32 devices in a mesh: batch: 2 (over x), row: 4 (over y, core), col: 4 (over z).
Axes of the slice: x: 2, y: 2, z: 4, core: 2. Of those that a mesh axis runs over, the one named last changes fastest.
Arguments:
- tokens_in: bfloat16 [4, 32, 32, 1152], P('batch', 'row', 'col'), may hold values from -6 to 6
- timesteps: int32 [4], replicated, may hold values from 0 to 999
- ada_weight: bfloat16 [2, 1152, 6912], P(None, 'batch'), may hold values from -0.1875 to 0.1875
- ada_bias: bfloat16 [2, 6912], P(None, 'batch'), may hold values from -3 to 3
- conv_taps: bfloat16 [2, 9, 1152], P(None, None, 'batch'), may hold values from -2 to 2
- qkv_weight: bfloat16 [2, 1152, 3456], P(None, 'batch'), may hold values from -0.1875 to 0.1875
- decay_weight: bfloat16 [2, 1152, 16], P(None, 'batch'), may hold values from -0.75 to 0.75
- decay_bias: bfloat16 [2, 16], P(None, 'batch'), may hold values from 1 to 5
- proj_weight: bfloat16 [2, 1152, 1152], P(None, 'batch'), may hold values from -0.1875 to 0.1875
- expand_weight: bfloat16 [2, 1152, 4608], P(None, 'batch'), may hold values from -0.1875 to 0.1875
- shrink_weight: bfloat16 [2, 4608, 1152], P(None, 'batch'), may hold values from -0.09375 to 0.09375
- cotangent: bfloat16 [4, 32, 32, 1152], P('batch', 'row', 'col'), may hold values from -6 to 6
Outputs:
- block_out: bfloat16 [4, 32, 32, 1152], P('batch', 'row', 'col')
- grad_tokens: bfloat16 [4, 32, 32, 1152], P('batch', 'row', 'col')
- grad_ada_weight: float32 [2, 1152, 6912], P(None, 'batch')
- grad_ada_bias: float32 [2, 6912], P(None, 'batch')
- grad_conv_taps: float32 [2, 9, 1152], P(None, None, 'batch')
- grad_qkv_weight: float32 [2, 1152, 3456], P(None, 'batch')
- grad_decay_weight: float32 [2, 1152, 16], P(None, 'batch')
- grad_decay_bias: float32 [2, 16], P(None, 'batch')
- grad_proj_weight: float32 [2, 1152, 1152], P(None, 'batch')
- grad_expand_weight: float32 [2, 1152, 4608], P(None, 'batch')
- grad_shrink_weight: float32 [2, 4608, 1152], P(None, 'batch')
The draws below stay inside these ranges and needn't reach their ends.
All inputs are finite; a program needn't handle non-finite values.
Results may differ from the reference program's by a relative error of at most 0.025.
The reference program's roundings to bfloat16 on the way count: a program that leaves them out, or rounds other values in their place, can miss the bound.
Values may be sent and summed in bfloat16 or wider, within the bound.
No kernel may reach another device: no remote copies, remote signals or barrier semaphores. Data moves between devices by JAX's collectives and lax.ppermute only.
A program may use at most 576 MiB of HBM per device.

```python
import jax
import jax.numpy as jnp
from jax import lax

D = 1152
H = 16
HD = 72
FF = 4608
GRID = 32
LAYERS = 2
NSTEPS = 1000
ITEMS = 4


def draw_timesteps(key, part):
    key = jax.random.fold_in(key, 7)
    first, second, third, fourth = jax.random.split(key, 4)
    early = jnp.minimum(jax.random.randint(first, (ITEMS,), 0, NSTEPS), jax.random.randint(second, (ITEMS,), 0, NSTEPS))
    early = jnp.minimum(early, jax.random.randint(third, (ITEMS,), 0, NSTEPS))
    order = jax.random.permutation(fourth, ITEMS)
    early = jnp.where(order == 0, NSTEPS - 1, early)
    return jnp.where(order == 1, 0, early).astype(jnp.int32)


def level_of(key, extent, pieces, low, top_value):
    gain = 1.0
    for dim, shards_of in pieces:
        heights = jax.random.uniform(jax.random.fold_in(jax.random.fold_in(key, 6), dim), (shards_of,), jnp.float32, low / len(pieces), top_value / len(pieces))
        gain = gain * jnp.repeat(jnp.exp(heights), extent[dim] // shards_of).reshape((-1,) + (1,) * (len(extent) - 1 - dim))
    return gain


def normal_values(stream_key, shape, deviation, reach, pieces=(), kind=jnp.bfloat16):
    entries = deviation * jax.random.normal(stream_key, shape, jnp.float32)
    if pieces:
        entries = entries * level_of(stream_key, shape, pieces, -0.22, 0.18)
    return jnp.clip(entries, -reach, reach).astype(kind)


def setup_inputs(seed: int = 0) -> dict:
    seeds = jax.random.split(jax.random.key(seed), 13)
    tokens_in = normal_values(seeds[0], (ITEMS, GRID, GRID, D), 1.0, 6.0, ((0, 2), (1, 4), (2, 4)))
    timesteps = draw_timesteps(jax.random.fold_in(seeds[12], 71), 0)
    ada_weight = normal_values(seeds[2], (LAYERS, D, 6 * D), D ** -0.5, 0.1875, ((1, 2),))
    ada_bias = normal_values(seeds[3], (LAYERS, 6 * D), 0.5, 3.0, ((1, 2),))
    conv_taps = normal_values(seeds[4], (LAYERS, 9, D), 9 ** -0.5, 2.0, ((2, 2),))
    qkv_weight = normal_values(seeds[5], (LAYERS, D, 3 * D), D ** -0.5, 0.1875, ((1, 2),))
    decay_weight = normal_values(seeds[6], (LAYERS, D, H), (D // 16) ** -0.5, 0.75, ((1, 2),))
    decay_bias = jnp.clip(1.0 + 4.0 * jax.random.uniform(seeds[7], (LAYERS, H), jnp.float32) ** level_of(seeds[7], (LAYERS, H), ((1, 2),), -0.2, 0.2), 1.0, 5.0).astype(jnp.bfloat16)
    proj_weight = normal_values(seeds[8], (LAYERS, D, D), D ** -0.5, 0.1875, ((1, 2),))
    expand_weight = normal_values(seeds[9], (LAYERS, D, FF), D ** -0.5, 0.1875, ((1, 2),))
    shrink_weight = normal_values(seeds[10], (LAYERS, FF, D), FF ** -0.5, 0.09375, ((1, 2),))
    cotangent = normal_values(seeds[11], (ITEMS, GRID, GRID, D), 1.0, 6.0, ((0, 2), (1, 4), (2, 4)))
    return dict(tokens_in=tokens_in, timesteps=timesteps, ada_weight=ada_weight, ada_bias=ada_bias, conv_taps=conv_taps, qkv_weight=qkv_weight, decay_weight=decay_weight, decay_bias=decay_bias, proj_weight=proj_weight, expand_weight=expand_weight, shrink_weight=shrink_weight, cotangent=cotangent)


EPS = 1e-06
ACCURATE = lax.Precision.HIGHEST

@jax.custom_vjp
def low(v):
    return lax.optimization_barrier(v.astype(jnp.bfloat16)).astype(jnp.float32)

@jax.custom_vjp
def low_back(v):
    return v

def low_keep(v):
    return (low(v), None)

def low_pass(kept, grad):
    return (grad,)

def back_keep(v):
    return (v, None)

def back_low(kept, grad):
    return (low(grad),)
low.defvjp(low_keep, low_pass)
low_back.defvjp(back_keep, back_low)

def embed_steps(steps):
    half = D // 2
    freqs = jnp.exp(-jnp.log(10000.0) * jnp.arange(half, dtype=jnp.float32) / half)
    angles = steps.astype(jnp.float32)[:, None] * freqs[None, :]
    return jnp.concatenate([jnp.cos(angles), jnp.sin(angles)], axis=1)

def layer_norm(values):
    center = values - lax.optimization_barrier(jnp.mean(values, axis=-1, keepdims=True))
    spread = lax.optimization_barrier(jnp.mean(center * center, axis=-1, keepdims=True))
    return center * lax.rsqrt(spread + EPS)

def recur(queries, keys_in, values_in, logdecay):
    scale = HD ** (-0.5)
    cumul = jnp.cumsum(logdecay, axis=1)
    trans = jnp.transpose(cumul, (0, 2, 1))
    gap = trans[:, :, :, None] - trans[:, :, None, :]
    length = logdecay.shape[1]
    lower = jnp.arange(length)[:, None] >= jnp.arange(length)[None, :]
    weights = jnp.where(lower, jnp.exp(jnp.minimum(gap, 0.0)), 0.0)
    scores = jnp.einsum('rthd,rshd->rhts', queries, keys_in, precision=ACCURATE) * scale
    return jnp.einsum('rhts,rshe->rthe', scores * weights, values_in, precision=ACCURATE)

def block(tokens, cond, weights, layer):
    ada_weight, ada_bias, conv_taps, qkv_weight, decay_weight, decay_bias, proj_weight, expand_weight, shrink_weight = weights
    rows, cols = (tokens.shape[0], tokens.shape[1])
    modulation = jnp.dot(low(jax.nn.silu(cond)), ada_weight, precision=ACCURATE) + ada_bias
    parts = modulation.reshape(6, D)
    hidden = low(layer_norm(tokens) * (1.0 + parts[1]) + parts[0])
    padded = jnp.pad(hidden, ((1, 1), (1, 1), (0, 0)))
    convolved = jnp.zeros((rows, cols, D), jnp.float32)
    for row_tap in range(3):
        for col_tap in range(3):
            convolved = convolved + conv_taps[3 * row_tap + col_tap] * padded[row_tap:row_tap + rows, col_tap:col_tap + cols]
    convolved = low_back(convolved)
    mixed = low(jax.nn.silu(convolved)).reshape(-1, D)
    project = low_back(jnp.dot(mixed, qkv_weight, precision=ACCURATE))
    logit = low_back(jnp.dot(mixed, decay_weight, precision=ACCURATE) + decay_bias[None, :])
    logdecay = jax.nn.log_sigmoid(logit).reshape(rows, cols, H)
    heads = project.reshape(rows, cols, 3, H, HD)
    queries, keys_in, values_in = (heads[:, :, 0], heads[:, :, 1], heads[:, :, 2])
    if layer % 2 == 1:
        queries, keys_in = (jnp.swapaxes(queries, 0, 1), jnp.swapaxes(keys_in, 0, 1))
        values_in, logdecay = (jnp.swapaxes(values_in, 0, 1), jnp.swapaxes(logdecay, 0, 1))
    attend = recur(queries, keys_in, values_in, logdecay)
    if layer % 2 == 1:
        attend = jnp.swapaxes(attend, 0, 1)
    attend = low(attend.reshape(-1, D))
    branch = low_back(jnp.dot(attend, proj_weight, precision=ACCURATE)).reshape(rows, cols, D)
    middle = tokens + parts[2] * branch
    second = low(layer_norm(middle) * (1.0 + parts[4]) + parts[3]).reshape(-1, D)
    inner = low_back(jnp.dot(second, expand_weight, precision=ACCURATE))
    active = low(jax.nn.gelu(inner, approximate=True))
    outer = low_back(jnp.dot(active, shrink_weight, precision=ACCURATE)).reshape(rows, cols, D)
    return middle + parts[5] * outer

def reference(tokens_in, timesteps, ada_weight, ada_bias, conv_taps, qkv_weight, decay_weight, decay_bias, proj_weight, expand_weight, shrink_weight, cotangent):
    weights = tuple((w.astype(jnp.float32) for w in (ada_weight, ada_bias, conv_taps, qkv_weight, decay_weight, decay_bias, proj_weight, expand_weight, shrink_weight)))
    cond = embed_steps(timesteps)

    def run(tokens, params):

        def one_item(pair):
            item, item_cond = pair
            for layer in range(LAYERS):
                item = block(item, item_cond, tuple((w[layer] for w in params)), layer)
            return item
        return lax.map(jax.checkpoint(one_item), (tokens, cond))
    result, pullback = jax.vjp(run, tokens_in.astype(jnp.float32), weights)
    delta_tokens, delta_weights = pullback(cotangent.astype(jnp.float32))
    return (result.astype(jnp.bfloat16), delta_tokens.astype(jnp.bfloat16), delta_weights[0], delta_weights[1], delta_weights[2], delta_weights[3], delta_weights[4], delta_weights[5], delta_weights[6], delta_weights[7], delta_weights[8])
```

```python
import jax
import jax.numpy as jnp
from jax import lax
from jax.experimental import pallas as pl
from jax.experimental.pallas import tpu as pltpu
from jax.sharding import PartitionSpec as P

D = 1152
H = 16
HD = 72
LAYERS = 2
EPS = 1e-06
ACCURATE = lax.Precision.HIGHEST
FLOAT = jnp.float32
BFLOAT = jnp.bfloat16
LANES = 128
VMEM_LIMIT = 48 * 1024 * 1024
GRID_AXES = ("row", "col")


def params():
    return pltpu.CompilerParams(vmem_limit_bytes=VMEM_LIMIT)


def padded_width(width):
    return -(-width // LANES) * LANES


def swap(value, axis="batch", bit=1):
    count = lax.axis_size(axis)
    return lax.ppermute(value, axis, [(i, i ^ bit) for i in range(count)])


def gather_items(own):
    if lax.axis_size("batch") == 2:
        return jnp.concatenate([own, swap(own)], axis=0)
    return lax.all_gather(own, "batch", axis=0, tiled=True)


def reduce_items(partial):
    if lax.axis_size("batch") == 2:
        items = partial.shape[0] // 2
        return partial[:items] + swap(partial[items:].astype(BFLOAT)).astype(FLOAT)
    return lax.psum_scatter(partial, "batch", scatter_dimension=0, tiled=True)


def lines_out(values, axis):
    count, place = lax.axis_size(axis), lax.axis_index(axis)
    groups = values.reshape((count, -1) + values.shape[1:])
    blocks = []
    for k in range(count):
        block = lax.dynamic_index_in_dim(groups, place ^ k, 0, keepdims=False)
        blocks.append(block if k == 0 else swap(block, axis, k))
    return blocks


def lines_back(blocks, axis):
    count, place = lax.axis_size(axis), lax.axis_index(axis)
    received = [blocks[0]] + [swap(blocks[k], axis, k) for k in range(1, count)]
    stacked = jnp.stack(received)
    return jnp.concatenate(
        [lax.dynamic_index_in_dim(stacked, place ^ j, 0, keepdims=False) for j in range(count)]
    )


def halo(cells):
    rows, cols = lax.axis_size("row"), lax.axis_size("col")
    down = [(i, i + 1) for i in range(rows - 1)]
    up = [(i + 1, i) for i in range(rows - 1)]
    top = lax.ppermute(cells[:, -1], "row", down)
    bottom = lax.ppermute(cells[:, 0], "row", up)
    edge = lambda at: jnp.concatenate([top[:, at][:, None], cells[:, :, at], bottom[:, at][:, None]], 1)
    left = lax.ppermute(edge(-1), "col", [(i, i + 1) for i in range(cols - 1)])
    right = lax.ppermute(edge(0), "col", [(i + 1, i) for i in range(cols - 1)])
    return top, bottom, left, right


def beside(cells, top, bottom, left, right, item):
    count = cells.shape[1]
    lefts, rights = left[item].astype(FLOAT), right[item].astype(FLOAT)
    width = cells.shape[2]
    at = lax.broadcasted_iota(jnp.int32, (width, cells.shape[3]), 0)
    rows = []
    for row in range(count + 2):
        if row == 0:
            here = top[item]
        elif row == count + 1:
            here = bottom[item]
        else:
            here = cells[item, row - 1]
        here = here.astype(FLOAT)
        before = jnp.where(at == 0, lefts[row : row + 1], pltpu.roll(here, 1, 0))
        after = jnp.where(at == width - 1, rights[row : row + 1], pltpu.roll(here, width - 1, 0))
        rows.append((before, here, after))
    return rows


def conv_forward_kernel(cells, top, bottom, left, right, taps, convolved, mixed):
    weights = taps[...].astype(FLOAT)
    for item in range(cells.shape[0]):
        rows = beside(cells, top, bottom, left, right, item)
        for row in range(cells.shape[1]):
            total = jnp.zeros(rows[0][1].shape, FLOAT)
            for a in range(3):
                for b in range(3):
                    total += weights[3 * a + b : 3 * a + b + 1] * rows[row + a][b]
            convolved[item, row] = total
            mixed[item, row] = (total * jax.nn.sigmoid(total)).astype(BFLOAT)


def conv_backward_kernel(
    cells, top, bottom, left, right, delta, dtop, dbottom, dleft, dright, taps, hidden, grads
):
    weights = taps[...].astype(FLOAT)
    sums = [jnp.zeros((cells.shape[2], cells.shape[3]), FLOAT) for _ in range(9)]
    for item in range(cells.shape[0]):
        rows = beside(cells, top, bottom, left, right, item)
        for row in range(cells.shape[1]):
            here = delta[item, row].astype(FLOAT)
            for a in range(3):
                for b in range(3):
                    sums[3 * a + b] += rows[row + a][b] * here
        rows = beside(delta, dtop, dbottom, dleft, dright, item)
        for row in range(cells.shape[1]):
            total = jnp.zeros(rows[0][1].shape, FLOAT)
            for a in range(3):
                for b in range(3):
                    total += weights[3 * a + b : 3 * a + b + 1] * rows[row + 2 - a][2 - b]
            hidden[item, row] = total
    for tap in range(9):
        grads[tap : tap + 1] = jnp.sum(sums[tap], axis=0, keepdims=True)


def conv_specs(items, rows, cols, block):
    cells = pl.BlockSpec((items, rows, cols, block), lambda i: (0, 0, 0, i))
    flat = pl.BlockSpec((items, cols, block), lambda i: (0, 0, i))
    side = pl.BlockSpec((items, rows + 2, block), lambda i: (0, 0, i))
    taps = pl.BlockSpec((9, block), lambda i: (0, i))
    return [cells, flat, flat, side, side], taps


def conv_forward(cells, sides, taps):
    items, rows, cols, width = cells.shape
    block = 3 * LANES
    specs, tap_spec = conv_specs(items, rows, cols, block)
    return pl.pallas_call(
        conv_forward_kernel,
        grid=(width // block,),
        in_specs=specs + [tap_spec],
        out_specs=[specs[0], specs[0]],
        out_shape=[
            jax.ShapeDtypeStruct(cells.shape, FLOAT),
            jax.ShapeDtypeStruct(cells.shape, BFLOAT),
        ],
        compiler_params=params(),
    )(cells, *sides, taps)


def conv_backward(cells, sides, delta, delta_sides, taps):
    items, rows, cols, width = cells.shape
    block = 3 * LANES
    specs, tap_spec = conv_specs(items, rows, cols, block)
    return pl.pallas_call(
        conv_backward_kernel,
        grid=(width // block,),
        in_specs=specs + specs + [tap_spec],
        out_specs=[specs[0], tap_spec],
        out_shape=[
            jax.ShapeDtypeStruct(cells.shape, FLOAT),
            jax.ShapeDtypeStruct((9, width), FLOAT),
        ],
        compiler_params=params(),
    )(cells, *sides, delta, *delta_sides, taps)


def scan_mask(place, rows, cols, along_cols, blocks):
    cells = rows * cols
    shape = (blocks * cells, blocks * cells)

    def line_and_position(index):
        block = index // cells
        inside = index - block * cells
        row = inside // cols
        col = inside - row * cols
        source = place ^ block
        if along_cols:
            return row, source * cols + col
        return col, source * rows + row

    line_t, at_t = line_and_position(lax.broadcasted_iota(jnp.int32, shape, 0))
    line_s, at_s = line_and_position(lax.broadcasted_iota(jnp.int32, shape, 1))
    return (line_t == line_s) & (at_s <= at_t)


def dot(left, right, contract=((1,), (0,)), precision=None):
    return lax.dot_general(
        left, right, (contract, ((), ())), precision=precision, preferred_element_type=FLOAT
    )


class Scan:
    def __init__(self, parts, mask, width):
        self.width = width
        self.padded = padded_width(width + 3 * (width // HD))
        self.heads = width // HD
        joined = jnp.concatenate([part[0] for part in parts], axis=0)
        size = self.padded
        self.queries = joined[:, :size]
        self.keys = joined[:, size : 2 * size]
        self.values = joined[:, 2 * size :]
        self.start = width - width // LANES * LANES
        self.block = width // LANES * LANES
        extra = self.queries[:, self.block : self.block + LANES].astype(FLOAT)
        logit = (
            extra
            + pltpu.roll(extra, LANES - self.heads, 1)
            + pltpu.roll(extra, LANES - 2 * self.heads, 1)
        )
        self.lane = lax.broadcasted_iota(jnp.int32, extra.shape, 1)
        self.is_logit = (self.lane >= self.start) & (self.lane < self.start + self.heads)
        self.logit = jnp.where(self.is_logit, logit, 0.0)
        small = jnp.exp(-jnp.abs(self.logit))
        logdecay = jnp.where(self.is_logit, jnp.minimum(self.logit, 0.0) - jnp.log(1.0 + small), 0.0)
        self.lower = jnp.where(mask, 1.0, 0.0).astype(FLOAT)
        self.mask = mask
        self.cumul = dot(self.lower, logdecay, precision=ACCURATE)
        self.cumul_rows = jnp.transpose(self.cumul)
        self.feature = lax.broadcasted_iota(jnp.int32, (1, size), 1)

    def of_head(self, head, array):
        inside = (self.feature >= head * HD) & (self.feature < head * HD + HD)
        return jnp.where(inside, array, jnp.zeros_like(array))

    def weights(self, head):
        at = self.start + head
        gap = self.cumul[:, at : at + 1] - self.cumul_rows[at : at + 1, :]
        return jnp.where(self.mask, jnp.exp(jnp.minimum(gap, 0.0)), 0.0)


SCALE = HD ** (-0.5)


def scan_forward_kernel(place, *refs, rows, cols, along_cols, width):
    count = len(refs) // 2
    parts, outs = refs[:count], refs[count:]
    mask = scan_mask(place[0], rows, cols, along_cols, count)
    scan = Scan(parts, mask, width)
    total = jnp.zeros(scan.queries.shape, FLOAT)
    for head in range(scan.heads):
        scores = dot(scan.of_head(head, scan.queries), scan.keys, ((1,), (1,))) * SCALE
        scores = (scores * scan.weights(head)).astype(BFLOAT)
        total += dot(scores, scan.of_head(head, scan.values))
    cells = rows * cols
    low = total.astype(BFLOAT)
    for k in range(count):
        outs[k][0] = low[k * cells : (k + 1) * cells, :width]


def scan_backward_kernel(place, *refs, rows, cols, along_cols, width):
    count = len(refs) // 3
    parts, deltas, outs = refs[:count], refs[count : 2 * count], refs[2 * count :]
    mask = scan_mask(place[0], rows, cols, along_cols, count)
    scan = Scan(parts, mask, width)
    joined = jnp.concatenate([part[0] for part in deltas], axis=0)
    short = scan.padded - width
    if short:
        joined = jnp.concatenate([joined, jnp.zeros((joined.shape[0], short), BFLOAT)], axis=1)
    shape = scan.queries.shape
    delta_query = jnp.zeros(shape, FLOAT)
    delta_key = jnp.zeros(shape, FLOAT)
    delta_value = jnp.zeros(shape, FLOAT)
    gap_rows = jnp.zeros(scan.lane.shape, FLOAT)
    gap_cols = jnp.zeros(scan.cumul_rows.shape, FLOAT)
    place_row = lax.broadcasted_iota(jnp.int32, gap_cols.shape, 0)
    for head in range(scan.heads):
        query = scan.of_head(head, scan.queries)
        delta = scan.of_head(head, joined)
        weights = scan.weights(head)
        scores = dot(query, scan.keys, ((1,), (1,))) * SCALE * weights
        delta_scores = dot(delta, scan.values, ((1,), (1,)))
        gap = delta_scores * scores
        at = scan.start + head
        gap_rows += jnp.where(scan.lane == at, jnp.sum(gap, axis=1, keepdims=True), 0.0)
        gap_cols += jnp.where(place_row == at, jnp.sum(gap, axis=0, keepdims=True), 0.0)
        inner = (delta_scores * weights * SCALE).astype(BFLOAT)
        delta_query += dot(inner, scan.of_head(head, scan.keys))
        delta_key += dot(inner, query, ((0,), (0,)))
        delta_value += dot(scores.astype(BFLOAT), delta, ((0,), (0,)))
    delta_cumul = gap_rows - jnp.transpose(gap_cols)
    delta_decay = dot(scan.lower, delta_cumul, ((0,), (0,)), ACCURATE)
    small = jnp.exp(-jnp.abs(scan.logit))
    keep = jnp.where(scan.logit >= 0.0, small, 1.0) / (1.0 + small)
    delta_logit = delta_decay * keep
    block = scan.block
    mixed = jnp.where(scan.is_logit, delta_logit, delta_query[:, block : block + LANES])
    pieces = [delta_query[:, :block]] if block else []
    pieces.append(mixed)
    if block + LANES < scan.padded:
        pieces.append(delta_query[:, block + LANES :])
    whole = jnp.concatenate(pieces + [delta_key, delta_value], axis=1).astype(BFLOAT)
    cells = rows * cols
    for k in range(count):
        outs[k][0] = whole[k * cells : (k + 1) * cells]


def scan_call(kernel, place, inputs, out_width, rows, cols, along_cols, width):
    count = lax.axis_size("col") if along_cols else lax.axis_size("row")
    items, cells = inputs[0].shape[:2]
    spec = lambda last: pl.BlockSpec((1, cells, last), lambda i, place: (i, 0, 0))

    def body(*refs):
        kernel(*refs, rows=rows, cols=cols, along_cols=along_cols, width=width)

    return pl.pallas_call(
        body,
        grid_spec=pltpu.PrefetchScalarGridSpec(
            num_scalar_prefetch=1,
            grid=(items,),
            in_specs=[spec(v.shape[2]) for v in inputs],
            out_specs=[spec(out_width)] * count,
        ),
        out_shape=[jax.ShapeDtypeStruct((items, cells, out_width), BFLOAT)] * count,
        compiler_params=params(),
    )(place.reshape(1).astype(jnp.int32), *inputs)


def pick(values, index):
    chosen = values[0]
    for k in range(1, len(values)):
        chosen = jnp.where(index == k, values[k], chosen)
    return chosen


def fetch_columns(pieces):
    count, place = lax.axis_size("batch"), lax.axis_index("batch")
    if count != 2:
        stacked = jnp.stack(pieces)
        return lax.all_to_all(stacked, "batch", 0, 0).reshape((-1,) + pieces[0].shape[1:])
    own, other = pick(pieces, place), pick(pieces, 1 - place)
    rows = own.shape[0]
    half = rows // 2
    core = lax.axis_index("row") % 2
    first = swap(lax.dynamic_slice_in_dim(other, core * half, half, 0))
    second = swap(first, "row", 1)
    whole = jnp.zeros((2 * rows,) + own.shape[1:], own.dtype)
    whole = lax.dynamic_update_slice_in_dim(whole, own, place * rows, 0)
    base = (1 - place) * rows
    whole = lax.dynamic_update_slice_in_dim(whole, first, base + core * half, 0)
    return lax.dynamic_update_slice_in_dim(whole, second, base + (1 - core) * half, 0)


def head_columns(qkv, decay, group, width):
    size = padded_width(width + 3 * (width // HD))
    heads = width // HD
    parts = []
    for j in range(3):
        piece = qkv[:, j * D + group * width : j * D + (group + 1) * width]
        filled = width
        parts.append(piece)
        if j == 0:
            parts.append(decay[:, group * heads : (group + 1) * heads])
            filled += heads
        if size > filled:
            parts.append(jnp.zeros((qkv.shape[0], size - filled), qkv.dtype))
    return jnp.concatenate(parts, axis=1)


def normalize(values):
    center = values - jnp.mean(values, axis=-1, keepdims=True)
    inverse = lax.rsqrt(jnp.mean(center * center, axis=-1, keepdims=True) + EPS)
    return center * inverse, inverse


def normalize_back(delta, normal, inverse):
    first = jnp.mean(delta, axis=-1, keepdims=True)
    second = jnp.mean(delta * normal, axis=-1, keepdims=True)
    return inverse * (delta - first - normal * second)


def embed_steps(steps):
    half = D // 2
    freqs = jnp.exp(-jnp.log(10000.0) * jnp.arange(half, dtype=FLOAT) / half)
    angles = steps.astype(FLOAT)[:, None] * freqs[None, :]
    return jnp.concatenate([jnp.cos(angles), jnp.sin(angles)], axis=1)


GELU_A = 0.7978845608028654
GELU_B = 0.044715


def gelu(z):
    return 0.5 * z * (1.0 + jnp.tanh(GELU_A * (z + GELU_B * z * z * z)))


def gelu_slope(z):
    t = jnp.tanh(GELU_A * (z + GELU_B * z * z * z))
    return 0.5 * (1.0 + t) + 0.5 * z * (1.0 - t * t) * GELU_A * (1.0 + 3.0 * GELU_B * z * z)


def matmul(left, right):
    return lax.dot_general(left, right, (((2,), (0,)), ((), ())), preferred_element_type=FLOAT)


def matmul_back(left, right):
    return lax.dot_general(left, right, (((2,), (1,)), ((), ())), preferred_element_type=FLOAT)


def weight_grad(left, right):
    return lax.dot_general(
        left, right, (((0, 1), (0, 1)), ((), ())), preferred_element_type=FLOAT
    )


def forward_layer(tokens, modulation, weights, layer, tile):
    taps, qkv, decay_bias, proj, expand, shrink = weights
    rows, cols = tile
    items, cells = tokens.shape[:2]
    width = proj.shape[0]
    heads = width // HD
    size = padded_width(width + 3 * heads)
    axis = "col" if layer % 2 == 0 else "row"
    mod = [modulation[:, k][:, None] for k in range(6)]
    normal, inverse = normalize(tokens)
    hidden = (normal * (1.0 + mod[1]) + mod[0]).astype(BFLOAT).reshape(items, rows, cols, D)
    sides = halo(hidden)
    convolved, mixed = conv_forward(hidden, sides, taps)
    mixed = gather_items(mixed.reshape(items, cells, D))
    project = matmul(mixed, qkv)
    logit = project[:, :, width : width + heads] + decay_bias.astype(FLOAT)
    high = logit.astype(BFLOAT)
    rest = logit - high.astype(FLOAT)
    middle_part = rest.astype(BFLOAT)
    low = (rest - middle_part.astype(FLOAT)).astype(BFLOAT)
    project = project.astype(BFLOAT)
    project = jnp.concatenate(
        [project[:, :, :width], high, middle_part, low, project[:, :, width + 3 * heads :]], axis=2
    )
    parts = lines_out(project, axis)
    place = lax.axis_index(axis)
    attends = scan_call(
        scan_forward_kernel, place, parts, width, rows, cols, layer % 2 == 0, width
    )
    attend = lines_back(attends, axis)
    branch = reduce_items(matmul(attend, proj))
    middle = tokens + mod[2] * branch
    normal2, inverse2 = normalize(middle)
    second = gather_items((normal2 * (1.0 + mod[4]) + mod[3]).astype(BFLOAT))
    inner = matmul(second, expand)
    active = gelu(inner).astype(BFLOAT)
    outer = reduce_items(matmul(active, shrink))
    result = middle + mod[5] * outer
    saved = (
        normal, inverse, hidden, sides, convolved, mixed, parts, attend, branch,
        normal2, inverse2, second, inner, active, outer,
    )
    return result, saved


def backward_layer(delta, saved, modulation, weights, layer, tile):
    taps, qkv, decay_bias, proj, expand, shrink = weights
    (
        normal, inverse, hidden, sides, convolved, mixed, parts, attend, branch,
        normal2, inverse2, second, inner, active, outer,
    ) = saved
    rows, cols = tile
    items, cells = delta.shape[:2]
    width = proj.shape[0]
    heads = width // HD
    size = padded_width(width + 3 * heads)
    axis = "col" if layer % 2 == 0 else "row"
    mod = [modulation[:, k][:, None] for k in range(6)]
    over = lambda v: jnp.sum(v, axis=1)
    delta_gate2 = over(delta * outer)
    outer_low = gather_items((mod[5] * delta).astype(BFLOAT))
    grad_shrink = weight_grad(active, outer_low)
    inner_low = (matmul_back(outer_low, shrink) * gelu_slope(inner)).astype(BFLOAT)
    grad_expand = weight_grad(second, inner_low)
    delta_second = reduce_items(matmul_back(inner_low, expand))
    delta_shift2 = over(delta_second)
    delta_scale2 = over(delta_second * normal2)
    delta_middle = delta + normalize_back(delta_second * (1.0 + mod[4]), normal2, inverse2)
    delta_gate1 = over(delta_middle * branch)
    branch_low = gather_items((mod[2] * delta_middle).astype(BFLOAT))
    grad_proj = weight_grad(attend, branch_low)
    delta_attend = matmul_back(branch_low, proj).astype(BFLOAT)
    delta_parts = lines_out(delta_attend, axis)
    place = lax.axis_index(axis)
    projects = scan_call(
        scan_backward_kernel, place, list(parts) + delta_parts, 3 * size, rows, cols,
        layer % 2 == 0, width,
    )
    delta_project = lines_back(projects, axis)
    grad_qkv = weight_grad(mixed, delta_project)
    grad_decay_bias = jnp.sum(delta_project[:, :, width : width + heads].astype(FLOAT), axis=(0, 1))
    delta_mixed = reduce_items(matmul_back(delta_project, qkv)).reshape(convolved.shape)
    gate = jax.nn.sigmoid(convolved)
    delta_conv = (delta_mixed * gate * (1.0 + convolved * (1.0 - gate))).astype(BFLOAT)
    delta_sides = halo(delta_conv)
    delta_hidden, grad_taps = conv_backward(hidden, sides, delta_conv, delta_sides, taps)
    delta_hidden = delta_hidden.reshape(items, cells, D)
    delta_shift1 = over(delta_hidden)
    delta_scale1 = over(delta_hidden * normal)
    delta_tokens = delta_middle + normalize_back(delta_hidden * (1.0 + mod[1]), normal, inverse)
    delta_mod = jnp.stack(
        [delta_shift1, delta_scale1, delta_gate1, delta_shift2, delta_scale2, delta_gate2], axis=1
    )
    return delta_tokens, (grad_shrink, grad_expand, grad_proj, grad_qkv), (
        delta_mod, grad_taps, grad_decay_bias,
    )


def sum_rows_here(grad):
    return lax.psum(grad.astype(BFLOAT), GRID_AXES).astype(FLOAT)


def sum_columns(grad):
    count = lax.axis_size("batch")
    low = grad.astype(BFLOAT).reshape((count, -1, grad.shape[1]))
    shares = lax.axis_size("row") * lax.axis_size("col")
    if count == 2 and low.shape[1] % shares == 0:
        share = lax.psum_scatter(low, GRID_AXES, scatter_dimension=1, tiled=True)
        place = lax.axis_index("batch")
        own = lax.dynamic_index_in_dim(share, place, 0, keepdims=False)
        other = swap(lax.dynamic_index_in_dim(share, 1 - place, 0, keepdims=False))
        both = jnp.stack([jnp.where(place == 0, own, other), jnp.where(place == 0, other, own)])
        return lax.all_gather(both, GRID_AXES, axis=1, tiled=True)
    total = lax.psum(low, GRID_AXES)
    return lax.all_to_all(total, "batch", 0, 0)


def per_device(
    tokens_in, timesteps, ada_weight, ada_bias, conv_taps, qkv_weight, decay_weight, decay_bias,
    proj_weight, expand_weight, shrink_weight, cotangent,
):
    count, place = lax.axis_size("batch"), lax.axis_index("batch")
    items, rows, cols = tokens_in.shape[:3]
    tile = (rows, cols)
    rows_here = ada_weight.shape[1]
    width = proj_weight.shape[1]
    heads = width // HD
    size = padded_width(width + 3 * heads)
    cond = jax.nn.silu(embed_steps(timesteps)).astype(BFLOAT)
    cond_slice = lax.dynamic_slice_in_dim(cond, place * rows_here, rows_here, 1)
    order = [0] if count != 2 else None
    if count == 2:
        cond_first = jnp.where(
            place == 0, cond_slice, jnp.concatenate([cond_slice[items:], cond_slice[:items]])
        )
    else:
        cond_first = cond_slice
    biases = lax.all_gather(ada_bias, "batch", axis=1, tiled=True).astype(FLOAT)
    taps_all = lax.all_gather(conv_taps, "batch", axis=2, tiled=True)
    weights, modulations = [], []
    partial = jnp.stack(
        [
            jnp.dot(cond_first, ada_weight[layer], preferred_element_type=FLOAT)
            for layer in range(LAYERS)
        ],
        axis=1,
    )
    if count == 2:
        total = partial[:items] + swap(partial[items:])
    else:
        total = lax.psum_scatter(partial, "batch", scatter_dimension=0, tiled=True)
    for layer in range(LAYERS):
        modulations.append((total[:, layer] + biases[layer]).reshape(items, 6, D))
    for layer in range(LAYERS):
        qkv = fetch_columns(
            [head_columns(qkv_weight[layer], decay_weight[layer], g, width) for g in range(count)]
        )
        inner = expand_weight.shape[2] // count
        expand = fetch_columns(
            [expand_weight[layer][:, g * inner : (g + 1) * inner] for g in range(count)]
        )
        weights.append(
            (taps_all[layer], qkv, decay_bias[layer], proj_weight[layer], expand, shrink_weight[layer])
        )
    tokens = tokens_in.astype(FLOAT).reshape(items, rows * cols, D)
    stored = []
    for layer in range(LAYERS):
        tokens, saved = forward_layer(tokens, modulations[layer], weights[layer], layer, tile)
        stored.append(saved)
    block_out = tokens.astype(BFLOAT).reshape(tokens_in.shape)
    delta = cotangent.astype(FLOAT).reshape(tokens.shape)
    bigs, smalls = [None] * LAYERS, [None] * LAYERS
    for layer in reversed(range(LAYERS)):
        delta, big, small = backward_layer(
            delta, stored[layer], modulations[layer], weights[layer], layer, tile
        )
        grad_shrink, grad_expand, grad_proj, grad_qkv = big
        bigs[layer] = (
            sum_rows_here(grad_shrink),
            sum_columns(grad_expand),
            sum_rows_here(grad_proj),
            sum_columns(grad_qkv),
        )
        smalls[layer] = small
    grad_tokens = delta.astype(BFLOAT).reshape(tokens_in.shape)
    delta_mods, taps_grads, bias_grads = lax.psum(
        tuple(jnp.stack([smalls[layer][k] for layer in range(LAYERS)]) for k in range(3)), GRID_AXES
    )
    every_mod = gather_items(delta_mods.transpose(1, 0, 2, 3)).reshape(count * items, LAYERS, 6 * D)
    if count == 2:
        taps_every = taps_grads + swap(taps_grads)
    else:
        taps_every = lax.psum(taps_grads, "batch")
    grad_taps = lax.dynamic_slice_in_dim(taps_every, place * width, width, 2)
    grad_ada = jnp.zeros((LAYERS, rows_here, 6 * D), FLOAT)
    for item in range(count * items):
        grad_ada += (
            cond_first[item].astype(FLOAT)[None, :, None] * every_mod[item][:, None, :]
        )
    bias_width = ada_bias.shape[1]
    grad_ada_bias = lax.dynamic_slice_in_dim(
        jnp.sum(every_mod, axis=0), place * bias_width, bias_width, 1
    )
    stack = lambda k: jnp.stack([bigs[layer][k] for layer in range(LAYERS)])
    grad_shrink, grad_proj = stack(0), stack(2)
    expand_parts, qkv_parts = stack(1), stack(3)
    grad_expand = jnp.concatenate([expand_parts[:, g] for g in range(count)], 2).astype(FLOAT)
    grad_qkv = jnp.concatenate(
        [
            qkv_parts[:, g, :, j * size : j * size + width]
            for j in range(3)
            for g in range(count)
        ],
        axis=2,
    ).astype(FLOAT)
    grad_decay = jnp.concatenate(
        [qkv_parts[:, g, :, width : width + heads] for g in range(count)], axis=2
    ).astype(FLOAT)
    return (
        block_out,
        grad_tokens,
        grad_ada,
        grad_ada_bias,
        grad_taps,
        grad_qkv,
        grad_decay,
        bias_grads,
        grad_proj,
        grad_expand,
        grad_shrink,
    )


def solution(mesh):
    return jax.shard_map(
        per_device,
        mesh=mesh,
        in_specs=(
            P("batch", "row", "col", None),
            P(),
            P(None, "batch", None),
            P(None, "batch"),
            P(None, None, "batch"),
            P(None, "batch", None),
            P(None, "batch", None),
            P(None, "batch"),
            P(None, "batch", None),
            P(None, "batch", None),
            P(None, "batch", None),
            P("batch", "row", "col", None),
        ),
        out_specs=(
            P("batch", "row", "col", None),
            P("batch", "row", "col", None),
            P(None, "batch", None),
            P(None, "batch"),
            P(None, None, "batch"),
            P(None, "batch", None),
            P(None, "batch", None),
            P(None, "batch"),
            P(None, "batch", None),
            P(None, "batch", None),
            P(None, "batch", None),
        ),
        check_vma=False,
    )
```

```python
import jax
import jax.numpy as jnp
from jax import lax
from jax.experimental import pallas as pl
from jax.experimental.pallas import tpu as pltpu
from jax.sharding import PartitionSpec as P

D = 1152
H = 16
HD = 72
LAYERS = 2
EPS = 1e-06
ACCURATE = lax.Precision.HIGHEST
FLOAT = jnp.float32
BFLOAT = jnp.bfloat16
LANES = 128
VMEM_LIMIT = 48 * 1024 * 1024
GRID_AXES = ("row", "col")
SMALL = pl.CostEstimate(flops=1, bytes_accessed=1, transcendentals=0)


def params():
    return pltpu.CompilerParams(vmem_limit_bytes=VMEM_LIMIT)


def padded_width(width):
    return -(-width // LANES) * LANES


def swap(value, axis="batch", bit=1):
    count = lax.axis_size(axis)
    return lax.ppermute(value, axis, [(i, i ^ bit) for i in range(count)])


def gather_items(own):
    if lax.axis_size("batch") == 2:
        return jnp.concatenate([own, swap(own)], axis=0)
    return lax.all_gather(own, "batch", axis=0, tiled=True)


def gather_last(own):
    if lax.axis_size("batch") == 2:
        other = swap(own)
        first = lax.axis_index("batch") == 0
        return jnp.concatenate([jnp.where(first, own, other), jnp.where(first, other, own)], -1)
    return lax.all_gather(own, "batch", axis=own.ndim - 1, tiled=True)


def reduce_items(partial):
    if lax.axis_size("batch") == 2:
        items = partial.shape[0] // 2
        return partial[:items] + swap(partial[items:].astype(BFLOAT)).astype(FLOAT)
    return lax.psum_scatter(partial, "batch", scatter_dimension=0, tiled=True)


def lines_out(values, axis):
    count, place = lax.axis_size(axis), lax.axis_index(axis)
    groups = values.reshape((count, -1) + values.shape[1:])
    blocks = []
    for k in range(count):
        block = lax.dynamic_index_in_dim(groups, place ^ k, 0, keepdims=False)
        blocks.append(block if k == 0 else swap(block, axis, k))
    return blocks


def lines_back(blocks, axis):
    count, place = lax.axis_size(axis), lax.axis_index(axis)
    received = [blocks[0]] + [swap(blocks[k], axis, k) for k in range(1, count)]
    stacked = jnp.stack(received)
    return jnp.concatenate(
        [lax.dynamic_index_in_dim(stacked, place ^ j, 0, keepdims=False) for j in range(count)]
    )


def halo(cells):
    return halo_edges([cells[:, 0], cells[:, -1], cells[:, :, 0], cells[:, :, -1]])


def beside(cells, sides, item):
    top, bottom, left, right = sides
    count, width = cells.shape[1], cells.shape[2]
    lefts, rights = left[item].astype(FLOAT), right[item].astype(FLOAT)
    at = lax.broadcasted_iota(jnp.int32, (width, cells.shape[3]), 0)
    rows = []
    for row in range(count + 2):
        if row == 0:
            here = top[item]
        elif row == count + 1:
            here = bottom[item]
        else:
            here = cells[item, row - 1]
        here = here.astype(FLOAT)
        before = jnp.where(at == 0, lefts[row : row + 1], pltpu.roll(here, 1, 0))
        after = jnp.where(at == width - 1, rights[row : row + 1], pltpu.roll(here, width - 1, 0))
        rows.append((before, here, after))
    return rows


def conv_forward_kernel(cells, *refs):
    sides, (taps, convolved, mixed) = refs[:4], refs[4:]
    weights = taps[...].astype(FLOAT)
    for item in range(cells.shape[0]):
        rows = beside(cells, sides, item)
        for row in range(cells.shape[1]):
            total = jnp.zeros(rows[0][1].shape, FLOAT)
            for a in range(3):
                for b in range(3):
                    total += weights[3 * a + b : 3 * a + b + 1] * rows[row + a][b]
            convolved[item, row] = total
            mixed[item, row] = (total * jax.nn.sigmoid(total)).astype(BFLOAT)


def conv_backward_kernel(cells, *refs):
    sides, delta, delta_sides, (taps, hidden, grads) = refs[:4], refs[4], refs[5:9], refs[9:]
    weights = taps[...].astype(FLOAT)
    sums = [jnp.zeros((cells.shape[2], cells.shape[3]), FLOAT) for _ in range(9)]
    for item in range(cells.shape[0]):
        rows = beside(cells, sides, item)
        for row in range(cells.shape[1]):
            here = delta[item, row].astype(FLOAT)
            for a in range(3):
                for b in range(3):
                    sums[3 * a + b] += rows[row + a][b] * here
        rows = beside(delta, delta_sides, item)
        for row in range(cells.shape[1]):
            total = jnp.zeros(rows[0][1].shape, FLOAT)
            for a in range(3):
                for b in range(3):
                    total += weights[3 * a + b : 3 * a + b + 1] * rows[row + 2 - a][2 - b]
            hidden[item, row] = total
    for tap in range(9):
        grads[tap : tap + 1] = jnp.sum(sums[tap], axis=0, keepdims=True)


def conv_specs(items, rows, cols, block):
    cells = pl.BlockSpec((items, rows, cols, block), lambda i: (0, 0, 0, i))
    side = lambda size: pl.BlockSpec((items, size, block), lambda i: (0, 0, i))
    taps = pl.BlockSpec((9, block), lambda i: (0, i))
    return [cells] + [side(size) for size in (cols, cols, rows + 2, rows + 2)], taps


def conv_forward(cells, sides, taps):
    items, rows, cols, width = cells.shape
    block = 3 * LANES
    specs, tap_spec = conv_specs(items, rows, cols, block)
    return pl.pallas_call(
        conv_forward_kernel,
        grid=(width // block,),
        in_specs=specs + [tap_spec],
        out_specs=[specs[0], specs[0]],
        out_shape=[
            jax.ShapeDtypeStruct(cells.shape, FLOAT),
            jax.ShapeDtypeStruct(cells.shape, BFLOAT),
        ],
        cost_estimate=SMALL,
        compiler_params=params(),
    )(cells, *sides, taps)


def conv_backward(cells, sides, delta, delta_sides, taps):
    items, rows, cols, width = cells.shape
    block = 3 * LANES
    specs, tap_spec = conv_specs(items, rows, cols, block)
    return pl.pallas_call(
        conv_backward_kernel,
        grid=(width // block,),
        in_specs=specs + specs + [tap_spec],
        out_specs=[specs[0], tap_spec],
        out_shape=[
            jax.ShapeDtypeStruct(cells.shape, FLOAT),
            jax.ShapeDtypeStruct((9, width), FLOAT),
        ],
        cost_estimate=SMALL,
        compiler_params=params(),
    )(cells, *sides, delta, *delta_sides, taps)


def scan_mask(place, rows, cols, along_cols, blocks):
    cells = rows * cols
    shape = (blocks * cells, blocks * cells)

    def line_and_position(index):
        block = index // cells
        inside = index - block * cells
        row = inside // cols
        col = inside - row * cols
        source = place ^ block
        if along_cols:
            return row, source * cols + col
        return col, source * rows + row

    line_t, at_t = line_and_position(lax.broadcasted_iota(jnp.int32, shape, 0))
    line_s, at_s = line_and_position(lax.broadcasted_iota(jnp.int32, shape, 1))
    return (line_t == line_s) & (at_s <= at_t)


def dot(left, right, contract=((1,), (0,)), precision=None):
    return lax.dot_general(
        left, right, (contract, ((), ())), precision=precision, preferred_element_type=FLOAT
    )


class Scan:
    def __init__(self, parts, mask, width):
        self.width = width
        self.padded = padded_width(width + 3 * (width // HD))
        self.heads = width // HD
        joined = jnp.concatenate([part[0] for part in parts], axis=0)
        size = self.padded
        self.queries = joined[:, :size]
        self.keys = joined[:, size : 2 * size]
        self.values = joined[:, 2 * size :]
        self.start = width - width // LANES * LANES
        self.block = width // LANES * LANES
        extra = self.queries[:, self.block : self.block + LANES].astype(FLOAT)
        logit = (
            extra
            + pltpu.roll(extra, LANES - self.heads, 1)
            + pltpu.roll(extra, LANES - 2 * self.heads, 1)
        )
        self.lane = lax.broadcasted_iota(jnp.int32, extra.shape, 1)
        self.is_logit = (self.lane >= self.start) & (self.lane < self.start + self.heads)
        self.logit = jnp.where(self.is_logit, logit, 0.0)
        small = jnp.exp(-jnp.abs(self.logit))
        logdecay = jnp.where(self.is_logit, jnp.minimum(self.logit, 0.0) - jnp.log(1.0 + small), 0.0)
        self.lower = jnp.where(mask, 1.0, 0.0).astype(FLOAT)
        self.mask = mask
        self.cumul = dot(self.lower, logdecay, precision=ACCURATE)
        self.cumul_rows = jnp.transpose(self.cumul)
        self.feature = lax.broadcasted_iota(jnp.int32, (1, size), 1)

    def of_head(self, head, array):
        inside = (self.feature >= head * HD) & (self.feature < head * HD + HD)
        return jnp.where(inside, array, jnp.zeros_like(array))

    def weights(self, head):
        at = self.start + head
        gap = self.cumul[:, at : at + 1] - self.cumul_rows[at : at + 1, :]
        return jnp.where(self.mask, jnp.exp(jnp.minimum(gap, 0.0)), 0.0)


SCALE = HD ** (-0.5)


def scan_forward_kernel(place, *refs, rows, cols, along_cols, width):
    count = len(refs) // 2
    parts, outs = refs[:count], refs[count:]
    mask = scan_mask(place[0], rows, cols, along_cols, count)
    scan = Scan(parts, mask, width)
    total = jnp.zeros(scan.queries.shape, FLOAT)
    for head in range(scan.heads):
        scores = dot(scan.of_head(head, scan.queries), scan.keys, ((1,), (1,))) * SCALE
        scores = (scores * scan.weights(head)).astype(BFLOAT)
        total += dot(scores, scan.of_head(head, scan.values))
    cells = rows * cols
    low = total.astype(BFLOAT)
    for k in range(count):
        outs[k][0] = low[k * cells : (k + 1) * cells, :width]


def scan_backward_kernel(place, *refs, rows, cols, along_cols, width):
    count = len(refs) // 3
    parts, deltas, outs = refs[:count], refs[count : 2 * count], refs[2 * count :]
    mask = scan_mask(place[0], rows, cols, along_cols, count)
    scan = Scan(parts, mask, width)
    joined = jnp.concatenate([part[0] for part in deltas], axis=0)
    short = scan.padded - width
    if short:
        joined = jnp.concatenate([joined, jnp.zeros((joined.shape[0], short), BFLOAT)], axis=1)
    shape = scan.queries.shape
    delta_query = jnp.zeros(shape, FLOAT)
    delta_key = jnp.zeros(shape, FLOAT)
    delta_value = jnp.zeros(shape, FLOAT)
    gap_rows = jnp.zeros(scan.lane.shape, FLOAT)
    gap_cols = jnp.zeros(scan.cumul_rows.shape, FLOAT)
    place_row = lax.broadcasted_iota(jnp.int32, gap_cols.shape, 0)
    for head in range(scan.heads):
        query = scan.of_head(head, scan.queries)
        delta = scan.of_head(head, joined)
        weights = scan.weights(head)
        scores = dot(query, scan.keys, ((1,), (1,))) * SCALE * weights
        delta_scores = dot(delta, scan.values, ((1,), (1,)))
        gap = delta_scores * scores
        at = scan.start + head
        gap_rows += jnp.where(scan.lane == at, jnp.sum(gap, axis=1, keepdims=True), 0.0)
        gap_cols += jnp.where(place_row == at, jnp.sum(gap, axis=0, keepdims=True), 0.0)
        inner = (delta_scores * weights * SCALE).astype(BFLOAT)
        delta_query += dot(inner, scan.of_head(head, scan.keys))
        delta_key += dot(inner, query, ((0,), (0,)))
        delta_value += dot(scores.astype(BFLOAT), delta, ((0,), (0,)))
    delta_cumul = gap_rows - jnp.transpose(gap_cols)
    delta_decay = dot(scan.lower, delta_cumul, ((0,), (0,)), ACCURATE)
    small = jnp.exp(-jnp.abs(scan.logit))
    keep = jnp.where(scan.logit >= 0.0, small, 1.0) / (1.0 + small)
    delta_logit = delta_decay * keep
    block = scan.block
    mixed = jnp.where(scan.is_logit, delta_logit, delta_query[:, block : block + LANES])
    pieces = [delta_query[:, :block]] if block else []
    pieces.append(mixed)
    if block + LANES < scan.padded:
        pieces.append(delta_query[:, block + LANES :])
    whole = jnp.concatenate(pieces + [delta_key, delta_value], axis=1).astype(BFLOAT)
    cells = rows * cols
    for k in range(count):
        outs[k][0] = whole[k * cells : (k + 1) * cells]


def scan_call(kernel, place, inputs, out_width, rows, cols, along_cols, width):
    count = lax.axis_size("col") if along_cols else lax.axis_size("row")
    items, cells = inputs[0].shape[:2]
    spec = lambda last: pl.BlockSpec((1, cells, last), lambda i, place: (i, 0, 0))

    def body(*refs):
        kernel(*refs, rows=rows, cols=cols, along_cols=along_cols, width=width)

    return pl.pallas_call(
        body,
        grid_spec=pltpu.PrefetchScalarGridSpec(
            num_scalar_prefetch=1,
            grid=(items,),
            in_specs=[spec(v.shape[2]) for v in inputs],
            out_specs=[spec(out_width)] * count,
        ),
        out_shape=[jax.ShapeDtypeStruct((items, cells, out_width), BFLOAT)] * count,
        cost_estimate=SMALL,
        compiler_params=params(),
    )(place.reshape(1).astype(jnp.int32), *inputs)


def pick(values, index):
    chosen = values[0]
    for k in range(1, len(values)):
        chosen = jnp.where(index == k, values[k], chosen)
    return chosen


def fetch_columns(pieces):
    count, place = lax.axis_size("batch"), lax.axis_index("batch")
    if count != 2:
        stacked = jnp.stack(pieces)
        return lax.all_to_all(stacked, "batch", 0, 0).reshape((-1,) + pieces[0].shape[1:])
    own, other = pick(pieces, place), pick(pieces, 1 - place)
    rows = own.shape[0]
    half = rows // 2
    core = lax.axis_index("row") % 2
    first = swap(lax.dynamic_slice_in_dim(other, core * half, half, 0))
    second = swap(first, "row", 1)
    whole = jnp.zeros((2 * rows,) + own.shape[1:], own.dtype)
    whole = lax.dynamic_update_slice_in_dim(whole, own, place * rows, 0)
    base = (1 - place) * rows
    whole = lax.dynamic_update_slice_in_dim(whole, first, base + core * half, 0)
    return lax.dynamic_update_slice_in_dim(whole, second, base + (1 - core) * half, 0)


def head_columns(qkv, decay, group, width):
    size = padded_width(width + 3 * (width // HD))
    heads = width // HD
    parts = []
    for j in range(3):
        piece = qkv[:, j * D + group * width : j * D + (group + 1) * width]
        filled = width
        parts.append(piece)
        if j == 0:
            parts.append(decay[:, group * heads : (group + 1) * heads])
            filled += heads
        if size > filled:
            parts.append(jnp.zeros((qkv.shape[0], size - filled), qkv.dtype))
    return jnp.concatenate(parts, axis=1)


def normalize(values):
    center = values - jnp.mean(values, axis=-1, keepdims=True)
    inverse = lax.rsqrt(jnp.mean(center * center, axis=-1, keepdims=True) + EPS)
    return center * inverse, inverse


def normalize_back(delta, normal, inverse):
    first = jnp.mean(delta, axis=-1, keepdims=True)
    second = jnp.mean(delta * normal, axis=-1, keepdims=True)
    return inverse * (delta - first - normal * second)


def embed_steps(steps):
    half = D // 2
    freqs = jnp.exp(-jnp.log(10000.0) * jnp.arange(half, dtype=FLOAT) / half)
    angles = steps.astype(FLOAT)[:, None] * freqs[None, :]
    return jnp.concatenate([jnp.cos(angles), jnp.sin(angles)], axis=1)


GELU_A = 0.7978845608028654
GELU_B = 0.044715


def gelu(z):
    return 0.5 * z * (1.0 + jnp.tanh(GELU_A * (z + GELU_B * z * z * z)))


def gelu_slope(z):
    t = jnp.tanh(GELU_A * (z + GELU_B * z * z * z))
    return 0.5 * (1.0 + t) + 0.5 * z * (1.0 - t * t) * GELU_A * (1.0 + 3.0 * GELU_B * z * z)


def matmul(left, right):
    return lax.dot_general(left, right, (((2,), (0,)), ((), ())), preferred_element_type=FLOAT)


def matmul_back(left, right):
    return lax.dot_general(left, right, (((2,), (1,)), ((), ())), preferred_element_type=FLOAT)


def weight_grad(left, right):
    return lax.dot_general(
        left, right, (((0, 1), (0, 1)), ((), ())), preferred_element_type=FLOAT
    )


SHARES = 16
SHARE_ROWS = 144
STAGES = (("row", 1), ("row", 2), ("col", 1), ("col", 2))


def share_place(stages):
    number = jnp.int32(0)
    for axis, bit in stages:
        number = 2 * number + (lax.axis_index(axis) // bit) % 2
    return number.reshape(1).astype(jnp.int32)


def product(act, delta):
    return lax.dot_general(act, delta, (((1,), (0,)), ((), ())), preferred_element_type=FLOAT)


def grad_send_kernel(place, act, delta, out):
    out[0] = product(act[0], delta[0]).astype(BFLOAT)


def grad_keep_kernel(place, act, delta, received, send, keep):
    value = (product(act[0], delta[0]) + received[0].astype(FLOAT)).astype(BFLOAT)
    first = pl.program_id(0) < SHARES // 4

    @pl.when(first)
    def _():
        send[0] = value

    @pl.when(jnp.logical_not(first))
    def _():
        keep[0] = value


class GradSum:
    def __init__(self, act, delta, act_index, delta_index, stages):
        self.act, self.delta, self.stages = act, delta, stages
        self.act_index, self.delta_index = act_index, delta_index
        self.place = share_place(stages)

    def call(self, kernel, position, extra, extra_specs, out_specs, out_shapes, through):
        tokens = self.act.shape[2]
        act_spec = pl.BlockSpec(
            (1, SHARE_ROWS, tokens), lambda i, m: self.act_index(position(i) ^ m[0])
        )
        delta_spec = pl.BlockSpec(
            (1, tokens, D), lambda i, m: self.delta_index(position(i) ^ m[0])
        )
        inputs = 3 + len(extra)

        def body(*refs):
            kernel(*refs[:inputs], *refs[inputs + 1 : -1])

        return pl.pallas_call(
            body,
            grid_spec=pltpu.PrefetchScalarGridSpec(
                num_scalar_prefetch=1,
                grid=(SHARES // 2,),
                in_specs=[act_spec, delta_spec] + extra_specs + [ANYWHERE],
                out_specs=out_specs + [ANYWHERE],
            ),
            out_shape=out_shapes + [jax.ShapeDtypeStruct(through.shape, through.dtype)],
            input_output_aliases={inputs: len(out_shapes)},
            cost_estimate=SMALL,
            compiler_params=params(),
        )(self.place, self.act, self.delta, *extra, through)

    def start(self, through):
        half = SHARES // 2
        block = (1, SHARE_ROWS, D)
        send, through = self.call(
            grad_send_kernel,
            lambda i: i + half,
            [],
            [],
            [pl.BlockSpec(block, lambda i, m: (i, 0, 0))],
            [jax.ShapeDtypeStruct((half, SHARE_ROWS, D), BFLOAT)],
            through,
        )
        self.flight = self.move(send, 0)
        return through

    def move(self, value, stage):
        axis, bit = self.stages[stage]
        return swap(value, axis, bit)

    def second(self, through):
        quarter = SHARES // 4
        block = (1, SHARE_ROWS, D)
        position = lambda i: i ^ quarter
        send, self.keep, through = self.call(
            grad_keep_kernel,
            position,
            [self.flight],
            [pl.BlockSpec(block, lambda i, m: (position(i), 0, 0))],
            [
                pl.BlockSpec(block, lambda i, m: (jnp.minimum(i, quarter - 1), 0, 0)),
                pl.BlockSpec(block, lambda i, m: (jnp.maximum(i - quarter, 0), 0, 0)),
            ],
            [jax.ShapeDtypeStruct((quarter, SHARE_ROWS, D), BFLOAT)] * 2,
            through,
        )
        self.flight = self.move(send, 1)
        self.state = 0
        return through

    works = ("halve", "halve", "add", "join", "join", "pass")
    own_state = 3
    offload = False

    def advanced(self, outs):
        work = self.works[self.state]
        self.state += 1
        if work == "pass":
            self.keep, self.flight = outs
            self.pieces = [self.keep, self.flight]
            self.pieces += [self.move(piece, 0) for piece in self.pieces]
            return
        self.keep = outs[0]
        if not (self.offload and self.state == self.own_state):
            self.flight = self.onward(self.state, outs[-1])

    def onward(self, state, value):
        return self.move(value, (None, 2, 3, 3, 2, 1)[state])

    def done(self):
        return self.state == len(self.works)


class CrossGradSum(GradSum):
    works = ("halve", "halve", "add", "take", "join", "join", "pass")
    own_state = 4

    def onward(self, state, value):
        if state == 3:
            return self.cross(value)
        return self.move(value, (None, 2, 3, None, 3, 2, 1)[state])

    def cross(self, value):
        rows, cols = lax.axis_size("row"), lax.axis_size("col")
        pairs = []
        for x in range(2):
            for r in range(rows):
                for z in range(cols):
                    stays = r % 2 == x
                    to_x, to_r = (x, r) if stays else (1 - x, r ^ 1)
                    pairs.append(((x * rows + r) * cols + z, (to_x * rows + to_r) * cols + z))
        return lax.ppermute(value, ("batch", "row", "col"), pairs)


class Gathered:
    def __init__(self, sums):
        self.sums = sums

    def gather(self):
        self.collect(jnp.concatenate([one.keep for one in self.sums]))

    def collect(self, shares):
        whole = lax.all_gather(shares, GRID_AXES)
        for slot, one in enumerate(self.sums):
            one.whole, one.slot = whole, slot

    @staticmethod
    def finish(sums, kinds, previous, layer, shapes, through):
        block = (1, SHARE_ROWS, D)
        scalar = lax.axis_index("batch").reshape(1).astype(jnp.int32)

        def source(slot):
            def index(i, m):
                core, y, low, high = i // 8, i // 4 % 2, i // 2 % 2, i % 2
                return ((y * 2 + core) * 4 + high * 2 + low, slot, 0, 0)

            return pl.BlockSpec((None,) + block, index)

        def expand(i, m):
            own = jnp.where(i // 8 == m[0], m[0], 1 - m[0])
            return (layer, i % 4, own * 2 + i // 4 % 2)

        indices = (
            lambda i, m: (layer, i, 0),
            expand,
            lambda i, m: (layer, i // 4, jnp.minimum(i % 4, 2)),
            lambda i, m: (layer, i // 4, 0),
        )
        targets = [k for kind in kinds for k in ((0,), (1,), (2, 3))["ABC".index(kind)]]
        earlier = [previous[k] for k in targets] if previous else []
        count, outs, given = len(earlier), len(targets), len(sums)

        def body(m, *refs):
            where = dict(zip(targets, refs[-1 - outs : -1]))
            last = pl.program_id(0) % 4 == 3
            for kind, ref in zip(kinds, refs):
                if kind != "C":
                    where["AB".index(kind)][0] = ref[0].astype(FLOAT)
                    continue

                @pl.when(last)
                def _(ref=ref):
                    where[3][0] = ref[0].astype(FLOAT)

                @pl.when(jnp.logical_not(last))
                def _(ref=ref):
                    where[2][0] = ref[0].astype(FLOAT)

        *results, through = pl.pallas_call(
            body,
            grid_spec=pltpu.PrefetchScalarGridSpec(
                num_scalar_prefetch=1,
                grid=(SHARES,),
                in_specs=[source(one.slot) for one in sums] + [ANYWHERE] * (count + 1),
                out_specs=[pl.BlockSpec(block, indices[k]) for k in targets] + [ANYWHERE],
            ),
            out_shape=[jax.ShapeDtypeStruct(shapes[k], FLOAT) for k in targets]
            + [jax.ShapeDtypeStruct(through.shape, through.dtype)],
            input_output_aliases={1 + given + k: k for k in range(count)}
            | {1 + given + count: outs},
            cost_estimate=SMALL,
            compiler_params=params(),
        )(scalar, *[one.whole for one in sums], *earlier, through)
        return dict(zip(targets, results)), through


class Scattered(Gathered):
    def __init__(self):
        self.sums, self.group, self.shares = [], [], []

    def add(self, one, through):
        slot, tokens, dim = len(self.group), one.act.shape[2], len(self.shares) % 2
        one.offload = True
        earlier = [self.buffer] if slot else []
        self.sums.append(one)
        self.group.append(one)
        count = len(earlier)
        width = 1 if dim else 2
        place = lambda d: (slot, d, 0, 0) if dim else (d, slot, 0, 0)
        shape = (width, SHARES) if dim else (SHARES, width)

        def share(d):
            row, col = d // 4, d % 4
            return row % 2 * 8 + row // 2 * 4 + col % 2 * 2 + col // 2

        def body(act, delta, *refs):
            refs[count + 1][0, 0] = product(act[0], delta[0]).astype(BFLOAT)

        self.buffer, through = pl.pallas_call(
            body,
            grid=(SHARES,),
            in_specs=[
                pl.BlockSpec((1, SHARE_ROWS, tokens), lambda d: one.act_index(share(d))),
                pl.BlockSpec((1, tokens, D), lambda d: one.delta_index(share(d))),
            ]
            + [ANYWHERE] * (count + 1),
            out_specs=[pl.BlockSpec((1, 1, SHARE_ROWS, D), place), ANYWHERE],
            out_shape=[
                jax.ShapeDtypeStruct(shape + (SHARE_ROWS, D), BFLOAT),
                jax.ShapeDtypeStruct(through.shape, through.dtype),
            ],
            input_output_aliases={2 + k: k for k in range(count)} | {2 + count: 1},
            cost_estimate=SMALL,
            compiler_params=params(),
        )(one.act, one.delta, *earlier, through)
        return through

    def reduce(self):
        dim = len(self.shares) % 2
        summed = lax.psum_scatter(self.buffer, GRID_AXES, scatter_dimension=dim, tiled=True)
        self.shares.append(summed.reshape(-1, SHARE_ROWS, D))
        self.group = []

    def gather(self, after):
        shares = passed_by(self.shares, [after])
        shares = [part[slot] for part in shares for slot in range(part.shape[0])]
        for slot, one in enumerate(self.sums):
            if isinstance(one, CrossGradSum):
                shares[slot] = one.cross(shares[slot])
        self.collect(jnp.stack(shares))


class SmallSum:
    works = ("sum",) * 4

    def __init__(self, value):
        self.value, self.state = value, 0

    def start(self, through):
        self.keep, self.flight = self.value, self.move(0, self.value)
        return through

    def move(self, stage, value):
        return swap(value, *STAGES[stage])

    def advanced(self, outs):
        self.state += 1
        (self.keep,) = outs
        self.flight = None if self.done() else self.move(self.state, self.keep)

    def done(self):
        return self.state == len(self.works)


def tick_kernel(*refs, works):
    at, out = 0, 2 * len(works)
    for work in works:
        keep, flight = refs[at], refs[at + 1]
        at += 2
        count = keep.shape[0]
        if work == "sum":
            refs[out][...] = keep[...] + flight[...]
            out += 1
            continue
        if work == "join":
            refs[out][:count] = keep[...]
            refs[out][count:] = flight[...]
            out += 1
            continue
        for row in range(count):
            value = (keep[row].astype(FLOAT) + flight[row].astype(FLOAT)).astype(BFLOAT)
            if work == "add":
                refs[out][row] = value
            elif row < count // 2:
                refs[out][row] = value
            else:
                refs[out + 1][row - count // 2] = value
        out += 1 if work == "add" else 2


def tick(sums, through):
    if not sums:
        return through
    light = ("pass", "take")
    working = [one for one in sums if one.works[one.state] not in light]
    passing = [one for one in sums if one.works[one.state] in light]
    operands, shapes, counts, works = [], [], [], []
    for one in working:
        operands += [one.keep, one.flight]
        work, count = one.works[one.state], one.keep.shape[0]
        works.append(work)
        sizes = {"halve": [count // 2] * 2, "join": [2 * count]}.get(work, [count])
        counts.append(len(sizes))
        shapes += [
            jax.ShapeDtypeStruct((k,) + one.keep.shape[1:], one.keep.dtype) for k in sizes
        ]
    kept = lambda one: [one.flight] if one.works[one.state] == "take" else [one.keep, one.flight]
    passed = [value for one in passing for value in kept(one)] + [through]

    def body(*refs):
        ins, outs = refs[: len(operands)], refs[len(operands) + len(passed) :]
        tick_kernel(*ins, *outs, works=works)

    outs = pl.pallas_call(
        body,
        in_specs=[WHOLE] * len(operands) + [ANYWHERE] * len(passed),
        out_specs=[WHOLE] * len(shapes) + [ANYWHERE] * len(passed),
        out_shape=shapes + [jax.ShapeDtypeStruct(v.shape, v.dtype) for v in passed],
        input_output_aliases={
            len(operands) + k: len(shapes) + k for k in range(len(passed))
        },
        cost_estimate=SMALL,
        compiler_params=params(),
    )(*operands, *passed)
    at = 0
    for one, count in zip(working, counts):
        one.advanced(outs[at : at + count])
        at += count
    for one in passing:
        count = len(kept(one))
        one.advanced(outs[at : at + count])
        at += count
    return outs[-1]


def sum_small(value):
    for axis, bit in STAGES:
        value = value + swap(value, axis, bit)
    return value


def turned(values):
    return jnp.transpose(values.reshape(-1, values.shape[2]))


def own_half(values):
    half = values.shape[-1] // 2
    return jnp.where(lax.axis_index("batch") == 0, values[..., :half], values[..., half:])


def spread(values):
    items = values.shape[0] // 2
    other = swap(values)
    return jnp.concatenate([other[items:], other[:items]], axis=0)


def shrink_sum(active, outer_low):
    act = turned(active)[None]
    delta = outer_low.reshape(1, -1, D)
    return GradSum(act, delta, lambda s: (0, s, 0), lambda s: (0, 0, 0), STAGES)


def expand_sum(second, inner_low):
    act = turned(second)[None]
    delta = inner_low.reshape(1, -1, inner_low.shape[-1])
    return CrossGradSum(
        act, delta, lambda s: (0, s // 8 * 4 + s % 4, 0), lambda s: (0, 0, s // 4 % 2), STAGES
    )


def mixer_delta(own, other, branch, branch_other, places, width, size):
    tokens = own.shape[0]
    block = tokens // 4
    heads = width // HD

    def body(places, mine, theirs, low, low_other, out, logits):
        first = places[0] == 0
        values = mine[...].astype(FLOAT), theirs[...].astype(FLOAT)
        left = jnp.where(first, values[0], values[1])
        right = jnp.where(first, values[1], values[0])
        for j in range(3):
            part = slice(j * size, j * size + width)
            out[:, j * D : (j + 1) * D] = jnp.concatenate(
                [left[:, part], right[:, part]], axis=1
            ).astype(BFLOAT)
        half = pl.program_id(0) < 2

        @pl.when(half)
        def _():
            out[:, 3 * D :] = low[...]

        @pl.when(jnp.logical_not(half))
        def _():
            out[:, 3 * D :] = low_other[...]

        part = slice(width, width + heads)
        rest = jnp.zeros((block, LANES - 2 * heads), FLOAT)
        logits[...] = jnp.concatenate([left[:, part], right[:, part], rest], axis=1).astype(BFLOAT)

    return pl.pallas_call(
        body,
        grid_spec=pltpu.PrefetchScalarGridSpec(
            num_scalar_prefetch=1,
            grid=(4,),
            in_specs=[
                pl.BlockSpec((block, 3 * size), lambda i, m: (i, 0)),
                pl.BlockSpec((block, 3 * size), lambda i, m: (i ^ 2, 0)),
                pl.BlockSpec((block, D), lambda i, m: (jnp.minimum(i, 1), 0)),
                pl.BlockSpec((block, D), lambda i, m: (jnp.maximum(i - 2, 0), 0)),
            ],
            out_specs=[
                pl.BlockSpec((block, 4 * D), lambda i, m: (i, 0)),
                pl.BlockSpec((block, LANES), lambda i, m: (i, 0)),
            ],
        ),
        out_shape=[
            jax.ShapeDtypeStruct((tokens, 4 * D), BFLOAT),
            jax.ShapeDtypeStruct((tokens, LANES), BFLOAT),
        ],
        cost_estimate=SMALL,
        compiler_params=params(),
    )(places, own, other, branch, branch_other)


def mixer_sum(mixed, delta_project, attend, branch, branch_other, places, width, size):
    act = jnp.stack([turned(own_half(mixed)[None]), turned(attend[None])])
    delta, logits = mixer_delta(
        delta_project, swap(delta_project), branch, branch_other, places, width, size
    )
    return (
        GradSum(
            act,
            delta[None],
            lambda s: (jnp.where(s % 4 == 3, 1, 0), s // 4, 0),
            lambda s: (0, 0, s % 4),
            STAGES,
        ),
        logits,
    )


ITEMS = 2
ANYWHERE = pl.BlockSpec(memory_space=pl.ANY)
WHOLE = pl.BlockSpec(memory_space=pltpu.VMEM)


def call(body, shapes, arrays, places=None, held=(), after=(), scratch=()):
    first = 0 if places is None else 1
    count, kept, tied = len(arrays), len(held), len(after)

    def whole(*refs):
        ins = refs[first : first + count]
        far = refs[first + count : first + count + kept]
        at = first + count + kept + tied
        outs = refs[at : at + len(shapes)]
        body(refs[0] if first else None, ins, far, outs, refs[at + len(shapes) :])

    return pl.pallas_call(
        whole,
        in_specs=[pl.BlockSpec(memory_space=pltpu.SMEM)] * first
        + [WHOLE] * count
        + [ANYWHERE] * (kept + tied),
        out_specs=[WHOLE] * len(shapes),
        out_shape=[jax.ShapeDtypeStruct(*shape) for shape in shapes],
        scratch_shapes=list(scratch),
        cost_estimate=SMALL,
        compiler_params=params(),
    )(*([] if places is None else [places]), *arrays, *held, *after)


def edge_shapes(tile):
    rows, cols = tile
    sizes = [cols, cols, rows, rows]
    return [((ITEMS, size, D), BFLOAT) for size in sizes]


def put_edges(value, item, refs, tile):
    rows, cols = tile
    lines = [value[0], value[rows - 1]]
    for at in (0, cols - 1):
        lines.append(jnp.concatenate([value[r][at : at + 1] for r in range(rows)], axis=0))
    for ref, line in zip(refs, lines):
        ref[item] = line.astype(BFLOAT)


def halo_edges(edges):
    rows, cols = lax.axis_size("row"), lax.axis_size("col")
    first_row, last_row, first_col, last_col = edges
    top = lax.ppermute(last_row, "row", [(i, i + 1) for i in range(rows - 1)])
    bottom = lax.ppermute(first_row, "row", [(i + 1, i) for i in range(rows - 1)])
    to_right = jnp.concatenate([top[:, -1:], last_col, bottom[:, -1:]], axis=1)
    to_left = jnp.concatenate([top[:, :1], first_col, bottom[:, :1]], axis=1)
    left = lax.ppermute(to_right, "col", [(i, i + 1) for i in range(cols - 1)])
    right = lax.ppermute(to_left, "col", [(i + 1, i) for i in range(cols - 1)])
    return top, bottom, left, right


def modulated(value, mod, shift, scale):
    normal, inverse = normalize(value)
    return normal * (1.0 + mod[scale : scale + 1]) + mod[shift : shift + 1]


def enter_first(tokens, mod, tile):
    cells = (ITEMS,) + tile + (D,)

    def body(_, ins, far, outs, scratch):
        for i in range(ITEMS):
            hidden = modulated(ins[0][i].astype(FLOAT), ins[1][i], 0, 1).reshape(cells[1:])
            outs[0][i] = hidden.astype(BFLOAT)
            put_edges(hidden, i, outs[1:], tile)

    hidden, *edges = call(body, [(cells, BFLOAT)] + edge_shapes(tile), [tokens, mod])
    return hidden, edges


def enter_next(middle, own, received, mod_before, mod, tile):
    cells = (ITEMS,) + tile + (D,)
    count = middle.shape[1]

    def body(_, ins, far, outs, scratch):
        for i in range(ITEMS):
            at = slice(i * count, (i + 1) * count)
            outer = ins[1][at] + ins[2][at].astype(FLOAT)
            outs[1][i] = outer
            value = ins[0][i] + ins[3][i][5:6] * outer
            outs[0][i] = value
            hidden = modulated(value, ins[4][i], 0, 1).reshape(cells[1:])
            outs[2][i] = hidden.astype(BFLOAT)
            put_edges(hidden, i, outs[3:], tile)

    shapes = [(middle.shape, FLOAT), (middle.shape, FLOAT), (cells, BFLOAT)] + edge_shapes(tile)
    value, outer, hidden, *edges = call(body, shapes, [middle, own, received, mod_before, mod])
    return value, outer, hidden, edges


def leave(middle, own, received, mod):
    count = middle.shape[1]

    def body(_, ins, far, outs, scratch):
        for i in range(ITEMS):
            at = slice(i * count, (i + 1) * count)
            outer = ins[1][at] + ins[2][at].astype(FLOAT)
            outs[1][i] = outer
            outs[0][i] = (ins[0][i] + ins[3][i][5:6] * outer).astype(BFLOAT)

    return call(
        body, [(middle.shape, BFLOAT), (middle.shape, FLOAT)], [middle, own, received, mod]
    )


def gather_weight(far, scratch, sems, places, own):
    batch, quarter = places[0], places[1]
    rows = own.shape[0]
    size = rows // 4
    base = (1 - batch) * rows
    parts = [(own, batch * rows, rows)]
    for k in range(4):
        parts.append((far[k], base + (quarter ^ k) * size, size))
    copies = []
    for k, (source, start, count) in enumerate(parts):
        target = scratch.at[pl.ds(pl.multiple_of(start, 16), count)]
        copy = pltpu.make_async_copy(source, target, sems.at[k])
        copy.start()
        copies.append(copy)
    return copies


def split_logit(block, start, heads):
    lane = lax.broadcasted_iota(jnp.int32, block.shape, 1)
    here = (lane >= start) & (lane < start + heads)
    high = block.astype(BFLOAT).astype(FLOAT)
    rest = jnp.where(here, block - high, 0.0)
    middle = rest.astype(BFLOAT).astype(FLOAT)
    low = rest - middle
    return (
        jnp.where(here, high, block) + pltpu.roll(middle, heads, 1) + pltpu.roll(low, 2 * heads, 1)
    )


def project_call(own, other, weight, bias, places, cells, width):
    size = weight[0].shape[1] // 3
    block = width // LANES * LANES
    total = 2 * own.shape[0]
    count = total // cells

    def body(places, ins, far, outs, scratch):
        whole, joined, result, sems = scratch
        copies = gather_weight(far[1:], whole, sems, places, far[0])
        joined[: total // 2] = ins[0][...]
        joined[total // 2 :] = ins[1][...]
        for copy in copies:
            copy.wait()
        for part in range(3):
            columns = slice(part * size, (part + 1) * size)
            value = dot(joined[...], whole[:, columns])
            if part == 0:
                last = split_logit(
                    value[:, block : block + LANES] + ins[2][...], width - block, width // HD
                )
                result[:, :block] = value[:, :block].astype(BFLOAT)
                result[:, block : block + LANES] = last.astype(BFLOAT)
            else:
                result[:, columns] = value.astype(BFLOAT)
        for k in range(count):
            start = pl.multiple_of((places[2] ^ k) * cells, cells)
            outs[k][0] = result[pl.ds(start, cells)]

    return call(
        body,
        [((1, cells, 3 * size), BFLOAT)] * count,
        [own, other, bias],
        places,
        weight,
        scratch=[
            pltpu.VMEM((D, 3 * size), BFLOAT),
            pltpu.VMEM((total, D), BFLOAT),
            pltpu.VMEM((total, 3 * size), BFLOAT),
            pltpu.SemaphoreType.DMA((5,)),
        ],
    )


def halves_out(value, outs, columns, items_here):
    outs[0][:, columns] = value[:items_here]
    outs[1][:, columns] = value[items_here:].astype(BFLOAT)


COLUMNS = 384


def attend_out_call(blocks, weight, layer, places, cells, width):
    count = len(blocks)
    total = count * cells

    def body(places, ins, far, outs, scratch):
        whole, sems = scratch
        copy = pltpu.make_async_copy(far[0].at[layer], whole, sems.at[0])
        copy.start()
        for k in range(count):
            start = pl.multiple_of((places[2] ^ k) * cells, cells)
            outs[2][pl.ds(start, cells)] = ins[k][0]
        copy.wait()
        for at in range(0, D, COLUMNS):
            columns = slice(at, at + COLUMNS)
            halves_out(dot(outs[2][...], whole[:, columns]), outs, columns, total // 2)

    return call(
        body,
        [((total // 2, D), FLOAT), ((total // 2, D), BFLOAT), ((total, width), BFLOAT)],
        blocks,
        places,
        [weight],
        scratch=[pltpu.VMEM((width, D), BFLOAT), pltpu.SemaphoreType.DMA((1,))],
    )


def middle_call(tokens, own, received, mod):
    count = tokens.shape[1]

    def body(_, ins, far, outs, scratch):
        for i in range(ITEMS):
            at = slice(i * count, (i + 1) * count)
            branch = ins[1][at] + ins[2][at].astype(FLOAT)
            outs[0][i] = branch
            middle = ins[0][i].astype(FLOAT) + ins[3][i][2:3] * branch
            outs[1][i] = middle
            outs[2][at] = modulated(middle, ins[3][i], 3, 4).astype(BFLOAT)

    shape = tokens.shape
    return call(
        body,
        [(shape, FLOAT), (shape, FLOAT), ((ITEMS * count, D), BFLOAT)],
        [tokens, own, received, mod],
    )


def feed_call(own, other, expand, shrink, layer, places):
    total = 2 * own.shape[0]
    inner = shrink.shape[1]
    rows = expand[0].shape[1]
    tile = 256

    def body(places, ins, far, outs, scratch):
        wide, back, joined, sems = scratch
        start = pl.multiple_of(places[0] * inner, LANES)
        source = far[0].at[layer, :, pl.ds(start, inner)]
        copies = gather_weight(far[1:5], wide, sems, places, source)
        last = pltpu.make_async_copy(far[5].at[layer], back, sems.at[5])
        last.start()
        joined[: total // 2] = ins[0][...]
        joined[total // 2 :] = ins[1][...]
        for copy in copies:
            copy.wait()
        for at in range(0, inner, tile):
            columns = slice(at, at + tile)
            value = dot(joined[...], wide[:, columns])
            outs[2][:, columns] = value
            outs[3][:, columns] = gelu(value).astype(BFLOAT)
        last.wait()
        for at in range(0, D, COLUMNS):
            columns = slice(at, at + COLUMNS)
            halves_out(dot(outs[3][...], back[:, columns]), outs, columns, total // 2)

    return call(
        body,
        [
            ((total // 2, D), FLOAT),
            ((total // 2, D), BFLOAT),
            ((total, inner), FLOAT),
            ((total, inner), BFLOAT),
        ],
        [own, other],
        places,
        list(expand) + [shrink],
        scratch=[
            pltpu.VMEM((2 * rows, inner), BFLOAT),
            pltpu.VMEM((inner, D), BFLOAT),
            pltpu.VMEM((total, D), BFLOAT),
            pltpu.SemaphoreType.DMA((6,)),
        ],
    )


def feed_back_call(own, other, inner_value, expand, shrink, layer, places):
    total = 2 * own.shape[0]
    inner = shrink.shape[1]
    rows = expand[0].shape[1]
    tile = 256

    def body(places, ins, far, outs, scratch):
        wide, back, joined, sems = scratch
        last = pltpu.make_async_copy(far[5].at[layer], back, sems.at[5])
        last.start()
        start = pl.multiple_of(places[0] * inner, LANES)
        source = far[0].at[layer, :, pl.ds(start, inner)]
        copies = gather_weight(far[1:5], wide, sems, places, source)
        joined[: total // 2] = ins[0][...]
        joined[total // 2 :] = ins[1][...]
        last.wait()
        for at in range(0, inner, tile):
            columns = slice(at, at + tile)
            value = dot(joined[...], back[at : at + tile], ((1,), (1,)))
            outs[2][:, columns] = (value * gelu_slope(ins[2][:, columns])).astype(BFLOAT)
        for copy in copies:
            copy.wait()
        for at in range(0, D, COLUMNS):
            columns = slice(at, at + COLUMNS)
            value = dot(outs[2][...], wide[at : at + COLUMNS], ((1,), (1,)))
            halves_out(value, outs, columns, total // 2)

    return call(
        body,
        [((total // 2, D), FLOAT), ((total // 2, D), BFLOAT), ((total, inner), BFLOAT)],
        [own, other, inner_value],
        places,
        list(expand) + [shrink],
        scratch=[
            pltpu.VMEM((2 * rows, inner), BFLOAT),
            pltpu.VMEM((inner, D), BFLOAT),
            pltpu.VMEM((total, D), BFLOAT),
            pltpu.SemaphoreType.DMA((6,)),
        ],
    )


def middle_back_call(delta, own, received, middle, branch, outer, mod):
    count = middle.shape[1]
    over = lambda v: jnp.sum(v, axis=0, keepdims=True)

    def body(_, ins, far, outs, scratch):
        for i in range(ITEMS):
            at = slice(i * count, (i + 1) * count)
            here = ins[0][i].astype(FLOAT)
            mod_here = ins[6][i]
            outs[2][i, 3:4] = over(here * ins[5][i])
            second = ins[1][at] + ins[2][at].astype(FLOAT)
            normal, inverse = normalize(ins[3][i])
            outs[2][i, 1:2] = over(second)
            outs[2][i, 2:3] = over(second * normal)
            total = here + normalize_back(second * (1.0 + mod_here[4:5]), normal, inverse)
            outs[0][i] = total
            outs[2][i, 0:1] = over(total * ins[4][i])
            outs[1][at] = (mod_here[2:3] * total).astype(BFLOAT)

    return call(
        body,
        [(middle.shape, FLOAT), ((ITEMS * count, D), BFLOAT), ((ITEMS, 4, D), FLOAT)],
        [delta, own, received, middle, branch, outer, mod],
    )


def attend_back_call(own, other, weight, layer, places, cells, width):
    total = 2 * own.shape[0]
    count = total // cells

    def body(places, ins, far, outs, scratch):
        whole, joined, result, sems = scratch
        copy = pltpu.make_async_copy(far[0].at[layer], whole, sems.at[0])
        copy.start()
        joined[: total // 2] = ins[0][...]
        joined[total // 2 :] = ins[1][...]
        copy.wait()
        result[...] = dot(joined[...], whole[...], ((1,), (1,))).astype(BFLOAT)
        for k in range(count):
            start = pl.multiple_of((places[2] ^ k) * cells, cells)
            outs[k][0] = result[pl.ds(start, cells)]

    return call(
        body,
        [((1, cells, width), BFLOAT)] * count,
        [own, other],
        places,
        [weight],
        scratch=[
            pltpu.VMEM((width, D), BFLOAT),
            pltpu.VMEM((total, D), BFLOAT),
            pltpu.VMEM((total, width), BFLOAT),
            pltpu.SemaphoreType.DMA((1,)),
        ],
    )


def project_back_call(blocks, weight, places, cells, width):
    count = len(blocks)
    total = count * cells
    wide = blocks[0].shape[2]

    def body(places, ins, far, outs, scratch):
        whole, sems = scratch
        copies = gather_weight(far[1:], whole, sems, places, far[0])
        for k in range(count):
            start = pl.multiple_of((places[2] ^ k) * cells, cells)
            outs[2][pl.ds(start, cells)] = ins[k][0]
        at = width // LANES * LANES
        logits = outs[2][:, at : at + LANES].astype(FLOAT)
        outs[3][...] = jnp.sum(logits, axis=0, keepdims=True)
        for copy in copies:
            copy.wait()
        for at in range(0, D, COLUMNS):
            columns = slice(at, at + COLUMNS)
            value = dot(outs[2][...], whole[at : at + COLUMNS], ((1,), (1,)))
            halves_out(value, outs, columns, total // 2)

    return call(
        body,
        [
            ((total // 2, D), FLOAT),
            ((total // 2, D), BFLOAT),
            ((total, wide), BFLOAT),
            ((1, LANES), FLOAT),
        ],
        blocks,
        places,
        weight,
        scratch=[pltpu.VMEM((D, wide), BFLOAT), pltpu.SemaphoreType.DMA((5,))],
    )


def conv_delta_call(own, received, convolved, tile):
    cells = convolved.shape
    count = tile[0] * tile[1]

    def body(_, ins, far, outs, scratch):
        for i in range(ITEMS):
            at = slice(i * count, (i + 1) * count)
            delta = (ins[0][at] + ins[1][at].astype(FLOAT)).reshape(cells[1:])
            value = ins[2][i]
            gate = jax.nn.sigmoid(value)
            delta = delta * gate * (1.0 + value * (1.0 - gate))
            outs[0][i] = delta.astype(BFLOAT)
            put_edges(delta, i, outs[1:], tile)

    delta, *edges = call(
        body, [(cells, BFLOAT)] + edge_shapes(tile), [own, received, convolved]
    )
    return delta, edges


def enter_back_call(delta_hidden, tokens, delta_middle, mod, mod_before):
    count = tokens.shape[1]
    over = lambda v: jnp.sum(v, axis=0, keepdims=True)
    lower = mod_before is not None

    def body(_, ins, far, outs, scratch):
        for i in range(ITEMS):
            at = slice(i * count, (i + 1) * count)
            here = ins[0][i].reshape(count, D)
            normal, inverse = normalize(ins[1][i].astype(FLOAT))
            outs[0][i, 0:1] = over(here)
            outs[0][i, 1:2] = over(here * normal)
            total = ins[2][i] + normalize_back(here * (1.0 + ins[3][i][1:2]), normal, inverse)
            if lower:
                outs[2][i] = total
                outs[1][at] = (ins[4][i][5:6] * total).astype(BFLOAT)
            else:
                outs[1][at] = total.astype(BFLOAT)

    shapes = [((ITEMS, 2, D), FLOAT), ((ITEMS * count, D), BFLOAT)]
    arrays = [delta_hidden, tokens, delta_middle, mod]
    if lower:
        shapes.append((tokens.shape, FLOAT))
        arrays.append(mod_before)
    return call(body, shapes, arrays)


def pack_kernel(places, qkv, decay, own, other, *, width):
    heads = width // HD
    size = padded_width(width + 3 * heads)
    value, extra = qkv[0].astype(FLOAT), decay[0].astype(FLOAT)
    rows = value.shape[0]
    pieces = []
    for group in range(2):
        parts = []
        for j in range(3):
            start = j * D + group * width
            parts.append(value[:, start : start + width])
            filled = width
            if j == 0:
                parts.append(extra[:, group * heads : (group + 1) * heads])
                filled += heads
            parts.append(jnp.zeros((rows, size - filled), FLOAT))
        pieces.append(jnp.concatenate(parts, axis=1).astype(BFLOAT))
    first = places[0] == 0
    own[...] = jnp.where(first, pieces[0], pieces[1])
    other[...] = jnp.where(first, pieces[1], pieces[0])


def pack_call(qkv, decay, layer, places, width):
    rows = qkv.shape[1]
    size = padded_width(width + 3 * (width // HD))

    def body(*refs):
        pack_kernel(*refs, width=width)

    out = pl.BlockSpec((SHARE_ROWS, 3 * size), lambda i, m: (i, 0))
    return pl.pallas_call(
        body,
        grid_spec=pltpu.PrefetchScalarGridSpec(
            num_scalar_prefetch=1,
            grid=(rows // SHARE_ROWS,),
            in_specs=[
                pl.BlockSpec((1, SHARE_ROWS, qkv.shape[2]), lambda i, m: (layer, i, 0)),
                pl.BlockSpec((1, SHARE_ROWS, decay.shape[2]), lambda i, m: (layer, i, 0)),
            ],
            out_specs=[out, out],
        ),
        out_shape=[jax.ShapeDtypeStruct((rows, 3 * size), BFLOAT)] * 2,
        cost_estimate=SMALL,
        compiler_params=params(),
    )(places, qkv, decay)


def passed_by(values, after):
    count = len(values)
    return pl.pallas_call(
        lambda *refs: None,
        in_specs=[ANYWHERE] * (count + len(after)),
        out_specs=[ANYWHERE] * count,
        out_shape=[jax.ShapeDtypeStruct(v.shape, v.dtype) for v in values],
        input_output_aliases={k: k for k in range(count)},
        cost_estimate=SMALL,
        compiler_params=params(),
    )(*values, *after)


def lines_swapped(blocks, axis):
    return [blocks[0]] + [swap(blocks[k], axis, k) for k in range(1, len(blocks))]


class Pair:
    def __init__(self, args, modulations, taps, tile):
        self.args, self.modulations, self.taps, self.tile = args, modulations, taps, tile
        self.cells = tile[0] * tile[1]
        self.width = args["proj"].shape[1]
        self.heads = self.width // HD
        self.size = padded_width(self.width + 3 * self.heads)
        batch, row = lax.axis_index("batch"), lax.axis_index("row")
        quarter = row % 2 * 2 + row // 2
        self.places = [
            jnp.stack([batch, quarter, lax.axis_index(axis)]).astype(jnp.int32)
            for axis in ("col", "row")
        ]
        self.qkv, self.expand, self.bias = [], [], []
        self.pieces = {}
        for layer in range(LAYERS):
            own, other = pack_call(
                args["qkv"], args["decay"], layer, self.places[0], self.width
            )
            part = own.shape[0] // 4
            piece = lax.dynamic_slice_in_dim(other, quarter * part, part, 0)
            self.pieces["qkv", layer] = piece
            self.qkv.append([own])
            inner = args["shrink"].shape[1]
            piece = lax.dynamic_slice(
                args["expand"], (layer, quarter * part, (1 - batch) * inner), (1, part, inner)
            )
            self.pieces["expand", layer] = piece[0]
            self.expand.append([args["expand"]])
            start = self.width - self.width // LANES * LANES
            self.bias.append(
                jnp.pad(
                    args["decay_bias"][layer].astype(FLOAT)[None],
                    ((0, 0), (start, LANES - start - self.heads)),
                )
            )
        for stage in range(3):
            self.fetch("qkv", 0, stage, [])

    def fetch(self, name, layer, stage, after):
        held = self.pieces[name, layer]
        if stage == 0:
            if after:
                (held,) = passed_by([held], after)
            self.pieces[name, layer] = [swap(held)]
        elif stage == 1:
            if after:
                held = passed_by(held, after)
            self.pieces[name, layer] = [held[0], swap(held[0], "row", 2)]
        else:
            if after:
                held = passed_by(held, after)
            into = self.qkv if name == "qkv" else self.expand
            into[layer] += list(held) + [swap(part, "row", 1) for part in held]

    def axis(self, layer):
        return "col" if layer % 2 == 0 else "row"

    def scan(self, kernel, layer, inputs, out_width):
        place = self.places[layer % 2][2]
        rows, cols = self.tile
        return scan_call(
            kernel, place, inputs, out_width, rows, cols, layer % 2 == 0, self.width
        )

    def forward(self, layer, hidden, edges, tokens):
        places, axis = self.places[layer % 2], self.axis(layer)
        mod = self.modulations[layer]
        sides = halo_edges(edges)
        convolved, mixed = conv_forward(hidden, sides, self.taps[layer])
        mixed = mixed.reshape(-1, D)
        mixed_other = swap(mixed)
        if layer == 0:
            self.fetch("expand", 0, 0, [hidden])
            self.fetch("expand", 0, 1, [mixed])
        else:
            self.fetch("expand", 1, 1, [mixed])
        parts = project_call(
            mixed, mixed_other, self.qkv[layer], self.bias[layer], places, self.cells, self.width
        )
        self.fetch("expand", layer, 2, [parts[0]])
        if layer + 1 < LAYERS:
            self.fetch("qkv", layer + 1, 0, [parts[0]])
        parts = lines_swapped(parts, axis)
        attends = self.scan(scan_forward_kernel, layer, parts, self.width)
        own, send, attend = attend_out_call(
            lines_swapped(attends, axis), self.args["proj"], layer, places, self.cells, self.width
        )
        if layer + 1 < LAYERS:
            self.fetch("qkv", layer + 1, 1, [own])
        branch, middle, second = middle_call(tokens, own, swap(send), mod)
        second_other = swap(second)
        if layer + 1 < LAYERS:
            self.fetch("qkv", layer + 1, 2, [second])
        own, send, inner, active = feed_call(
            second, second_other, self.expand[layer], self.args["shrink"], layer, places
        )
        if layer + 1 < LAYERS:
            self.fetch("expand", layer + 1, 0, [own])
        saved = dict(
            tokens=tokens, hidden=hidden, sides=sides, convolved=convolved, mixed=mixed,
            mixed_other=mixed_other, parts=parts, attend=attend, branch=branch, middle=middle,
            second=second, second_other=second_other, inner=inner, active=active,
        )
        return middle, own, swap(send), saved

    def backward(self, layer, delta, outer_low, outer_other, saved, tick):
        places, axis = self.places[layer % 2], self.axis(layer)
        mod = self.modulations[layer]
        both = lambda own, other: jnp.concatenate([own, other], axis=0)
        own, send, inner_low = feed_back_call(
            outer_low, outer_other, saved["inner"], self.expand[layer], self.args["shrink"],
            layer, places,
        )
        received = swap(send)
        shrink_pipe = shrink_sum(saved["active"][None], both(outer_low, outer_other))
        own = tick("P1", {"A": shrink_pipe}, own)
        delta_middle, branch_low, mod_b = middle_back_call(
            delta, own, received, saved["middle"], saved["branch"], saved["outer"], mod
        )
        branch_other = swap(branch_low)
        paired = lambda v: v.reshape(2, -1, v.shape[-1])
        expand_pipe = expand_sum(
            paired(both(saved["second"], saved["second_other"])), paired(inner_low)
        )
        branch_low = tick("P2", {"B": expand_pipe}, branch_low)
        blocks = attend_back_call(
            branch_low, branch_other, self.args["proj"], layer, places, self.cells, self.width
        )
        sent = lines_swapped(blocks, axis)
        sent[0] = tick("P3", {}, sent[0])
        projects = self.scan(
            scan_backward_kernel, layer, list(saved["parts"]) + sent, 3 * self.size
        )
        sent = lines_swapped(projects, axis)
        sent[0] = tick("P4", {}, sent[0])
        own, send, delta_project, grad_bias = project_back_call(
            sent, self.qkv[layer], places, self.cells, self.width
        )
        received = swap(send)
        mixed = both(saved["mixed"], saved["mixed_other"])

        def mixer(after):
            (value,) = passed_by([delta_project], after)
            pipe, logits = mixer_sum(
                mixed, value, saved["attend"], branch_low, branch_other, places,
                self.width, self.size,
            )
            return pipe, dot(logits, own_half(mixed), ((0,), (0,)))[: 2 * self.heads]

        if not layer:
            mixer_pipe, grad_decay = mixer([])
        own = tick("P5", {}, own)
        delta_conv, edges = conv_delta_call(own, received, saved["convolved"], self.tile)
        delta_sides = halo_edges(edges)
        delta_conv = tick("P6", {}, delta_conv)
        if layer:
            mixer_pipe, grad_decay = mixer([delta_conv])
        top, bottom, left, right = delta_sides
        left = tick("P8", {"C": mixer_pipe}, left)
        delta_sides = (top, bottom, left, right)
        delta_hidden, grad_taps = conv_backward(
            saved["hidden"], saved["sides"], delta_conv, delta_sides, self.taps[layer]
        )
        before = self.modulations[layer - 1] if layer else None
        mod_a, low, *rest = enter_back_call(
            delta_hidden, saved["tokens"], delta_middle, mod, before
        )
        low_other = swap(low) if rest else None

        small = SmallSum(join_smalls(mod_a, mod_b, grad_taps, grad_decay, grad_bias))
        low = tick("P7", {"S": small}, low)
        return rest[0] if rest else None, low, low_other


def pair_forward_backward(pair, tokens_in, cotangent, tick):
    tile = pair.tile
    shape = (ITEMS, pair.cells, D)
    tokens = tokens_in.reshape(shape)
    delta = cotangent.reshape(shape)
    outer_low = (pair.modulations[-1][:, 5:6] * delta.astype(FLOAT)).astype(BFLOAT)
    hidden, edges = enter_first(tokens, pair.modulations[0], tile)
    stored = []
    for layer in range(LAYERS):
        middle, own, received, saved = pair.forward(layer, hidden, edges, tokens)
        stored.append(saved)
        mod = pair.modulations[layer]
        if layer + 1 < LAYERS:
            tokens, saved["outer"], hidden, edges = enter_next(
                middle, own, received, mod, pair.modulations[layer + 1], tile
            )
        else:
            block_out, saved["outer"] = leave(middle, own, received, mod)
    outer_low = outer_low.reshape(-1, D)
    outer_other = swap(outer_low)
    for layer in reversed(range(LAYERS)):
        delta, outer_low, outer_other = pair.backward(
            layer, delta, outer_low, outer_other, stored[layer],
            lambda point, fresh, through, layer=layer: tick(layer, point, fresh, through),
        )
    return block_out, outer_low


def forward_layer(tokens, modulation, weights, layer, tile):
    taps, qkv, decay_bias, proj, expand, shrink = weights
    rows, cols = tile
    items, cells = tokens.shape[:2]
    width = proj.shape[0]
    heads = width // HD
    size = padded_width(width + 3 * heads)
    axis = "col" if layer % 2 == 0 else "row"
    mod = [modulation[:, k][:, None] for k in range(6)]
    normal, inverse = normalize(tokens)
    hidden = (normal * (1.0 + mod[1]) + mod[0]).astype(BFLOAT).reshape(items, rows, cols, D)
    sides = halo(hidden)
    convolved, mixed = conv_forward(hidden, sides, taps)
    mixed = gather_items(mixed.reshape(items, cells, D))
    project = matmul(mixed, qkv)
    logit = project[:, :, width : width + heads] + decay_bias.astype(FLOAT)
    high = logit.astype(BFLOAT)
    rest = logit - high.astype(FLOAT)
    middle_part = rest.astype(BFLOAT)
    low = (rest - middle_part.astype(FLOAT)).astype(BFLOAT)
    project = project.astype(BFLOAT)
    project = jnp.concatenate(
        [project[:, :, :width], high, middle_part, low, project[:, :, width + 3 * heads :]], axis=2
    )
    parts = lines_out(project, axis)
    place = lax.axis_index(axis)
    attends = scan_call(
        scan_forward_kernel, place, parts, width, rows, cols, layer % 2 == 0, width
    )
    attend = lines_back(attends, axis)
    branch = reduce_items(matmul(attend, proj))
    middle = tokens + mod[2] * branch
    normal2, inverse2 = normalize(middle)
    second = gather_items((normal2 * (1.0 + mod[4]) + mod[3]).astype(BFLOAT))
    inner = matmul(second, expand)
    active = gelu(inner).astype(BFLOAT)
    outer = reduce_items(matmul(active, shrink))
    result = middle + mod[5] * outer
    saved = (
        normal, inverse, hidden, sides, convolved, mixed, parts, attend, branch,
        normal2, inverse2, second, inner, active, outer,
    )
    return result, saved


def pipelined(width):
    shares = lax.axis_size("row") * lax.axis_size("col")
    square = lax.axis_size("row") == 4 and lax.axis_size("col") == 4
    return lax.axis_size("batch") == 2 and square and width == 4 * SHARE_ROWS and shares == SHARES


def backward_layer(delta, saved, modulation, weights, layer, tile):
    taps, qkv, decay_bias, proj, expand, shrink = weights
    (
        normal, inverse, hidden, sides, convolved, mixed, parts, attend, branch,
        normal2, inverse2, second, inner, active, outer,
    ) = saved
    rows, cols = tile
    items, cells = delta.shape[:2]
    width = proj.shape[0]
    heads = width // HD
    size = padded_width(width + 3 * heads)
    axis = "col" if layer % 2 == 0 else "row"
    mod = [modulation[:, k][:, None] for k in range(6)]
    over = lambda v: jnp.sum(v, axis=1)
    delta_gate2 = over(delta * outer)
    outer_low = gather_items((mod[5] * delta).astype(BFLOAT))
    grad_shrink = weight_grad(active, outer_low)
    inner_low = (matmul_back(outer_low, shrink) * gelu_slope(inner)).astype(BFLOAT)
    grad_expand = weight_grad(second, inner_low)
    delta_second = reduce_items(matmul_back(inner_low, expand))
    delta_shift2 = over(delta_second)
    delta_scale2 = over(delta_second * normal2)
    delta_middle = delta + normalize_back(delta_second * (1.0 + mod[4]), normal2, inverse2)
    delta_gate1 = over(delta_middle * branch)
    branch_low = gather_items((mod[2] * delta_middle).astype(BFLOAT))
    grad_proj = weight_grad(attend, branch_low)
    delta_attend = matmul_back(branch_low, proj).astype(BFLOAT)
    delta_parts = lines_out(delta_attend, axis)
    place = lax.axis_index(axis)
    projects = scan_call(
        scan_backward_kernel, place, list(parts) + delta_parts, 3 * size, rows, cols,
        layer % 2 == 0, width,
    )
    delta_project = lines_back(projects, axis)
    grad_qkv = weight_grad(mixed, delta_project)
    sums = (grad_shrink, grad_expand, grad_proj, grad_qkv)
    grad_decay_bias = jnp.sum(delta_project[:, :, width : width + heads].astype(FLOAT), axis=(0, 1))
    delta_mixed = reduce_items(matmul_back(delta_project, qkv)).reshape(convolved.shape)
    gate = jax.nn.sigmoid(convolved)
    delta_conv = (delta_mixed * gate * (1.0 + convolved * (1.0 - gate))).astype(BFLOAT)
    delta_sides = halo(delta_conv)
    delta_hidden, grad_taps = conv_backward(hidden, sides, delta_conv, delta_sides, taps)
    delta_hidden = delta_hidden.reshape(items, cells, D)
    delta_shift1 = over(delta_hidden)
    delta_scale1 = over(delta_hidden * normal)
    delta_tokens = delta_middle + normalize_back(delta_hidden * (1.0 + mod[1]), normal, inverse)
    delta_mod = jnp.stack(
        [delta_shift1, delta_scale1, delta_gate1, delta_shift2, delta_scale2, delta_gate2], axis=1
    )
    return delta_tokens, sums, (delta_mod, grad_taps, None, grad_decay_bias)


def sum_rows_here(grad):
    return lax.psum(grad.astype(BFLOAT), GRID_AXES).astype(FLOAT)


def sum_columns(grad):
    count = lax.axis_size("batch")
    low = grad.astype(BFLOAT).reshape((count, -1, grad.shape[1]))
    shares = lax.axis_size("row") * lax.axis_size("col")
    if count == 2 and low.shape[1] % shares == 0:
        share = lax.psum_scatter(low, GRID_AXES, scatter_dimension=1, tiled=True)
        place = lax.axis_index("batch")
        own = lax.dynamic_index_in_dim(share, place, 0, keepdims=False)
        other = swap(lax.dynamic_index_in_dim(share, 1 - place, 0, keepdims=False))
        both = jnp.stack([jnp.where(place == 0, own, other), jnp.where(place == 0, other, own)])
        return lax.all_gather(both, GRID_AXES, axis=1, tiled=True)
    total = lax.psum(low, GRID_AXES)
    return lax.all_to_all(total, "batch", 0, 0)


def ada_call(cond, mods, previous, layer, through):
    items, rows = cond.shape
    wide = mods.shape[1]
    block = 64
    previous = [] if previous is None else [previous]

    def body(columns, values, *refs):
        out = refs[-2]
        for at in range(0, wide, D):
            part = slice(at, at + D)
            total = columns[:, 0:1] * values[0:1, part]
            for item in range(1, items):
                total += columns[:, item : item + 1] * values[item : item + 1, part]
            out[0, :, part] = total

    count = len(previous)
    return pl.pallas_call(
        body,
        grid=(rows // block,),
        in_specs=[
            pl.BlockSpec((block, items), lambda i: (i, 0)),
            pl.BlockSpec((items, wide), lambda i: (0, 0)),
        ]
        + [ANYWHERE] * (count + 1),
        out_specs=[pl.BlockSpec((1, block, wide), lambda i: (layer, i, 0)), ANYWHERE],
        out_shape=[
            jax.ShapeDtypeStruct((LAYERS, rows, wide), FLOAT),
            jax.ShapeDtypeStruct(through.shape, through.dtype),
        ],
        input_output_aliases={2 + k: k for k in range(count)} | {2 + count: 1},
        cost_estimate=SMALL,
        compiler_params=params(),
    )(jnp.transpose(cond.astype(FLOAT)), mods, *previous, through)


SCHEDULE = {
    (1, "P1"): "aA1",
    (1, "P2"): "aB1rL1",
    (1, "P7"): "sC1sS1",
    (0, "P1"): "kC1sA0",
    (0, "P2"): "tS1kA0sB0",
    (0, "P3"): "gL1kB0",
    (0, "P4"): "tS1",
    (0, "P5"): "tC1tS1",
    (0, "P8"): "tC1tA0tS1sC0",
    (0, "P7"): "tC1tA0tB0kC0sS0",
}
TAIL = (
    "tA0tB0tS0",
    "mS1",
    "tB0tC0tS0",
    "tB0tC0tS0",
    "tC0tS0gL0",
    "fAB1",
    "mS0",
    "fC1",
    "fABC0",
)


SMALL_ROWS = 32


def join_smalls(mod_a, mod_b, grad_taps, grad_decay, grad_bias):
    heads = grad_decay.shape[0] // 2

    def body(_, ins, far, outs, scratch):
        out = outs[0]
        for i in range(ITEMS):
            out[6 * i : 6 * i + 2] = ins[0][i]
            out[6 * i + 2 : 6 * i + 6] = ins[1][i]
        out[12:21] = ins[2][...]
        out[21 : 21 + heads] = jnp.concatenate([ins[3][:heads], ins[3][heads:]], axis=1)
        bias = jnp.concatenate([ins[4][...], jnp.zeros((1, D - LANES), FLOAT)], axis=1)
        out[21 + heads : 22 + heads] = bias
        out[22 + heads :] = jnp.zeros((SMALL_ROWS - 22 - heads, D), FLOAT)

    return call(
        body, [((SMALL_ROWS, D), FLOAT)], [mod_a, mod_b, grad_taps, grad_decay, grad_bias]
    )[0]


def split_smalls(flat, items, heads, width):
    start = width - width // LANES * LANES
    decay = flat[21 : 21 + heads]
    return (
        flat[: items * 6].reshape(items, 6 * D),
        flat[12:21],
        jnp.concatenate([decay[:, :width], decay[:, width:]], axis=0),
        flat[21 + heads, start : start + heads],
    )


def general_forward_backward(
    tokens_in, cotangent, modulations, taps_all, qkv_weight, decay_weight, decay_bias,
    proj_weight, expand_weight, shrink_weight,
):
    count = lax.axis_size("batch")
    items, rows, cols = tokens_in.shape[:3]
    tile = (rows, cols)
    width = proj_weight.shape[1]
    weights = []
    for layer in range(LAYERS):
        qkv = fetch_columns(
            [head_columns(qkv_weight[layer], decay_weight[layer], g, width) for g in range(count)]
        )
        inner = expand_weight.shape[2] // count
        expand = fetch_columns(
            [expand_weight[layer][:, g * inner : (g + 1) * inner] for g in range(count)]
        )
        weights.append(
            (taps_all[layer], qkv, decay_bias[layer], proj_weight[layer], expand, shrink_weight[layer])
        )
    tokens = tokens_in.astype(FLOAT).reshape(items, rows * cols, D)
    stored = []
    for layer in range(LAYERS):
        tokens, saved = forward_layer(tokens, modulations[layer], weights[layer], layer, tile)
        stored.append(saved)
    delta = cotangent.astype(FLOAT).reshape(tokens.shape)
    bigs, smalls = [None] * LAYERS, [None] * LAYERS
    for layer in reversed(range(LAYERS)):
        delta, big, small = backward_layer(
            delta, stored[layer], modulations[layer], weights[layer], layer, tile
        )
        grad_shrink, grad_expand, grad_proj, grad_qkv = big
        bigs[layer] = (
            sum_rows_here(grad_shrink),
            sum_columns(grad_expand),
            sum_rows_here(grad_proj),
            sum_columns(grad_qkv),
        )
        smalls[layer] = tuple(
            None if part is None else lax.psum(part, GRID_AXES) for part in small
        )
    return tokens.astype(BFLOAT), delta.astype(BFLOAT), bigs, smalls


def per_device(
    tokens_in, timesteps, ada_weight, ada_bias, conv_taps, qkv_weight, decay_weight, decay_bias,
    proj_weight, expand_weight, shrink_weight, cotangent,
):
    count, place = lax.axis_size("batch"), lax.axis_index("batch")
    items, rows, cols = tokens_in.shape[:3]
    tile = (rows, cols)
    rows_here = ada_weight.shape[1]
    width = proj_weight.shape[1]
    heads = width // HD
    size = padded_width(width + 3 * heads)
    cond = jax.nn.silu(embed_steps(timesteps)).astype(BFLOAT)
    cond_slice = lax.dynamic_slice_in_dim(cond, place * rows_here, rows_here, 1)
    order = [0] if count != 2 else None
    if count == 2:
        cond_first = jnp.where(
            place == 0, cond_slice, jnp.concatenate([cond_slice[items:], cond_slice[:items]])
        )
    else:
        cond_first = cond_slice
    biases = gather_last(ada_bias).astype(FLOAT)
    taps_all = gather_last(conv_taps)
    weights, modulations = [], []
    partial = jnp.stack(
        [
            jnp.dot(cond_first, ada_weight[layer], preferred_element_type=FLOAT)
            for layer in range(LAYERS)
        ],
        axis=1,
    )
    if count == 2:
        total = partial[:items] + swap(partial[items:])
    else:
        total = lax.psum_scatter(partial, "batch", scatter_dimension=0, tiled=True)
    for layer in range(LAYERS):
        modulations.append((total[:, layer] + biases[layer]).reshape(items, 6, D))
    fast = pipelined(width) and count * items == 4 and tile == (8, 8)
    hidden_units = shrink_weight.shape[1]
    if fast:
        moving = {}
        upper_sums = Scattered()

        def act(names, through):
            names = [names[at : at + 3] for at in range(0, len(names), 3)]
            steps = [moving[name[1:]] for name in names if name[0] == "t"]
            through = tick(steps, through)
            for name in names:
                one = moving.get(name[1:])
                if name[0] == "s":
                    through = one.start(through)
                elif name[0] == "k":
                    through = one.second(through)
                elif name == "gL1":
                    upper_sums.gather(through)
                elif name == "gL0":
                    Gathered([moving[name] for name in ("C1", "A0", "B0", "C0")]).gather()
                elif name[0] == "a":
                    through = upper_sums.add(one, through)
                elif name[0] == "r":
                    upper_sums.reduce()
            return through

        def step(layer, point, fresh, through):
            for name, one in fresh.items():
                moving[name if len(name) == 2 else name + str(layer)] = one
                if name in "ABC":
                    one.offload = True
            return act(SCHEDULE.get((layer, point), ""), through)

        pair = Pair(
            dict(
                qkv=qkv_weight, decay=decay_weight, decay_bias=decay_bias, proj=proj_weight,
                expand=expand_weight, shrink=shrink_weight,
            ),
            modulations,
            taps_all,
            tile,
        )
        block_out, through = pair_forward_backward(pair, tokens_in, cotangent, step)
        shapes = [
            (LAYERS, hidden_units, D),
            (LAYERS, rows_here, expand_weight.shape[2]),
            (LAYERS, rows_here, 3 * D),
            (LAYERS, width, D),
        ]
        finished = None
        grad_ada = None
        smalls = [None] * LAYERS
        for names in TAIL:
            if names[0] == "f":
                kinds = names[1:-1]
                layer = int(names[-1])
                made, through = Gathered.finish(
                    [moving[kind + names[-1]] for kind in kinds], kinds,
                    None if layer else finished, layer, shapes, through,
                )
                finished = (finished or {}) | made
            elif names[0] == "m":
                layer = int(names[2])
                smalls[layer] = list(split_smalls(moving[names[1:]].keep, items, heads, width))
                mods = gather_items(smalls[layer][0])
                smalls[layer][0] = mods
                grad_ada, through = ada_call(cond_first, mods, grad_ada, layer, through)
            else:
                through = act(names, through)
        grad_tokens = through
    else:
        block_out, grad_tokens, bigs, smalls = general_forward_backward(
            tokens_in, cotangent, modulations, taps_all, qkv_weight, decay_weight, decay_bias,
            proj_weight, expand_weight, shrink_weight,
        )
    block_out = block_out.reshape(tokens_in.shape)
    grad_tokens = grad_tokens.reshape(tokens_in.shape)
    delta_mods, taps_grads, bias_grads = (
        jnp.stack([smalls[layer][k] for layer in range(LAYERS)]) for k in (0, 1, 3)
    )
    if fast:
        every_mod = delta_mods.transpose(1, 0, 2)
    else:
        every_mod = gather_items(delta_mods.transpose(1, 0, 2, 3)).reshape(
            count * items, LAYERS, 6 * D
        )
    if count == 2:
        taps_every = taps_grads + swap(taps_grads)
    else:
        taps_every = lax.psum(taps_grads, "batch")
    grad_taps = lax.dynamic_slice_in_dim(taps_every, place * width, width, 2)
    if not fast:
        grad_ada = jnp.zeros((LAYERS, rows_here, 6 * D), FLOAT)
        for item in range(count * items):
            grad_ada += (
                cond_first[item].astype(FLOAT)[None, :, None] * every_mod[item][:, None, :]
            )
    bias_width = ada_bias.shape[1]
    grad_ada_bias = lax.dynamic_slice_in_dim(
        jnp.sum(every_mod, axis=0), place * bias_width, bias_width, 1
    )
    if fast:
        grad_shrink, grad_expand, grad_qkv, grad_proj = (finished[k] for k in range(4))
        grad_decay = jnp.stack([jnp.transpose(smalls[layer][2]) for layer in range(LAYERS)])
    else:
        stack = lambda k: jnp.stack([bigs[layer][k] for layer in range(LAYERS)])
        grad_shrink, grad_proj = stack(0), stack(2)
        expand_parts, qkv_parts = stack(1), stack(3)
        grad_expand = jnp.concatenate([expand_parts[:, g] for g in range(count)], 2).astype(FLOAT)
        grad_qkv = jnp.concatenate(
            [
                qkv_parts[:, g, :, j * size : j * size + width]
                for j in range(3)
                for g in range(count)
            ],
            axis=2,
        ).astype(FLOAT)
        grad_decay = jnp.concatenate(
            [qkv_parts[:, g, :, width : width + heads] for g in range(count)], axis=2
        ).astype(FLOAT)
    return (
        block_out,
        grad_tokens,
        grad_ada,
        grad_ada_bias,
        grad_taps,
        grad_qkv,
        grad_decay,
        bias_grads,
        grad_proj,
        grad_expand,
        grad_shrink,
    )


def solution(mesh):
    return jax.shard_map(
        per_device,
        mesh=mesh,
        in_specs=(
            P("batch", "row", "col", None),
            P(),
            P(None, "batch", None),
            P(None, "batch"),
            P(None, None, "batch"),
            P(None, "batch", None),
            P(None, "batch", None),
            P(None, "batch"),
            P(None, "batch", None),
            P(None, "batch", None),
            P(None, "batch", None),
            P("batch", "row", "col", None),
        ),
        out_specs=(
            P("batch", "row", "col", None),
            P("batch", "row", "col", None),
            P(None, "batch", None),
            P(None, "batch"),
            P(None, None, "batch"),
            P(None, "batch", None),
            P(None, "batch", None),
            P(None, "batch"),
            P(None, "batch", None),
            P(None, "batch", None),
            P(None, "batch", None),
        ),
        check_vma=False,
    )
```

```python
import jax
import jax.numpy as jnp
from jax import lax
from jax.experimental import pallas as pl
from jax.experimental.pallas import tpu as pltpu
from jax.sharding import PartitionSpec as P

D = 1152
H = 16
HD = 72
LAYERS = 2
EPS = 1e-06
ACCURATE = lax.Precision.HIGHEST
FLOAT = jnp.float32
BFLOAT = jnp.bfloat16
LANES = 128
VMEM_LIMIT = 48 * 1024 * 1024
GRID_AXES = ("row", "col")
SMALL = pl.CostEstimate(flops=1, bytes_accessed=1, transcendentals=0)


def params():
    return pltpu.CompilerParams(vmem_limit_bytes=VMEM_LIMIT)


def padded_width(width):
    return -(-width // LANES) * LANES


def swap(value, axis="batch", bit=1):
    count = lax.axis_size(axis)
    return lax.ppermute(value, axis, [(i, i ^ bit) for i in range(count)])


def gather_items(own):
    if lax.axis_size("batch") == 2:
        return jnp.concatenate([own, swap(own)], axis=0)
    return lax.all_gather(own, "batch", axis=0, tiled=True)


def gather_last(own):
    if lax.axis_size("batch") == 2:
        other = swap(own)
        first = lax.axis_index("batch") == 0
        return jnp.concatenate([jnp.where(first, own, other), jnp.where(first, other, own)], -1)
    return lax.all_gather(own, "batch", axis=own.ndim - 1, tiled=True)


def reduce_items(partial):
    if lax.axis_size("batch") == 2:
        items = partial.shape[0] // 2
        return partial[:items] + swap(partial[items:].astype(BFLOAT)).astype(FLOAT)
    return lax.psum_scatter(partial, "batch", scatter_dimension=0, tiled=True)


def lines_out(values, axis):
    count, place = lax.axis_size(axis), lax.axis_index(axis)
    groups = values.reshape((count, -1) + values.shape[1:])
    blocks = []
    for k in range(count):
        block = lax.dynamic_index_in_dim(groups, place ^ k, 0, keepdims=False)
        blocks.append(block if k == 0 else swap(block, axis, k))
    return blocks


def lines_back(blocks, axis):
    count, place = lax.axis_size(axis), lax.axis_index(axis)
    received = [blocks[0]] + [swap(blocks[k], axis, k) for k in range(1, count)]
    stacked = jnp.stack(received)
    return jnp.concatenate(
        [lax.dynamic_index_in_dim(stacked, place ^ j, 0, keepdims=False) for j in range(count)]
    )


def halo(cells):
    return halo_edges([cells[:, 0], cells[:, -1], cells[:, :, 0], cells[:, :, -1]])


def beside(cells, sides, item):
    top, bottom, left, right = sides
    count, width = cells.shape[1], cells.shape[2]
    lefts, rights = left[item].astype(FLOAT), right[item].astype(FLOAT)
    at = lax.broadcasted_iota(jnp.int32, (width, cells.shape[3]), 0)
    rows = []
    for row in range(count + 2):
        if row == 0:
            here = top[item]
        elif row == count + 1:
            here = bottom[item]
        else:
            here = cells[item, row - 1]
        here = here.astype(FLOAT)
        before = jnp.where(at == 0, lefts[row : row + 1], pltpu.roll(here, 1, 0))
        after = jnp.where(at == width - 1, rights[row : row + 1], pltpu.roll(here, width - 1, 0))
        rows.append((before, here, after))
    return rows


def conv_forward_kernel(cells, *refs):
    sides, (taps, convolved, mixed) = refs[:4], refs[4:]
    weights = taps[...].astype(FLOAT)
    for item in range(cells.shape[0]):
        rows = beside(cells, sides, item)
        for row in range(cells.shape[1]):
            total = jnp.zeros(rows[0][1].shape, FLOAT)
            for a in range(3):
                for b in range(3):
                    total += weights[3 * a + b : 3 * a + b + 1] * rows[row + a][b]
            convolved[item, row] = total
            mixed[item, row] = (total * jax.nn.sigmoid(total)).astype(BFLOAT)


def conv_backward_kernel(cells, *refs):
    sides, delta, delta_sides, (taps, hidden, grads) = refs[:4], refs[4], refs[5:9], refs[9:]
    weights = taps[...].astype(FLOAT)
    sums = [jnp.zeros((cells.shape[2], cells.shape[3]), FLOAT) for _ in range(9)]
    for item in range(cells.shape[0]):
        rows = beside(cells, sides, item)
        for row in range(cells.shape[1]):
            here = delta[item, row].astype(FLOAT)
            for a in range(3):
                for b in range(3):
                    sums[3 * a + b] += rows[row + a][b] * here
        rows = beside(delta, delta_sides, item)
        for row in range(cells.shape[1]):
            total = jnp.zeros(rows[0][1].shape, FLOAT)
            for a in range(3):
                for b in range(3):
                    total += weights[3 * a + b : 3 * a + b + 1] * rows[row + 2 - a][2 - b]
            hidden[item, row] = total
    for tap in range(9):
        grads[tap : tap + 1] = jnp.sum(sums[tap], axis=0, keepdims=True)


def conv_specs(items, rows, cols, block):
    cells = pl.BlockSpec((items, rows, cols, block), lambda i: (0, 0, 0, i))
    side = lambda size: pl.BlockSpec((items, size, block), lambda i: (0, 0, i))
    taps = pl.BlockSpec((9, block), lambda i: (0, i))
    return [cells] + [side(size) for size in (cols, cols, rows + 2, rows + 2)], taps


def conv_forward(cells, sides, taps):
    items, rows, cols, width = cells.shape
    block = 3 * LANES
    specs, tap_spec = conv_specs(items, rows, cols, block)
    return pl.pallas_call(
        conv_forward_kernel,
        grid=(width // block,),
        in_specs=specs + [tap_spec],
        out_specs=[specs[0], specs[0]],
        out_shape=[
            jax.ShapeDtypeStruct(cells.shape, FLOAT),
            jax.ShapeDtypeStruct(cells.shape, BFLOAT),
        ],
        cost_estimate=SMALL,
        compiler_params=params(),
    )(cells, *sides, taps)


def conv_backward(cells, sides, delta, delta_sides, taps):
    items, rows, cols, width = cells.shape
    block = 3 * LANES
    specs, tap_spec = conv_specs(items, rows, cols, block)
    return pl.pallas_call(
        conv_backward_kernel,
        grid=(width // block,),
        in_specs=specs + specs + [tap_spec],
        out_specs=[specs[0], tap_spec],
        out_shape=[
            jax.ShapeDtypeStruct(cells.shape, FLOAT),
            jax.ShapeDtypeStruct((9, width), FLOAT),
        ],
        cost_estimate=SMALL,
        compiler_params=params(),
    )(cells, *sides, delta, *delta_sides, taps)


def scan_mask(place, rows, cols, along_cols, blocks):
    cells = rows * cols
    shape = (blocks * cells, blocks * cells)

    def line_and_position(index):
        block = index // cells
        inside = index - block * cells
        row = inside // cols
        col = inside - row * cols
        source = place ^ block
        if along_cols:
            return row, source * cols + col
        return col, source * rows + row

    line_t, at_t = line_and_position(lax.broadcasted_iota(jnp.int32, shape, 0))
    line_s, at_s = line_and_position(lax.broadcasted_iota(jnp.int32, shape, 1))
    return (line_t == line_s) & (at_s <= at_t)


def dot(left, right, contract=((1,), (0,)), precision=None):
    return lax.dot_general(
        left, right, (contract, ((), ())), precision=precision, preferred_element_type=FLOAT
    )


class Scan:
    def __init__(self, parts, mask, width):
        self.width = width
        self.padded = padded_width(width + 3 * (width // HD))
        self.heads = width // HD
        joined = jnp.concatenate([part[0] for part in parts], axis=0)
        size = self.padded
        self.queries = joined[:, :size]
        self.keys = joined[:, size : 2 * size]
        self.values = joined[:, 2 * size :]
        self.start = width - width // LANES * LANES
        self.block = width // LANES * LANES
        extra = self.queries[:, self.block : self.block + LANES].astype(FLOAT)
        logit = (
            extra
            + pltpu.roll(extra, LANES - self.heads, 1)
            + pltpu.roll(extra, LANES - 2 * self.heads, 1)
        )
        self.lane = lax.broadcasted_iota(jnp.int32, extra.shape, 1)
        self.is_logit = (self.lane >= self.start) & (self.lane < self.start + self.heads)
        self.logit = jnp.where(self.is_logit, logit, 0.0)
        small = jnp.exp(-jnp.abs(self.logit))
        logdecay = jnp.where(self.is_logit, jnp.minimum(self.logit, 0.0) - jnp.log(1.0 + small), 0.0)
        self.lower = jnp.where(mask, 1.0, 0.0).astype(FLOAT)
        self.mask = mask
        self.cumul = dot(self.lower, logdecay, precision=ACCURATE)
        self.cumul_rows = jnp.transpose(self.cumul)
        self.feature = lax.broadcasted_iota(jnp.int32, (1, size), 1)

    def of_head(self, head, array):
        inside = (self.feature >= head * HD) & (self.feature < head * HD + HD)
        return jnp.where(inside, array, jnp.zeros_like(array))

    def weights(self, head):
        at = self.start + head
        gap = self.cumul[:, at : at + 1] - self.cumul_rows[at : at + 1, :]
        return jnp.where(self.mask, jnp.exp(jnp.minimum(gap, 0.0)), 0.0)


SCALE = HD ** (-0.5)


def scan_forward_kernel(place, *refs, rows, cols, along_cols, width):
    count = len(refs) // 2
    parts, outs = refs[:count], refs[count:]
    mask = scan_mask(place[0], rows, cols, along_cols, count)
    scan = Scan(parts, mask, width)
    total = jnp.zeros(scan.queries.shape, FLOAT)
    for head in range(scan.heads):
        scores = dot(scan.of_head(head, scan.queries), scan.keys, ((1,), (1,))) * SCALE
        scores = (scores * scan.weights(head)).astype(BFLOAT)
        total += dot(scores, scan.of_head(head, scan.values))
    cells = rows * cols
    low = total.astype(BFLOAT)
    for k in range(count):
        outs[k][0] = low[k * cells : (k + 1) * cells, :width]


def scan_backward_kernel(place, *refs, rows, cols, along_cols, width):
    count = len(refs) // 3
    parts, deltas, outs = refs[:count], refs[count : 2 * count], refs[2 * count :]
    mask = scan_mask(place[0], rows, cols, along_cols, count)
    scan = Scan(parts, mask, width)
    joined = jnp.concatenate([part[0] for part in deltas], axis=0)
    short = scan.padded - width
    if short:
        joined = jnp.concatenate([joined, jnp.zeros((joined.shape[0], short), BFLOAT)], axis=1)
    shape = scan.queries.shape
    delta_query = jnp.zeros(shape, FLOAT)
    delta_key = jnp.zeros(shape, FLOAT)
    delta_value = jnp.zeros(shape, FLOAT)
    gap_rows = jnp.zeros(scan.lane.shape, FLOAT)
    gap_cols = jnp.zeros(scan.cumul_rows.shape, FLOAT)
    place_row = lax.broadcasted_iota(jnp.int32, gap_cols.shape, 0)
    for head in range(scan.heads):
        query = scan.of_head(head, scan.queries)
        delta = scan.of_head(head, joined)
        weights = scan.weights(head)
        scores = dot(query, scan.keys, ((1,), (1,))) * SCALE * weights
        delta_scores = dot(delta, scan.values, ((1,), (1,)))
        gap = delta_scores * scores
        at = scan.start + head
        gap_rows += jnp.where(scan.lane == at, jnp.sum(gap, axis=1, keepdims=True), 0.0)
        gap_cols += jnp.where(place_row == at, jnp.sum(gap, axis=0, keepdims=True), 0.0)
        inner = (delta_scores * weights * SCALE).astype(BFLOAT)
        delta_query += dot(inner, scan.of_head(head, scan.keys))
        delta_key += dot(inner, query, ((0,), (0,)))
        delta_value += dot(scores.astype(BFLOAT), delta, ((0,), (0,)))
    delta_cumul = gap_rows - jnp.transpose(gap_cols)
    delta_decay = dot(scan.lower, delta_cumul, ((0,), (0,)), ACCURATE)
    small = jnp.exp(-jnp.abs(scan.logit))
    keep = jnp.where(scan.logit >= 0.0, small, 1.0) / (1.0 + small)
    delta_logit = delta_decay * keep
    block = scan.block
    mixed = jnp.where(scan.is_logit, delta_logit, delta_query[:, block : block + LANES])
    pieces = [delta_query[:, :block]] if block else []
    pieces.append(mixed)
    if block + LANES < scan.padded:
        pieces.append(delta_query[:, block + LANES :])
    whole = jnp.concatenate(pieces + [delta_key, delta_value], axis=1).astype(BFLOAT)
    cells = rows * cols
    for k in range(count):
        outs[k][0] = whole[k * cells : (k + 1) * cells]


def scan_call(kernel, place, inputs, out_width, rows, cols, along_cols, width):
    count = lax.axis_size("col") if along_cols else lax.axis_size("row")
    items, cells = inputs[0].shape[:2]
    spec = lambda last: pl.BlockSpec((1, cells, last), lambda i, place: (i, 0, 0))

    def body(*refs):
        kernel(*refs, rows=rows, cols=cols, along_cols=along_cols, width=width)

    return pl.pallas_call(
        body,
        grid_spec=pltpu.PrefetchScalarGridSpec(
            num_scalar_prefetch=1,
            grid=(items,),
            in_specs=[spec(v.shape[2]) for v in inputs],
            out_specs=[spec(out_width)] * count,
        ),
        out_shape=[jax.ShapeDtypeStruct((items, cells, out_width), BFLOAT)] * count,
        cost_estimate=SMALL,
        compiler_params=params(),
    )(place.reshape(1).astype(jnp.int32), *inputs)


def pick(values, index):
    chosen = values[0]
    for k in range(1, len(values)):
        chosen = jnp.where(index == k, values[k], chosen)
    return chosen


def fetch_columns(pieces):
    count, place = lax.axis_size("batch"), lax.axis_index("batch")
    if count != 2:
        stacked = jnp.stack(pieces)
        return lax.all_to_all(stacked, "batch", 0, 0).reshape((-1,) + pieces[0].shape[1:])
    own, other = pick(pieces, place), pick(pieces, 1 - place)
    rows = own.shape[0]
    half = rows // 2
    core = lax.axis_index("row") % 2
    first = swap(lax.dynamic_slice_in_dim(other, core * half, half, 0))
    second = swap(first, "row", 1)
    whole = jnp.zeros((2 * rows,) + own.shape[1:], own.dtype)
    whole = lax.dynamic_update_slice_in_dim(whole, own, place * rows, 0)
    base = (1 - place) * rows
    whole = lax.dynamic_update_slice_in_dim(whole, first, base + core * half, 0)
    return lax.dynamic_update_slice_in_dim(whole, second, base + (1 - core) * half, 0)


def head_columns(qkv, decay, group, width):
    size = padded_width(width + 3 * (width // HD))
    heads = width // HD
    parts = []
    for j in range(3):
        piece = qkv[:, j * D + group * width : j * D + (group + 1) * width]
        filled = width
        parts.append(piece)
        if j == 0:
            parts.append(decay[:, group * heads : (group + 1) * heads])
            filled += heads
        if size > filled:
            parts.append(jnp.zeros((qkv.shape[0], size - filled), qkv.dtype))
    return jnp.concatenate(parts, axis=1)


def normalize(values):
    center = values - jnp.mean(values, axis=-1, keepdims=True)
    inverse = lax.rsqrt(jnp.mean(center * center, axis=-1, keepdims=True) + EPS)
    return center * inverse, inverse


def normalize_back(delta, normal, inverse):
    first = jnp.mean(delta, axis=-1, keepdims=True)
    second = jnp.mean(delta * normal, axis=-1, keepdims=True)
    return inverse * (delta - first - normal * second)


def embed_steps(steps):
    half = D // 2
    freqs = jnp.exp(-jnp.log(10000.0) * jnp.arange(half, dtype=FLOAT) / half)
    angles = steps.astype(FLOAT)[:, None] * freqs[None, :]
    return jnp.concatenate([jnp.cos(angles), jnp.sin(angles)], axis=1)


GELU_A = 0.7978845608028654
GELU_B = 0.044715


def gelu(z):
    return 0.5 * z * (1.0 + jnp.tanh(GELU_A * (z + GELU_B * z * z * z)))


def gelu_slope(z):
    t = jnp.tanh(GELU_A * (z + GELU_B * z * z * z))
    return 0.5 * (1.0 + t) + 0.5 * z * (1.0 - t * t) * GELU_A * (1.0 + 3.0 * GELU_B * z * z)


def matmul(left, right):
    return lax.dot_general(left, right, (((2,), (0,)), ((), ())), preferred_element_type=FLOAT)


def matmul_back(left, right):
    return lax.dot_general(left, right, (((2,), (1,)), ((), ())), preferred_element_type=FLOAT)


def weight_grad(left, right):
    return lax.dot_general(
        left, right, (((0, 1), (0, 1)), ((), ())), preferred_element_type=FLOAT
    )


SHARES = 16
SHARE_ROWS = 144
STAGES = (("row", 1), ("row", 2), ("col", 1), ("col", 2))


def share_place(stages):
    number = jnp.int32(0)
    for axis, bit in stages:
        number = 2 * number + (lax.axis_index(axis) // bit) % 2
    return number.reshape(1).astype(jnp.int32)


def product(act, delta):
    return lax.dot_general(act, delta, (((1,), (0,)), ((), ())), preferred_element_type=FLOAT)


def grad_send_kernel(place, act, delta, out):
    out[0] = product(act[0], delta[0]).astype(BFLOAT)


def grad_keep_kernel(place, act, delta, received, send, keep):
    value = (product(act[0], delta[0]) + received[0].astype(FLOAT)).astype(BFLOAT)
    first = pl.program_id(0) < SHARES // 4

    @pl.when(first)
    def _():
        send[0] = value

    @pl.when(jnp.logical_not(first))
    def _():
        keep[0] = value


class GradSum:
    def __init__(self, act, delta, act_index, delta_index, stages):
        self.act, self.delta, self.stages = act, delta, stages
        self.act_index, self.delta_index = act_index, delta_index
        self.place = share_place(stages)

    def call(self, kernel, position, extra, extra_specs, out_specs, out_shapes, through):
        tokens = self.act.shape[2]
        act_spec = pl.BlockSpec(
            (1, SHARE_ROWS, tokens), lambda i, m: self.act_index(position(i) ^ m[0])
        )
        delta_spec = pl.BlockSpec(
            (1, tokens, D), lambda i, m: self.delta_index(position(i) ^ m[0])
        )
        inputs = 3 + len(extra)

        def body(*refs):
            kernel(*refs[:inputs], *refs[inputs + 1 : -1])

        return pl.pallas_call(
            body,
            grid_spec=pltpu.PrefetchScalarGridSpec(
                num_scalar_prefetch=1,
                grid=(SHARES // 2,),
                in_specs=[act_spec, delta_spec] + extra_specs + [ANYWHERE],
                out_specs=out_specs + [ANYWHERE],
            ),
            out_shape=out_shapes + [jax.ShapeDtypeStruct(through.shape, through.dtype)],
            input_output_aliases={inputs: len(out_shapes)},
            cost_estimate=SMALL,
            compiler_params=params(),
        )(self.place, self.act, self.delta, *extra, through)

    def start(self, through):
        half = SHARES // 2
        block = (1, SHARE_ROWS, D)
        send, through = self.call(
            grad_send_kernel,
            lambda i: i + half,
            [],
            [],
            [pl.BlockSpec(block, lambda i, m: (i, 0, 0))],
            [jax.ShapeDtypeStruct((half, SHARE_ROWS, D), BFLOAT)],
            through,
        )
        self.flight = self.move(send, 0)
        return through

    def move(self, value, stage):
        axis, bit = self.stages[stage]
        return swap(value, axis, bit)

    def second(self, through):
        quarter = SHARES // 4
        block = (1, SHARE_ROWS, D)
        position = lambda i: i ^ quarter
        send, self.keep, through = self.call(
            grad_keep_kernel,
            position,
            [self.flight],
            [pl.BlockSpec(block, lambda i, m: (position(i), 0, 0))],
            [
                pl.BlockSpec(block, lambda i, m: (jnp.minimum(i, quarter - 1), 0, 0)),
                pl.BlockSpec(block, lambda i, m: (jnp.maximum(i - quarter, 0), 0, 0)),
            ],
            [jax.ShapeDtypeStruct((quarter, SHARE_ROWS, D), BFLOAT)] * 2,
            through,
        )
        self.flight = self.move(send, 1)
        self.state = 0
        return through

    works = ("halve", "halve", "add", "join", "join", "pass")
    own_state = 3
    offload = False

    def advanced(self, outs):
        work = self.works[self.state]
        self.state += 1
        if work == "pass":
            self.keep, self.flight = outs
            self.pieces = [self.keep, self.flight]
            self.pieces += [self.move(piece, 0) for piece in self.pieces]
            return
        self.keep = outs[0]
        if not (self.offload and self.state == self.own_state):
            self.flight = self.onward(self.state, outs[-1])

    def onward(self, state, value):
        return self.move(value, (None, 2, 3, 3, 2, 1)[state])

    def done(self):
        return self.state == len(self.works)


class CrossGradSum(GradSum):
    works = ("halve", "halve", "add", "take", "join", "join", "pass")
    own_state = 4

    def onward(self, state, value):
        if state == 3:
            return self.cross(value)
        return self.move(value, (None, 2, 3, None, 3, 2, 1)[state])

    def cross(self, value):
        rows, cols = lax.axis_size("row"), lax.axis_size("col")
        pairs = []
        for x in range(2):
            for r in range(rows):
                for z in range(cols):
                    stays = r % 2 == x
                    to_x, to_r = (x, r) if stays else (1 - x, r ^ 1)
                    pairs.append(((x * rows + r) * cols + z, (to_x * rows + to_r) * cols + z))
        return lax.ppermute(value, ("batch", "row", "col"), pairs)


class Gathered:
    def __init__(self, sums):
        self.sums = sums

    def gather(self):
        self.collect(jnp.concatenate([one.keep for one in self.sums]))

    def collect(self, shares):
        whole = lax.all_gather(shares, GRID_AXES)
        for slot, one in enumerate(self.sums):
            one.whole, one.slot = whole, slot

    @staticmethod
    def finish(sums, kinds, previous, layer, shapes, through):
        block = (1, SHARE_ROWS, D)
        scalar = lax.axis_index("batch").reshape(1).astype(jnp.int32)

        def source(slot):
            def index(i, m):
                core, y, low, high = i // 8, i // 4 % 2, i // 2 % 2, i % 2
                return ((y * 2 + core) * 4 + high * 2 + low, slot, 0, 0)

            return pl.BlockSpec((None,) + block, index)

        def expand(i, m):
            own = jnp.where(i // 8 == m[0], m[0], 1 - m[0])
            return (layer, i % 4, own * 2 + i // 4 % 2)

        indices = (
            lambda i, m: (layer, i, 0),
            expand,
            lambda i, m: (0, i // 4, jnp.minimum(i % 4, 2)),
            lambda i, m: (0, i // 4, 0),
        )
        blocks = (block, block, (LAYERS,) + block[1:], (LAYERS,) + block[1:])
        targets = [k for kind in kinds[:3] for k in ((0,), (1,), (2, 3))["ABC".index(kind)]]
        kept = [k for k in targets if previous and k in previous]
        earlier = [previous[k] for k in kept]
        count, outs, given = len(earlier), len(targets), len(sums)

        def body(m, *refs):
            where = dict(zip(targets, refs[-1 - outs : -1]))
            last = pl.program_id(0) % 4 == 3
            done = 0
            for kind, ref in zip(kinds, refs):
                if kind != "C":
                    where["AB".index(kind)][0] = ref[0].astype(FLOAT)
                    continue

                at, done = done, done + 1

                @pl.when(last)
                def _(ref=ref, at=at):
                    where[3][at] = ref[0].astype(FLOAT)

                @pl.when(jnp.logical_not(last))
                def _(ref=ref, at=at):
                    where[2][at] = ref[0].astype(FLOAT)

        *results, through = pl.pallas_call(
            body,
            grid_spec=pltpu.PrefetchScalarGridSpec(
                num_scalar_prefetch=1,
                grid=(SHARES,),
                in_specs=[source(one.slot) for one in sums] + [ANYWHERE] * (count + 1),
                out_specs=[pl.BlockSpec(blocks[k], indices[k]) for k in targets] + [ANYWHERE],
            ),
            out_shape=[jax.ShapeDtypeStruct(shapes[k], FLOAT) for k in targets]
            + [jax.ShapeDtypeStruct(through.shape, through.dtype)],
            input_output_aliases={1 + given + j: targets.index(k) for j, k in enumerate(kept)}
            | {1 + given + count: outs},
            cost_estimate=SMALL,
            compiler_params=params(),
        )(scalar, *[one.whole for one in sums], *earlier, through)
        return dict(zip(targets, results)), through


class Scattered(Gathered):
    def __init__(self):
        self.sums, self.group, self.shares = [], [], []

    def add(self, one, through):
        slot, tokens, dim = len(self.group), one.act.shape[2], len(self.shares) % 2
        one.offload = True
        earlier = [self.buffer] if slot else []
        self.sums.append(one)
        self.group.append(one)
        count = len(earlier)
        width = 1 if dim else 2
        place = lambda d: (slot, d, 0, 0) if dim else (d, slot, 0, 0)
        shape = (width, SHARES) if dim else (SHARES, width)

        def share(d):
            row, col = d // 4, d % 4
            return row % 2 * 8 + row // 2 * 4 + col % 2 * 2 + col // 2

        def body(act, delta, *refs):
            refs[count + 1][0, 0] = product(act[0], delta[0]).astype(BFLOAT)

        self.buffer, through = pl.pallas_call(
            body,
            grid=(SHARES,),
            in_specs=[
                pl.BlockSpec((1, SHARE_ROWS, tokens), lambda d: one.act_index(share(d))),
                pl.BlockSpec((1, tokens, D), lambda d: one.delta_index(share(d))),
            ]
            + [ANYWHERE] * (count + 1),
            out_specs=[pl.BlockSpec((1, 1, SHARE_ROWS, D), place), ANYWHERE],
            out_shape=[
                jax.ShapeDtypeStruct(shape + (SHARE_ROWS, D), BFLOAT),
                jax.ShapeDtypeStruct(through.shape, through.dtype),
            ],
            input_output_aliases={2 + k: k for k in range(count)} | {2 + count: 1},
            cost_estimate=SMALL,
            compiler_params=params(),
        )(one.act, one.delta, *earlier, through)
        return through

    def reduce(self):
        dim = len(self.shares) % 2
        summed = lax.psum_scatter(self.buffer, GRID_AXES, scatter_dimension=dim, tiled=True)
        self.shares.append(summed.reshape(-1, SHARE_ROWS, D))
        self.group = []

    def gather(self, after):
        shares = passed_by(self.shares, [after])
        shares = [part[slot] for part in shares for slot in range(part.shape[0])]
        for slot, one in enumerate(self.sums):
            if isinstance(one, CrossGradSum):
                shares[slot] = one.cross(shares[slot])
        self.collect(jnp.stack(shares))


class SmallSum:
    works = ("sum",) * 4

    def __init__(self, value):
        self.value, self.state = value, 0

    def start(self, through):
        self.keep, self.flight = self.value, self.move(0, self.value)
        return through

    def move(self, stage, value):
        return swap(value, *STAGES[stage])

    def advanced(self, outs):
        self.state += 1
        (self.keep,) = outs
        self.flight = None if self.done() else self.move(self.state, self.keep)

    def done(self):
        return self.state == len(self.works)


def tick_kernel(*refs, works):
    at, out = 0, 2 * len(works)
    for work in works:
        keep, flight = refs[at], refs[at + 1]
        at += 2
        count = keep.shape[0]
        if work == "sum":
            refs[out][...] = keep[...] + flight[...]
            out += 1
            continue
        if work == "join":
            refs[out][:count] = keep[...]
            refs[out][count:] = flight[...]
            out += 1
            continue
        for row in range(count):
            value = (keep[row].astype(FLOAT) + flight[row].astype(FLOAT)).astype(BFLOAT)
            if work == "add":
                refs[out][row] = value
            elif row < count // 2:
                refs[out][row] = value
            else:
                refs[out + 1][row - count // 2] = value
        out += 1 if work == "add" else 2


def tick(sums, through):
    if not sums:
        return through
    light = ("pass", "take")
    working = [one for one in sums if one.works[one.state] not in light]
    passing = [one for one in sums if one.works[one.state] in light]
    operands, shapes, counts, works = [], [], [], []
    for one in working:
        operands += [one.keep, one.flight]
        work, count = one.works[one.state], one.keep.shape[0]
        works.append(work)
        sizes = {"halve": [count // 2] * 2, "join": [2 * count]}.get(work, [count])
        counts.append(len(sizes))
        shapes += [
            jax.ShapeDtypeStruct((k,) + one.keep.shape[1:], one.keep.dtype) for k in sizes
        ]
    kept = lambda one: [one.flight] if one.works[one.state] == "take" else [one.keep, one.flight]
    passed = [value for one in passing for value in kept(one)] + [through]

    def body(*refs):
        ins, outs = refs[: len(operands)], refs[len(operands) + len(passed) :]
        tick_kernel(*ins, *outs, works=works)

    outs = pl.pallas_call(
        body,
        in_specs=[WHOLE] * len(operands) + [ANYWHERE] * len(passed),
        out_specs=[WHOLE] * len(shapes) + [ANYWHERE] * len(passed),
        out_shape=shapes + [jax.ShapeDtypeStruct(v.shape, v.dtype) for v in passed],
        input_output_aliases={
            len(operands) + k: len(shapes) + k for k in range(len(passed))
        },
        cost_estimate=SMALL,
        compiler_params=params(),
    )(*operands, *passed)
    at = 0
    for one, count in zip(working, counts):
        one.advanced(outs[at : at + count])
        at += count
    for one in passing:
        count = len(kept(one))
        one.advanced(outs[at : at + count])
        at += count
    return outs[-1]


def sum_small(value):
    for axis, bit in STAGES:
        value = value + swap(value, axis, bit)
    return value


def shrink_sum(act, outer_low):
    return GradSum(act[None], outer_low[None], lambda s: (0, s, 0), lambda s: (0, 0, 0), STAGES)


def expand_sum(act, inner_low):
    return CrossGradSum(
        act[None],
        inner_low[None],
        lambda s: (0, s // 8 * 4 + s % 4, 0),
        lambda s: (0, 0, s // 4 % 2),
        STAGES,
    )


def mixer_delta(own, other, branch, branch_other, places, width, size):
    tokens = own.shape[0]
    block = tokens // 4
    heads = width // HD

    def body(places, mine, theirs, low, low_other, out, logits):
        first = places[0] == 0
        values = mine[...].astype(FLOAT), theirs[...].astype(FLOAT)
        left = jnp.where(first, values[0], values[1])
        right = jnp.where(first, values[1], values[0])
        for j in range(3):
            part = slice(j * size, j * size + width)
            out[:, j * D : (j + 1) * D] = jnp.concatenate(
                [left[:, part], right[:, part]], axis=1
            ).astype(BFLOAT)
        half = pl.program_id(0) < 2

        @pl.when(half)
        def _():
            out[:, 3 * D :] = low[...]

        @pl.when(jnp.logical_not(half))
        def _():
            out[:, 3 * D :] = low_other[...]

        part = slice(width, width + heads)
        rest = jnp.zeros((block, LANES - 2 * heads), FLOAT)
        logits[...] = jnp.concatenate([left[:, part], right[:, part], rest], axis=1).astype(BFLOAT)

    return pl.pallas_call(
        body,
        grid_spec=pltpu.PrefetchScalarGridSpec(
            num_scalar_prefetch=1,
            grid=(4,),
            in_specs=[
                pl.BlockSpec((block, 3 * size), lambda i, m: (i, 0)),
                pl.BlockSpec((block, 3 * size), lambda i, m: (i ^ 2, 0)),
                pl.BlockSpec((block, D), lambda i, m: (jnp.minimum(i, 1), 0)),
                pl.BlockSpec((block, D), lambda i, m: (jnp.maximum(i - 2, 0), 0)),
            ],
            out_specs=[
                pl.BlockSpec((block, 4 * D), lambda i, m: (i, 0)),
                pl.BlockSpec((block, LANES), lambda i, m: (i, 0)),
            ],
        ),
        out_shape=[
            jax.ShapeDtypeStruct((tokens, 4 * D), BFLOAT),
            jax.ShapeDtypeStruct((tokens, LANES), BFLOAT),
        ],
        cost_estimate=SMALL,
        compiler_params=params(),
    )(places, own, other, branch, branch_other)


def mixer_sum(act, delta_project, branch, branch_other, places, width, size):
    delta, logits = mixer_delta(
        delta_project, swap(delta_project), branch, branch_other, places, width, size
    )
    return (
        GradSum(
            act,
            delta[None],
            lambda s: (jnp.where(s % 4 == 3, 1, 0), s // 4, 0),
            lambda s: (0, 0, s % 4),
            STAGES,
        ),
        logits,
    )


ITEMS = 2
ANYWHERE = pl.BlockSpec(memory_space=pl.ANY)
WHOLE = pl.BlockSpec(memory_space=pltpu.VMEM)


def call(body, shapes, arrays, places=None, held=(), after=(), scratch=()):
    first = 0 if places is None else 1
    count, kept, tied = len(arrays), len(held), len(after)

    def whole(*refs):
        ins = refs[first : first + count]
        far = refs[first + count : first + count + kept]
        at = first + count + kept + tied
        outs = refs[at : at + len(shapes)]
        body(refs[0] if first else None, ins, far, outs, refs[at + len(shapes) :])

    return pl.pallas_call(
        whole,
        in_specs=[pl.BlockSpec(memory_space=pltpu.SMEM)] * first
        + [WHOLE] * count
        + [ANYWHERE] * (kept + tied),
        out_specs=[WHOLE] * len(shapes),
        out_shape=[jax.ShapeDtypeStruct(*shape) for shape in shapes],
        scratch_shapes=list(scratch),
        cost_estimate=SMALL,
        compiler_params=params(),
    )(*([] if places is None else [places]), *arrays, *held, *after)


def edge_shapes(tile):
    rows, cols = tile
    sizes = [cols, cols, rows, rows]
    return [((ITEMS, size, D), BFLOAT) for size in sizes]


def put_edges(value, item, refs, tile):
    rows, cols = tile
    lines = [value[0], value[rows - 1]]
    for at in (0, cols - 1):
        lines.append(jnp.concatenate([value[r][at : at + 1] for r in range(rows)], axis=0))
    for ref, line in zip(refs, lines):
        ref[item] = line.astype(BFLOAT)


def halo_edges(edges):
    rows, cols = lax.axis_size("row"), lax.axis_size("col")
    first_row, last_row, first_col, last_col = edges
    top = lax.ppermute(last_row, "row", [(i, i + 1) for i in range(rows - 1)])
    bottom = lax.ppermute(first_row, "row", [(i + 1, i) for i in range(rows - 1)])
    to_right = jnp.concatenate([top[:, -1:], last_col, bottom[:, -1:]], axis=1)
    to_left = jnp.concatenate([top[:, :1], first_col, bottom[:, :1]], axis=1)
    left = lax.ppermute(to_right, "col", [(i, i + 1) for i in range(cols - 1)])
    right = lax.ppermute(to_left, "col", [(i + 1, i) for i in range(cols - 1)])
    return top, bottom, left, right


def modulated(value, mod, shift, scale):
    normal, inverse = normalize(value)
    return normal * (1.0 + mod[scale : scale + 1]) + mod[shift : shift + 1]


def enter_first(tokens, mod, tile):
    cells = (ITEMS,) + tile + (D,)

    def body(_, ins, far, outs, scratch):
        for i in range(ITEMS):
            hidden = modulated(ins[0][i].astype(FLOAT), ins[1][i], 0, 1).reshape(cells[1:])
            outs[0][i] = hidden.astype(BFLOAT)
            put_edges(hidden, i, outs[1:], tile)

    hidden, *edges = call(body, [(cells, BFLOAT)] + edge_shapes(tile), [tokens, mod])
    return hidden, edges


def enter_next(middle, own, received, mod_before, mod, tile):
    cells = (ITEMS,) + tile + (D,)
    count = middle.shape[1]

    def body(_, ins, far, outs, scratch):
        for i in range(ITEMS):
            at = slice(i * count, (i + 1) * count)
            outer = ins[1][at] + ins[2][at].astype(FLOAT)
            outs[1][i] = outer
            value = ins[0][i] + ins[3][i][5:6] * outer
            outs[0][i] = value
            hidden = modulated(value, ins[4][i], 0, 1).reshape(cells[1:])
            outs[2][i] = hidden.astype(BFLOAT)
            put_edges(hidden, i, outs[3:], tile)

    shapes = [(middle.shape, FLOAT), (middle.shape, FLOAT), (cells, BFLOAT)] + edge_shapes(tile)
    value, outer, hidden, *edges = call(body, shapes, [middle, own, received, mod_before, mod])
    return value, outer, hidden, edges


def leave(middle, own, received, mod):
    count = middle.shape[1]

    def body(_, ins, far, outs, scratch):
        for i in range(ITEMS):
            at = slice(i * count, (i + 1) * count)
            outer = ins[1][at] + ins[2][at].astype(FLOAT)
            outs[1][i] = outer
            outs[0][i] = (ins[0][i] + ins[3][i][5:6] * outer).astype(BFLOAT)

    return call(
        body, [(middle.shape, BFLOAT), (middle.shape, FLOAT)], [middle, own, received, mod]
    )


def gather_weight(far, scratch, sems, places, own):
    batch, quarter = places[0], places[1]
    rows = own.shape[0]
    size = rows // 4
    base = (1 - batch) * rows
    parts = [(own, batch * rows, rows)]
    for k in range(4):
        parts.append((far[k], base + (quarter ^ k) * size, size))
    copies = []
    for k, (source, start, count) in enumerate(parts):
        target = scratch.at[pl.ds(pl.multiple_of(start, 16), count)]
        copy = pltpu.make_async_copy(source, target, sems.at[k])
        copy.start()
        copies.append(copy)
    return copies


def split_logit(block, start, heads):
    lane = lax.broadcasted_iota(jnp.int32, block.shape, 1)
    here = (lane >= start) & (lane < start + heads)
    high = block.astype(BFLOAT).astype(FLOAT)
    rest = jnp.where(here, block - high, 0.0)
    middle = rest.astype(BFLOAT).astype(FLOAT)
    low = rest - middle
    return (
        jnp.where(here, high, block) + pltpu.roll(middle, heads, 1) + pltpu.roll(low, 2 * heads, 1)
    )


def project_call(own, other, weight, bias, places, cells, width):
    size = weight[0].shape[1] // 3
    block = width // LANES * LANES
    total = 2 * own.shape[0]
    count = total // cells

    def body(places, ins, far, outs, scratch):
        whole, joined, result, sems = scratch
        copies = gather_weight(far[1:], whole, sems, places, far[0])
        joined[: total // 2] = ins[0][...]
        joined[total // 2 :] = ins[1][...]
        for copy in copies:
            copy.wait()
        for part in range(3):
            columns = slice(part * size, (part + 1) * size)
            value = dot(joined[...], whole[:, columns])
            if part == 0:
                last = split_logit(
                    value[:, block : block + LANES] + ins[2][...], width - block, width // HD
                )
                result[:, :block] = value[:, :block].astype(BFLOAT)
                result[:, block : block + LANES] = last.astype(BFLOAT)
            else:
                result[:, columns] = value.astype(BFLOAT)
        for k in range(count):
            start = pl.multiple_of((places[2] ^ k) * cells, cells)
            outs[k][0] = result[pl.ds(start, cells)]

    return call(
        body,
        [((1, cells, 3 * size), BFLOAT)] * count,
        [own, other, bias],
        places,
        weight,
        scratch=[
            pltpu.VMEM((D, 3 * size), BFLOAT),
            pltpu.VMEM((total, D), BFLOAT),
            pltpu.VMEM((total, 3 * size), BFLOAT),
            pltpu.SemaphoreType.DMA((5,)),
        ],
    )


def halves_out(value, outs, columns, items_here):
    outs[0][:, columns] = value[:items_here]
    outs[1][:, columns] = value[items_here:].astype(BFLOAT)


COLUMNS = 384


def attend_out_call(blocks, weight, layer, places, cells, width):
    count = len(blocks)
    total = count * cells

    def body(places, ins, far, outs, scratch):
        whole, sems = scratch
        copy = pltpu.make_async_copy(far[0].at[layer], whole, sems.at[0])
        copy.start()
        for k in range(count):
            start = pl.multiple_of((places[2] ^ k) * cells, cells)
            outs[2][pl.ds(start, cells)] = ins[k][0]
        copy.wait()
        for at in range(0, D, COLUMNS):
            columns = slice(at, at + COLUMNS)
            halves_out(dot(outs[2][...], whole[:, columns]), outs, columns, total // 2)

    return call(
        body,
        [((total // 2, D), FLOAT), ((total // 2, D), BFLOAT), ((total, width), BFLOAT)],
        blocks,
        places,
        [weight],
        scratch=[pltpu.VMEM((width, D), BFLOAT), pltpu.SemaphoreType.DMA((1,))],
    )


def middle_call(tokens, own, received, mod):
    count = tokens.shape[1]

    def body(_, ins, far, outs, scratch):
        for i in range(ITEMS):
            at = slice(i * count, (i + 1) * count)
            branch = ins[1][at] + ins[2][at].astype(FLOAT)
            outs[0][i] = branch
            middle = ins[0][i].astype(FLOAT) + ins[3][i][2:3] * branch
            outs[1][i] = middle
            outs[2][at] = modulated(middle, ins[3][i], 3, 4).astype(BFLOAT)

    shape = tokens.shape
    return call(
        body,
        [(shape, FLOAT), (shape, FLOAT), ((ITEMS * count, D), BFLOAT)],
        [tokens, own, received, mod],
    )


def feed_call(own, other, expand, shrink, layer, places):
    total = 2 * own.shape[0]
    inner = shrink.shape[1]
    rows = expand[0].shape[1]
    tile = 256

    def body(places, ins, far, outs, scratch):
        wide, back, joined, sems = scratch
        start = pl.multiple_of(places[0] * inner, LANES)
        source = far[0].at[layer, :, pl.ds(start, inner)]
        copies = gather_weight(far[1:5], wide, sems, places, source)
        last = pltpu.make_async_copy(far[5].at[layer], back, sems.at[5])
        last.start()
        joined[: total // 2] = ins[0][...]
        joined[total // 2 :] = ins[1][...]
        for copy in copies:
            copy.wait()
        for at in range(0, inner, tile):
            columns = slice(at, at + tile)
            value = dot(joined[...], wide[:, columns])
            outs[2][:, columns] = value
            outs[3][:, columns] = gelu(value).astype(BFLOAT)
        last.wait()
        for at in range(0, D, COLUMNS):
            columns = slice(at, at + COLUMNS)
            halves_out(dot(outs[3][...], back[:, columns]), outs, columns, total // 2)

    return call(
        body,
        [
            ((total // 2, D), FLOAT),
            ((total // 2, D), BFLOAT),
            ((total, inner), FLOAT),
            ((total, inner), BFLOAT),
        ],
        [own, other],
        places,
        list(expand) + [shrink],
        scratch=[
            pltpu.VMEM((2 * rows, inner), BFLOAT),
            pltpu.VMEM((inner, D), BFLOAT),
            pltpu.VMEM((total, D), BFLOAT),
            pltpu.SemaphoreType.DMA((6,)),
        ],
    )


def turn_call(mixed, mixed_other, attend, second, second_other, active, places, through):
    tokens = attend.shape[0]
    width = attend.shape[1]
    padded = padded_width(width)
    inner = active.shape[1]
    half = mixed.shape[0]

    def turn(value):
        return jnp.transpose(value.astype(FLOAT)).astype(BFLOAT)

    def body(places, one, two, three, four, five, six, _, mixer, wide, long, __):
        first = places[0] == 0
        for ref, at in ((one, 0), (two, half)):
            value = turn(ref[...])
            mixer[0, :, at : at + half] = jnp.where(first, value[:width], value[width:])
        blank = jnp.zeros((tokens, padded - width), FLOAT)
        value = jnp.concatenate([three[...].astype(FLOAT), blank], axis=1)
        mixer[1] = jnp.transpose(value)[:width].astype(BFLOAT)
        wide[:, :half] = turn(four[...])
        wide[:, half:] = turn(five[...])
        for at in range(0, inner, 256):
            long[at : at + 256] = turn(six[:, at : at + 256])

    return pl.pallas_call(
        body,
        in_specs=[pl.BlockSpec(memory_space=pltpu.SMEM)] + [WHOLE] * 6 + [ANYWHERE],
        out_specs=[WHOLE] * 3 + [ANYWHERE],
        out_shape=[
            jax.ShapeDtypeStruct((2, width, tokens), BFLOAT),
            jax.ShapeDtypeStruct((D, tokens), BFLOAT),
            jax.ShapeDtypeStruct((inner, tokens), BFLOAT),
            jax.ShapeDtypeStruct(through.shape, through.dtype),
        ],
        input_output_aliases={7: 3},
        cost_estimate=SMALL,
        compiler_params=params(),
    )(places, mixed, mixed_other, attend, second, second_other, active, through)


def feed_back_call(own, other, inner_value, expand, shrink, layer, places):
    total = 2 * own.shape[0]
    inner = shrink.shape[1]
    rows = expand[0].shape[1]
    tile = 256

    def body(places, ins, far, outs, scratch):
        wide, back, joined, sems = scratch
        last = pltpu.make_async_copy(far[5].at[layer], back, sems.at[5])
        last.start()
        start = pl.multiple_of(places[0] * inner, LANES)
        source = far[0].at[layer, :, pl.ds(start, inner)]
        copies = gather_weight(far[1:5], wide, sems, places, source)
        joined[: total // 2] = ins[0][...]
        joined[total // 2 :] = ins[1][...]
        last.wait()
        for at in range(0, inner, tile):
            columns = slice(at, at + tile)
            value = dot(joined[...], back[at : at + tile], ((1,), (1,)))
            outs[2][:, columns] = (value * gelu_slope(ins[2][:, columns])).astype(BFLOAT)
        for copy in copies:
            copy.wait()
        for at in range(0, D, COLUMNS):
            columns = slice(at, at + COLUMNS)
            value = dot(outs[2][...], wide[at : at + COLUMNS], ((1,), (1,)))
            halves_out(value, outs, columns, total // 2)

    return call(
        body,
        [((total // 2, D), FLOAT), ((total // 2, D), BFLOAT), ((total, inner), BFLOAT)],
        [own, other, inner_value],
        places,
        list(expand) + [shrink],
        scratch=[
            pltpu.VMEM((2 * rows, inner), BFLOAT),
            pltpu.VMEM((inner, D), BFLOAT),
            pltpu.VMEM((total, D), BFLOAT),
            pltpu.SemaphoreType.DMA((6,)),
        ],
    )


def middle_back_call(delta, own, received, middle, branch, outer, mod):
    count = middle.shape[1]
    over = lambda v: jnp.sum(v, axis=0, keepdims=True)

    def body(_, ins, far, outs, scratch):
        for i in range(ITEMS):
            at = slice(i * count, (i + 1) * count)
            here = ins[0][i].astype(FLOAT)
            mod_here = ins[6][i]
            outs[2][i, 3:4] = over(here * ins[5][i])
            second = ins[1][at] + ins[2][at].astype(FLOAT)
            normal, inverse = normalize(ins[3][i])
            outs[2][i, 1:2] = over(second)
            outs[2][i, 2:3] = over(second * normal)
            total = here + normalize_back(second * (1.0 + mod_here[4:5]), normal, inverse)
            outs[0][i] = total
            outs[2][i, 0:1] = over(total * ins[4][i])
            outs[1][at] = (mod_here[2:3] * total).astype(BFLOAT)

    return call(
        body,
        [(middle.shape, FLOAT), ((ITEMS * count, D), BFLOAT), ((ITEMS, 4, D), FLOAT)],
        [delta, own, received, middle, branch, outer, mod],
    )


def attend_back_call(own, other, weight, layer, places, cells, width):
    total = 2 * own.shape[0]
    count = total // cells

    def body(places, ins, far, outs, scratch):
        whole, joined, result, sems = scratch
        copy = pltpu.make_async_copy(far[0].at[layer], whole, sems.at[0])
        copy.start()
        joined[: total // 2] = ins[0][...]
        joined[total // 2 :] = ins[1][...]
        copy.wait()
        result[...] = dot(joined[...], whole[...], ((1,), (1,))).astype(BFLOAT)
        for k in range(count):
            start = pl.multiple_of((places[2] ^ k) * cells, cells)
            outs[k][0] = result[pl.ds(start, cells)]

    return call(
        body,
        [((1, cells, width), BFLOAT)] * count,
        [own, other],
        places,
        [weight],
        scratch=[
            pltpu.VMEM((width, D), BFLOAT),
            pltpu.VMEM((total, D), BFLOAT),
            pltpu.VMEM((total, width), BFLOAT),
            pltpu.SemaphoreType.DMA((1,)),
        ],
    )


def project_back_call(blocks, weight, places, cells, width):
    count = len(blocks)
    total = count * cells
    wide = blocks[0].shape[2]

    def body(places, ins, far, outs, scratch):
        whole, sems = scratch
        copies = gather_weight(far[1:], whole, sems, places, far[0])
        for k in range(count):
            start = pl.multiple_of((places[2] ^ k) * cells, cells)
            outs[2][pl.ds(start, cells)] = ins[k][0]
        at = width // LANES * LANES
        logits = outs[2][:, at : at + LANES].astype(FLOAT)
        outs[3][...] = jnp.sum(logits, axis=0, keepdims=True)
        for copy in copies:
            copy.wait()
        for at in range(0, D, COLUMNS):
            columns = slice(at, at + COLUMNS)
            value = dot(outs[2][...], whole[at : at + COLUMNS], ((1,), (1,)))
            halves_out(value, outs, columns, total // 2)

    return call(
        body,
        [
            ((total // 2, D), FLOAT),
            ((total // 2, D), BFLOAT),
            ((total, wide), BFLOAT),
            ((1, LANES), FLOAT),
        ],
        blocks,
        places,
        weight,
        scratch=[pltpu.VMEM((D, wide), BFLOAT), pltpu.SemaphoreType.DMA((5,))],
    )


def conv_delta_call(own, received, convolved, tile):
    cells = convolved.shape
    count = tile[0] * tile[1]

    def body(_, ins, far, outs, scratch):
        for i in range(ITEMS):
            at = slice(i * count, (i + 1) * count)
            delta = (ins[0][at] + ins[1][at].astype(FLOAT)).reshape(cells[1:])
            value = ins[2][i]
            gate = jax.nn.sigmoid(value)
            delta = delta * gate * (1.0 + value * (1.0 - gate))
            outs[0][i] = delta.astype(BFLOAT)
            put_edges(delta, i, outs[1:], tile)

    delta, *edges = call(
        body, [(cells, BFLOAT)] + edge_shapes(tile), [own, received, convolved]
    )
    return delta, edges


def enter_back_call(delta_hidden, tokens, delta_middle, mod, mod_before):
    count = tokens.shape[1]
    over = lambda v: jnp.sum(v, axis=0, keepdims=True)
    lower = mod_before is not None

    def body(_, ins, far, outs, scratch):
        for i in range(ITEMS):
            at = slice(i * count, (i + 1) * count)
            here = ins[0][i].reshape(count, D)
            normal, inverse = normalize(ins[1][i].astype(FLOAT))
            outs[0][i, 0:1] = over(here)
            outs[0][i, 1:2] = over(here * normal)
            total = ins[2][i] + normalize_back(here * (1.0 + ins[3][i][1:2]), normal, inverse)
            if lower:
                outs[2][i] = total
                outs[1][at] = (ins[4][i][5:6] * total).astype(BFLOAT)
            else:
                outs[1][at] = total.astype(BFLOAT)

    shapes = [((ITEMS, 2, D), FLOAT), ((ITEMS * count, D), BFLOAT)]
    arrays = [delta_hidden, tokens, delta_middle, mod]
    if lower:
        shapes.append((tokens.shape, FLOAT))
        arrays.append(mod_before)
    return call(body, shapes, arrays)


def pack_kernel(places, qkv, decay, own, other, *, width):
    heads = width // HD
    size = padded_width(width + 3 * heads)
    value, extra = qkv[0].astype(FLOAT), decay[0].astype(FLOAT)
    rows = value.shape[0]
    pieces = []
    for group in range(2):
        parts = []
        for j in range(3):
            start = j * D + group * width
            parts.append(value[:, start : start + width])
            filled = width
            if j == 0:
                parts.append(extra[:, group * heads : (group + 1) * heads])
                filled += heads
            parts.append(jnp.zeros((rows, size - filled), FLOAT))
        pieces.append(jnp.concatenate(parts, axis=1).astype(BFLOAT))
    first = places[0] == 0
    own[...] = jnp.where(first, pieces[0], pieces[1])
    other[...] = jnp.where(first, pieces[1], pieces[0])


def pack_call(qkv, decay, layer, places, width):
    rows = qkv.shape[1]
    size = padded_width(width + 3 * (width // HD))

    def body(*refs):
        pack_kernel(*refs, width=width)

    out = pl.BlockSpec((SHARE_ROWS, 3 * size), lambda i, m: (i, 0))
    return pl.pallas_call(
        body,
        grid_spec=pltpu.PrefetchScalarGridSpec(
            num_scalar_prefetch=1,
            grid=(rows // SHARE_ROWS,),
            in_specs=[
                pl.BlockSpec((1, SHARE_ROWS, qkv.shape[2]), lambda i, m: (layer, i, 0)),
                pl.BlockSpec((1, SHARE_ROWS, decay.shape[2]), lambda i, m: (layer, i, 0)),
            ],
            out_specs=[out, out],
        ),
        out_shape=[jax.ShapeDtypeStruct((rows, 3 * size), BFLOAT)] * 2,
        cost_estimate=SMALL,
        compiler_params=params(),
    )(places, qkv, decay)


def passed_by(values, after):
    count = len(values)
    return pl.pallas_call(
        lambda *refs: None,
        in_specs=[ANYWHERE] * (count + len(after)),
        out_specs=[ANYWHERE] * count,
        out_shape=[jax.ShapeDtypeStruct(v.shape, v.dtype) for v in values],
        input_output_aliases={k: k for k in range(count)},
        cost_estimate=SMALL,
        compiler_params=params(),
    )(*values, *after)


def lines_swapped(blocks, axis):
    return [blocks[0]] + [swap(blocks[k], axis, k) for k in range(1, len(blocks))]


class Pair:
    def __init__(self, args, modulations, taps, tile):
        self.args, self.modulations, self.taps, self.tile = args, modulations, taps, tile
        self.cells = tile[0] * tile[1]
        self.width = args["proj"].shape[1]
        self.heads = self.width // HD
        self.size = padded_width(self.width + 3 * self.heads)
        batch, row = lax.axis_index("batch"), lax.axis_index("row")
        quarter = row % 2 * 2 + row // 2
        self.places = [
            jnp.stack([batch, quarter, lax.axis_index(axis)]).astype(jnp.int32)
            for axis in ("col", "row")
        ]
        self.qkv, self.expand, self.bias = [], [], []
        self.pieces = {}
        for layer in range(LAYERS):
            own, other = pack_call(
                args["qkv"], args["decay"], layer, self.places[0], self.width
            )
            part = own.shape[0] // 4
            piece = lax.dynamic_slice_in_dim(other, quarter * part, part, 0)
            self.pieces["qkv", layer] = piece
            self.qkv.append([own])
            inner = args["shrink"].shape[1]
            piece = lax.dynamic_slice(
                args["expand"], (layer, quarter * part, (1 - batch) * inner), (1, part, inner)
            )
            self.pieces["expand", layer] = piece[0]
            self.expand.append([args["expand"]])
            start = self.width - self.width // LANES * LANES
            self.bias.append(
                jnp.pad(
                    args["decay_bias"][layer].astype(FLOAT)[None],
                    ((0, 0), (start, LANES - start - self.heads)),
                )
            )
        for stage in range(3):
            self.fetch("qkv", 0, stage, [])

    def fetch(self, name, layer, stage, after):
        held = self.pieces[name, layer]
        if stage == 0:
            if after:
                (held,) = passed_by([held], after)
            self.pieces[name, layer] = [swap(held)]
        elif stage == 1:
            if after:
                held = passed_by(held, after)
            self.pieces[name, layer] = [held[0], swap(held[0], "row", 2)]
        else:
            if after:
                held = passed_by(held, after)
            into = self.qkv if name == "qkv" else self.expand
            into[layer] += list(held) + [swap(part, "row", 1) for part in held]

    def axis(self, layer):
        return "col" if layer % 2 == 0 else "row"

    def scan(self, kernel, layer, inputs, out_width):
        place = self.places[layer % 2][2]
        rows, cols = self.tile
        return scan_call(
            kernel, place, inputs, out_width, rows, cols, layer % 2 == 0, self.width
        )

    def forward(self, layer, hidden, edges, tokens):
        places, axis = self.places[layer % 2], self.axis(layer)
        mod = self.modulations[layer]
        sides = halo_edges(edges)
        convolved, mixed = conv_forward(hidden, sides, self.taps[layer])
        mixed = mixed.reshape(-1, D)
        mixed_other = swap(mixed)
        if layer == 0:
            self.fetch("expand", 0, 0, [hidden])
            self.fetch("expand", 0, 1, [mixed])
        else:
            self.fetch("expand", 1, 1, [mixed])
        parts = project_call(
            mixed, mixed_other, self.qkv[layer], self.bias[layer], places, self.cells, self.width
        )
        self.fetch("expand", layer, 2, [parts[0]])
        if layer + 1 < LAYERS:
            self.fetch("qkv", layer + 1, 0, [parts[0]])
        parts = lines_swapped(parts, axis)
        attends = self.scan(scan_forward_kernel, layer, parts, self.width)
        own, send, attend = attend_out_call(
            lines_swapped(attends, axis), self.args["proj"], layer, places, self.cells, self.width
        )
        if layer + 1 < LAYERS:
            self.fetch("qkv", layer + 1, 1, [own])
        branch, middle, second = middle_call(tokens, own, swap(send), mod)
        second_other = swap(second)
        if layer + 1 < LAYERS:
            self.fetch("qkv", layer + 1, 2, [second])
        own, send, inner, active = feed_call(
            second, second_other, self.expand[layer], self.args["shrink"], layer, places
        )
        if layer + 1 < LAYERS:
            self.fetch("expand", layer + 1, 0, [own])
        received = swap(send)
        mixer_act, second_act, active_act, own = turn_call(
            mixed, mixed_other, attend, second, second_other, active, places, own
        )
        saved = dict(
            tokens=tokens, hidden=hidden, sides=sides, convolved=convolved, parts=parts,
            branch=branch, middle=middle, inner=inner, mixer_act=mixer_act,
            second_act=second_act, active_act=active_act,
        )
        return middle, own, received, saved

    def backward(self, layer, delta, outer_low, outer_other, saved, tick):
        places, axis = self.places[layer % 2], self.axis(layer)
        mod = self.modulations[layer]
        both = lambda own, other: jnp.concatenate([own, other], axis=0)
        own, send, inner_low = feed_back_call(
            outer_low, outer_other, saved["inner"], self.expand[layer], self.args["shrink"],
            layer, places,
        )
        received = swap(send)
        shrink_pipe = shrink_sum(saved["active_act"], both(outer_low, outer_other))
        own = tick("P1", {"A": shrink_pipe}, own)
        delta_middle, branch_low, mod_b = middle_back_call(
            delta, own, received, saved["middle"], saved["branch"], saved["outer"], mod
        )
        branch_other = swap(branch_low)
        expand_pipe = expand_sum(saved["second_act"], inner_low)
        branch_low = tick("P2", {"B": expand_pipe}, branch_low)
        blocks = attend_back_call(
            branch_low, branch_other, self.args["proj"], layer, places, self.cells, self.width
        )
        sent = lines_swapped(blocks, axis)
        sent[0] = tick("P3", {}, sent[0])
        projects = self.scan(
            scan_backward_kernel, layer, list(saved["parts"]) + sent, 3 * self.size
        )
        sent = lines_swapped(projects, axis)
        sent[0] = tick("P4", {}, sent[0])
        own, send, delta_project, grad_bias = project_back_call(
            sent, self.qkv[layer], places, self.cells, self.width
        )
        received = swap(send)
        def mixer(after):
            (value,) = passed_by([delta_project], after)
            act = saved["mixer_act"]
            pipe, logits = mixer_sum(
                act, value, branch_low, branch_other, places, self.width, self.size
            )
            return pipe, dot(logits, act[0], ((0,), (1,)))[: 2 * self.heads]

        if not layer:
            mixer_pipe, grad_decay = mixer([])
        own = tick("P5", {}, own)
        delta_conv, edges = conv_delta_call(own, received, saved["convolved"], self.tile)
        delta_sides = halo_edges(edges)
        delta_conv = tick("P6", {}, delta_conv)
        if layer:
            mixer_pipe, grad_decay = mixer([delta_conv])
        top, bottom, left, right = delta_sides
        left = tick("P8", {"C": mixer_pipe}, left)
        delta_sides = (top, bottom, left, right)
        delta_hidden, grad_taps = conv_backward(
            saved["hidden"], saved["sides"], delta_conv, delta_sides, self.taps[layer]
        )
        before = self.modulations[layer - 1] if layer else None
        mod_a, low, *rest = enter_back_call(
            delta_hidden, saved["tokens"], delta_middle, mod, before
        )
        low_other = swap(low) if rest else None

        small = SmallSum(join_smalls(mod_a, mod_b, grad_taps, grad_decay, grad_bias))
        low = tick("P7", {"S": small}, low)
        return rest[0] if rest else None, low, low_other


def pair_forward_backward(pair, tokens_in, cotangent, tick):
    tile = pair.tile
    shape = (ITEMS, pair.cells, D)
    tokens = tokens_in.reshape(shape)
    delta = cotangent.reshape(shape)
    outer_low = (pair.modulations[-1][:, 5:6] * delta.astype(FLOAT)).astype(BFLOAT)
    hidden, edges = enter_first(tokens, pair.modulations[0], tile)
    stored = []
    for layer in range(LAYERS):
        middle, own, received, saved = pair.forward(layer, hidden, edges, tokens)
        stored.append(saved)
        mod = pair.modulations[layer]
        if layer + 1 < LAYERS:
            tokens, saved["outer"], hidden, edges = enter_next(
                middle, own, received, mod, pair.modulations[layer + 1], tile
            )
        else:
            block_out, saved["outer"] = leave(middle, own, received, mod)
    outer_low = outer_low.reshape(-1, D)
    outer_other = swap(outer_low)
    for layer in reversed(range(LAYERS)):
        delta, outer_low, outer_other = pair.backward(
            layer, delta, outer_low, outer_other, stored[layer],
            lambda point, fresh, through, layer=layer: tick(layer, point, fresh, through),
        )
    return block_out, outer_low


def forward_layer(tokens, modulation, weights, layer, tile):
    taps, qkv, decay_bias, proj, expand, shrink = weights
    rows, cols = tile
    items, cells = tokens.shape[:2]
    width = proj.shape[0]
    heads = width // HD
    size = padded_width(width + 3 * heads)
    axis = "col" if layer % 2 == 0 else "row"
    mod = [modulation[:, k][:, None] for k in range(6)]
    normal, inverse = normalize(tokens)
    hidden = (normal * (1.0 + mod[1]) + mod[0]).astype(BFLOAT).reshape(items, rows, cols, D)
    sides = halo(hidden)
    convolved, mixed = conv_forward(hidden, sides, taps)
    mixed = gather_items(mixed.reshape(items, cells, D))
    project = matmul(mixed, qkv)
    logit = project[:, :, width : width + heads] + decay_bias.astype(FLOAT)
    high = logit.astype(BFLOAT)
    rest = logit - high.astype(FLOAT)
    middle_part = rest.astype(BFLOAT)
    low = (rest - middle_part.astype(FLOAT)).astype(BFLOAT)
    project = project.astype(BFLOAT)
    project = jnp.concatenate(
        [project[:, :, :width], high, middle_part, low, project[:, :, width + 3 * heads :]], axis=2
    )
    parts = lines_out(project, axis)
    place = lax.axis_index(axis)
    attends = scan_call(
        scan_forward_kernel, place, parts, width, rows, cols, layer % 2 == 0, width
    )
    attend = lines_back(attends, axis)
    branch = reduce_items(matmul(attend, proj))
    middle = tokens + mod[2] * branch
    normal2, inverse2 = normalize(middle)
    second = gather_items((normal2 * (1.0 + mod[4]) + mod[3]).astype(BFLOAT))
    inner = matmul(second, expand)
    active = gelu(inner).astype(BFLOAT)
    outer = reduce_items(matmul(active, shrink))
    result = middle + mod[5] * outer
    saved = (
        normal, inverse, hidden, sides, convolved, mixed, parts, attend, branch,
        normal2, inverse2, second, inner, active, outer,
    )
    return result, saved


def pipelined(width):
    shares = lax.axis_size("row") * lax.axis_size("col")
    square = lax.axis_size("row") == 4 and lax.axis_size("col") == 4
    return lax.axis_size("batch") == 2 and square and width == 4 * SHARE_ROWS and shares == SHARES


def backward_layer(delta, saved, modulation, weights, layer, tile):
    taps, qkv, decay_bias, proj, expand, shrink = weights
    (
        normal, inverse, hidden, sides, convolved, mixed, parts, attend, branch,
        normal2, inverse2, second, inner, active, outer,
    ) = saved
    rows, cols = tile
    items, cells = delta.shape[:2]
    width = proj.shape[0]
    heads = width // HD
    size = padded_width(width + 3 * heads)
    axis = "col" if layer % 2 == 0 else "row"
    mod = [modulation[:, k][:, None] for k in range(6)]
    over = lambda v: jnp.sum(v, axis=1)
    delta_gate2 = over(delta * outer)
    outer_low = gather_items((mod[5] * delta).astype(BFLOAT))
    grad_shrink = weight_grad(active, outer_low)
    inner_low = (matmul_back(outer_low, shrink) * gelu_slope(inner)).astype(BFLOAT)
    grad_expand = weight_grad(second, inner_low)
    delta_second = reduce_items(matmul_back(inner_low, expand))
    delta_shift2 = over(delta_second)
    delta_scale2 = over(delta_second * normal2)
    delta_middle = delta + normalize_back(delta_second * (1.0 + mod[4]), normal2, inverse2)
    delta_gate1 = over(delta_middle * branch)
    branch_low = gather_items((mod[2] * delta_middle).astype(BFLOAT))
    grad_proj = weight_grad(attend, branch_low)
    delta_attend = matmul_back(branch_low, proj).astype(BFLOAT)
    delta_parts = lines_out(delta_attend, axis)
    place = lax.axis_index(axis)
    projects = scan_call(
        scan_backward_kernel, place, list(parts) + delta_parts, 3 * size, rows, cols,
        layer % 2 == 0, width,
    )
    delta_project = lines_back(projects, axis)
    grad_qkv = weight_grad(mixed, delta_project)
    sums = (grad_shrink, grad_expand, grad_proj, grad_qkv)
    grad_decay_bias = jnp.sum(delta_project[:, :, width : width + heads].astype(FLOAT), axis=(0, 1))
    delta_mixed = reduce_items(matmul_back(delta_project, qkv)).reshape(convolved.shape)
    gate = jax.nn.sigmoid(convolved)
    delta_conv = (delta_mixed * gate * (1.0 + convolved * (1.0 - gate))).astype(BFLOAT)
    delta_sides = halo(delta_conv)
    delta_hidden, grad_taps = conv_backward(hidden, sides, delta_conv, delta_sides, taps)
    delta_hidden = delta_hidden.reshape(items, cells, D)
    delta_shift1 = over(delta_hidden)
    delta_scale1 = over(delta_hidden * normal)
    delta_tokens = delta_middle + normalize_back(delta_hidden * (1.0 + mod[1]), normal, inverse)
    delta_mod = jnp.stack(
        [delta_shift1, delta_scale1, delta_gate1, delta_shift2, delta_scale2, delta_gate2], axis=1
    )
    return delta_tokens, sums, (delta_mod, grad_taps, None, grad_decay_bias)


def sum_rows_here(grad):
    return lax.psum(grad.astype(BFLOAT), GRID_AXES).astype(FLOAT)


def sum_columns(grad):
    count = lax.axis_size("batch")
    low = grad.astype(BFLOAT).reshape((count, -1, grad.shape[1]))
    shares = lax.axis_size("row") * lax.axis_size("col")
    if count == 2 and low.shape[1] % shares == 0:
        share = lax.psum_scatter(low, GRID_AXES, scatter_dimension=1, tiled=True)
        place = lax.axis_index("batch")
        own = lax.dynamic_index_in_dim(share, place, 0, keepdims=False)
        other = swap(lax.dynamic_index_in_dim(share, 1 - place, 0, keepdims=False))
        both = jnp.stack([jnp.where(place == 0, own, other), jnp.where(place == 0, other, own)])
        return lax.all_gather(both, GRID_AXES, axis=1, tiled=True)
    total = lax.psum(low, GRID_AXES)
    return lax.all_to_all(total, "batch", 0, 0)


def ada_call(cond, mods, previous, layer, through):
    items, rows = cond.shape
    wide = mods.shape[1]
    block = 64
    previous = [] if previous is None else [previous]

    def body(columns, values, *refs):
        out = refs[-2]
        for at in range(0, wide, D):
            part = slice(at, at + D)
            total = columns[:, 0:1] * values[0:1, part]
            for item in range(1, items):
                total += columns[:, item : item + 1] * values[item : item + 1, part]
            out[0, :, part] = total

    count = len(previous)
    return pl.pallas_call(
        body,
        grid=(rows // block,),
        in_specs=[
            pl.BlockSpec((block, items), lambda i: (i, 0)),
            pl.BlockSpec((items, wide), lambda i: (0, 0)),
        ]
        + [ANYWHERE] * (count + 1),
        out_specs=[pl.BlockSpec((1, block, wide), lambda i: (layer, i, 0)), ANYWHERE],
        out_shape=[
            jax.ShapeDtypeStruct((LAYERS, rows, wide), FLOAT),
            jax.ShapeDtypeStruct(through.shape, through.dtype),
        ],
        input_output_aliases={2 + k: k for k in range(count)} | {2 + count: 1},
        cost_estimate=SMALL,
        compiler_params=params(),
    )(jnp.transpose(cond.astype(FLOAT)), mods, *previous, through)


SCHEDULE = {
    (1, "P1"): "aA1",
    (1, "P2"): "aB1rL1",
    (1, "P7"): "sC1sS1",
    (0, "P1"): "kC1sA0",
    (0, "P2"): "tS1kA0sB0",
    (0, "P3"): "gL1kB0",
    (0, "P4"): "tS1",
    (0, "P5"): "tC1tS1",
    (0, "P8"): "tC1tA0tS1sC0",
    (0, "P7"): "tC1tA0tB0kC0sS0",
}
TAIL = (
    "tA0tB0tS0",
    "mS1",
    "tB0tC0tS0",
    "tB0tC0tS0",
    "tC0tS0gL0",
    "fAB1",
    "mS0",
    "fABC0",
)


SMALL_ROWS = 32


def join_smalls(mod_a, mod_b, grad_taps, grad_decay, grad_bias):
    heads = grad_decay.shape[0] // 2

    def body(_, ins, far, outs, scratch):
        out = outs[0]
        for i in range(ITEMS):
            out[6 * i : 6 * i + 2] = ins[0][i]
            out[6 * i + 2 : 6 * i + 6] = ins[1][i]
        out[12:21] = ins[2][...]
        out[21 : 21 + heads] = jnp.concatenate([ins[3][:heads], ins[3][heads:]], axis=1)
        bias = jnp.concatenate([ins[4][...], jnp.zeros((1, D - LANES), FLOAT)], axis=1)
        out[21 + heads : 22 + heads] = bias
        out[22 + heads :] = jnp.zeros((SMALL_ROWS - 22 - heads, D), FLOAT)

    return call(
        body, [((SMALL_ROWS, D), FLOAT)], [mod_a, mod_b, grad_taps, grad_decay, grad_bias]
    )[0]


def split_smalls(flat, items, heads, width):
    start = width - width // LANES * LANES
    decay = flat[21 : 21 + heads]
    return (
        flat[: items * 6].reshape(items, 6 * D),
        flat[12:21],
        jnp.concatenate([decay[:, :width], decay[:, width:]], axis=0),
        flat[21 + heads, start : start + heads],
    )


def general_forward_backward(
    tokens_in, cotangent, modulations, taps_all, qkv_weight, decay_weight, decay_bias,
    proj_weight, expand_weight, shrink_weight,
):
    count = lax.axis_size("batch")
    items, rows, cols = tokens_in.shape[:3]
    tile = (rows, cols)
    width = proj_weight.shape[1]
    weights = []
    for layer in range(LAYERS):
        qkv = fetch_columns(
            [head_columns(qkv_weight[layer], decay_weight[layer], g, width) for g in range(count)]
        )
        inner = expand_weight.shape[2] // count
        expand = fetch_columns(
            [expand_weight[layer][:, g * inner : (g + 1) * inner] for g in range(count)]
        )
        weights.append(
            (taps_all[layer], qkv, decay_bias[layer], proj_weight[layer], expand, shrink_weight[layer])
        )
    tokens = tokens_in.astype(FLOAT).reshape(items, rows * cols, D)
    stored = []
    for layer in range(LAYERS):
        tokens, saved = forward_layer(tokens, modulations[layer], weights[layer], layer, tile)
        stored.append(saved)
    delta = cotangent.astype(FLOAT).reshape(tokens.shape)
    bigs, smalls = [None] * LAYERS, [None] * LAYERS
    for layer in reversed(range(LAYERS)):
        delta, big, small = backward_layer(
            delta, stored[layer], modulations[layer], weights[layer], layer, tile
        )
        grad_shrink, grad_expand, grad_proj, grad_qkv = big
        bigs[layer] = (
            sum_rows_here(grad_shrink),
            sum_columns(grad_expand),
            sum_rows_here(grad_proj),
            sum_columns(grad_qkv),
        )
        smalls[layer] = tuple(
            None if part is None else lax.psum(part, GRID_AXES) for part in small
        )
    return tokens.astype(BFLOAT), delta.astype(BFLOAT), bigs, smalls


def per_device(
    tokens_in, timesteps, ada_weight, ada_bias, conv_taps, qkv_weight, decay_weight, decay_bias,
    proj_weight, expand_weight, shrink_weight, cotangent,
):
    count, place = lax.axis_size("batch"), lax.axis_index("batch")
    items, rows, cols = tokens_in.shape[:3]
    tile = (rows, cols)
    rows_here = ada_weight.shape[1]
    width = proj_weight.shape[1]
    heads = width // HD
    size = padded_width(width + 3 * heads)
    cond = jax.nn.silu(embed_steps(timesteps)).astype(BFLOAT)
    cond_slice = lax.dynamic_slice_in_dim(cond, place * rows_here, rows_here, 1)
    order = [0] if count != 2 else None
    if count == 2:
        cond_first = jnp.where(
            place == 0, cond_slice, jnp.concatenate([cond_slice[items:], cond_slice[:items]])
        )
    else:
        cond_first = cond_slice
    biases = gather_last(ada_bias).astype(FLOAT)
    taps_all = gather_last(conv_taps)
    weights, modulations = [], []
    partial = jnp.stack(
        [
            jnp.dot(cond_first, ada_weight[layer], preferred_element_type=FLOAT)
            for layer in range(LAYERS)
        ],
        axis=1,
    )
    if count == 2:
        total = partial[:items] + swap(partial[items:])
    else:
        total = lax.psum_scatter(partial, "batch", scatter_dimension=0, tiled=True)
    for layer in range(LAYERS):
        modulations.append((total[:, layer] + biases[layer]).reshape(items, 6, D))
    fast = pipelined(width) and count * items == 4 and tile == (8, 8)
    hidden_units = shrink_weight.shape[1]
    if fast:
        moving = {}
        upper_sums = Scattered()

        def act(names, through):
            names = [names[at : at + 3] for at in range(0, len(names), 3)]
            steps = [moving[name[1:]] for name in names if name[0] == "t"]
            through = tick(steps, through)
            for name in names:
                one = moving.get(name[1:])
                if name[0] == "s":
                    through = one.start(through)
                elif name[0] == "k":
                    through = one.second(through)
                elif name == "gL1":
                    upper_sums.gather(through)
                elif name == "gL0":
                    Gathered([moving[name] for name in ("C1", "A0", "B0", "C0")]).gather()
                elif name[0] == "a":
                    through = upper_sums.add(one, through)
                elif name[0] == "r":
                    upper_sums.reduce()
            return through

        def step(layer, point, fresh, through):
            for name, one in fresh.items():
                moving[name if len(name) == 2 else name + str(layer)] = one
                if name in "ABC":
                    one.offload = True
            return act(SCHEDULE.get((layer, point), ""), through)

        pair = Pair(
            dict(
                qkv=qkv_weight, decay=decay_weight, decay_bias=decay_bias, proj=proj_weight,
                expand=expand_weight, shrink=shrink_weight,
            ),
            modulations,
            taps_all,
            tile,
        )
        block_out, through = pair_forward_backward(pair, tokens_in, cotangent, step)
        shapes = [
            (LAYERS, hidden_units, D),
            (LAYERS, rows_here, expand_weight.shape[2]),
            (LAYERS, rows_here, 3 * D),
            (LAYERS, width, D),
        ]
        finished = None
        grad_ada = None
        smalls = [None] * LAYERS
        for names in TAIL:
            if names[0] == "f":
                kinds = names[1:-1]
                layer = int(names[-1])
                sums = [moving[kind + names[-1]] for kind in kinds]
                if kinds[-1] == "C":
                    kinds, sums = kinds + "C", sums + [moving["C1"]]
                made, through = Gathered.finish(
                    sums, kinds,
                    None if layer else finished, layer, shapes, through,
                )
                finished = (finished or {}) | made
            elif names[0] == "m":
                layer = int(names[2])
                smalls[layer] = list(split_smalls(moving[names[1:]].keep, items, heads, width))
                mods = gather_items(smalls[layer][0])
                smalls[layer][0] = mods
                grad_ada, through = ada_call(cond_first, mods, grad_ada, layer, through)
            else:
                through = act(names, through)
        grad_tokens = through
    else:
        block_out, grad_tokens, bigs, smalls = general_forward_backward(
            tokens_in, cotangent, modulations, taps_all, qkv_weight, decay_weight, decay_bias,
            proj_weight, expand_weight, shrink_weight,
        )
    block_out = block_out.reshape(tokens_in.shape)
    grad_tokens = grad_tokens.reshape(tokens_in.shape)
    delta_mods, taps_grads, bias_grads = (
        jnp.stack([smalls[layer][k] for layer in range(LAYERS)]) for k in (0, 1, 3)
    )
    if fast:
        every_mod = delta_mods.transpose(1, 0, 2)
    else:
        every_mod = gather_items(delta_mods.transpose(1, 0, 2, 3)).reshape(
            count * items, LAYERS, 6 * D
        )
    if count == 2:
        taps_every = taps_grads + swap(taps_grads)
    else:
        taps_every = lax.psum(taps_grads, "batch")
    grad_taps = lax.dynamic_slice_in_dim(taps_every, place * width, width, 2)
    if not fast:
        grad_ada = jnp.zeros((LAYERS, rows_here, 6 * D), FLOAT)
        for item in range(count * items):
            grad_ada += (
                cond_first[item].astype(FLOAT)[None, :, None] * every_mod[item][:, None, :]
            )
    bias_width = ada_bias.shape[1]
    grad_ada_bias = lax.dynamic_slice_in_dim(
        jnp.sum(every_mod, axis=0), place * bias_width, bias_width, 1
    )
    if fast:
        grad_shrink, grad_expand, grad_qkv, grad_proj = (finished[k] for k in range(4))
        grad_decay = jnp.stack([jnp.transpose(smalls[layer][2]) for layer in range(LAYERS)])
    else:
        stack = lambda k: jnp.stack([bigs[layer][k] for layer in range(LAYERS)])
        grad_shrink, grad_proj = stack(0), stack(2)
        expand_parts, qkv_parts = stack(1), stack(3)
        grad_expand = jnp.concatenate([expand_parts[:, g] for g in range(count)], 2).astype(FLOAT)
        grad_qkv = jnp.concatenate(
            [
                qkv_parts[:, g, :, j * size : j * size + width]
                for j in range(3)
                for g in range(count)
            ],
            axis=2,
        ).astype(FLOAT)
        grad_decay = jnp.concatenate(
            [qkv_parts[:, g, :, width : width + heads] for g in range(count)], axis=2
        ).astype(FLOAT)
    return (
        block_out,
        grad_tokens,
        grad_ada,
        grad_ada_bias,
        grad_taps,
        grad_qkv,
        grad_decay,
        bias_grads,
        grad_proj,
        grad_expand,
        grad_shrink,
    )


def solution(mesh):
    return jax.shard_map(
        per_device,
        mesh=mesh,
        in_specs=(
            P("batch", "row", "col", None),
            P(),
            P(None, "batch", None),
            P(None, "batch"),
            P(None, None, "batch"),
            P(None, "batch", None),
            P(None, "batch", None),
            P(None, "batch"),
            P(None, "batch", None),
            P(None, "batch", None),
            P(None, "batch", None),
            P("batch", "row", "col", None),
        ),
        out_specs=(
            P("batch", "row", "col", None),
            P("batch", "row", "col", None),
            P(None, "batch", None),
            P(None, "batch"),
            P(None, None, "batch"),
            P(None, "batch", None),
            P(None, "batch", None),
            P(None, "batch"),
            P(None, "batch", None),
            P(None, "batch", None),
            P(None, "batch", None),
        ),
        check_vma=False,
    )
```

```python
import jax
import jax.numpy as jnp
from jax import lax
from jax.experimental import pallas as pl
from jax.experimental.pallas import tpu as pltpu
from jax.sharding import PartitionSpec as P

D = 1152
H = 16
HD = 72
LAYERS = 2
EPS = 1e-06
ACCURATE = lax.Precision.HIGHEST
FLOAT = jnp.float32
BFLOAT = jnp.bfloat16
LANES = 128
VMEM_LIMIT = 48 * 1024 * 1024
GRID_AXES = ("row", "col")
SMALL = pl.CostEstimate(flops=1, bytes_accessed=1, transcendentals=0)


def params():
    return pltpu.CompilerParams(vmem_limit_bytes=VMEM_LIMIT)


def padded_width(width):
    return -(-width // LANES) * LANES


def swap(value, axis="batch", bit=1):
    count = lax.axis_size(axis)
    return lax.ppermute(value, axis, [(i, i ^ bit) for i in range(count)])


def gather_items(own):
    if lax.axis_size("batch") == 2:
        return jnp.concatenate([own, swap(own)], axis=0)
    return lax.all_gather(own, "batch", axis=0, tiled=True)


def gather_last(own):
    if lax.axis_size("batch") == 2:
        other = swap(own)
        first = lax.axis_index("batch") == 0
        return jnp.concatenate([jnp.where(first, own, other), jnp.where(first, other, own)], -1)
    return lax.all_gather(own, "batch", axis=own.ndim - 1, tiled=True)


def reduce_items(partial):
    if lax.axis_size("batch") == 2:
        items = partial.shape[0] // 2
        return partial[:items] + swap(partial[items:].astype(BFLOAT)).astype(FLOAT)
    return lax.psum_scatter(partial, "batch", scatter_dimension=0, tiled=True)


def lines_out(values, axis):
    count, place = lax.axis_size(axis), lax.axis_index(axis)
    groups = values.reshape((count, -1) + values.shape[1:])
    blocks = []
    for k in range(count):
        block = lax.dynamic_index_in_dim(groups, place ^ k, 0, keepdims=False)
        blocks.append(block if k == 0 else swap(block, axis, k))
    return blocks


def lines_back(blocks, axis):
    count, place = lax.axis_size(axis), lax.axis_index(axis)
    received = [blocks[0]] + [swap(blocks[k], axis, k) for k in range(1, count)]
    stacked = jnp.stack(received)
    return jnp.concatenate(
        [lax.dynamic_index_in_dim(stacked, place ^ j, 0, keepdims=False) for j in range(count)]
    )


def halo(cells):
    return halo_edges([cells[:, 0], cells[:, -1], cells[:, :, 0], cells[:, :, -1]])


def beside(cells, sides, item):
    top, bottom, left, right = sides
    count, width = cells.shape[1], cells.shape[2]
    lefts, rights = left[item].astype(FLOAT), right[item].astype(FLOAT)
    at = lax.broadcasted_iota(jnp.int32, (width, cells.shape[3]), 0)
    rows = []
    for row in range(count + 2):
        if row == 0:
            here = top[item]
        elif row == count + 1:
            here = bottom[item]
        else:
            here = cells[item, row - 1]
        here = here.astype(FLOAT)
        before = jnp.where(at == 0, lefts[row : row + 1], pltpu.roll(here, 1, 0))
        after = jnp.where(at == width - 1, rights[row : row + 1], pltpu.roll(here, width - 1, 0))
        rows.append((before, here, after))
    return rows


def conv_forward_kernel(cells, *refs):
    sides, (taps, convolved, mixed) = refs[:4], refs[4:]
    weights = taps[...].astype(FLOAT)
    for item in range(cells.shape[0]):
        rows = beside(cells, sides, item)
        for row in range(cells.shape[1]):
            total = jnp.zeros(rows[0][1].shape, FLOAT)
            for a in range(3):
                for b in range(3):
                    total += weights[3 * a + b : 3 * a + b + 1] * rows[row + a][b]
            convolved[item, row] = total
            mixed[item, row] = (total * jax.nn.sigmoid(total)).astype(BFLOAT)


def conv_backward_kernel(cells, *refs):
    sides, delta, delta_sides, (taps, hidden, grads) = refs[:4], refs[4], refs[5:9], refs[9:]
    weights = taps[...].astype(FLOAT)
    sums = [jnp.zeros((cells.shape[2], cells.shape[3]), FLOAT) for _ in range(9)]
    for item in range(cells.shape[0]):
        rows = beside(cells, sides, item)
        for row in range(cells.shape[1]):
            here = delta[item, row].astype(FLOAT)
            for a in range(3):
                for b in range(3):
                    sums[3 * a + b] += rows[row + a][b] * here
        rows = beside(delta, delta_sides, item)
        for row in range(cells.shape[1]):
            total = jnp.zeros(rows[0][1].shape, FLOAT)
            for a in range(3):
                for b in range(3):
                    total += weights[3 * a + b : 3 * a + b + 1] * rows[row + 2 - a][2 - b]
            hidden[item, row] = total
    for tap in range(9):
        grads[tap : tap + 1] = jnp.sum(sums[tap], axis=0, keepdims=True)


def conv_specs(items, rows, cols, block):
    cells = pl.BlockSpec((items, rows, cols, block), lambda i: (0, 0, 0, i))
    side = lambda size: pl.BlockSpec((items, size, block), lambda i: (0, 0, i))
    taps = pl.BlockSpec((9, block), lambda i: (0, i))
    return [cells] + [side(size) for size in (cols, cols, rows + 2, rows + 2)], taps


def conv_forward(cells, sides, taps):
    items, rows, cols, width = cells.shape
    block = 3 * LANES
    specs, tap_spec = conv_specs(items, rows, cols, block)
    return pl.pallas_call(
        conv_forward_kernel,
        grid=(width // block,),
        in_specs=specs + [tap_spec],
        out_specs=[specs[0], specs[0]],
        out_shape=[
            jax.ShapeDtypeStruct(cells.shape, FLOAT),
            jax.ShapeDtypeStruct(cells.shape, BFLOAT),
        ],
        cost_estimate=SMALL,
        compiler_params=params(),
    )(cells, *sides, taps)


def conv_backward(cells, sides, delta, delta_sides, taps):
    items, rows, cols, width = cells.shape
    block = 3 * LANES
    specs, tap_spec = conv_specs(items, rows, cols, block)
    return pl.pallas_call(
        conv_backward_kernel,
        grid=(width // block,),
        in_specs=specs + specs + [tap_spec],
        out_specs=[specs[0], tap_spec],
        out_shape=[
            jax.ShapeDtypeStruct(cells.shape, FLOAT),
            jax.ShapeDtypeStruct((9, width), FLOAT),
        ],
        cost_estimate=SMALL,
        compiler_params=params(),
    )(cells, *sides, delta, *delta_sides, taps)


def scan_mask(place, rows, cols, along_cols, blocks):
    cells = rows * cols
    shape = (blocks * cells, blocks * cells)

    def line_and_position(index):
        block = index // cells
        inside = index - block * cells
        row = inside // cols
        col = inside - row * cols
        source = place ^ block
        if along_cols:
            return row, source * cols + col
        return col, source * rows + row

    line_t, at_t = line_and_position(lax.broadcasted_iota(jnp.int32, shape, 0))
    line_s, at_s = line_and_position(lax.broadcasted_iota(jnp.int32, shape, 1))
    return (line_t == line_s) & (at_s <= at_t)


def dot(left, right, contract=((1,), (0,)), precision=None):
    return lax.dot_general(
        left, right, (contract, ((), ())), precision=precision, preferred_element_type=FLOAT
    )


class Scan:
    def __init__(self, parts, mask, width):
        self.width = width
        self.padded = padded_width(width + 3 * (width // HD))
        self.heads = width // HD
        joined = jnp.concatenate([part[0] for part in parts], axis=0)
        size = self.padded
        self.queries = joined[:, :size]
        self.keys = joined[:, size : 2 * size]
        self.values = joined[:, 2 * size :]
        self.start = width - width // LANES * LANES
        self.block = width // LANES * LANES
        extra = self.queries[:, self.block : self.block + LANES].astype(FLOAT)
        logit = (
            extra
            + pltpu.roll(extra, LANES - self.heads, 1)
            + pltpu.roll(extra, LANES - 2 * self.heads, 1)
        )
        self.lane = lax.broadcasted_iota(jnp.int32, extra.shape, 1)
        self.is_logit = (self.lane >= self.start) & (self.lane < self.start + self.heads)
        self.logit = jnp.where(self.is_logit, logit, 0.0)
        small = jnp.exp(-jnp.abs(self.logit))
        logdecay = jnp.where(self.is_logit, jnp.minimum(self.logit, 0.0) - jnp.log(1.0 + small), 0.0)
        self.lower = jnp.where(mask, 1.0, 0.0).astype(FLOAT)
        self.mask = mask
        self.cumul = dot(self.lower, logdecay, precision=ACCURATE)
        self.cumul_rows = jnp.transpose(self.cumul)
        self.feature = lax.broadcasted_iota(jnp.int32, (1, size), 1)

    def of_head(self, head, array):
        inside = (self.feature >= head * HD) & (self.feature < head * HD + HD)
        return jnp.where(inside, array, jnp.zeros_like(array))

    def weights(self, head):
        at = self.start + head
        gap = self.cumul[:, at : at + 1] - self.cumul_rows[at : at + 1, :]
        return jnp.where(self.mask, jnp.exp(jnp.minimum(gap, 0.0)), 0.0)


SCALE = HD ** (-0.5)


def scan_forward_kernel(place, *refs, rows, cols, along_cols, width):
    count = len(refs) // 2
    parts, outs = refs[:count], refs[count:]
    mask = scan_mask(place[0], rows, cols, along_cols, count)
    scan = Scan(parts, mask, width)
    total = jnp.zeros(scan.queries.shape, FLOAT)
    for head in range(scan.heads):
        scores = dot(scan.of_head(head, scan.queries), scan.keys, ((1,), (1,))) * SCALE
        scores = (scores * scan.weights(head)).astype(BFLOAT)
        total += dot(scores, scan.of_head(head, scan.values))
    cells = rows * cols
    low = total.astype(BFLOAT)
    for k in range(count):
        outs[k][0] = low[k * cells : (k + 1) * cells, :width]


def scan_backward_kernel(place, *refs, rows, cols, along_cols, width):
    count = len(refs) // 3
    parts, deltas, outs = refs[:count], refs[count : 2 * count], refs[2 * count :]
    mask = scan_mask(place[0], rows, cols, along_cols, count)
    scan = Scan(parts, mask, width)
    joined = jnp.concatenate([part[0] for part in deltas], axis=0)
    short = scan.padded - width
    if short:
        joined = jnp.concatenate([joined, jnp.zeros((joined.shape[0], short), BFLOAT)], axis=1)
    shape = scan.queries.shape
    delta_query = jnp.zeros(shape, FLOAT)
    delta_key = jnp.zeros(shape, FLOAT)
    delta_value = jnp.zeros(shape, FLOAT)
    gap_rows = jnp.zeros(scan.lane.shape, FLOAT)
    gap_cols = jnp.zeros(scan.cumul_rows.shape, FLOAT)
    place_row = lax.broadcasted_iota(jnp.int32, gap_cols.shape, 0)
    for head in range(scan.heads):
        query = scan.of_head(head, scan.queries)
        delta = scan.of_head(head, joined)
        weights = scan.weights(head)
        scores = dot(query, scan.keys, ((1,), (1,))) * SCALE * weights
        delta_scores = dot(delta, scan.values, ((1,), (1,)))
        gap = delta_scores * scores
        at = scan.start + head
        gap_rows += jnp.where(scan.lane == at, jnp.sum(gap, axis=1, keepdims=True), 0.0)
        gap_cols += jnp.where(place_row == at, jnp.sum(gap, axis=0, keepdims=True), 0.0)
        inner = (delta_scores * weights * SCALE).astype(BFLOAT)
        delta_query += dot(inner, scan.of_head(head, scan.keys))
        delta_key += dot(inner, query, ((0,), (0,)))
        delta_value += dot(scores.astype(BFLOAT), delta, ((0,), (0,)))
    delta_cumul = gap_rows - jnp.transpose(gap_cols)
    delta_decay = dot(scan.lower, delta_cumul, ((0,), (0,)), ACCURATE)
    small = jnp.exp(-jnp.abs(scan.logit))
    keep = jnp.where(scan.logit >= 0.0, small, 1.0) / (1.0 + small)
    delta_logit = delta_decay * keep
    block = scan.block
    mixed = jnp.where(scan.is_logit, delta_logit, delta_query[:, block : block + LANES])
    pieces = [delta_query[:, :block]] if block else []
    pieces.append(mixed)
    if block + LANES < scan.padded:
        pieces.append(delta_query[:, block + LANES :])
    whole = jnp.concatenate(pieces + [delta_key, delta_value], axis=1).astype(BFLOAT)
    cells = rows * cols
    for k in range(count):
        outs[k][0] = whole[k * cells : (k + 1) * cells]


def scan_call(kernel, place, inputs, out_width, rows, cols, along_cols, width):
    count = lax.axis_size("col") if along_cols else lax.axis_size("row")
    items, cells = inputs[0].shape[:2]
    spec = lambda last: pl.BlockSpec((1, cells, last), lambda i, place: (i, 0, 0))

    def body(*refs):
        kernel(*refs, rows=rows, cols=cols, along_cols=along_cols, width=width)

    return pl.pallas_call(
        body,
        grid_spec=pltpu.PrefetchScalarGridSpec(
            num_scalar_prefetch=1,
            grid=(items,),
            in_specs=[spec(v.shape[2]) for v in inputs],
            out_specs=[spec(out_width)] * count,
        ),
        out_shape=[jax.ShapeDtypeStruct((items, cells, out_width), BFLOAT)] * count,
        cost_estimate=SMALL,
        compiler_params=params(),
    )(place.reshape(1).astype(jnp.int32), *inputs)


def pick(values, index):
    chosen = values[0]
    for k in range(1, len(values)):
        chosen = jnp.where(index == k, values[k], chosen)
    return chosen


def fetch_columns(pieces):
    count, place = lax.axis_size("batch"), lax.axis_index("batch")
    if count != 2:
        stacked = jnp.stack(pieces)
        return lax.all_to_all(stacked, "batch", 0, 0).reshape((-1,) + pieces[0].shape[1:])
    own, other = pick(pieces, place), pick(pieces, 1 - place)
    rows = own.shape[0]
    half = rows // 2
    core = lax.axis_index("row") % 2
    first = swap(lax.dynamic_slice_in_dim(other, core * half, half, 0))
    second = swap(first, "row", 1)
    whole = jnp.zeros((2 * rows,) + own.shape[1:], own.dtype)
    whole = lax.dynamic_update_slice_in_dim(whole, own, place * rows, 0)
    base = (1 - place) * rows
    whole = lax.dynamic_update_slice_in_dim(whole, first, base + core * half, 0)
    return lax.dynamic_update_slice_in_dim(whole, second, base + (1 - core) * half, 0)


def head_columns(qkv, decay, group, width):
    size = padded_width(width + 3 * (width // HD))
    heads = width // HD
    parts = []
    for j in range(3):
        piece = qkv[:, j * D + group * width : j * D + (group + 1) * width]
        filled = width
        parts.append(piece)
        if j == 0:
            parts.append(decay[:, group * heads : (group + 1) * heads])
            filled += heads
        if size > filled:
            parts.append(jnp.zeros((qkv.shape[0], size - filled), qkv.dtype))
    return jnp.concatenate(parts, axis=1)


def normalize(values):
    center = values - jnp.mean(values, axis=-1, keepdims=True)
    inverse = lax.rsqrt(jnp.mean(center * center, axis=-1, keepdims=True) + EPS)
    return center * inverse, inverse


def normalize_back(delta, normal, inverse):
    first = jnp.mean(delta, axis=-1, keepdims=True)
    second = jnp.mean(delta * normal, axis=-1, keepdims=True)
    return inverse * (delta - first - normal * second)


def embed_steps(steps):
    half = D // 2
    freqs = jnp.exp(-jnp.log(10000.0) * jnp.arange(half, dtype=FLOAT) / half)
    angles = steps.astype(FLOAT)[:, None] * freqs[None, :]
    return jnp.concatenate([jnp.cos(angles), jnp.sin(angles)], axis=1)


GELU_A = 0.7978845608028654
GELU_B = 0.044715


def gelu(z):
    return 0.5 * z * (1.0 + jnp.tanh(GELU_A * (z + GELU_B * z * z * z)))


def gelu_slope(z):
    t = jnp.tanh(GELU_A * (z + GELU_B * z * z * z))
    return 0.5 * (1.0 + t) + 0.5 * z * (1.0 - t * t) * GELU_A * (1.0 + 3.0 * GELU_B * z * z)


def matmul(left, right):
    return lax.dot_general(left, right, (((2,), (0,)), ((), ())), preferred_element_type=FLOAT)


def matmul_back(left, right):
    return lax.dot_general(left, right, (((2,), (1,)), ((), ())), preferred_element_type=FLOAT)


def weight_grad(left, right):
    return lax.dot_general(
        left, right, (((0, 1), (0, 1)), ((), ())), preferred_element_type=FLOAT
    )


SHARES = 16
SHARE_ROWS = 144
STAGES = (("row", 1), ("row", 2), ("col", 1), ("col", 2))


def share_place(stages):
    number = jnp.int32(0)
    for axis, bit in stages:
        number = 2 * number + (lax.axis_index(axis) // bit) % 2
    return number.reshape(1).astype(jnp.int32)


def product(act, delta):
    return lax.dot_general(act, delta, (((1,), (0,)), ((), ())), preferred_element_type=FLOAT)


def grad_send_kernel(place, act, delta, out):
    out[0] = product(act[0], delta[0]).astype(BFLOAT)


def grad_keep_kernel(place, act, delta, received, send, keep):
    value = (product(act[0], delta[0]) + received[0].astype(FLOAT)).astype(BFLOAT)
    first = pl.program_id(0) < SHARES // 4

    @pl.when(first)
    def _():
        send[0] = value

    @pl.when(jnp.logical_not(first))
    def _():
        keep[0] = value


class GradSum:
    def __init__(self, act, delta, act_index, delta_index, stages):
        self.act, self.delta, self.stages = act, delta, stages
        self.act_index, self.delta_index = act_index, delta_index
        self.place = share_place(stages)

    def call(self, kernel, position, extra, extra_specs, out_specs, out_shapes, through):
        tokens = self.act.shape[2]
        act_spec = pl.BlockSpec(
            (1, SHARE_ROWS, tokens), lambda i, m: self.act_index(position(i) ^ m[0])
        )
        delta_spec = pl.BlockSpec(
            (1, tokens, D), lambda i, m: self.delta_index(position(i) ^ m[0])
        )
        inputs = 3 + len(extra)

        def body(*refs):
            kernel(*refs[:inputs], *refs[inputs + 1 : -1])

        return pl.pallas_call(
            body,
            grid_spec=pltpu.PrefetchScalarGridSpec(
                num_scalar_prefetch=1,
                grid=(SHARES // 2,),
                in_specs=[act_spec, delta_spec] + extra_specs + [ANYWHERE],
                out_specs=out_specs + [ANYWHERE],
            ),
            out_shape=out_shapes + [jax.ShapeDtypeStruct(through.shape, through.dtype)],
            input_output_aliases={inputs: len(out_shapes)},
            cost_estimate=SMALL,
            compiler_params=params(),
        )(self.place, self.act, self.delta, *extra, through)

    def start(self, through):
        half = SHARES // 2
        block = (1, SHARE_ROWS, D)
        send, through = self.call(
            grad_send_kernel,
            lambda i: i + half,
            [],
            [],
            [pl.BlockSpec(block, lambda i, m: (i, 0, 0))],
            [jax.ShapeDtypeStruct((half, SHARE_ROWS, D), BFLOAT)],
            through,
        )
        self.flight = self.move(send, 0)
        return through

    def move(self, value, stage):
        axis, bit = self.stages[stage]
        return swap(value, axis, bit)

    def second(self, through):
        quarter = SHARES // 4
        block = (1, SHARE_ROWS, D)
        position = lambda i: i ^ quarter
        send, self.keep, through = self.call(
            grad_keep_kernel,
            position,
            [self.flight],
            [pl.BlockSpec(block, lambda i, m: (position(i), 0, 0))],
            [
                pl.BlockSpec(block, lambda i, m: (jnp.minimum(i, quarter - 1), 0, 0)),
                pl.BlockSpec(block, lambda i, m: (jnp.maximum(i - quarter, 0), 0, 0)),
            ],
            [jax.ShapeDtypeStruct((quarter, SHARE_ROWS, D), BFLOAT)] * 2,
            through,
        )
        self.flight = self.move(send, 1)
        self.state = 0
        return through

    works = ("halve", "halve", "add", "join", "join", "pass")
    own_state = 3
    offload = natural = False

    def advanced(self, outs):
        work = self.works[self.state]
        self.state += 1
        if work == "pass":
            self.keep, self.flight = outs
            self.pieces = [self.keep, self.flight]
            self.pieces += [self.move(piece, 0) for piece in self.pieces]
            return
        self.keep = outs[0]
        if not (self.offload and self.state == self.own_state):
            self.flight = self.onward(self.state, outs[-1])

    def onward(self, state, value):
        return self.move(value, (None, 2, 3, 3, 2, 1)[state])

    def done(self):
        return self.state == len(self.works)


class CrossGradSum(GradSum):
    works = ("halve", "halve", "add", "take", "join", "join", "pass")
    own_state = 4

    def onward(self, state, value):
        if state == 3:
            return self.cross(value)
        return self.move(value, (None, 2, 3, None, 3, 2, 1)[state])

    def cross(self, value):
        rows, cols = lax.axis_size("row"), lax.axis_size("col")
        pairs = []
        for x in range(2):
            for r in range(rows):
                for z in range(cols):
                    stays = r % 2 == x
                    to_x, to_r = (x, r) if stays else (1 - x, r ^ 1)
                    pairs.append(((x * rows + r) * cols + z, (to_x * rows + to_r) * cols + z))
        return lax.ppermute(value, ("batch", "row", "col"), pairs)


class Gathered:
    def __init__(self, sums):
        self.sums = sums

    def gather(self):
        self.collect(jnp.concatenate([one.keep for one in self.sums]))

    def collect(self, shares):
        whole = lax.all_gather(shares, GRID_AXES)
        for slot, one in enumerate(self.sums):
            one.whole, one.slot = whole, slot

    @staticmethod
    def finish(sums, kinds, previous, layer, shapes, through):
        block = (1, SHARE_ROWS, D)
        scalar = lax.axis_index("batch").reshape(1).astype(jnp.int32)

        def source(one):
            def index(i, m):
                core, y, low, high = i // 8, i // 4 % 2, i // 2 % 2, i % 2
                device = i if one.natural else (y * 2 + core) * 4 + high * 2 + low
                return (device, one.slot, 0, 0)

            return pl.BlockSpec((None,) + block, index)

        natural = sums[0].natural

        def expand(i, m):
            core, y = (i // 4 % 2, i // 8) if natural else (i // 8, i // 4 % 2)
            own = jnp.where(core == m[0], m[0], 1 - m[0])
            return (layer, i % 4, own * 2 + y)

        indices = (
            lambda i, m: (layer, i, 0),
            expand,
            lambda i, m: (0, i // 4, jnp.minimum(i % 4, 2)),
            lambda i, m: (0, i // 4, 0),
        )
        blocks = (block, block, (LAYERS,) + block[1:], (LAYERS,) + block[1:])
        targets = [k for kind in kinds[:3] for k in ((0,), (1,), (2, 3))["ABC".index(kind)]]
        kept = [k for k in targets if previous and k in previous]
        earlier = [previous[k] for k in kept]
        count, outs, given = len(earlier), len(targets), len(sums)

        def body(m, *refs):
            where = dict(zip(targets, refs[-1 - outs : -1]))
            last = pl.program_id(0) % 4 == 3
            done = 0
            for kind, ref in zip(kinds, refs):
                if kind != "C":
                    where["AB".index(kind)][0] = ref[0].astype(FLOAT)
                    continue

                at, done = done, done + 1

                @pl.when(last)
                def _(ref=ref, at=at):
                    where[3][at] = ref[0].astype(FLOAT)

                @pl.when(jnp.logical_not(last))
                def _(ref=ref, at=at):
                    where[2][at] = ref[0].astype(FLOAT)

        *results, through = pl.pallas_call(
            body,
            grid_spec=pltpu.PrefetchScalarGridSpec(
                num_scalar_prefetch=1,
                grid=(SHARES,),
                in_specs=[source(one) for one in sums] + [ANYWHERE] * (count + 1),
                out_specs=[pl.BlockSpec(blocks[k], indices[k]) for k in targets] + [ANYWHERE],
            ),
            out_shape=[jax.ShapeDtypeStruct(shapes[k], FLOAT) for k in targets]
            + [jax.ShapeDtypeStruct(through.shape, through.dtype)],
            input_output_aliases={1 + given + j: targets.index(k) for j, k in enumerate(kept)}
            | {1 + given + count: outs},
            cost_estimate=SMALL,
            compiler_params=params(),
        )(scalar, *[one.whole for one in sums], *earlier, through)
        return dict(zip(targets, results)), through


class Scattered(Gathered):
    def __init__(self):
        self.sums, self.group, self.shares = [], [], []

    def add(self, one, through):
        slot, tokens, dim = len(self.group), one.act.shape[2], len(self.shares) % 2
        one.offload = one.natural = True
        earlier = [self.buffer] if slot else []
        self.sums.append(one)
        self.group.append(one)
        count = len(earlier)
        shape = (1, SHARES) if dim else (SHARES, 2)
        place = lambda j: (slot, j, 0, 0) if dim else (j, slot, 0, 0)
        block = (1, 2) if dim else (2, 1)
        cross = isinstance(one, CrossGradSum)

        def body(act, delta, *refs):
            value = product(act[0], delta[0]).astype(BFLOAT)
            for k in range(2):
                part = value[k * SHARE_ROWS : (k + 1) * SHARE_ROWS]
                refs[count + 1][(0, k) if dim else (k, 0)] = part

        self.buffer, through = pl.pallas_call(
            body,
            grid=(SHARES // 2,),
            in_specs=[
                pl.BlockSpec(
                    (1, 2 * SHARE_ROWS, tokens), lambda j: (0, j % 4 if cross else j, 0)
                ),
                pl.BlockSpec((1, tokens, D), lambda j: (0, 0, j // 4 if cross else 0)),
            ]
            + [ANYWHERE] * (count + 1),
            out_specs=[pl.BlockSpec(block + (SHARE_ROWS, D), place), ANYWHERE],
            out_shape=[
                jax.ShapeDtypeStruct(shape + (SHARE_ROWS, D), BFLOAT),
                jax.ShapeDtypeStruct(through.shape, through.dtype),
            ],
            input_output_aliases={2 + k: k for k in range(count)} | {2 + count: 1},
            cost_estimate=SMALL,
            compiler_params=params(),
        )(one.act, one.delta, *earlier, through)
        return through

    def reduce(self):
        dim = len(self.shares) % 2
        summed = lax.psum_scatter(self.buffer, GRID_AXES, scatter_dimension=dim, tiled=True)
        self.shares.append(summed.reshape(-1, SHARE_ROWS, D))
        self.group = []

    def gather(self, after):
        shares = passed_by(self.shares, [after])
        shares = [part[slot] for part in shares for slot in range(part.shape[0])]
        for slot, one in enumerate(self.sums):
            if isinstance(one, CrossGradSum):
                shares[slot] = one.cross(shares[slot])
        self.collect(jnp.stack(shares))


class SmallSum:
    works = ("sum",) * 4

    def __init__(self, value):
        self.value, self.state = value, 0

    def start(self, through):
        self.keep, self.flight = self.value, self.move(0, self.value)
        return through

    def move(self, stage, value):
        return swap(value, *STAGES[stage])

    def advanced(self, outs):
        self.state += 1
        (self.keep,) = outs
        self.flight = None if self.done() else self.move(self.state, self.keep)

    def done(self):
        return self.state == len(self.works)


def tick_kernel(*refs, works):
    at, out = 0, 2 * len(works)
    for work in works:
        keep, flight = refs[at], refs[at + 1]
        at += 2
        count = keep.shape[0]
        if work == "sum":
            refs[out][...] = keep[...] + flight[...]
            out += 1
            continue
        if work == "join":
            refs[out][:count] = keep[...]
            refs[out][count:] = flight[...]
            out += 1
            continue
        for row in range(count):
            value = (keep[row].astype(FLOAT) + flight[row].astype(FLOAT)).astype(BFLOAT)
            if work == "add":
                refs[out][row] = value
            elif row < count // 2:
                refs[out][row] = value
            else:
                refs[out + 1][row - count // 2] = value
        out += 1 if work == "add" else 2


def tick(sums, through):
    if not sums:
        return through
    light = ("pass", "take")
    working = [one for one in sums if one.works[one.state] not in light]
    passing = [one for one in sums if one.works[one.state] in light]
    operands, shapes, counts, works = [], [], [], []
    for one in working:
        operands += [one.keep, one.flight]
        work, count = one.works[one.state], one.keep.shape[0]
        works.append(work)
        sizes = {"halve": [count // 2] * 2, "join": [2 * count]}.get(work, [count])
        counts.append(len(sizes))
        shapes += [
            jax.ShapeDtypeStruct((k,) + one.keep.shape[1:], one.keep.dtype) for k in sizes
        ]
    kept = lambda one: [one.flight] if one.works[one.state] == "take" else [one.keep, one.flight]
    passed = [value for one in passing for value in kept(one)] + [through]

    def body(*refs):
        ins, outs = refs[: len(operands)], refs[len(operands) + len(passed) :]
        tick_kernel(*ins, *outs, works=works)

    outs = pl.pallas_call(
        body,
        in_specs=[WHOLE] * len(operands) + [ANYWHERE] * len(passed),
        out_specs=[WHOLE] * len(shapes) + [ANYWHERE] * len(passed),
        out_shape=shapes + [jax.ShapeDtypeStruct(v.shape, v.dtype) for v in passed],
        input_output_aliases={
            len(operands) + k: len(shapes) + k for k in range(len(passed))
        },
        cost_estimate=SMALL,
        compiler_params=params(),
    )(*operands, *passed)
    at = 0
    for one, count in zip(working, counts):
        one.advanced(outs[at : at + count])
        at += count
    for one in passing:
        count = len(kept(one))
        one.advanced(outs[at : at + count])
        at += count
    return outs[-1]


def sum_small(value):
    for axis, bit in STAGES:
        value = value + swap(value, axis, bit)
    return value


def shrink_sum(act, outer_low):
    return GradSum(act[None], outer_low[None], lambda s: (0, s, 0), lambda s: (0, 0, 0), STAGES)


def expand_sum(act, inner_low):
    return CrossGradSum(
        act[None],
        inner_low[None],
        lambda s: (0, s // 8 * 4 + s % 4, 0),
        lambda s: (0, 0, s // 4 % 2),
        STAGES,
    )


def mixer_delta(own, other, branch, branch_other, places, width, size):
    tokens = own.shape[0]
    block = tokens // 4
    heads = width // HD

    def body(places, mine, theirs, low, low_other, out, logits):
        first = places[0] == 0
        values = mine[...].astype(FLOAT), theirs[...].astype(FLOAT)
        left = jnp.where(first, values[0], values[1])
        right = jnp.where(first, values[1], values[0])
        for j in range(3):
            part = slice(j * size, j * size + width)
            out[:, j * D : (j + 1) * D] = jnp.concatenate(
                [left[:, part], right[:, part]], axis=1
            ).astype(BFLOAT)
        half = pl.program_id(0) < 2

        @pl.when(half)
        def _():
            out[:, 3 * D :] = low[...]

        @pl.when(jnp.logical_not(half))
        def _():
            out[:, 3 * D :] = low_other[...]

        part = slice(width, width + heads)
        rest = jnp.zeros((block, LANES - 2 * heads), FLOAT)
        logits[...] = jnp.concatenate([left[:, part], right[:, part], rest], axis=1).astype(BFLOAT)

    return pl.pallas_call(
        body,
        grid_spec=pltpu.PrefetchScalarGridSpec(
            num_scalar_prefetch=1,
            grid=(4,),
            in_specs=[
                pl.BlockSpec((block, 3 * size), lambda i, m: (i, 0)),
                pl.BlockSpec((block, 3 * size), lambda i, m: (i ^ 2, 0)),
                pl.BlockSpec((block, D), lambda i, m: (jnp.minimum(i, 1), 0)),
                pl.BlockSpec((block, D), lambda i, m: (jnp.maximum(i - 2, 0), 0)),
            ],
            out_specs=[
                pl.BlockSpec((block, 4 * D), lambda i, m: (i, 0)),
                pl.BlockSpec((block, LANES), lambda i, m: (i, 0)),
            ],
        ),
        out_shape=[
            jax.ShapeDtypeStruct((tokens, 4 * D), BFLOAT),
            jax.ShapeDtypeStruct((tokens, LANES), BFLOAT),
        ],
        cost_estimate=SMALL,
        compiler_params=params(),
    )(places, own, other, branch, branch_other)


def mixer_sum(act, delta_project, branch, branch_other, places, width, size):
    delta, logits = mixer_delta(
        delta_project, swap(delta_project), branch, branch_other, places, width, size
    )
    return (
        GradSum(
            act,
            delta[None],
            lambda s: (jnp.where(s % 4 == 3, 1, 0), s // 4, 0),
            lambda s: (0, 0, s % 4),
            STAGES,
        ),
        logits,
    )


ITEMS = 2
ANYWHERE = pl.BlockSpec(memory_space=pl.ANY)
WHOLE = pl.BlockSpec(memory_space=pltpu.VMEM)


def call(body, shapes, arrays, places=None, held=(), after=(), scratch=()):
    first = 0 if places is None else 1
    count, kept, tied = len(arrays), len(held), len(after)

    def whole(*refs):
        ins = refs[first : first + count]
        far = refs[first + count : first + count + kept]
        at = first + count + kept + tied
        outs = refs[at : at + len(shapes)]
        body(refs[0] if first else None, ins, far, outs, refs[at + len(shapes) :])

    return pl.pallas_call(
        whole,
        in_specs=[pl.BlockSpec(memory_space=pltpu.SMEM)] * first
        + [WHOLE] * count
        + [ANYWHERE] * (kept + tied),
        out_specs=[WHOLE] * len(shapes),
        out_shape=[jax.ShapeDtypeStruct(*shape) for shape in shapes],
        scratch_shapes=list(scratch),
        cost_estimate=SMALL,
        compiler_params=params(),
    )(*([] if places is None else [places]), *arrays, *held, *after)


def edge_shapes(tile):
    rows, cols = tile
    sizes = [cols, cols, rows, rows]
    return [((ITEMS, size, D), BFLOAT) for size in sizes]


def put_edges(value, item, refs, tile):
    rows, cols = tile
    lines = [value[0], value[rows - 1]]
    for at in (0, cols - 1):
        lines.append(jnp.concatenate([value[r][at : at + 1] for r in range(rows)], axis=0))
    for ref, line in zip(refs, lines):
        ref[item] = line.astype(BFLOAT)


def halo_edges(edges):
    rows, cols = lax.axis_size("row"), lax.axis_size("col")
    first_row, last_row, first_col, last_col = edges
    top = lax.ppermute(last_row, "row", [(i, i + 1) for i in range(rows - 1)])
    bottom = lax.ppermute(first_row, "row", [(i + 1, i) for i in range(rows - 1)])
    to_right = jnp.concatenate([top[:, -1:], last_col, bottom[:, -1:]], axis=1)
    to_left = jnp.concatenate([top[:, :1], first_col, bottom[:, :1]], axis=1)
    left = lax.ppermute(to_right, "col", [(i, i + 1) for i in range(cols - 1)])
    right = lax.ppermute(to_left, "col", [(i + 1, i) for i in range(cols - 1)])
    return top, bottom, left, right


def modulated(value, mod, shift, scale):
    normal, inverse = normalize(value)
    return normal * (1.0 + mod[scale : scale + 1]) + mod[shift : shift + 1]


def enter_first(tokens, mod, tile):
    cells = (ITEMS,) + tile + (D,)

    def body(_, ins, far, outs, scratch):
        for i in range(ITEMS):
            hidden = modulated(ins[0][i].astype(FLOAT), ins[1][i], 0, 1).reshape(cells[1:])
            outs[0][i] = hidden.astype(BFLOAT)
            put_edges(hidden, i, outs[1:], tile)

    hidden, *edges = call(body, [(cells, BFLOAT)] + edge_shapes(tile), [tokens, mod])
    return hidden, edges


def enter_next(middle, own, received, mod_before, mod, tile):
    cells = (ITEMS,) + tile + (D,)
    count = middle.shape[1]

    def body(_, ins, far, outs, scratch):
        for i in range(ITEMS):
            at = slice(i * count, (i + 1) * count)
            outer = ins[1][at] + ins[2][at].astype(FLOAT)
            outs[1][i] = outer
            value = ins[0][i] + ins[3][i][5:6] * outer
            outs[0][i] = value
            hidden = modulated(value, ins[4][i], 0, 1).reshape(cells[1:])
            outs[2][i] = hidden.astype(BFLOAT)
            put_edges(hidden, i, outs[3:], tile)

    shapes = [(middle.shape, FLOAT), (middle.shape, FLOAT), (cells, BFLOAT)] + edge_shapes(tile)
    value, outer, hidden, *edges = call(body, shapes, [middle, own, received, mod_before, mod])
    return value, outer, hidden, edges


def leave(middle, own, received, mod):
    count = middle.shape[1]

    def body(_, ins, far, outs, scratch):
        for i in range(ITEMS):
            at = slice(i * count, (i + 1) * count)
            outer = ins[1][at] + ins[2][at].astype(FLOAT)
            outs[1][i] = outer
            outs[0][i] = (ins[0][i] + ins[3][i][5:6] * outer).astype(BFLOAT)

    return call(
        body, [(middle.shape, BFLOAT), (middle.shape, FLOAT)], [middle, own, received, mod]
    )


def gather_weight(far, scratch, sems, places, own):
    batch, quarter = places[0], places[1]
    rows = own.shape[0]
    size = rows // 4
    base = (1 - batch) * rows
    parts = [(own, batch * rows, rows)]
    for k in range(4):
        parts.append((far[k], base + (quarter ^ k) * size, size))
    copies = []
    for k, (source, start, count) in enumerate(parts):
        target = scratch.at[pl.ds(pl.multiple_of(start, 16), count)]
        copy = pltpu.make_async_copy(source, target, sems.at[k])
        copy.start()
        copies.append(copy)
    return copies


def split_logit(block, start, heads):
    lane = lax.broadcasted_iota(jnp.int32, block.shape, 1)
    here = (lane >= start) & (lane < start + heads)
    high = block.astype(BFLOAT).astype(FLOAT)
    rest = jnp.where(here, block - high, 0.0)
    middle = rest.astype(BFLOAT).astype(FLOAT)
    low = rest - middle
    return (
        jnp.where(here, high, block) + pltpu.roll(middle, heads, 1) + pltpu.roll(low, 2 * heads, 1)
    )


def project_call(own, other, weight, bias, places, cells, width):
    size = weight[0].shape[1] // 3
    block = width // LANES * LANES
    total = 2 * own.shape[0]
    count = total // cells

    def body(places, ins, far, outs, scratch):
        whole, joined, result, sems = scratch
        copies = gather_weight(far[1:], whole, sems, places, far[0])
        joined[: total // 2] = ins[0][...]
        joined[total // 2 :] = ins[1][...]
        for copy in copies:
            copy.wait()
        for part in range(3):
            columns = slice(part * size, (part + 1) * size)
            value = dot(joined[...], whole[:, columns])
            if part == 0:
                last = split_logit(
                    value[:, block : block + LANES] + ins[2][...], width - block, width // HD
                )
                result[:, :block] = value[:, :block].astype(BFLOAT)
                result[:, block : block + LANES] = last.astype(BFLOAT)
            else:
                result[:, columns] = value.astype(BFLOAT)
        for k in range(count):
            start = pl.multiple_of((places[2] ^ k) * cells, cells)
            outs[k][0] = result[pl.ds(start, cells)]

    return call(
        body,
        [((1, cells, 3 * size), BFLOAT)] * count,
        [own, other, bias],
        places,
        weight,
        scratch=[
            pltpu.VMEM((D, 3 * size), BFLOAT),
            pltpu.VMEM((total, D), BFLOAT),
            pltpu.VMEM((total, 3 * size), BFLOAT),
            pltpu.SemaphoreType.DMA((5,)),
        ],
    )


def halves_out(value, outs, columns, items_here):
    outs[0][:, columns] = value[:items_here]
    outs[1][:, columns] = value[items_here:].astype(BFLOAT)


COLUMNS = 384


def attend_out_call(blocks, weight, layer, places, cells, width):
    count = len(blocks)
    total = count * cells

    def body(places, ins, far, outs, scratch):
        whole, sems = scratch
        copy = pltpu.make_async_copy(far[0].at[layer], whole, sems.at[0])
        copy.start()
        for k in range(count):
            start = pl.multiple_of((places[2] ^ k) * cells, cells)
            outs[2][pl.ds(start, cells)] = ins[k][0]
        copy.wait()
        for at in range(0, D, COLUMNS):
            columns = slice(at, at + COLUMNS)
            halves_out(dot(outs[2][...], whole[:, columns]), outs, columns, total // 2)

    return call(
        body,
        [((total // 2, D), FLOAT), ((total // 2, D), BFLOAT), ((total, width), BFLOAT)],
        blocks,
        places,
        [weight],
        scratch=[pltpu.VMEM((width, D), BFLOAT), pltpu.SemaphoreType.DMA((1,))],
    )


def middle_call(tokens, own, received, mod):
    count = tokens.shape[1]

    def body(_, ins, far, outs, scratch):
        for i in range(ITEMS):
            at = slice(i * count, (i + 1) * count)
            branch = ins[1][at] + ins[2][at].astype(FLOAT)
            outs[0][i] = branch
            middle = ins[0][i].astype(FLOAT) + ins[3][i][2:3] * branch
            outs[1][i] = middle
            outs[2][at] = modulated(middle, ins[3][i], 3, 4).astype(BFLOAT)

    shape = tokens.shape
    return call(
        body,
        [(shape, FLOAT), (shape, FLOAT), ((ITEMS * count, D), BFLOAT)],
        [tokens, own, received, mod],
    )


def feed_call(own, other, expand, shrink, layer, places):
    total = 2 * own.shape[0]
    inner = shrink.shape[1]
    rows = expand[0].shape[1]
    tile = 256

    def body(places, ins, far, outs, scratch):
        wide, back, joined, sems = scratch
        start = pl.multiple_of(places[0] * inner, LANES)
        source = far[0].at[layer, :, pl.ds(start, inner)]
        copies = gather_weight(far[1:5], wide, sems, places, source)
        last = pltpu.make_async_copy(far[5].at[layer], back, sems.at[5])
        last.start()
        joined[: total // 2] = ins[0][...]
        joined[total // 2 :] = ins[1][...]
        for copy in copies:
            copy.wait()
        for at in range(0, inner, tile):
            columns = slice(at, at + tile)
            value = dot(joined[...], wide[:, columns])
            outs[2][:, columns] = value
            outs[3][:, columns] = gelu(value).astype(BFLOAT)
        last.wait()
        for at in range(0, D, COLUMNS):
            columns = slice(at, at + COLUMNS)
            halves_out(dot(outs[3][...], back[:, columns]), outs, columns, total // 2)

    return call(
        body,
        [
            ((total // 2, D), FLOAT),
            ((total // 2, D), BFLOAT),
            ((total, inner), FLOAT),
            ((total, inner), BFLOAT),
        ],
        [own, other],
        places,
        list(expand) + [shrink],
        scratch=[
            pltpu.VMEM((2 * rows, inner), BFLOAT),
            pltpu.VMEM((inner, D), BFLOAT),
            pltpu.VMEM((total, D), BFLOAT),
            pltpu.SemaphoreType.DMA((6,)),
        ],
    )


def turn_call(mixed, mixed_other, attend, second, second_other, active, places, through):
    tokens = attend.shape[0]
    width = attend.shape[1]
    padded = padded_width(width)
    inner = active.shape[1]
    half = mixed.shape[0]

    def turn(value):
        return jnp.transpose(value.astype(FLOAT)).astype(BFLOAT)

    def body(places, one, two, three, four, five, six, _, mixer, wide, long, __):
        first = places[0] == 0
        for ref, at in ((one, 0), (two, half)):
            value = turn(ref[...])
            mixer[0, :, at : at + half] = jnp.where(first, value[:width], value[width:])
        blank = jnp.zeros((tokens, padded - width), FLOAT)
        value = jnp.concatenate([three[...].astype(FLOAT), blank], axis=1)
        mixer[1] = jnp.transpose(value)[:width].astype(BFLOAT)
        wide[:, :half] = turn(four[...])
        wide[:, half:] = turn(five[...])
        for at in range(0, inner, 256):
            long[at : at + 256] = turn(six[:, at : at + 256])

    return pl.pallas_call(
        body,
        in_specs=[pl.BlockSpec(memory_space=pltpu.SMEM)] + [WHOLE] * 6 + [ANYWHERE],
        out_specs=[WHOLE] * 3 + [ANYWHERE],
        out_shape=[
            jax.ShapeDtypeStruct((2, width, tokens), BFLOAT),
            jax.ShapeDtypeStruct((D, tokens), BFLOAT),
            jax.ShapeDtypeStruct((inner, tokens), BFLOAT),
            jax.ShapeDtypeStruct(through.shape, through.dtype),
        ],
        input_output_aliases={7: 3},
        cost_estimate=SMALL,
        compiler_params=params(),
    )(places, mixed, mixed_other, attend, second, second_other, active, through)


def feed_back_call(own, other, inner_value, expand, shrink, layer, places):
    total = 2 * own.shape[0]
    inner = shrink.shape[1]
    rows = expand[0].shape[1]
    tile = 256

    def body(places, ins, far, outs, scratch):
        wide, back, joined, sems = scratch
        last = pltpu.make_async_copy(far[5].at[layer], back, sems.at[5])
        last.start()
        start = pl.multiple_of(places[0] * inner, LANES)
        source = far[0].at[layer, :, pl.ds(start, inner)]
        copies = gather_weight(far[1:5], wide, sems, places, source)
        joined[: total // 2] = ins[0][...]
        joined[total // 2 :] = ins[1][...]
        last.wait()
        for at in range(0, inner, tile):
            columns = slice(at, at + tile)
            value = dot(joined[...], back[at : at + tile], ((1,), (1,)))
            outs[2][:, columns] = (value * gelu_slope(ins[2][:, columns])).astype(BFLOAT)
        for copy in copies:
            copy.wait()
        for at in range(0, D, COLUMNS):
            columns = slice(at, at + COLUMNS)
            value = dot(outs[2][...], wide[at : at + COLUMNS], ((1,), (1,)))
            halves_out(value, outs, columns, total // 2)

    return call(
        body,
        [((total // 2, D), FLOAT), ((total // 2, D), BFLOAT), ((total, inner), BFLOAT)],
        [own, other, inner_value],
        places,
        list(expand) + [shrink],
        scratch=[
            pltpu.VMEM((2 * rows, inner), BFLOAT),
            pltpu.VMEM((inner, D), BFLOAT),
            pltpu.VMEM((total, D), BFLOAT),
            pltpu.SemaphoreType.DMA((6,)),
        ],
    )


def middle_back_call(delta, own, received, middle, branch, outer, mod):
    count = middle.shape[1]
    over = lambda v: jnp.sum(v, axis=0, keepdims=True)

    def body(_, ins, far, outs, scratch):
        for i in range(ITEMS):
            at = slice(i * count, (i + 1) * count)
            here = ins[0][i].astype(FLOAT)
            mod_here = ins[6][i]
            outs[2][i, 3:4] = over(here * ins[5][i])
            second = ins[1][at] + ins[2][at].astype(FLOAT)
            normal, inverse = normalize(ins[3][i])
            outs[2][i, 1:2] = over(second)
            outs[2][i, 2:3] = over(second * normal)
            total = here + normalize_back(second * (1.0 + mod_here[4:5]), normal, inverse)
            outs[0][i] = total
            outs[2][i, 0:1] = over(total * ins[4][i])
            outs[1][at] = (mod_here[2:3] * total).astype(BFLOAT)

    return call(
        body,
        [(middle.shape, FLOAT), ((ITEMS * count, D), BFLOAT), ((ITEMS, 4, D), FLOAT)],
        [delta, own, received, middle, branch, outer, mod],
    )


def attend_back_call(own, other, weight, layer, places, cells, width):
    total = 2 * own.shape[0]
    count = total // cells

    def body(places, ins, far, outs, scratch):
        whole, joined, result, sems = scratch
        copy = pltpu.make_async_copy(far[0].at[layer], whole, sems.at[0])
        copy.start()
        joined[: total // 2] = ins[0][...]
        joined[total // 2 :] = ins[1][...]
        copy.wait()
        result[...] = dot(joined[...], whole[...], ((1,), (1,))).astype(BFLOAT)
        for k in range(count):
            start = pl.multiple_of((places[2] ^ k) * cells, cells)
            outs[k][0] = result[pl.ds(start, cells)]

    return call(
        body,
        [((1, cells, width), BFLOAT)] * count,
        [own, other],
        places,
        [weight],
        scratch=[
            pltpu.VMEM((width, D), BFLOAT),
            pltpu.VMEM((total, D), BFLOAT),
            pltpu.VMEM((total, width), BFLOAT),
            pltpu.SemaphoreType.DMA((1,)),
        ],
    )


def project_back_call(blocks, weight, places, cells, width):
    count = len(blocks)
    total = count * cells
    wide = blocks[0].shape[2]

    def body(places, ins, far, outs, scratch):
        whole, sems = scratch
        copies = gather_weight(far[1:], whole, sems, places, far[0])
        for k in range(count):
            start = pl.multiple_of((places[2] ^ k) * cells, cells)
            outs[2][pl.ds(start, cells)] = ins[k][0]
        at = width // LANES * LANES
        logits = outs[2][:, at : at + LANES].astype(FLOAT)
        outs[3][...] = jnp.sum(logits, axis=0, keepdims=True)
        for copy in copies:
            copy.wait()
        for at in range(0, D, COLUMNS):
            columns = slice(at, at + COLUMNS)
            value = dot(outs[2][...], whole[at : at + COLUMNS], ((1,), (1,)))
            halves_out(value, outs, columns, total // 2)

    return call(
        body,
        [
            ((total // 2, D), FLOAT),
            ((total // 2, D), BFLOAT),
            ((total, wide), BFLOAT),
            ((1, LANES), FLOAT),
        ],
        blocks,
        places,
        weight,
        scratch=[pltpu.VMEM((D, wide), BFLOAT), pltpu.SemaphoreType.DMA((5,))],
    )


def conv_delta_call(own, received, convolved, tile):
    cells = convolved.shape
    count = tile[0] * tile[1]

    def body(_, ins, far, outs, scratch):
        for i in range(ITEMS):
            at = slice(i * count, (i + 1) * count)
            delta = (ins[0][at] + ins[1][at].astype(FLOAT)).reshape(cells[1:])
            value = ins[2][i]
            gate = jax.nn.sigmoid(value)
            delta = delta * gate * (1.0 + value * (1.0 - gate))
            outs[0][i] = delta.astype(BFLOAT)
            put_edges(delta, i, outs[1:], tile)

    delta, *edges = call(
        body, [(cells, BFLOAT)] + edge_shapes(tile), [own, received, convolved]
    )
    return delta, edges


def enter_back_call(delta_hidden, tokens, delta_middle, mod, mod_before):
    count = tokens.shape[1]
    over = lambda v: jnp.sum(v, axis=0, keepdims=True)
    lower = mod_before is not None

    def body(_, ins, far, outs, scratch):
        for i in range(ITEMS):
            at = slice(i * count, (i + 1) * count)
            here = ins[0][i].reshape(count, D)
            normal, inverse = normalize(ins[1][i].astype(FLOAT))
            outs[0][i, 0:1] = over(here)
            outs[0][i, 1:2] = over(here * normal)
            total = ins[2][i] + normalize_back(here * (1.0 + ins[3][i][1:2]), normal, inverse)
            if lower:
                outs[2][i] = total
                outs[1][at] = (ins[4][i][5:6] * total).astype(BFLOAT)
            else:
                outs[1][at] = total.astype(BFLOAT)

    shapes = [((ITEMS, 2, D), FLOAT), ((ITEMS * count, D), BFLOAT)]
    arrays = [delta_hidden, tokens, delta_middle, mod]
    if lower:
        shapes.append((tokens.shape, FLOAT))
        arrays.append(mod_before)
    return call(body, shapes, arrays)


def pack_kernel(places, qkv, decay, own, other, *, width):
    heads = width // HD
    size = padded_width(width + 3 * heads)
    value, extra = qkv[0].astype(FLOAT), decay[0].astype(FLOAT)
    rows = value.shape[0]
    pieces = []
    for group in range(2):
        parts = []
        for j in range(3):
            start = j * D + group * width
            parts.append(value[:, start : start + width])
            filled = width
            if j == 0:
                parts.append(extra[:, group * heads : (group + 1) * heads])
                filled += heads
            parts.append(jnp.zeros((rows, size - filled), FLOAT))
        pieces.append(jnp.concatenate(parts, axis=1).astype(BFLOAT))
    first = places[0] == 0
    own[...] = jnp.where(first, pieces[0], pieces[1])
    other[...] = jnp.where(first, pieces[1], pieces[0])


def pack_call(qkv, decay, layer, places, width):
    rows = qkv.shape[1]
    size = padded_width(width + 3 * (width // HD))

    def body(*refs):
        pack_kernel(*refs, width=width)

    out = pl.BlockSpec((SHARE_ROWS, 3 * size), lambda i, m: (i, 0))
    return pl.pallas_call(
        body,
        grid_spec=pltpu.PrefetchScalarGridSpec(
            num_scalar_prefetch=1,
            grid=(rows // SHARE_ROWS,),
            in_specs=[
                pl.BlockSpec((1, SHARE_ROWS, qkv.shape[2]), lambda i, m: (layer, i, 0)),
                pl.BlockSpec((1, SHARE_ROWS, decay.shape[2]), lambda i, m: (layer, i, 0)),
            ],
            out_specs=[out, out],
        ),
        out_shape=[jax.ShapeDtypeStruct((rows, 3 * size), BFLOAT)] * 2,
        cost_estimate=SMALL,
        compiler_params=params(),
    )(places, qkv, decay)


def passed_by(values, after):
    count = len(values)
    return pl.pallas_call(
        lambda *refs: None,
        in_specs=[ANYWHERE] * (count + len(after)),
        out_specs=[ANYWHERE] * count,
        out_shape=[jax.ShapeDtypeStruct(v.shape, v.dtype) for v in values],
        input_output_aliases={k: k for k in range(count)},
        cost_estimate=SMALL,
        compiler_params=params(),
    )(*values, *after)


def lines_swapped(blocks, axis):
    return [blocks[0]] + [swap(blocks[k], axis, k) for k in range(1, len(blocks))]


class Pair:
    def __init__(self, args, taps, tile):
        self.args, self.taps, self.tile = args, taps, tile
        self.modulations = [None] * LAYERS
        self.cells = tile[0] * tile[1]
        self.width = args["proj"].shape[1]
        self.heads = self.width // HD
        self.size = padded_width(self.width + 3 * self.heads)
        batch, row = lax.axis_index("batch"), lax.axis_index("row")
        quarter = row % 2 * 2 + row // 2
        self.places = [
            jnp.stack([batch, quarter, lax.axis_index(axis)]).astype(jnp.int32)
            for axis in ("col", "row")
        ]
        self.qkv, self.expand, self.bias = [], [], []
        self.pieces = {}
        self.quarter, self.batch = quarter, batch
        self.modulate()
        for layer in range(LAYERS):
            self.prepare(layer)
        for stage in range(3):
            self.fetch("qkv", 0, stage, [])

    def prepare(self, layer):
        args = self.args
        own, other = pack_call(args["qkv"], args["decay"], layer, self.places[0], self.width)
        part = own.shape[0] // 4
        self.pieces["qkv", layer] = lax.dynamic_slice_in_dim(other, self.quarter * part, part, 0)
        self.qkv.append([own])
        inner = args["shrink"].shape[1]
        piece = lax.dynamic_slice(
            args["expand"],
            (layer, self.quarter * part, (1 - self.batch) * inner),
            (1, part, inner),
        )
        self.pieces["expand", layer] = piece[0]
        self.expand.append([args["expand"]])
        start = self.width - self.width // LANES * LANES
        self.bias.append(
            jnp.pad(
                args["decay_bias"][layer].astype(FLOAT)[None],
                ((0, 0), (start, LANES - start - self.heads)),
            )
        )

    def modulate(self):
        cond = self.args["cond"]
        partial = jnp.stack(
            [
                jnp.dot(cond, self.args["ada"][layer], preferred_element_type=FLOAT)
                for layer in range(LAYERS)
            ],
            axis=1,
        )
        total = partial[:ITEMS] + swap(partial[ITEMS:])
        for layer in range(LAYERS):
            value = total[:, layer] + self.args["ada_bias"][layer]
            self.modulations[layer] = value.reshape(ITEMS, 6, D)

    def fetch(self, name, layer, stage, after):
        held = self.pieces[name, layer]
        if stage == 0:
            if after:
                (held,) = passed_by([held], after)
            self.pieces[name, layer] = [swap(held)]
        elif stage == 1:
            if after:
                held = passed_by(held, after)
            self.pieces[name, layer] = [held[0], swap(held[0], "row", 2)]
        else:
            if after:
                held = passed_by(held, after)
            into = self.qkv if name == "qkv" else self.expand
            into[layer] += list(held) + [swap(part, "row", 1) for part in held]

    def axis(self, layer):
        return "col" if layer % 2 == 0 else "row"

    def scan(self, kernel, layer, inputs, out_width):
        place = self.places[layer % 2][2]
        rows, cols = self.tile
        return scan_call(
            kernel, place, inputs, out_width, rows, cols, layer % 2 == 0, self.width
        )

    def forward(self, layer, hidden, edges, tokens):
        places, axis = self.places[layer % 2], self.axis(layer)
        mod = self.modulations[layer]
        sides = halo_edges(edges)
        convolved, mixed = conv_forward(hidden, sides, self.taps[layer])
        mixed = mixed.reshape(-1, D)
        mixed_other = swap(mixed)
        if layer == 0:
            self.fetch("expand", 0, 0, [hidden])
            self.fetch("expand", 0, 1, [mixed])
        else:
            self.fetch("expand", 1, 1, [mixed])
        parts = project_call(
            mixed, mixed_other, self.qkv[layer], self.bias[layer], places, self.cells, self.width
        )
        parts = list(parts)
        self.fetch("expand", layer, 2, [parts[0]])
        if layer + 1 < LAYERS:
            self.fetch("qkv", layer + 1, 0, [parts[0]])
        parts = lines_swapped(parts, axis)
        attends = self.scan(scan_forward_kernel, layer, parts, self.width)
        own, send, attend = attend_out_call(
            lines_swapped(attends, axis), self.args["proj"], layer, places, self.cells, self.width
        )
        if layer + 1 < LAYERS:
            self.fetch("qkv", layer + 1, 1, [own])
        branch, middle, second = middle_call(tokens, own, swap(send), mod)
        second_other = swap(second)
        if layer + 1 < LAYERS:
            self.fetch("qkv", layer + 1, 2, [second])
        own, send, inner, active = feed_call(
            second, second_other, self.expand[layer], self.args["shrink"], layer, places
        )
        if layer + 1 < LAYERS:
            self.fetch("expand", layer + 1, 0, [own])
        received = swap(send)
        mixer_act, second_act, active_act, own = turn_call(
            mixed, mixed_other, attend, second, second_other, active, places, own
        )
        saved = dict(
            tokens=tokens, hidden=hidden, sides=sides, convolved=convolved, parts=parts,
            branch=branch, middle=middle, inner=inner, mixer_act=mixer_act,
            second_act=second_act, active_act=active_act,
        )
        return middle, own, received, saved

    def backward(self, layer, delta, outer_low, outer_other, saved, tick):
        places, axis = self.places[layer % 2], self.axis(layer)
        mod = self.modulations[layer]
        both = lambda own, other: jnp.concatenate([own, other], axis=0)
        own, send, inner_low = feed_back_call(
            outer_low, outer_other, saved["inner"], self.expand[layer], self.args["shrink"],
            layer, places,
        )
        received = swap(send)
        shrink_pipe = shrink_sum(saved["active_act"], both(outer_low, outer_other))
        own = tick("P1", {"A": shrink_pipe}, own)
        delta_middle, branch_low, mod_b = middle_back_call(
            delta, own, received, saved["middle"], saved["branch"], saved["outer"], mod
        )
        branch_other = swap(branch_low)
        expand_pipe = expand_sum(saved["second_act"], inner_low)
        branch_low = tick("P2", {"B": expand_pipe}, branch_low)
        blocks = attend_back_call(
            branch_low, branch_other, self.args["proj"], layer, places, self.cells, self.width
        )
        sent = lines_swapped(blocks, axis)
        sent[0] = tick("P3", {}, sent[0])
        projects = self.scan(
            scan_backward_kernel, layer, list(saved["parts"]) + sent, 3 * self.size
        )
        sent = lines_swapped(projects, axis)
        sent[0] = tick("P4", {}, sent[0])
        own, send, delta_project, grad_bias = project_back_call(
            sent, self.qkv[layer], places, self.cells, self.width
        )
        received = swap(send)
        def mixer(after):
            (value,) = passed_by([delta_project], after)
            act = saved["mixer_act"]
            pipe, logits = mixer_sum(
                act, value, branch_low, branch_other, places, self.width, self.size
            )
            return pipe, dot(logits, act[0], ((0,), (1,)))[: 2 * self.heads]

        if not layer:
            mixer_pipe, grad_decay = mixer([])
        own = tick("P5", {}, own)
        delta_conv, edges = conv_delta_call(own, received, saved["convolved"], self.tile)
        delta_sides = halo_edges(edges)
        delta_conv = tick("P6", {}, delta_conv)
        if layer:
            mixer_pipe, grad_decay = mixer([delta_conv])
        top, bottom, left, right = delta_sides
        (left,) = passed_by([left], [right])
        left = tick("P8", {"C": mixer_pipe}, left)
        delta_sides = (top, bottom, left, right)
        delta_hidden, grad_taps = conv_backward(
            saved["hidden"], saved["sides"], delta_conv, delta_sides, self.taps[layer]
        )
        before = self.modulations[layer - 1] if layer else None
        mod_a, low, *rest = enter_back_call(
            delta_hidden, saved["tokens"], delta_middle, mod, before
        )
        low_other = swap(low) if rest else None

        small = SmallSum(join_smalls(mod_a, mod_b, grad_taps, grad_decay, grad_bias))
        low = tick("P7", {"S": small}, low)
        return rest[0] if rest else None, low, low_other


def pair_forward_backward(pair, tokens_in, cotangent, tick):
    tile = pair.tile
    shape = (ITEMS, pair.cells, D)
    tokens = tokens_in.reshape(shape)
    delta = cotangent.reshape(shape)
    hidden, edges = enter_first(tokens, pair.modulations[0], tile)
    stored = []
    for layer in range(LAYERS):
        middle, own, received, saved = pair.forward(layer, hidden, edges, tokens)
        stored.append(saved)
        mod = pair.modulations[layer]
        if layer + 1 < LAYERS:
            tokens, saved["outer"], hidden, edges = enter_next(
                middle, own, received, mod, pair.modulations[layer + 1], tile
            )
        else:
            block_out, saved["outer"] = leave(middle, own, received, mod)
    outer_low = (pair.modulations[-1][:, 5:6] * delta.astype(FLOAT)).astype(BFLOAT)
    outer_low = outer_low.reshape(-1, D)
    outer_other = swap(outer_low)
    for layer in reversed(range(LAYERS)):
        delta, outer_low, outer_other = pair.backward(
            layer, delta, outer_low, outer_other, stored[layer],
            lambda point, fresh, through, layer=layer: tick(layer, point, fresh, through),
        )
    return block_out, outer_low


def forward_layer(tokens, modulation, weights, layer, tile):
    taps, qkv, decay_bias, proj, expand, shrink = weights
    rows, cols = tile
    items, cells = tokens.shape[:2]
    width = proj.shape[0]
    heads = width // HD
    size = padded_width(width + 3 * heads)
    axis = "col" if layer % 2 == 0 else "row"
    mod = [modulation[:, k][:, None] for k in range(6)]
    normal, inverse = normalize(tokens)
    hidden = (normal * (1.0 + mod[1]) + mod[0]).astype(BFLOAT).reshape(items, rows, cols, D)
    sides = halo(hidden)
    convolved, mixed = conv_forward(hidden, sides, taps)
    mixed = gather_items(mixed.reshape(items, cells, D))
    project = matmul(mixed, qkv)
    logit = project[:, :, width : width + heads] + decay_bias.astype(FLOAT)
    high = logit.astype(BFLOAT)
    rest = logit - high.astype(FLOAT)
    middle_part = rest.astype(BFLOAT)
    low = (rest - middle_part.astype(FLOAT)).astype(BFLOAT)
    project = project.astype(BFLOAT)
    project = jnp.concatenate(
        [project[:, :, :width], high, middle_part, low, project[:, :, width + 3 * heads :]], axis=2
    )
    parts = lines_out(project, axis)
    place = lax.axis_index(axis)
    attends = scan_call(
        scan_forward_kernel, place, parts, width, rows, cols, layer % 2 == 0, width
    )
    attend = lines_back(attends, axis)
    branch = reduce_items(matmul(attend, proj))
    middle = tokens + mod[2] * branch
    normal2, inverse2 = normalize(middle)
    second = gather_items((normal2 * (1.0 + mod[4]) + mod[3]).astype(BFLOAT))
    inner = matmul(second, expand)
    active = gelu(inner).astype(BFLOAT)
    outer = reduce_items(matmul(active, shrink))
    result = middle + mod[5] * outer
    saved = (
        normal, inverse, hidden, sides, convolved, mixed, parts, attend, branch,
        normal2, inverse2, second, inner, active, outer,
    )
    return result, saved


def pipelined(width):
    shares = lax.axis_size("row") * lax.axis_size("col")
    square = lax.axis_size("row") == 4 and lax.axis_size("col") == 4
    return lax.axis_size("batch") == 2 and square and width == 4 * SHARE_ROWS and shares == SHARES


def backward_layer(delta, saved, modulation, weights, layer, tile):
    taps, qkv, decay_bias, proj, expand, shrink = weights
    (
        normal, inverse, hidden, sides, convolved, mixed, parts, attend, branch,
        normal2, inverse2, second, inner, active, outer,
    ) = saved
    rows, cols = tile
    items, cells = delta.shape[:2]
    width = proj.shape[0]
    heads = width // HD
    size = padded_width(width + 3 * heads)
    axis = "col" if layer % 2 == 0 else "row"
    mod = [modulation[:, k][:, None] for k in range(6)]
    over = lambda v: jnp.sum(v, axis=1)
    delta_gate2 = over(delta * outer)
    outer_low = gather_items((mod[5] * delta).astype(BFLOAT))
    grad_shrink = weight_grad(active, outer_low)
    inner_low = (matmul_back(outer_low, shrink) * gelu_slope(inner)).astype(BFLOAT)
    grad_expand = weight_grad(second, inner_low)
    delta_second = reduce_items(matmul_back(inner_low, expand))
    delta_shift2 = over(delta_second)
    delta_scale2 = over(delta_second * normal2)
    delta_middle = delta + normalize_back(delta_second * (1.0 + mod[4]), normal2, inverse2)
    delta_gate1 = over(delta_middle * branch)
    branch_low = gather_items((mod[2] * delta_middle).astype(BFLOAT))
    grad_proj = weight_grad(attend, branch_low)
    delta_attend = matmul_back(branch_low, proj).astype(BFLOAT)
    delta_parts = lines_out(delta_attend, axis)
    place = lax.axis_index(axis)
    projects = scan_call(
        scan_backward_kernel, place, list(parts) + delta_parts, 3 * size, rows, cols,
        layer % 2 == 0, width,
    )
    delta_project = lines_back(projects, axis)
    grad_qkv = weight_grad(mixed, delta_project)
    sums = (grad_shrink, grad_expand, grad_proj, grad_qkv)
    grad_decay_bias = jnp.sum(delta_project[:, :, width : width + heads].astype(FLOAT), axis=(0, 1))
    delta_mixed = reduce_items(matmul_back(delta_project, qkv)).reshape(convolved.shape)
    gate = jax.nn.sigmoid(convolved)
    delta_conv = (delta_mixed * gate * (1.0 + convolved * (1.0 - gate))).astype(BFLOAT)
    delta_sides = halo(delta_conv)
    delta_hidden, grad_taps = conv_backward(hidden, sides, delta_conv, delta_sides, taps)
    delta_hidden = delta_hidden.reshape(items, cells, D)
    delta_shift1 = over(delta_hidden)
    delta_scale1 = over(delta_hidden * normal)
    delta_tokens = delta_middle + normalize_back(delta_hidden * (1.0 + mod[1]), normal, inverse)
    delta_mod = jnp.stack(
        [delta_shift1, delta_scale1, delta_gate1, delta_shift2, delta_scale2, delta_gate2], axis=1
    )
    return delta_tokens, sums, (delta_mod, grad_taps, None, grad_decay_bias)


def sum_rows_here(grad):
    return lax.psum(grad.astype(BFLOAT), GRID_AXES).astype(FLOAT)


def sum_columns(grad):
    count = lax.axis_size("batch")
    low = grad.astype(BFLOAT).reshape((count, -1, grad.shape[1]))
    shares = lax.axis_size("row") * lax.axis_size("col")
    if count == 2 and low.shape[1] % shares == 0:
        share = lax.psum_scatter(low, GRID_AXES, scatter_dimension=1, tiled=True)
        place = lax.axis_index("batch")
        own = lax.dynamic_index_in_dim(share, place, 0, keepdims=False)
        other = swap(lax.dynamic_index_in_dim(share, 1 - place, 0, keepdims=False))
        both = jnp.stack([jnp.where(place == 0, own, other), jnp.where(place == 0, other, own)])
        return lax.all_gather(both, GRID_AXES, axis=1, tiled=True)
    total = lax.psum(low, GRID_AXES)
    return lax.all_to_all(total, "batch", 0, 0)


def ada_call(cond, mods, previous, layer, through):
    items, rows = cond.shape
    wide = mods.shape[1]
    block = 64
    previous = [] if previous is None else [previous]

    def body(columns, values, *refs):
        out = refs[-2]
        for at in range(0, wide, D):
            part = slice(at, at + D)
            total = columns[:, 0:1] * values[0:1, part]
            for item in range(1, items):
                total += columns[:, item : item + 1] * values[item : item + 1, part]
            out[0, :, part] = total

    count = len(previous)
    return pl.pallas_call(
        body,
        grid=(rows // block,),
        in_specs=[
            pl.BlockSpec((block, items), lambda i: (i, 0)),
            pl.BlockSpec((items, wide), lambda i: (0, 0)),
        ]
        + [ANYWHERE] * (count + 1),
        out_specs=[pl.BlockSpec((1, block, wide), lambda i: (layer, i, 0)), ANYWHERE],
        out_shape=[
            jax.ShapeDtypeStruct((LAYERS, rows, wide), FLOAT),
            jax.ShapeDtypeStruct(through.shape, through.dtype),
        ],
        input_output_aliases={2 + k: k for k in range(count)} | {2 + count: 1},
        cost_estimate=SMALL,
        compiler_params=params(),
    )(jnp.transpose(cond.astype(FLOAT)), mods, *previous, through)


SCHEDULE = {
    (1, "P1"): "aA1",
    (1, "P2"): "aB1rL1",
    (1, "P7"): "sC1",
    (0, "P1"): "kC1sA0",
    (0, "P2"): "kA0sB0",
    (0, "P3"): "gL1kB0",
    (0, "P5"): "tC1",
    (0, "P8"): "sC0kC0tC1tA0",
    (0, "P7"): "tC1tA0tB0sS0",
}
TAIL = (
    "tA0tB0tC0tS0",
    "tB0tC0tS0",
    "tB0tC0tS0gL0",
    "tS0",
    "mS1",
    "fAB1",
    "mS0",
    "fABC0",
)


SMALL_ROWS = 32


def join_smalls(mod_a, mod_b, grad_taps, grad_decay, grad_bias):
    heads = grad_decay.shape[0] // 2

    def body(_, ins, far, outs, scratch):
        out = outs[0]
        for i in range(ITEMS):
            out[6 * i : 6 * i + 2] = ins[0][i]
            out[6 * i + 2 : 6 * i + 6] = ins[1][i]
        out[12:21] = ins[2][...]
        out[21 : 21 + heads] = jnp.concatenate([ins[3][:heads], ins[3][heads:]], axis=1)
        bias = jnp.concatenate([ins[4][...], jnp.zeros((1, D - LANES), FLOAT)], axis=1)
        out[21 + heads : 22 + heads] = bias
        out[22 + heads :] = jnp.zeros((SMALL_ROWS - 22 - heads, D), FLOAT)

    return call(
        body, [((SMALL_ROWS, D), FLOAT)], [mod_a, mod_b, grad_taps, grad_decay, grad_bias]
    )[0]


def split_smalls(flat, items, heads, width):
    start = width - width // LANES * LANES
    decay = flat[21 : 21 + heads]
    return (
        flat[: items * 6].reshape(items, 6 * D),
        flat[12:21],
        jnp.concatenate([decay[:, :width], decay[:, width:]], axis=0),
        flat[21 + heads, start : start + heads],
    )


def general_forward_backward(
    tokens_in, cotangent, modulations, taps_all, qkv_weight, decay_weight, decay_bias,
    proj_weight, expand_weight, shrink_weight,
):
    count = lax.axis_size("batch")
    items, rows, cols = tokens_in.shape[:3]
    tile = (rows, cols)
    width = proj_weight.shape[1]
    weights = []
    for layer in range(LAYERS):
        qkv = fetch_columns(
            [head_columns(qkv_weight[layer], decay_weight[layer], g, width) for g in range(count)]
        )
        inner = expand_weight.shape[2] // count
        expand = fetch_columns(
            [expand_weight[layer][:, g * inner : (g + 1) * inner] for g in range(count)]
        )
        weights.append(
            (taps_all[layer], qkv, decay_bias[layer], proj_weight[layer], expand, shrink_weight[layer])
        )
    tokens = tokens_in.astype(FLOAT).reshape(items, rows * cols, D)
    stored = []
    for layer in range(LAYERS):
        tokens, saved = forward_layer(tokens, modulations[layer], weights[layer], layer, tile)
        stored.append(saved)
    delta = cotangent.astype(FLOAT).reshape(tokens.shape)
    bigs, smalls = [None] * LAYERS, [None] * LAYERS
    for layer in reversed(range(LAYERS)):
        delta, big, small = backward_layer(
            delta, stored[layer], modulations[layer], weights[layer], layer, tile
        )
        grad_shrink, grad_expand, grad_proj, grad_qkv = big
        bigs[layer] = (
            sum_rows_here(grad_shrink),
            sum_columns(grad_expand),
            sum_rows_here(grad_proj),
            sum_columns(grad_qkv),
        )
        smalls[layer] = tuple(
            None if part is None else lax.psum(part, GRID_AXES) for part in small
        )
    return tokens.astype(BFLOAT), delta.astype(BFLOAT), bigs, smalls


def per_device(
    tokens_in, timesteps, ada_weight, ada_bias, conv_taps, qkv_weight, decay_weight, decay_bias,
    proj_weight, expand_weight, shrink_weight, cotangent,
):
    count, place = lax.axis_size("batch"), lax.axis_index("batch")
    items, rows, cols = tokens_in.shape[:3]
    tile = (rows, cols)
    rows_here = ada_weight.shape[1]
    width = proj_weight.shape[1]
    heads = width // HD
    size = padded_width(width + 3 * heads)
    cond = jax.nn.silu(embed_steps(timesteps)).astype(BFLOAT)
    cond_slice = lax.dynamic_slice_in_dim(cond, place * rows_here, rows_here, 1)
    order = [0] if count != 2 else None
    if count == 2:
        cond_first = jnp.where(
            place == 0, cond_slice, jnp.concatenate([cond_slice[items:], cond_slice[:items]])
        )
    else:
        cond_first = cond_slice
    biases = gather_last(ada_bias).astype(FLOAT)
    taps_all = gather_last(conv_taps)
    fast = pipelined(width) and count * items == 4 and tile == (8, 8)
    hidden_units = shrink_weight.shape[1]
    if fast:
        moving = {}
        upper_sums = Scattered()

        def act(names, through):
            names = [names[at : at + 3] for at in range(0, len(names), 3)]
            steps = []
            for name in names + ["end"]:
                if name[0] == "t":
                    steps.append(moving[name[1:]])
                    continue
                through = tick(steps, through)
                steps = []
                one = moving.get(name[1:])
                if name[0] == "s":
                    through = one.start(through)
                elif name[0] == "k":
                    through = one.second(through)
                elif name == "gL1":
                    upper_sums.gather(through)
                elif name == "gL0":
                    Gathered([moving[name] for name in ("C1", "A0", "B0", "C0")]).gather()
                elif name[0] == "a":
                    through = upper_sums.add(one, through)
                elif name[0] == "r":
                    upper_sums.reduce()
            return through

        def step(layer, point, fresh, through):
            for name, one in fresh.items():
                moving[name if len(name) == 2 else name + str(layer)] = one
                if name in "ABC":
                    one.offload = True
            if "S" in fresh and not layer:
                moving["S0"] = SmallSum(
                    jnp.concatenate([moving["S0"].value, moving["S1"].value], axis=0)
                )
            return act(SCHEDULE.get((layer, point), ""), through)

        pair = Pair(
            dict(
                qkv=qkv_weight, decay=decay_weight, decay_bias=decay_bias, proj=proj_weight,
                expand=expand_weight, shrink=shrink_weight, cond=cond_first, ada=ada_weight,
                ada_bias=biases,
            ),
            taps_all,
            tile,
        )
        block_out, through = pair_forward_backward(pair, tokens_in, cotangent, step)
        shapes = [
            (LAYERS, hidden_units, D),
            (LAYERS, rows_here, expand_weight.shape[2]),
            (LAYERS, rows_here, 3 * D),
            (LAYERS, width, D),
        ]
        finished = None
        grad_ada = None
        smalls = [None] * LAYERS
        for names in TAIL:
            if names[0] == "f":
                kinds = names[1:-1]
                layer = int(names[-1])
                sums = [moving[kind + names[-1]] for kind in kinds]
                if kinds[-1] == "C":
                    kinds, sums = kinds + "C", sums + [moving["C1"]]
                made, through = Gathered.finish(
                    sums, kinds,
                    None if layer else finished, layer, shapes, through,
                )
                finished = (finished or {}) | made
            elif names[0] == "m":
                layer = int(names[2])
                flat = moving["S0"].keep[layer * SMALL_ROWS : (layer + 1) * SMALL_ROWS]
                smalls[layer] = list(split_smalls(flat, items, heads, width))
                mods = gather_items(smalls[layer][0])
                smalls[layer][0] = mods
                grad_ada, through = ada_call(cond_first, mods, grad_ada, layer, through)
            else:
                through = act(names, through)
        grad_tokens = through
    else:
        partial = jnp.stack(
            [
                jnp.dot(cond_first, ada_weight[layer], preferred_element_type=FLOAT)
                for layer in range(LAYERS)
            ],
            axis=1,
        )
        if count == 2:
            total = partial[:items] + swap(partial[items:])
        else:
            total = lax.psum_scatter(partial, "batch", scatter_dimension=0, tiled=True)
        modulations = [
            (total[:, layer] + biases[layer]).reshape(items, 6, D) for layer in range(LAYERS)
        ]
        block_out, grad_tokens, bigs, smalls = general_forward_backward(
            tokens_in, cotangent, modulations, taps_all, qkv_weight, decay_weight, decay_bias,
            proj_weight, expand_weight, shrink_weight,
        )
    block_out = block_out.reshape(tokens_in.shape)
    grad_tokens = grad_tokens.reshape(tokens_in.shape)
    delta_mods, taps_grads, bias_grads = (
        jnp.stack([smalls[layer][k] for layer in range(LAYERS)]) for k in (0, 1, 3)
    )
    if fast:
        every_mod = delta_mods.transpose(1, 0, 2)
    else:
        every_mod = gather_items(delta_mods.transpose(1, 0, 2, 3)).reshape(
            count * items, LAYERS, 6 * D
        )
    if count == 2:
        taps_every = taps_grads + swap(taps_grads)
    else:
        taps_every = lax.psum(taps_grads, "batch")
    grad_taps = lax.dynamic_slice_in_dim(taps_every, place * width, width, 2)
    if not fast:
        grad_ada = jnp.zeros((LAYERS, rows_here, 6 * D), FLOAT)
        for item in range(count * items):
            grad_ada += (
                cond_first[item].astype(FLOAT)[None, :, None] * every_mod[item][:, None, :]
            )
    bias_width = ada_bias.shape[1]
    grad_ada_bias = lax.dynamic_slice_in_dim(
        jnp.sum(every_mod, axis=0), place * bias_width, bias_width, 1
    )
    if fast:
        grad_shrink, grad_expand, grad_qkv, grad_proj = (finished[k] for k in range(4))
        grad_decay = jnp.stack([jnp.transpose(smalls[layer][2]) for layer in range(LAYERS)])
    else:
        stack = lambda k: jnp.stack([bigs[layer][k] for layer in range(LAYERS)])
        grad_shrink, grad_proj = stack(0), stack(2)
        expand_parts, qkv_parts = stack(1), stack(3)
        grad_expand = jnp.concatenate([expand_parts[:, g] for g in range(count)], 2).astype(FLOAT)
        grad_qkv = jnp.concatenate(
            [
                qkv_parts[:, g, :, j * size : j * size + width]
                for j in range(3)
                for g in range(count)
            ],
            axis=2,
        ).astype(FLOAT)
        grad_decay = jnp.concatenate(
            [qkv_parts[:, g, :, width : width + heads] for g in range(count)], axis=2
        ).astype(FLOAT)
    return (
        block_out,
        grad_tokens,
        grad_ada,
        grad_ada_bias,
        grad_taps,
        grad_qkv,
        grad_decay,
        bias_grads,
        grad_proj,
        grad_expand,
        grad_shrink,
    )


def solution(mesh):
    return jax.shard_map(
        per_device,
        mesh=mesh,
        in_specs=(
            P("batch", "row", "col", None),
            P(),
            P(None, "batch", None),
            P(None, "batch"),
            P(None, None, "batch"),
            P(None, "batch", None),
            P(None, "batch", None),
            P(None, "batch"),
            P(None, "batch", None),
            P(None, "batch", None),
            P(None, "batch", None),
            P("batch", "row", "col", None),
        ),
        out_specs=(
            P("batch", "row", "col", None),
            P("batch", "row", "col", None),
            P(None, "batch", None),
            P(None, "batch"),
            P(None, None, "batch"),
            P(None, "batch", None),
            P(None, "batch", None),
            P(None, "batch"),
            P(None, "batch", None),
            P(None, "batch", None),
            P(None, "batch", None),
        ),
        check_vma=False,
    )
```

```python
import jax
import jax.numpy as jnp
from jax import lax
from jax.experimental import pallas as pl
from jax.experimental.pallas import tpu as pltpu
from jax.sharding import PartitionSpec as P

D = 1152
H = 16
HD = 72
LAYERS = 2
EPS = 1e-06
ACCURATE = lax.Precision.HIGHEST
FLOAT = jnp.float32
BFLOAT = jnp.bfloat16
LANES = 128
VMEM_LIMIT = 48 * 1024 * 1024
GRID_AXES = ("row", "col")
SMALL = pl.CostEstimate(flops=1, bytes_accessed=1, transcendentals=0)


def params():
    return pltpu.CompilerParams(vmem_limit_bytes=VMEM_LIMIT)


def padded_width(width):
    return -(-width // LANES) * LANES


def swap(value, axis="batch", bit=1):
    count = lax.axis_size(axis)
    return lax.ppermute(value, axis, [(i, i ^ bit) for i in range(count)])


def gather_items(own):
    if lax.axis_size("batch") == 2:
        return jnp.concatenate([own, swap(own)], axis=0)
    return lax.all_gather(own, "batch", axis=0, tiled=True)


def gather_last(own):
    if lax.axis_size("batch") == 2:
        other = swap(own)
        first = lax.axis_index("batch") == 0
        return jnp.concatenate([jnp.where(first, own, other), jnp.where(first, other, own)], -1)
    return lax.all_gather(own, "batch", axis=own.ndim - 1, tiled=True)


def reduce_items(partial):
    if lax.axis_size("batch") == 2:
        items = partial.shape[0] // 2
        return partial[:items] + swap(partial[items:].astype(BFLOAT)).astype(FLOAT)
    return lax.psum_scatter(partial, "batch", scatter_dimension=0, tiled=True)


def lines_out(values, axis):
    count, place = lax.axis_size(axis), lax.axis_index(axis)
    groups = values.reshape((count, -1) + values.shape[1:])
    blocks = []
    for k in range(count):
        block = lax.dynamic_index_in_dim(groups, place ^ k, 0, keepdims=False)
        blocks.append(block if k == 0 else swap(block, axis, k))
    return blocks


def lines_back(blocks, axis):
    count, place = lax.axis_size(axis), lax.axis_index(axis)
    received = [blocks[0]] + [swap(blocks[k], axis, k) for k in range(1, count)]
    stacked = jnp.stack(received)
    return jnp.concatenate(
        [lax.dynamic_index_in_dim(stacked, place ^ j, 0, keepdims=False) for j in range(count)]
    )


def halo(cells):
    return halo_edges([cells[:, 0], cells[:, -1], cells[:, :, 0], cells[:, :, -1]])


def beside(cells, sides, item):
    top, bottom, left, right = sides
    count, width = cells.shape[1], cells.shape[2]
    lefts, rights = left[item].astype(FLOAT), right[item].astype(FLOAT)
    at = lax.broadcasted_iota(jnp.int32, (width, cells.shape[3]), 0)
    rows = []
    for row in range(count + 2):
        if row == 0:
            here = top[item]
        elif row == count + 1:
            here = bottom[item]
        else:
            here = cells[item, row - 1]
        here = here.astype(FLOAT)
        before = jnp.where(at == 0, lefts[row : row + 1], pltpu.roll(here, 1, 0))
        after = jnp.where(at == width - 1, rights[row : row + 1], pltpu.roll(here, width - 1, 0))
        rows.append((before, here, after))
    return rows


def conv_forward_kernel(cells, *refs):
    sides, (taps, convolved, mixed) = refs[:4], refs[4:]
    weights = taps[...].astype(FLOAT)
    for item in range(cells.shape[0]):
        rows = beside(cells, sides, item)
        for row in range(cells.shape[1]):
            total = jnp.zeros(rows[0][1].shape, FLOAT)
            for a in range(3):
                for b in range(3):
                    total += weights[3 * a + b : 3 * a + b + 1] * rows[row + a][b]
            convolved[item, row] = total
            mixed[item, row] = (total * jax.nn.sigmoid(total)).astype(BFLOAT)


def conv_backward_kernel(cells, *refs):
    sides, delta, delta_sides, (taps, hidden, grads) = refs[:4], refs[4], refs[5:9], refs[9:]
    weights = taps[...].astype(FLOAT)
    sums = [jnp.zeros((cells.shape[2], cells.shape[3]), FLOAT) for _ in range(9)]
    for item in range(cells.shape[0]):
        rows = beside(cells, sides, item)
        for row in range(cells.shape[1]):
            here = delta[item, row].astype(FLOAT)
            for a in range(3):
                for b in range(3):
                    sums[3 * a + b] += rows[row + a][b] * here
        rows = beside(delta, delta_sides, item)
        for row in range(cells.shape[1]):
            total = jnp.zeros(rows[0][1].shape, FLOAT)
            for a in range(3):
                for b in range(3):
                    total += weights[3 * a + b : 3 * a + b + 1] * rows[row + 2 - a][2 - b]
            hidden[item, row] = total
    for tap in range(9):
        grads[tap : tap + 1] = jnp.sum(sums[tap], axis=0, keepdims=True)


def conv_specs(items, rows, cols, block):
    cells = pl.BlockSpec((items, rows, cols, block), lambda i: (0, 0, 0, i))
    side = lambda size: pl.BlockSpec((items, size, block), lambda i: (0, 0, i))
    taps = pl.BlockSpec((9, block), lambda i: (0, i))
    return [cells] + [side(size) for size in (cols, cols, rows + 2, rows + 2)], taps


def conv_forward(cells, sides, taps):
    items, rows, cols, width = cells.shape
    block = 3 * LANES
    specs, tap_spec = conv_specs(items, rows, cols, block)
    return pl.pallas_call(
        conv_forward_kernel,
        grid=(width // block,),
        in_specs=specs + [tap_spec],
        out_specs=[specs[0], specs[0]],
        out_shape=[
            jax.ShapeDtypeStruct(cells.shape, FLOAT),
            jax.ShapeDtypeStruct(cells.shape, BFLOAT),
        ],
        cost_estimate=SMALL,
        compiler_params=params(),
    )(cells, *sides, taps)


def conv_backward(cells, sides, delta, delta_sides, taps):
    items, rows, cols, width = cells.shape
    block = 3 * LANES
    specs, tap_spec = conv_specs(items, rows, cols, block)
    return pl.pallas_call(
        conv_backward_kernel,
        grid=(width // block,),
        in_specs=specs + specs + [tap_spec],
        out_specs=[specs[0], tap_spec],
        out_shape=[
            jax.ShapeDtypeStruct(cells.shape, FLOAT),
            jax.ShapeDtypeStruct((9, width), FLOAT),
        ],
        cost_estimate=SMALL,
        compiler_params=params(),
    )(cells, *sides, delta, *delta_sides, taps)


def scan_mask(place, rows, cols, along_cols, blocks):
    cells = rows * cols
    shape = (blocks * cells, blocks * cells)

    def line_and_position(index):
        block = index // cells
        inside = index - block * cells
        row = inside // cols
        col = inside - row * cols
        source = place ^ block
        if along_cols:
            return row, source * cols + col
        return col, source * rows + row

    line_t, at_t = line_and_position(lax.broadcasted_iota(jnp.int32, shape, 0))
    line_s, at_s = line_and_position(lax.broadcasted_iota(jnp.int32, shape, 1))
    return (line_t == line_s) & (at_s <= at_t)


def dot(left, right, contract=((1,), (0,)), precision=None):
    return lax.dot_general(
        left, right, (contract, ((), ())), precision=precision, preferred_element_type=FLOAT
    )


class Scan:
    def __init__(self, parts, mask, width):
        self.width = width
        self.padded = padded_width(width + 3 * (width // HD))
        self.heads = width // HD
        joined = jnp.concatenate([part[0] for part in parts], axis=0)
        size = self.padded
        self.queries = joined[:, :size]
        self.keys = joined[:, size : 2 * size]
        self.values = joined[:, 2 * size :]
        self.start = width - width // LANES * LANES
        self.block = width // LANES * LANES
        extra = self.queries[:, self.block : self.block + LANES].astype(FLOAT)
        logit = (
            extra
            + pltpu.roll(extra, LANES - self.heads, 1)
            + pltpu.roll(extra, LANES - 2 * self.heads, 1)
        )
        self.lane = lax.broadcasted_iota(jnp.int32, extra.shape, 1)
        self.is_logit = (self.lane >= self.start) & (self.lane < self.start + self.heads)
        self.logit = jnp.where(self.is_logit, logit, 0.0)
        small = jnp.exp(-jnp.abs(self.logit))
        logdecay = jnp.where(self.is_logit, jnp.minimum(self.logit, 0.0) - jnp.log(1.0 + small), 0.0)
        self.lower = jnp.where(mask, 1.0, 0.0).astype(FLOAT)
        self.mask = mask
        self.cumul = dot(self.lower, logdecay, precision=ACCURATE)
        self.cumul_rows = jnp.transpose(self.cumul)
        self.feature = lax.broadcasted_iota(jnp.int32, (1, size), 1)

    def of_head(self, head, array):
        inside = (self.feature >= head * HD) & (self.feature < head * HD + HD)
        return jnp.where(inside, array, jnp.zeros_like(array))

    def weights(self, head):
        at = self.start + head
        gap = self.cumul[:, at : at + 1] - self.cumul_rows[at : at + 1, :]
        return jnp.where(self.mask, jnp.exp(jnp.minimum(gap, 0.0)), 0.0)


SCALE = HD ** (-0.5)


def scan_forward_kernel(place, *refs, rows, cols, along_cols, width):
    count = len(refs) // 2
    parts, outs = refs[:count], refs[count:]
    mask = scan_mask(place[0], rows, cols, along_cols, count)
    scan = Scan(parts, mask, width)
    total = jnp.zeros(scan.queries.shape, FLOAT)
    for head in range(scan.heads):
        scores = dot(scan.of_head(head, scan.queries), scan.keys, ((1,), (1,))) * SCALE
        scores = (scores * scan.weights(head)).astype(BFLOAT)
        total += dot(scores, scan.of_head(head, scan.values))
    cells = rows * cols
    low = total.astype(BFLOAT)
    for k in range(count):
        outs[k][0] = low[k * cells : (k + 1) * cells, :width]


def scan_backward_kernel(place, *refs, rows, cols, along_cols, width):
    count = len(refs) // 3
    parts, deltas, outs = refs[:count], refs[count : 2 * count], refs[2 * count :]
    mask = scan_mask(place[0], rows, cols, along_cols, count)
    scan = Scan(parts, mask, width)
    joined = jnp.concatenate([part[0] for part in deltas], axis=0)
    short = scan.padded - width
    if short:
        joined = jnp.concatenate([joined, jnp.zeros((joined.shape[0], short), BFLOAT)], axis=1)
    shape = scan.queries.shape
    delta_query = jnp.zeros(shape, FLOAT)
    delta_key = jnp.zeros(shape, FLOAT)
    delta_value = jnp.zeros(shape, FLOAT)
    gap_rows = jnp.zeros(scan.lane.shape, FLOAT)
    gap_cols = jnp.zeros(scan.cumul_rows.shape, FLOAT)
    place_row = lax.broadcasted_iota(jnp.int32, gap_cols.shape, 0)
    for head in range(scan.heads):
        query = scan.of_head(head, scan.queries)
        delta = scan.of_head(head, joined)
        weights = scan.weights(head)
        scores = dot(query, scan.keys, ((1,), (1,))) * SCALE * weights
        delta_scores = dot(delta, scan.values, ((1,), (1,)))
        gap = delta_scores * scores
        at = scan.start + head
        gap_rows += jnp.where(scan.lane == at, jnp.sum(gap, axis=1, keepdims=True), 0.0)
        gap_cols += jnp.where(place_row == at, jnp.sum(gap, axis=0, keepdims=True), 0.0)
        inner = (delta_scores * weights * SCALE).astype(BFLOAT)
        delta_query += dot(inner, scan.of_head(head, scan.keys))
        delta_key += dot(inner, query, ((0,), (0,)))
        delta_value += dot(scores.astype(BFLOAT), delta, ((0,), (0,)))
    delta_cumul = gap_rows - jnp.transpose(gap_cols)
    delta_decay = dot(scan.lower, delta_cumul, ((0,), (0,)), ACCURATE)
    small = jnp.exp(-jnp.abs(scan.logit))
    keep = jnp.where(scan.logit >= 0.0, small, 1.0) / (1.0 + small)
    delta_logit = delta_decay * keep
    block = scan.block
    mixed = jnp.where(scan.is_logit, delta_logit, delta_query[:, block : block + LANES])
    pieces = [delta_query[:, :block]] if block else []
    pieces.append(mixed)
    if block + LANES < scan.padded:
        pieces.append(delta_query[:, block + LANES :])
    whole = jnp.concatenate(pieces + [delta_key, delta_value], axis=1).astype(BFLOAT)
    cells = rows * cols
    for k in range(count):
        outs[k][0] = whole[k * cells : (k + 1) * cells]


def scan_call(kernel, place, inputs, out_width, rows, cols, along_cols, width):
    count = lax.axis_size("col") if along_cols else lax.axis_size("row")
    items, cells = inputs[0].shape[:2]
    spec = lambda last: pl.BlockSpec((1, cells, last), lambda i, place: (i, 0, 0))

    def body(*refs):
        kernel(*refs, rows=rows, cols=cols, along_cols=along_cols, width=width)

    return pl.pallas_call(
        body,
        grid_spec=pltpu.PrefetchScalarGridSpec(
            num_scalar_prefetch=1,
            grid=(items,),
            in_specs=[spec(v.shape[2]) for v in inputs],
            out_specs=[spec(out_width)] * count,
        ),
        out_shape=[jax.ShapeDtypeStruct((items, cells, out_width), BFLOAT)] * count,
        cost_estimate=SMALL,
        compiler_params=params(),
    )(place.reshape(1).astype(jnp.int32), *inputs)


def pick(values, index):
    chosen = values[0]
    for k in range(1, len(values)):
        chosen = jnp.where(index == k, values[k], chosen)
    return chosen


def fetch_columns(pieces):
    count, place = lax.axis_size("batch"), lax.axis_index("batch")
    if count != 2:
        stacked = jnp.stack(pieces)
        return lax.all_to_all(stacked, "batch", 0, 0).reshape((-1,) + pieces[0].shape[1:])
    own, other = pick(pieces, place), pick(pieces, 1 - place)
    rows = own.shape[0]
    half = rows // 2
    core = lax.axis_index("row") % 2
    first = swap(lax.dynamic_slice_in_dim(other, core * half, half, 0))
    second = swap(first, "row", 1)
    whole = jnp.zeros((2 * rows,) + own.shape[1:], own.dtype)
    whole = lax.dynamic_update_slice_in_dim(whole, own, place * rows, 0)
    base = (1 - place) * rows
    whole = lax.dynamic_update_slice_in_dim(whole, first, base + core * half, 0)
    return lax.dynamic_update_slice_in_dim(whole, second, base + (1 - core) * half, 0)


def head_columns(qkv, decay, group, width):
    size = padded_width(width + 3 * (width // HD))
    heads = width // HD
    parts = []
    for j in range(3):
        piece = qkv[:, j * D + group * width : j * D + (group + 1) * width]
        filled = width
        parts.append(piece)
        if j == 0:
            parts.append(decay[:, group * heads : (group + 1) * heads])
            filled += heads
        if size > filled:
            parts.append(jnp.zeros((qkv.shape[0], size - filled), qkv.dtype))
    return jnp.concatenate(parts, axis=1)


def normalize(values):
    center = values - jnp.mean(values, axis=-1, keepdims=True)
    inverse = lax.rsqrt(jnp.mean(center * center, axis=-1, keepdims=True) + EPS)
    return center * inverse, inverse


def normalize_back(delta, normal, inverse):
    first = jnp.mean(delta, axis=-1, keepdims=True)
    second = jnp.mean(delta * normal, axis=-1, keepdims=True)
    return inverse * (delta - first - normal * second)


def embed_steps(steps):
    half = D // 2
    freqs = jnp.exp(-jnp.log(10000.0) * jnp.arange(half, dtype=FLOAT) / half)
    angles = steps.astype(FLOAT)[:, None] * freqs[None, :]
    return jnp.concatenate([jnp.cos(angles), jnp.sin(angles)], axis=1)


GELU_A = 0.7978845608028654
GELU_B = 0.044715


def gelu(z):
    return 0.5 * z * (1.0 + jnp.tanh(GELU_A * (z + GELU_B * z * z * z)))


def gelu_slope(z):
    t = jnp.tanh(GELU_A * (z + GELU_B * z * z * z))
    return 0.5 * (1.0 + t) + 0.5 * z * (1.0 - t * t) * GELU_A * (1.0 + 3.0 * GELU_B * z * z)


def matmul(left, right):
    return lax.dot_general(left, right, (((2,), (0,)), ((), ())), preferred_element_type=FLOAT)


def matmul_back(left, right):
    return lax.dot_general(left, right, (((2,), (1,)), ((), ())), preferred_element_type=FLOAT)


def weight_grad(left, right):
    return lax.dot_general(
        left, right, (((0, 1), (0, 1)), ((), ())), preferred_element_type=FLOAT
    )


SHARES = 16
SHARE_ROWS = 144
STAGES = (("row", 1), ("row", 2), ("col", 1), ("col", 2))


def share_place(stages):
    number = jnp.int32(0)
    for axis, bit in stages:
        number = 2 * number + (lax.axis_index(axis) // bit) % 2
    return number.reshape(1).astype(jnp.int32)


def product(act, delta):
    return lax.dot_general(act, delta, (((1,), (0,)), ((), ())), preferred_element_type=FLOAT)


def grad_send_kernel(place, act, delta, out):
    out[0] = product(act[0], delta[0]).astype(BFLOAT)


def grad_keep_kernel(place, act, delta, received, send, keep):
    value = (product(act[0], delta[0]) + received[0].astype(FLOAT)).astype(BFLOAT)
    first = pl.program_id(0) < SHARES // 4

    @pl.when(first)
    def _():
        send[0] = value

    @pl.when(jnp.logical_not(first))
    def _():
        keep[0] = value


class GradSum:
    def __init__(self, act, delta, act_index, delta_index, stages):
        self.act, self.delta, self.stages = act, delta, stages
        self.act_index, self.delta_index = act_index, delta_index
        self.place = share_place(stages)

    def call(self, kernel, position, extra, extra_specs, out_specs, out_shapes, through):
        tokens = self.act.shape[2]
        act_spec = pl.BlockSpec(
            (1, SHARE_ROWS, tokens), lambda i, m: self.act_index(position(i) ^ m[0])
        )
        delta_spec = pl.BlockSpec(
            (1, tokens, D), lambda i, m: self.delta_index(position(i) ^ m[0])
        )
        inputs = 3 + len(extra)

        def body(*refs):
            kernel(*refs[:inputs], *refs[inputs + 1 : -1])

        return pl.pallas_call(
            body,
            grid_spec=pltpu.PrefetchScalarGridSpec(
                num_scalar_prefetch=1,
                grid=(SHARES // 2,),
                in_specs=[act_spec, delta_spec] + extra_specs + [ANYWHERE],
                out_specs=out_specs + [ANYWHERE],
            ),
            out_shape=out_shapes + [jax.ShapeDtypeStruct(through.shape, through.dtype)],
            input_output_aliases={inputs: len(out_shapes)},
            cost_estimate=SMALL,
            compiler_params=params(),
        )(self.place, self.act, self.delta, *extra, through)

    def start(self, through):
        half = SHARES // 2
        block = (1, SHARE_ROWS, D)
        send, through = self.call(
            grad_send_kernel,
            lambda i: i + half,
            [],
            [],
            [pl.BlockSpec(block, lambda i, m: (i, 0, 0))],
            [jax.ShapeDtypeStruct((half, SHARE_ROWS, D), BFLOAT)],
            through,
        )
        self.flight = self.move(send, 0)
        return through

    def move(self, value, stage):
        axis, bit = self.stages[stage]
        return swap(value, axis, bit)

    def second(self, through):
        quarter = SHARES // 4
        block = (1, SHARE_ROWS, D)
        position = lambda i: i ^ quarter
        send, self.keep, through = self.call(
            grad_keep_kernel,
            position,
            [self.flight],
            [pl.BlockSpec(block, lambda i, m: (position(i), 0, 0))],
            [
                pl.BlockSpec(block, lambda i, m: (jnp.minimum(i, quarter - 1), 0, 0)),
                pl.BlockSpec(block, lambda i, m: (jnp.maximum(i - quarter, 0), 0, 0)),
            ],
            [jax.ShapeDtypeStruct((quarter, SHARE_ROWS, D), BFLOAT)] * 2,
            through,
        )
        self.flight = self.move(send, 1)
        self.state = 0
        return through

    works = ("halve", "halve", "add", "join", "join", "pass")
    own_state = 3
    offload = natural = False

    def advanced(self, outs):
        work = self.works[self.state]
        self.state += 1
        if work == "pass":
            self.keep, self.flight = outs
            self.pieces = [self.keep, self.flight]
            self.pieces += [self.move(piece, 0) for piece in self.pieces]
            return
        self.keep = outs[0]
        if not (self.offload and self.state == self.own_state):
            self.flight = self.onward(self.state, outs[-1])

    def onward(self, state, value):
        return self.move(value, (None, 2, 3, 3, 2, 1)[state])

    def done(self):
        return self.state == len(self.works)


class CrossGradSum(GradSum):
    works = ("halve", "halve", "add", "take", "join", "join", "pass")
    own_state = 4

    def onward(self, state, value):
        if state == 3:
            return self.cross(value)
        return self.move(value, (None, 2, 3, None, 3, 2, 1)[state])

    def cross(self, value):
        rows, cols = lax.axis_size("row"), lax.axis_size("col")
        pairs = []
        for x in range(2):
            for r in range(rows):
                for z in range(cols):
                    stays = r % 2 == x
                    to_x, to_r = (x, r) if stays else (1 - x, r ^ 1)
                    pairs.append(((x * rows + r) * cols + z, (to_x * rows + to_r) * cols + z))
        return lax.ppermute(value, ("batch", "row", "col"), pairs)


class Gathered:
    def __init__(self, sums):
        self.sums = sums

    def gather(self):
        self.collect(jnp.concatenate([one.keep for one in self.sums]))

    def collect(self, shares):
        whole = lax.all_gather(shares, GRID_AXES)
        for slot, one in enumerate(self.sums):
            one.whole, one.slot = whole, slot

    @staticmethod
    def finish(sums, kinds, previous, layer, shapes, through):
        block = (1, SHARE_ROWS, D)
        scalar = lax.axis_index("batch").reshape(1).astype(jnp.int32)

        def source(one):
            def index(i, m):
                core, y, low, high = i // 8, i // 4 % 2, i // 2 % 2, i % 2
                device = i if one.natural else (y * 2 + core) * 4 + high * 2 + low
                return (device, one.slot, 0, 0)

            return pl.BlockSpec((None,) + block, index)

        natural = sums[0].natural

        def expand(i, m):
            core, y = (i // 4 % 2, i // 8) if natural else (i // 8, i // 4 % 2)
            own = jnp.where(core == m[0], m[0], 1 - m[0])
            return (layer, i % 4, own * 2 + y)

        indices = (
            lambda i, m: (layer, i, 0),
            expand,
            lambda i, m: (0, i // 4, jnp.minimum(i % 4, 2)),
            lambda i, m: (0, i // 4, 0),
        )
        blocks = (block, block, (LAYERS,) + block[1:], (LAYERS,) + block[1:])
        targets = [k for kind in kinds[:3] for k in ((0,), (1,), (2, 3))["ABC".index(kind)]]
        kept = [k for k in targets if previous and k in previous]
        earlier = [previous[k] for k in kept]
        count, outs, given = len(earlier), len(targets), len(sums)

        def body(m, *refs):
            where = dict(zip(targets, refs[-1 - outs : -1]))
            last = pl.program_id(0) % 4 == 3
            done = 0
            for kind, ref in zip(kinds, refs):
                if kind != "C":
                    where["AB".index(kind)][0] = ref[0].astype(FLOAT)
                    continue

                at, done = done, done + 1

                @pl.when(last)
                def _(ref=ref, at=at):
                    where[3][at] = ref[0].astype(FLOAT)

                @pl.when(jnp.logical_not(last))
                def _(ref=ref, at=at):
                    where[2][at] = ref[0].astype(FLOAT)

        *results, through = pl.pallas_call(
            body,
            grid_spec=pltpu.PrefetchScalarGridSpec(
                num_scalar_prefetch=1,
                grid=(SHARES,),
                in_specs=[source(one) for one in sums] + [ANYWHERE] * (count + 1),
                out_specs=[pl.BlockSpec(blocks[k], indices[k]) for k in targets] + [ANYWHERE],
            ),
            out_shape=[jax.ShapeDtypeStruct(shapes[k], FLOAT) for k in targets]
            + [jax.ShapeDtypeStruct(through.shape, through.dtype)],
            input_output_aliases={1 + given + j: targets.index(k) for j, k in enumerate(kept)}
            | {1 + given + count: outs},
            cost_estimate=SMALL,
            compiler_params=params(),
        )(scalar, *[one.whole for one in sums], *earlier, through)
        return dict(zip(targets, results)), through


class Scattered(Gathered):
    def __init__(self):
        self.sums, self.group, self.shares = [], [], []

    def add(self, one, through):
        slot, tokens, dim = len(self.group), one.act.shape[2], len(self.shares) % 2
        one.offload = one.natural = True
        earlier = [self.buffer] if slot else []
        self.sums.append(one)
        self.group.append(one)
        count = len(earlier)
        shape = (1, SHARES) if dim else (SHARES, 2)
        place = lambda j: (slot, j, 0, 0) if dim else (j, slot, 0, 0)
        block = (1, 2) if dim else (2, 1)
        cross = isinstance(one, CrossGradSum)

        def body(act, delta, *refs):
            value = product(act[0], delta[0]).astype(BFLOAT)
            for k in range(2):
                part = value[k * SHARE_ROWS : (k + 1) * SHARE_ROWS]
                refs[count + 1][(0, k) if dim else (k, 0)] = part

        self.buffer, through = pl.pallas_call(
            body,
            grid=(SHARES // 2,),
            in_specs=[
                pl.BlockSpec(
                    (1, 2 * SHARE_ROWS, tokens), lambda j: (0, j % 4 if cross else j, 0)
                ),
                pl.BlockSpec((1, tokens, D), lambda j: (0, 0, j // 4 if cross else 0)),
            ]
            + [ANYWHERE] * (count + 1),
            out_specs=[pl.BlockSpec(block + (SHARE_ROWS, D), place), ANYWHERE],
            out_shape=[
                jax.ShapeDtypeStruct(shape + (SHARE_ROWS, D), BFLOAT),
                jax.ShapeDtypeStruct(through.shape, through.dtype),
            ],
            input_output_aliases={2 + k: k for k in range(count)} | {2 + count: 1},
            cost_estimate=SMALL,
            compiler_params=params(),
        )(one.act, one.delta, *earlier, through)
        return through

    def reduce(self):
        dim = len(self.shares) % 2
        summed = lax.psum_scatter(self.buffer, GRID_AXES, scatter_dimension=dim, tiled=True)
        self.shares.append(summed.reshape(-1, SHARE_ROWS, D))
        self.group = []

    def gather(self, after):
        shares = passed_by(self.shares, [after])
        shares = [part[slot] for part in shares for slot in range(part.shape[0])]
        for slot, one in enumerate(self.sums):
            if isinstance(one, CrossGradSum):
                shares[slot] = one.cross(shares[slot])
        self.collect(jnp.stack(shares))


class SmallSum:
    works = ("sum",) * 4

    def __init__(self, value):
        self.value, self.state = value, 0

    def start(self, through):
        self.keep, self.flight = self.value, self.move(0, self.value)
        return through

    def move(self, stage, value):
        return swap(value, *STAGES[stage])

    def advanced(self, outs):
        self.state += 1
        (self.keep,) = outs
        self.flight = None if self.done() else self.move(self.state, self.keep)

    def done(self):
        return self.state == len(self.works)


def tick_kernel(*refs, works):
    at, out = 0, 2 * len(works)
    for work in works:
        keep, flight = refs[at], refs[at + 1]
        at += 2
        count = keep.shape[0]
        if work == "sum":
            refs[out][...] = keep[...] + flight[...]
            out += 1
            continue
        if work == "join":
            refs[out][:count] = keep[...]
            refs[out][count:] = flight[...]
            out += 1
            continue
        for row in range(count):
            value = (keep[row].astype(FLOAT) + flight[row].astype(FLOAT)).astype(BFLOAT)
            if work == "add":
                refs[out][row] = value
            elif row < count // 2:
                refs[out][row] = value
            else:
                refs[out + 1][row - count // 2] = value
        out += 1 if work == "add" else 2


def tick(sums, through):
    if not sums:
        return through
    light = ("pass", "take")
    working = [one for one in sums if one.works[one.state] not in light]
    passing = [one for one in sums if one.works[one.state] in light]
    operands, shapes, counts, works = [], [], [], []
    for one in working:
        operands += [one.keep, one.flight]
        work, count = one.works[one.state], one.keep.shape[0]
        works.append(work)
        sizes = {"halve": [count // 2] * 2, "join": [2 * count]}.get(work, [count])
        counts.append(len(sizes))
        shapes += [
            jax.ShapeDtypeStruct((k,) + one.keep.shape[1:], one.keep.dtype) for k in sizes
        ]
    kept = lambda one: [one.flight] if one.works[one.state] == "take" else [one.keep, one.flight]
    passed = [value for one in passing for value in kept(one)] + [through]

    def body(*refs):
        ins, outs = refs[: len(operands)], refs[len(operands) + len(passed) :]
        tick_kernel(*ins, *outs, works=works)

    outs = pl.pallas_call(
        body,
        in_specs=[WHOLE] * len(operands) + [ANYWHERE] * len(passed),
        out_specs=[WHOLE] * len(shapes) + [ANYWHERE] * len(passed),
        out_shape=shapes + [jax.ShapeDtypeStruct(v.shape, v.dtype) for v in passed],
        input_output_aliases={
            len(operands) + k: len(shapes) + k for k in range(len(passed))
        },
        cost_estimate=SMALL,
        compiler_params=params(),
    )(*operands, *passed)
    at = 0
    for one, count in zip(working, counts):
        one.advanced(outs[at : at + count])
        at += count
    for one in passing:
        count = len(kept(one))
        one.advanced(outs[at : at + count])
        at += count
    return outs[-1]


def sum_small(value):
    for axis, bit in STAGES:
        value = value + swap(value, axis, bit)
    return value


def shrink_sum(act, outer_low):
    return GradSum(act[None], outer_low[None], lambda s: (0, s, 0), lambda s: (0, 0, 0), STAGES)


def expand_sum(act, inner_low):
    return CrossGradSum(
        act[None],
        inner_low[None],
        lambda s: (0, s // 8 * 4 + s % 4, 0),
        lambda s: (0, 0, s // 4 % 2),
        STAGES,
    )


def mixer_delta(own, other, branch, branch_other, places, width, size):
    tokens = own.shape[0]
    block = tokens // 4
    heads = width // HD

    def body(places, mine, theirs, low, low_other, out, logits):
        first = places[0] == 0
        values = mine[...].astype(FLOAT), theirs[...].astype(FLOAT)
        left = jnp.where(first, values[0], values[1])
        right = jnp.where(first, values[1], values[0])
        for j in range(3):
            part = slice(j * size, j * size + width)
            out[:, j * D : (j + 1) * D] = jnp.concatenate(
                [left[:, part], right[:, part]], axis=1
            ).astype(BFLOAT)
        half = pl.program_id(0) < 2

        @pl.when(half)
        def _():
            out[:, 3 * D :] = low[...]

        @pl.when(jnp.logical_not(half))
        def _():
            out[:, 3 * D :] = low_other[...]

        part = slice(width, width + heads)
        rest = jnp.zeros((block, LANES - 2 * heads), FLOAT)
        logits[...] = jnp.concatenate([left[:, part], right[:, part], rest], axis=1).astype(BFLOAT)

    return pl.pallas_call(
        body,
        grid_spec=pltpu.PrefetchScalarGridSpec(
            num_scalar_prefetch=1,
            grid=(4,),
            in_specs=[
                pl.BlockSpec((block, 3 * size), lambda i, m: (i, 0)),
                pl.BlockSpec((block, 3 * size), lambda i, m: (i ^ 2, 0)),
                pl.BlockSpec((block, D), lambda i, m: (jnp.minimum(i, 1), 0)),
                pl.BlockSpec((block, D), lambda i, m: (jnp.maximum(i - 2, 0), 0)),
            ],
            out_specs=[
                pl.BlockSpec((block, 4 * D), lambda i, m: (i, 0)),
                pl.BlockSpec((block, LANES), lambda i, m: (i, 0)),
            ],
        ),
        out_shape=[
            jax.ShapeDtypeStruct((tokens, 4 * D), BFLOAT),
            jax.ShapeDtypeStruct((tokens, LANES), BFLOAT),
        ],
        cost_estimate=SMALL,
        compiler_params=params(),
    )(places, own, other, branch, branch_other)


def mixer_sum(act, delta_project, branch, branch_other, places, width, size):
    delta, logits = mixer_delta(
        delta_project, swap(delta_project), branch, branch_other, places, width, size
    )
    return (
        GradSum(
            act,
            delta[None],
            lambda s: (jnp.where(s % 4 == 3, 1, 0), s // 4, 0),
            lambda s: (0, 0, s % 4),
            STAGES,
        ),
        logits,
    )


ITEMS = 2
ANYWHERE = pl.BlockSpec(memory_space=pl.ANY)
WHOLE = pl.BlockSpec(memory_space=pltpu.VMEM)


def call(body, shapes, arrays, places=None, held=(), after=(), scratch=()):
    first = 0 if places is None else 1
    count, kept, tied = len(arrays), len(held), len(after)

    def whole(*refs):
        ins = refs[first : first + count]
        far = refs[first + count : first + count + kept]
        at = first + count + kept + tied
        outs = refs[at : at + len(shapes)]
        body(refs[0] if first else None, ins, far, outs, refs[at + len(shapes) :])

    return pl.pallas_call(
        whole,
        in_specs=[pl.BlockSpec(memory_space=pltpu.SMEM)] * first
        + [WHOLE] * count
        + [ANYWHERE] * (kept + tied),
        out_specs=[WHOLE] * len(shapes),
        out_shape=[jax.ShapeDtypeStruct(*shape) for shape in shapes],
        scratch_shapes=list(scratch),
        cost_estimate=SMALL,
        compiler_params=params(),
    )(*([] if places is None else [places]), *arrays, *held, *after)


def edge_shapes(tile):
    rows, cols = tile
    sizes = [cols, cols, rows, rows]
    return [((ITEMS, size, D), BFLOAT) for size in sizes]


def put_edges(value, item, refs, tile):
    rows, cols = tile
    lines = [value[0], value[rows - 1]]
    for at in (0, cols - 1):
        lines.append(jnp.concatenate([value[r][at : at + 1] for r in range(rows)], axis=0))
    for ref, line in zip(refs, lines):
        ref[item] = line.astype(BFLOAT)


def halo_edges(edges):
    rows, cols = lax.axis_size("row"), lax.axis_size("col")
    first_row, last_row, first_col, last_col = edges
    top = lax.ppermute(last_row, "row", [(i, i + 1) for i in range(rows - 1)])
    bottom = lax.ppermute(first_row, "row", [(i + 1, i) for i in range(rows - 1)])
    to_right = jnp.concatenate([top[:, -1:], last_col, bottom[:, -1:]], axis=1)
    to_left = jnp.concatenate([top[:, :1], first_col, bottom[:, :1]], axis=1)
    left = lax.ppermute(to_right, "col", [(i, i + 1) for i in range(cols - 1)])
    right = lax.ppermute(to_left, "col", [(i + 1, i) for i in range(cols - 1)])
    return top, bottom, left, right


def modulated(value, mod, shift, scale):
    normal, inverse = normalize(value)
    return normal * (1.0 + mod[scale : scale + 1]) + mod[shift : shift + 1]


def enter_first(tokens, mod, tile):
    cells = (ITEMS,) + tile + (D,)

    def body(_, ins, far, outs, scratch):
        for i in range(ITEMS):
            hidden = modulated(ins[0][i].astype(FLOAT), ins[1][i], 0, 1).reshape(cells[1:])
            outs[0][i] = hidden.astype(BFLOAT)
            put_edges(hidden, i, outs[1:], tile)

    hidden, *edges = call(body, [(cells, BFLOAT)] + edge_shapes(tile), [tokens, mod])
    return hidden, edges


def enter_next(middle, own, received, mod_before, mod, tile):
    cells = (ITEMS,) + tile + (D,)
    count = middle.shape[1]

    def body(_, ins, far, outs, scratch):
        for i in range(ITEMS):
            at = slice(i * count, (i + 1) * count)
            outer = ins[1][at] + ins[2][at].astype(FLOAT)
            outs[1][i] = outer
            value = ins[0][i] + ins[3][i][5:6] * outer
            outs[0][i] = value
            hidden = modulated(value, ins[4][i], 0, 1).reshape(cells[1:])
            outs[2][i] = hidden.astype(BFLOAT)
            put_edges(hidden, i, outs[3:], tile)

    shapes = [(middle.shape, FLOAT), (middle.shape, FLOAT), (cells, BFLOAT)] + edge_shapes(tile)
    value, outer, hidden, *edges = call(body, shapes, [middle, own, received, mod_before, mod])
    return value, outer, hidden, edges


def leave(middle, own, received, mod):
    count = middle.shape[1]

    def body(_, ins, far, outs, scratch):
        for i in range(ITEMS):
            at = slice(i * count, (i + 1) * count)
            outer = ins[1][at] + ins[2][at].astype(FLOAT)
            outs[1][i] = outer
            outs[0][i] = (ins[0][i] + ins[3][i][5:6] * outer).astype(BFLOAT)

    return call(
        body, [(middle.shape, BFLOAT), (middle.shape, FLOAT)], [middle, own, received, mod]
    )


def gather_weight(far, scratch, sems, places, own):
    batch, quarter = places[0], places[1]
    rows = own.shape[0]
    size = rows // 4
    base = (1 - batch) * rows
    parts = [(own, batch * rows, rows)]
    for k in range(4):
        parts.append((far[k], base + (quarter ^ k) * size, size))
    copies = []
    for k, (source, start, count) in enumerate(parts):
        target = scratch.at[pl.ds(pl.multiple_of(start, 16), count)]
        copy = pltpu.make_async_copy(source, target, sems.at[k])
        copy.start()
        copies.append(copy)
    return copies


def split_logit(block, start, heads):
    lane = lax.broadcasted_iota(jnp.int32, block.shape, 1)
    here = (lane >= start) & (lane < start + heads)
    high = block.astype(BFLOAT).astype(FLOAT)
    rest = jnp.where(here, block - high, 0.0)
    middle = rest.astype(BFLOAT).astype(FLOAT)
    low = rest - middle
    return (
        jnp.where(here, high, block) + pltpu.roll(middle, heads, 1) + pltpu.roll(low, 2 * heads, 1)
    )


def project_call(own, other, weight, bias, places, cells, width):
    size = weight[0].shape[1] // 3
    block = width // LANES * LANES
    total = 2 * own.shape[0]
    count = total // cells

    def body(places, ins, far, outs, scratch):
        whole, joined, result, sems = scratch
        copies = gather_weight(far[1:], whole, sems, places, far[0])
        joined[: total // 2] = ins[0][...]
        joined[total // 2 :] = ins[1][...]
        for copy in copies:
            copy.wait()
        for part in range(3):
            columns = slice(part * size, (part + 1) * size)
            value = dot(joined[...], whole[:, columns])
            if part == 0:
                last = split_logit(
                    value[:, block : block + LANES] + ins[2][...], width - block, width // HD
                )
                result[:, :block] = value[:, :block].astype(BFLOAT)
                result[:, block : block + LANES] = last.astype(BFLOAT)
            else:
                result[:, columns] = value.astype(BFLOAT)
        for k in range(count):
            start = pl.multiple_of((places[2] ^ k) * cells, cells)
            outs[k][0] = result[pl.ds(start, cells)]

    return call(
        body,
        [((1, cells, 3 * size), BFLOAT)] * count,
        [own, other, bias],
        places,
        weight,
        scratch=[
            pltpu.VMEM((D, 3 * size), BFLOAT),
            pltpu.VMEM((total, D), BFLOAT),
            pltpu.VMEM((total, 3 * size), BFLOAT),
            pltpu.SemaphoreType.DMA((5,)),
        ],
    )


def halves_out(value, outs, columns, items_here):
    outs[0][:, columns] = value[:items_here]
    outs[1][:, columns] = value[items_here:].astype(BFLOAT)


COLUMNS = 384


def attend_out_call(blocks, weight, layer, places, cells, width):
    count = len(blocks)
    total = count * cells

    def body(places, ins, far, outs, scratch):
        whole, sems = scratch
        copy = pltpu.make_async_copy(far[0].at[layer], whole, sems.at[0])
        copy.start()
        for k in range(count):
            start = pl.multiple_of((places[2] ^ k) * cells, cells)
            outs[2][pl.ds(start, cells)] = ins[k][0]
        copy.wait()
        for at in range(0, D, COLUMNS):
            columns = slice(at, at + COLUMNS)
            halves_out(dot(outs[2][...], whole[:, columns]), outs, columns, total // 2)

    return call(
        body,
        [((total // 2, D), FLOAT), ((total // 2, D), BFLOAT), ((total, width), BFLOAT)],
        blocks,
        places,
        [weight],
        scratch=[pltpu.VMEM((width, D), BFLOAT), pltpu.SemaphoreType.DMA((1,))],
    )


def middle_call(tokens, own, received, mod):
    count = tokens.shape[1]

    def body(_, ins, far, outs, scratch):
        for i in range(ITEMS):
            at = slice(i * count, (i + 1) * count)
            branch = ins[1][at] + ins[2][at].astype(FLOAT)
            outs[0][i] = branch
            middle = ins[0][i].astype(FLOAT) + ins[3][i][2:3] * branch
            outs[1][i] = middle
            outs[2][at] = modulated(middle, ins[3][i], 3, 4).astype(BFLOAT)

    shape = tokens.shape
    return call(
        body,
        [(shape, FLOAT), (shape, FLOAT), ((ITEMS * count, D), BFLOAT)],
        [tokens, own, received, mod],
    )


def feed_call(own, other, expand, shrink, layer, places):
    total = 2 * own.shape[0]
    inner = shrink.shape[1]
    rows = expand[0].shape[1]
    tile = 256

    def body(places, ins, far, outs, scratch):
        wide, back, joined, sems = scratch
        start = pl.multiple_of(places[0] * inner, LANES)
        source = far[0].at[layer, :, pl.ds(start, inner)]
        copies = gather_weight(far[1:5], wide, sems, places, source)
        last = pltpu.make_async_copy(far[5].at[layer], back, sems.at[5])
        last.start()
        joined[: total // 2] = ins[0][...]
        joined[total // 2 :] = ins[1][...]
        for copy in copies:
            copy.wait()
        for at in range(0, inner, tile):
            columns = slice(at, at + tile)
            value = dot(joined[...], wide[:, columns])
            outs[2][:, columns] = value
            outs[3][:, columns] = gelu(value).astype(BFLOAT)
        last.wait()
        for at in range(0, D, COLUMNS):
            columns = slice(at, at + COLUMNS)
            halves_out(dot(outs[3][...], back[:, columns]), outs, columns, total // 2)

    return call(
        body,
        [
            ((total // 2, D), FLOAT),
            ((total // 2, D), BFLOAT),
            ((total, inner), FLOAT),
            ((total, inner), BFLOAT),
        ],
        [own, other],
        places,
        list(expand) + [shrink],
        scratch=[
            pltpu.VMEM((2 * rows, inner), BFLOAT),
            pltpu.VMEM((inner, D), BFLOAT),
            pltpu.VMEM((total, D), BFLOAT),
            pltpu.SemaphoreType.DMA((6,)),
        ],
    )


def turn_call(mixed, mixed_other, attend, second, second_other, active, places, through):
    tokens = attend.shape[0]
    width = attend.shape[1]
    padded = padded_width(width)
    inner = active.shape[1]
    half = mixed.shape[0]

    def turn(value):
        return jnp.transpose(value.astype(FLOAT)).astype(BFLOAT)

    def body(places, one, two, three, four, five, six, _, mixer, wide, long, __):
        first = places[0] == 0
        for ref, at in ((one, 0), (two, half)):
            value = turn(ref[...])
            mixer[0, :, at : at + half] = jnp.where(first, value[:width], value[width:])
        blank = jnp.zeros((tokens, padded - width), FLOAT)
        value = jnp.concatenate([three[...].astype(FLOAT), blank], axis=1)
        mixer[1] = jnp.transpose(value)[:width].astype(BFLOAT)
        wide[:, :half] = turn(four[...])
        wide[:, half:] = turn(five[...])
        for at in range(0, inner, 256):
            long[at : at + 256] = turn(six[:, at : at + 256])

    return pl.pallas_call(
        body,
        in_specs=[pl.BlockSpec(memory_space=pltpu.SMEM)] + [WHOLE] * 6 + [ANYWHERE],
        out_specs=[WHOLE] * 3 + [ANYWHERE],
        out_shape=[
            jax.ShapeDtypeStruct((2, width, tokens), BFLOAT),
            jax.ShapeDtypeStruct((D, tokens), BFLOAT),
            jax.ShapeDtypeStruct((inner, tokens), BFLOAT),
            jax.ShapeDtypeStruct(through.shape, through.dtype),
        ],
        input_output_aliases={7: 3},
        cost_estimate=SMALL,
        compiler_params=params(),
    )(places, mixed, mixed_other, attend, second, second_other, active, through)


def feed_back_call(own, other, inner_value, expand, shrink, layer, places):
    total = 2 * own.shape[0]
    inner = shrink.shape[1]
    rows = expand[0].shape[1]
    tile = 256

    def body(places, ins, far, outs, scratch):
        wide, back, joined, sems = scratch
        last = pltpu.make_async_copy(far[5].at[layer], back, sems.at[5])
        last.start()
        start = pl.multiple_of(places[0] * inner, LANES)
        source = far[0].at[layer, :, pl.ds(start, inner)]
        copies = gather_weight(far[1:5], wide, sems, places, source)
        joined[: total // 2] = ins[0][...]
        joined[total // 2 :] = ins[1][...]
        last.wait()
        for at in range(0, inner, tile):
            columns = slice(at, at + tile)
            value = dot(joined[...], back[at : at + tile], ((1,), (1,)))
            outs[2][:, columns] = (value * gelu_slope(ins[2][:, columns])).astype(BFLOAT)
        for copy in copies:
            copy.wait()
        for at in range(0, D, COLUMNS):
            columns = slice(at, at + COLUMNS)
            value = dot(outs[2][...], wide[at : at + COLUMNS], ((1,), (1,)))
            halves_out(value, outs, columns, total // 2)

    return call(
        body,
        [((total // 2, D), FLOAT), ((total // 2, D), BFLOAT), ((total, inner), BFLOAT)],
        [own, other, inner_value],
        places,
        list(expand) + [shrink],
        scratch=[
            pltpu.VMEM((2 * rows, inner), BFLOAT),
            pltpu.VMEM((inner, D), BFLOAT),
            pltpu.VMEM((total, D), BFLOAT),
            pltpu.SemaphoreType.DMA((6,)),
        ],
    )


def middle_back_call(delta, own, received, middle, branch, outer, mod):
    count = middle.shape[1]
    over = lambda v: jnp.sum(v, axis=0, keepdims=True)

    def body(_, ins, far, outs, scratch):
        for i in range(ITEMS):
            at = slice(i * count, (i + 1) * count)
            here = ins[0][i].astype(FLOAT)
            mod_here = ins[6][i]
            outs[2][i, 3:4] = over(here * ins[5][i])
            second = ins[1][at] + ins[2][at].astype(FLOAT)
            normal, inverse = normalize(ins[3][i])
            outs[2][i, 1:2] = over(second)
            outs[2][i, 2:3] = over(second * normal)
            total = here + normalize_back(second * (1.0 + mod_here[4:5]), normal, inverse)
            outs[0][i] = total
            outs[2][i, 0:1] = over(total * ins[4][i])
            outs[1][at] = (mod_here[2:3] * total).astype(BFLOAT)

    return call(
        body,
        [(middle.shape, FLOAT), ((ITEMS * count, D), BFLOAT), ((ITEMS, 4, D), FLOAT)],
        [delta, own, received, middle, branch, outer, mod],
    )


def attend_back_call(own, other, weight, layer, places, cells, width):
    total = 2 * own.shape[0]
    count = total // cells

    def body(places, ins, far, outs, scratch):
        whole, joined, result, sems = scratch
        copy = pltpu.make_async_copy(far[0].at[layer], whole, sems.at[0])
        copy.start()
        joined[: total // 2] = ins[0][...]
        joined[total // 2 :] = ins[1][...]
        copy.wait()
        result[...] = dot(joined[...], whole[...], ((1,), (1,))).astype(BFLOAT)
        for k in range(count):
            start = pl.multiple_of((places[2] ^ k) * cells, cells)
            outs[k][0] = result[pl.ds(start, cells)]

    return call(
        body,
        [((1, cells, width), BFLOAT)] * count,
        [own, other],
        places,
        [weight],
        scratch=[
            pltpu.VMEM((width, D), BFLOAT),
            pltpu.VMEM((total, D), BFLOAT),
            pltpu.VMEM((total, width), BFLOAT),
            pltpu.SemaphoreType.DMA((1,)),
        ],
    )


def project_back_call(blocks, weight, places, cells, width):
    count = len(blocks)
    total = count * cells
    wide = blocks[0].shape[2]

    def body(places, ins, far, outs, scratch):
        whole, sems = scratch
        copies = gather_weight(far[1:], whole, sems, places, far[0])
        for k in range(count):
            start = pl.multiple_of((places[2] ^ k) * cells, cells)
            outs[2][pl.ds(start, cells)] = ins[k][0]
        at = width // LANES * LANES
        logits = outs[2][:, at : at + LANES].astype(FLOAT)
        outs[3][...] = jnp.sum(logits, axis=0, keepdims=True)
        for copy in copies:
            copy.wait()
        for at in range(0, D, COLUMNS):
            columns = slice(at, at + COLUMNS)
            value = dot(outs[2][...], whole[at : at + COLUMNS], ((1,), (1,)))
            halves_out(value, outs, columns, total // 2)

    return call(
        body,
        [
            ((total // 2, D), FLOAT),
            ((total // 2, D), BFLOAT),
            ((total, wide), BFLOAT),
            ((1, LANES), FLOAT),
        ],
        blocks,
        places,
        weight,
        scratch=[pltpu.VMEM((D, wide), BFLOAT), pltpu.SemaphoreType.DMA((5,))],
    )


def conv_delta_call(own, received, convolved, tile):
    cells = convolved.shape
    count = tile[0] * tile[1]

    def body(_, ins, far, outs, scratch):
        for i in range(ITEMS):
            at = slice(i * count, (i + 1) * count)
            delta = (ins[0][at] + ins[1][at].astype(FLOAT)).reshape(cells[1:])
            value = ins[2][i]
            gate = jax.nn.sigmoid(value)
            delta = delta * gate * (1.0 + value * (1.0 - gate))
            outs[0][i] = delta.astype(BFLOAT)
            put_edges(delta, i, outs[1:], tile)

    delta, *edges = call(
        body, [(cells, BFLOAT)] + edge_shapes(tile), [own, received, convolved]
    )
    return delta, edges


def enter_back_call(delta_hidden, tokens, delta_middle, mod, mod_before):
    count = tokens.shape[1]
    over = lambda v: jnp.sum(v, axis=0, keepdims=True)
    lower = mod_before is not None

    def body(_, ins, far, outs, scratch):
        for i in range(ITEMS):
            at = slice(i * count, (i + 1) * count)
            here = ins[0][i].reshape(count, D)
            normal, inverse = normalize(ins[1][i].astype(FLOAT))
            outs[0][i, 0:1] = over(here)
            outs[0][i, 1:2] = over(here * normal)
            total = ins[2][i] + normalize_back(here * (1.0 + ins[3][i][1:2]), normal, inverse)
            if lower:
                outs[2][i] = total
                outs[1][at] = (ins[4][i][5:6] * total).astype(BFLOAT)
            else:
                outs[1][at] = total.astype(BFLOAT)

    shapes = [((ITEMS, 2, D), FLOAT), ((ITEMS * count, D), BFLOAT)]
    arrays = [delta_hidden, tokens, delta_middle, mod]
    if lower:
        shapes.append((tokens.shape, FLOAT))
        arrays.append(mod_before)
    return call(body, shapes, arrays)


def pack_kernel(places, qkv, decay, own, other, *, width):
    heads = width // HD
    size = padded_width(width + 3 * heads)
    value, extra = qkv[0].astype(FLOAT), decay[0].astype(FLOAT)
    rows = value.shape[0]
    pieces = []
    for group in range(2):
        parts = []
        for j in range(3):
            start = j * D + group * width
            parts.append(value[:, start : start + width])
            filled = width
            if j == 0:
                parts.append(extra[:, group * heads : (group + 1) * heads])
                filled += heads
            parts.append(jnp.zeros((rows, size - filled), FLOAT))
        pieces.append(jnp.concatenate(parts, axis=1).astype(BFLOAT))
    first = places[0] == 0
    own[...] = jnp.where(first, pieces[0], pieces[1])
    other[...] = jnp.where(first, pieces[1], pieces[0])


def pack_call(qkv, decay, layer, places, width):
    rows = qkv.shape[1]
    size = padded_width(width + 3 * (width // HD))

    def body(*refs):
        pack_kernel(*refs, width=width)

    out = pl.BlockSpec((SHARE_ROWS, 3 * size), lambda i, m: (i, 0))
    return pl.pallas_call(
        body,
        grid_spec=pltpu.PrefetchScalarGridSpec(
            num_scalar_prefetch=1,
            grid=(rows // SHARE_ROWS,),
            in_specs=[
                pl.BlockSpec((1, SHARE_ROWS, qkv.shape[2]), lambda i, m: (layer, i, 0)),
                pl.BlockSpec((1, SHARE_ROWS, decay.shape[2]), lambda i, m: (layer, i, 0)),
            ],
            out_specs=[out, out],
        ),
        out_shape=[jax.ShapeDtypeStruct((rows, 3 * size), BFLOAT)] * 2,
        cost_estimate=SMALL,
        compiler_params=params(),
    )(places, qkv, decay)


def passed_by(values, after):
    count = len(values)
    return pl.pallas_call(
        lambda *refs: None,
        in_specs=[ANYWHERE] * (count + len(after)),
        out_specs=[ANYWHERE] * count,
        out_shape=[jax.ShapeDtypeStruct(v.shape, v.dtype) for v in values],
        input_output_aliases={k: k for k in range(count)},
        cost_estimate=SMALL,
        compiler_params=params(),
    )(*values, *after)


def lines_swapped(blocks, axis):
    return [blocks[0]] + [swap(blocks[k], axis, k) for k in range(1, len(blocks))]


class Pair:
    def __init__(self, args, taps, tile):
        self.args, self.taps, self.tile = args, taps, tile
        self.modulations = [None] * LAYERS
        self.cells = tile[0] * tile[1]
        self.width = args["proj"].shape[1]
        self.heads = self.width // HD
        self.size = padded_width(self.width + 3 * self.heads)
        batch, row = lax.axis_index("batch"), lax.axis_index("row")
        quarter = row % 2 * 2 + row // 2
        self.places = [
            jnp.stack([batch, quarter, lax.axis_index(axis)]).astype(jnp.int32)
            for axis in ("col", "row")
        ]
        self.qkv, self.expand, self.bias = [], [], []
        self.pieces = {}
        self.quarter, self.batch = quarter, batch
        self.modulate()
        for layer in range(LAYERS):
            self.prepare(layer)
        for stage in range(3):
            self.fetch("qkv", 0, stage, [])

    def prepare(self, layer):
        args = self.args
        own, other = pack_call(args["qkv"], args["decay"], layer, self.places[0], self.width)
        part = own.shape[0] // 4
        self.pieces["qkv", layer] = lax.dynamic_slice_in_dim(other, self.quarter * part, part, 0)
        self.qkv.append([own])
        inner = args["shrink"].shape[1]
        piece = lax.dynamic_slice(
            args["expand"],
            (layer, self.quarter * part, (1 - self.batch) * inner),
            (1, part, inner),
        )
        self.pieces["expand", layer] = piece[0]
        self.expand.append([args["expand"]])
        start = self.width - self.width // LANES * LANES
        self.bias.append(
            jnp.pad(
                args["decay_bias"][layer].astype(FLOAT)[None],
                ((0, 0), (start, LANES - start - self.heads)),
            )
        )

    def modulate(self):
        cond = self.args["cond"]
        partial = jnp.stack(
            [
                jnp.dot(cond, self.args["ada"][layer], preferred_element_type=FLOAT)
                for layer in range(LAYERS)
            ],
            axis=1,
        )
        total = partial[:ITEMS] + swap(partial[ITEMS:])
        for layer in range(LAYERS):
            value = total[:, layer] + self.args["ada_bias"][layer]
            self.modulations[layer] = value.reshape(ITEMS, 6, D)

    def fetch(self, name, layer, stage, after):
        held = self.pieces[name, layer]
        if stage == 0:
            if after:
                (held,) = passed_by([held], after)
            self.pieces[name, layer] = [swap(held)]
        elif stage == 1:
            if after:
                held = passed_by(held, after)
            self.pieces[name, layer] = [held[0], swap(held[0], "row", 2)]
        else:
            if after:
                held = passed_by(held, after)
            into = self.qkv if name == "qkv" else self.expand
            into[layer] += list(held) + [swap(part, "row", 1) for part in held]

    def axis(self, layer):
        return "col" if layer % 2 == 0 else "row"

    def scan(self, kernel, layer, inputs, out_width):
        place = self.places[layer % 2][2]
        rows, cols = self.tile
        return scan_call(
            kernel, place, inputs, out_width, rows, cols, layer % 2 == 0, self.width
        )

    def forward(self, layer, hidden, edges, tokens):
        places, axis = self.places[layer % 2], self.axis(layer)
        mod = self.modulations[layer]
        sides = halo_edges(edges)
        convolved, mixed = conv_forward(hidden, sides, self.taps[layer])
        mixed = mixed.reshape(-1, D)
        mixed_other = swap(mixed)
        if layer == 0:
            self.fetch("expand", 0, 0, [hidden])
            self.fetch("expand", 0, 1, [mixed])
        else:
            self.fetch("expand", 1, 1, [mixed])
        parts = project_call(
            mixed, mixed_other, self.qkv[layer], self.bias[layer], places, self.cells, self.width
        )
        parts = list(parts)
        self.fetch("expand", layer, 2, [parts[0]])
        if layer + 1 < LAYERS:
            self.fetch("qkv", layer + 1, 0, [parts[0]])
        parts = lines_swapped(parts, axis)
        attends = self.scan(scan_forward_kernel, layer, parts, self.width)
        own, send, attend = attend_out_call(
            lines_swapped(attends, axis), self.args["proj"], layer, places, self.cells, self.width
        )
        if layer + 1 < LAYERS:
            self.fetch("qkv", layer + 1, 1, [own])
        branch, middle, second = middle_call(tokens, own, swap(send), mod)
        second_other = swap(second)
        if layer + 1 < LAYERS:
            self.fetch("qkv", layer + 1, 2, [second])
        own, send, inner, active = feed_call(
            second, second_other, self.expand[layer], self.args["shrink"], layer, places
        )
        if layer + 1 < LAYERS:
            self.fetch("expand", layer + 1, 0, [own])
        received = swap(send)
        mixer_act, second_act, active_act, own = turn_call(
            mixed, mixed_other, attend, second, second_other, active, places, own
        )
        saved = dict(
            tokens=tokens, hidden=hidden, sides=sides, convolved=convolved, parts=parts,
            branch=branch, middle=middle, inner=inner, mixer_act=mixer_act,
            second_act=second_act, active_act=active_act,
        )
        return middle, own, received, saved

    def backward(self, layer, delta, outer_low, outer_other, saved, tick):
        places, axis = self.places[layer % 2], self.axis(layer)
        mod = self.modulations[layer]
        both = lambda own, other: jnp.concatenate([own, other], axis=0)
        own, send, inner_low = feed_back_call(
            outer_low, outer_other, saved["inner"], self.expand[layer], self.args["shrink"],
            layer, places,
        )
        received = swap(send)
        shrink_pipe = shrink_sum(saved["active_act"], both(outer_low, outer_other))
        own = tick("P1", {"A": shrink_pipe}, own)
        delta_middle, branch_low, mod_b = middle_back_call(
            delta, own, received, saved["middle"], saved["branch"], saved["outer"], mod
        )
        branch_other = swap(branch_low)
        expand_pipe = expand_sum(saved["second_act"], inner_low)
        branch_low = tick("P2", {"B": expand_pipe}, branch_low)
        blocks = attend_back_call(
            branch_low, branch_other, self.args["proj"], layer, places, self.cells, self.width
        )
        sent = lines_swapped(blocks, axis)
        sent[0] = tick("P3", {}, sent[0])
        projects = self.scan(
            scan_backward_kernel, layer, list(saved["parts"]) + sent, 3 * self.size
        )
        sent = lines_swapped(projects, axis)
        sent[0] = tick("P4", {}, sent[0])
        own, send, delta_project, grad_bias = project_back_call(
            sent, self.qkv[layer], places, self.cells, self.width
        )
        received = swap(send)
        def mixer(after):
            (value,) = passed_by([delta_project], after)
            act = saved["mixer_act"]
            pipe, logits = mixer_sum(
                act, value, branch_low, branch_other, places, self.width, self.size
            )
            return pipe, dot(logits, act[0], ((0,), (1,)))[: 2 * self.heads]

        if not layer:
            mixer_pipe, grad_decay = mixer([])
        own = tick("P5", {}, own)
        delta_conv, edges = conv_delta_call(own, received, saved["convolved"], self.tile)
        delta_sides = halo_edges(edges)
        delta_conv = tick("P6", {}, delta_conv)
        if layer:
            mixer_pipe, grad_decay = mixer([delta_conv])
        top, bottom, left, right = delta_sides
        (left,) = passed_by([left], [right])
        left = tick("P8", {"C": mixer_pipe}, left)
        delta_sides = (top, bottom, left, right)
        delta_hidden, grad_taps = conv_backward(
            saved["hidden"], saved["sides"], delta_conv, delta_sides, self.taps[layer]
        )
        before = self.modulations[layer - 1] if layer else None
        mod_a, low, *rest = enter_back_call(
            delta_hidden, saved["tokens"], delta_middle, mod, before
        )
        low_other = swap(low) if rest else None

        small = SmallSum(join_smalls(mod_a, mod_b, grad_taps, grad_decay, grad_bias))
        low = tick("P7", {"S": small}, low)
        return rest[0] if rest else None, low, low_other


def pair_forward_backward(pair, tokens_in, cotangent, tick):
    tile = pair.tile
    shape = (ITEMS, pair.cells, D)
    tokens = tokens_in.reshape(shape)
    delta = cotangent.reshape(shape)
    hidden, edges = enter_first(tokens, pair.modulations[0], tile)
    stored = []
    for layer in range(LAYERS):
        middle, own, received, saved = pair.forward(layer, hidden, edges, tokens)
        stored.append(saved)
        mod = pair.modulations[layer]
        if layer + 1 < LAYERS:
            tokens, saved["outer"], hidden, edges = enter_next(
                middle, own, received, mod, pair.modulations[layer + 1], tile
            )
        else:
            block_out, saved["outer"] = leave(middle, own, received, mod)
    outer_low = (pair.modulations[-1][:, 5:6] * delta.astype(FLOAT)).astype(BFLOAT)
    outer_low = outer_low.reshape(-1, D)
    outer_other = swap(outer_low)
    for layer in reversed(range(LAYERS)):
        delta, outer_low, outer_other = pair.backward(
            layer, delta, outer_low, outer_other, stored[layer],
            lambda point, fresh, through, layer=layer: tick(layer, point, fresh, through),
        )
    return block_out, outer_low


def forward_layer(tokens, modulation, weights, layer, tile):
    taps, qkv, decay_bias, proj, expand, shrink = weights
    rows, cols = tile
    items, cells = tokens.shape[:2]
    width = proj.shape[0]
    heads = width // HD
    size = padded_width(width + 3 * heads)
    axis = "col" if layer % 2 == 0 else "row"
    mod = [modulation[:, k][:, None] for k in range(6)]
    normal, inverse = normalize(tokens)
    hidden = (normal * (1.0 + mod[1]) + mod[0]).astype(BFLOAT).reshape(items, rows, cols, D)
    sides = halo(hidden)
    convolved, mixed = conv_forward(hidden, sides, taps)
    mixed = gather_items(mixed.reshape(items, cells, D))
    project = matmul(mixed, qkv)
    logit = project[:, :, width : width + heads] + decay_bias.astype(FLOAT)
    high = logit.astype(BFLOAT)
    rest = logit - high.astype(FLOAT)
    middle_part = rest.astype(BFLOAT)
    low = (rest - middle_part.astype(FLOAT)).astype(BFLOAT)
    project = project.astype(BFLOAT)
    project = jnp.concatenate(
        [project[:, :, :width], high, middle_part, low, project[:, :, width + 3 * heads :]], axis=2
    )
    parts = lines_out(project, axis)
    place = lax.axis_index(axis)
    attends = scan_call(
        scan_forward_kernel, place, parts, width, rows, cols, layer % 2 == 0, width
    )
    attend = lines_back(attends, axis)
    branch = reduce_items(matmul(attend, proj))
    middle = tokens + mod[2] * branch
    normal2, inverse2 = normalize(middle)
    second = gather_items((normal2 * (1.0 + mod[4]) + mod[3]).astype(BFLOAT))
    inner = matmul(second, expand)
    active = gelu(inner).astype(BFLOAT)
    outer = reduce_items(matmul(active, shrink))
    result = middle + mod[5] * outer
    saved = (
        normal, inverse, hidden, sides, convolved, mixed, parts, attend, branch,
        normal2, inverse2, second, inner, active, outer,
    )
    return result, saved


def pipelined(width):
    shares = lax.axis_size("row") * lax.axis_size("col")
    square = lax.axis_size("row") == 4 and lax.axis_size("col") == 4
    return lax.axis_size("batch") == 2 and square and width == 4 * SHARE_ROWS and shares == SHARES


def backward_layer(delta, saved, modulation, weights, layer, tile):
    taps, qkv, decay_bias, proj, expand, shrink = weights
    (
        normal, inverse, hidden, sides, convolved, mixed, parts, attend, branch,
        normal2, inverse2, second, inner, active, outer,
    ) = saved
    rows, cols = tile
    items, cells = delta.shape[:2]
    width = proj.shape[0]
    heads = width // HD
    size = padded_width(width + 3 * heads)
    axis = "col" if layer % 2 == 0 else "row"
    mod = [modulation[:, k][:, None] for k in range(6)]
    over = lambda v: jnp.sum(v, axis=1)
    delta_gate2 = over(delta * outer)
    outer_low = gather_items((mod[5] * delta).astype(BFLOAT))
    grad_shrink = weight_grad(active, outer_low)
    inner_low = (matmul_back(outer_low, shrink) * gelu_slope(inner)).astype(BFLOAT)
    grad_expand = weight_grad(second, inner_low)
    delta_second = reduce_items(matmul_back(inner_low, expand))
    delta_shift2 = over(delta_second)
    delta_scale2 = over(delta_second * normal2)
    delta_middle = delta + normalize_back(delta_second * (1.0 + mod[4]), normal2, inverse2)
    delta_gate1 = over(delta_middle * branch)
    branch_low = gather_items((mod[2] * delta_middle).astype(BFLOAT))
    grad_proj = weight_grad(attend, branch_low)
    delta_attend = matmul_back(branch_low, proj).astype(BFLOAT)
    delta_parts = lines_out(delta_attend, axis)
    place = lax.axis_index(axis)
    projects = scan_call(
        scan_backward_kernel, place, list(parts) + delta_parts, 3 * size, rows, cols,
        layer % 2 == 0, width,
    )
    delta_project = lines_back(projects, axis)
    grad_qkv = weight_grad(mixed, delta_project)
    sums = (grad_shrink, grad_expand, grad_proj, grad_qkv)
    grad_decay_bias = jnp.sum(delta_project[:, :, width : width + heads].astype(FLOAT), axis=(0, 1))
    delta_mixed = reduce_items(matmul_back(delta_project, qkv)).reshape(convolved.shape)
    gate = jax.nn.sigmoid(convolved)
    delta_conv = (delta_mixed * gate * (1.0 + convolved * (1.0 - gate))).astype(BFLOAT)
    delta_sides = halo(delta_conv)
    delta_hidden, grad_taps = conv_backward(hidden, sides, delta_conv, delta_sides, taps)
    delta_hidden = delta_hidden.reshape(items, cells, D)
    delta_shift1 = over(delta_hidden)
    delta_scale1 = over(delta_hidden * normal)
    delta_tokens = delta_middle + normalize_back(delta_hidden * (1.0 + mod[1]), normal, inverse)
    delta_mod = jnp.stack(
        [delta_shift1, delta_scale1, delta_gate1, delta_shift2, delta_scale2, delta_gate2], axis=1
    )
    return delta_tokens, sums, (delta_mod, grad_taps, None, grad_decay_bias)


def sum_rows_here(grad):
    return lax.psum(grad.astype(BFLOAT), GRID_AXES).astype(FLOAT)


def sum_columns(grad):
    count = lax.axis_size("batch")
    low = grad.astype(BFLOAT).reshape((count, -1, grad.shape[1]))
    shares = lax.axis_size("row") * lax.axis_size("col")
    if count == 2 and low.shape[1] % shares == 0:
        share = lax.psum_scatter(low, GRID_AXES, scatter_dimension=1, tiled=True)
        place = lax.axis_index("batch")
        own = lax.dynamic_index_in_dim(share, place, 0, keepdims=False)
        other = swap(lax.dynamic_index_in_dim(share, 1 - place, 0, keepdims=False))
        both = jnp.stack([jnp.where(place == 0, own, other), jnp.where(place == 0, other, own)])
        return lax.all_gather(both, GRID_AXES, axis=1, tiled=True)
    total = lax.psum(low, GRID_AXES)
    return lax.all_to_all(total, "batch", 0, 0)


def ada_call(cond, mods, previous, layer, through):
    items, rows = cond.shape
    wide = mods.shape[1]
    block = 64
    previous = [] if previous is None else [previous]

    def body(columns, values, *refs):
        out = refs[-2]
        for at in range(0, wide, D):
            part = slice(at, at + D)
            total = columns[:, 0:1] * values[0:1, part]
            for item in range(1, items):
                total += columns[:, item : item + 1] * values[item : item + 1, part]
            out[0, :, part] = total

    count = len(previous)
    return pl.pallas_call(
        body,
        grid=(rows // block,),
        in_specs=[
            pl.BlockSpec((block, items), lambda i: (i, 0)),
            pl.BlockSpec((items, wide), lambda i: (0, 0)),
        ]
        + [ANYWHERE] * (count + 1),
        out_specs=[pl.BlockSpec((1, block, wide), lambda i: (layer, i, 0)), ANYWHERE],
        out_shape=[
            jax.ShapeDtypeStruct((LAYERS, rows, wide), FLOAT),
            jax.ShapeDtypeStruct(through.shape, through.dtype),
        ],
        input_output_aliases={2 + k: k for k in range(count)} | {2 + count: 1},
        cost_estimate=SMALL,
        compiler_params=params(),
    )(jnp.transpose(cond.astype(FLOAT)), mods, *previous, through)


SCHEDULE = {
    (1, "P1"): "aA1",
    (1, "P2"): "aB1rL1",
    (1, "P7"): "sC1",
    (0, "P1"): "kC1sA0",
    (0, "P2"): "kA0sB0gL1",
    (0, "P3"): "kB0",
    (0, "P5"): "tC1",
    (0, "P8"): "sC0kC0tC1tA0",
    (0, "P7"): "tC1tA0tB0sS0",
}
TAIL = (
    "tA0tB0tC0tS0",
    "tB0tC0tS0",
    "tB0tC0tS0gL0",
    "tS0",
    "mS1",
    "fAB1",
    "mS0",
    "fABC0",
)


SMALL_ROWS = 32


def join_smalls(mod_a, mod_b, grad_taps, grad_decay, grad_bias):
    heads = grad_decay.shape[0] // 2

    def body(_, ins, far, outs, scratch):
        out = outs[0]
        for i in range(ITEMS):
            out[6 * i : 6 * i + 2] = ins[0][i]
            out[6 * i + 2 : 6 * i + 6] = ins[1][i]
        out[12:21] = ins[2][...]
        out[21 : 21 + heads] = jnp.concatenate([ins[3][:heads], ins[3][heads:]], axis=1)
        bias = jnp.concatenate([ins[4][...], jnp.zeros((1, D - LANES), FLOAT)], axis=1)
        out[21 + heads : 22 + heads] = bias
        out[22 + heads :] = jnp.zeros((SMALL_ROWS - 22 - heads, D), FLOAT)

    return call(
        body, [((SMALL_ROWS, D), FLOAT)], [mod_a, mod_b, grad_taps, grad_decay, grad_bias]
    )[0]


def split_smalls(flat, items, heads, width):
    start = width - width // LANES * LANES
    decay = flat[21 : 21 + heads]
    return (
        flat[: items * 6].reshape(items, 6 * D),
        flat[12:21],
        jnp.concatenate([decay[:, :width], decay[:, width:]], axis=0),
        flat[21 + heads, start : start + heads],
    )


def general_forward_backward(
    tokens_in, cotangent, modulations, taps_all, qkv_weight, decay_weight, decay_bias,
    proj_weight, expand_weight, shrink_weight,
):
    count = lax.axis_size("batch")
    items, rows, cols = tokens_in.shape[:3]
    tile = (rows, cols)
    width = proj_weight.shape[1]
    weights = []
    for layer in range(LAYERS):
        qkv = fetch_columns(
            [head_columns(qkv_weight[layer], decay_weight[layer], g, width) for g in range(count)]
        )
        inner = expand_weight.shape[2] // count
        expand = fetch_columns(
            [expand_weight[layer][:, g * inner : (g + 1) * inner] for g in range(count)]
        )
        weights.append(
            (taps_all[layer], qkv, decay_bias[layer], proj_weight[layer], expand, shrink_weight[layer])
        )
    tokens = tokens_in.astype(FLOAT).reshape(items, rows * cols, D)
    stored = []
    for layer in range(LAYERS):
        tokens, saved = forward_layer(tokens, modulations[layer], weights[layer], layer, tile)
        stored.append(saved)
    delta = cotangent.astype(FLOAT).reshape(tokens.shape)
    bigs, smalls = [None] * LAYERS, [None] * LAYERS
    for layer in reversed(range(LAYERS)):
        delta, big, small = backward_layer(
            delta, stored[layer], modulations[layer], weights[layer], layer, tile
        )
        grad_shrink, grad_expand, grad_proj, grad_qkv = big
        bigs[layer] = (
            sum_rows_here(grad_shrink),
            sum_columns(grad_expand),
            sum_rows_here(grad_proj),
            sum_columns(grad_qkv),
        )
        smalls[layer] = tuple(
            None if part is None else lax.psum(part, GRID_AXES) for part in small
        )
    return tokens.astype(BFLOAT), delta.astype(BFLOAT), bigs, smalls


def per_device(
    tokens_in, timesteps, ada_weight, ada_bias, conv_taps, qkv_weight, decay_weight, decay_bias,
    proj_weight, expand_weight, shrink_weight, cotangent,
):
    count, place = lax.axis_size("batch"), lax.axis_index("batch")
    items, rows, cols = tokens_in.shape[:3]
    tile = (rows, cols)
    rows_here = ada_weight.shape[1]
    width = proj_weight.shape[1]
    heads = width // HD
    size = padded_width(width + 3 * heads)
    cond = jax.nn.silu(embed_steps(timesteps)).astype(BFLOAT)
    cond_slice = lax.dynamic_slice_in_dim(cond, place * rows_here, rows_here, 1)
    order = [0] if count != 2 else None
    if count == 2:
        cond_first = jnp.where(
            place == 0, cond_slice, jnp.concatenate([cond_slice[items:], cond_slice[:items]])
        )
    else:
        cond_first = cond_slice
    biases = gather_last(ada_bias).astype(FLOAT)
    taps_all = gather_last(conv_taps)
    fast = pipelined(width) and count * items == 4 and tile == (8, 8)
    hidden_units = shrink_weight.shape[1]
    if fast:
        moving = {}
        upper_sums = Scattered()

        def act(names, through):
            names = [names[at : at + 3] for at in range(0, len(names), 3)]
            steps = []
            for name in names + ["end"]:
                if name[0] == "t":
                    steps.append(moving[name[1:]])
                    continue
                through = tick(steps, through)
                steps = []
                one = moving.get(name[1:])
                if name[0] == "s":
                    through = one.start(through)
                elif name[0] == "k":
                    through = one.second(through)
                elif name == "gL1":
                    upper_sums.gather(through)
                elif name == "gL0":
                    Gathered([moving[name] for name in ("C1", "A0", "B0", "C0")]).gather()
                elif name[0] == "a":
                    through = upper_sums.add(one, through)
                elif name[0] == "r":
                    upper_sums.reduce()
            return through

        def step(layer, point, fresh, through):
            for name, one in fresh.items():
                moving[name if len(name) == 2 else name + str(layer)] = one
                if name in "ABC":
                    one.offload = True
            if "S" in fresh and not layer:
                moving["S0"] = SmallSum(
                    jnp.concatenate([moving["S0"].value, moving["S1"].value], axis=0)
                )
            return act(SCHEDULE.get((layer, point), ""), through)

        pair = Pair(
            dict(
                qkv=qkv_weight, decay=decay_weight, decay_bias=decay_bias, proj=proj_weight,
                expand=expand_weight, shrink=shrink_weight, cond=cond_first, ada=ada_weight,
                ada_bias=biases,
            ),
            taps_all,
            tile,
        )
        block_out, through = pair_forward_backward(pair, tokens_in, cotangent, step)
        shapes = [
            (LAYERS, hidden_units, D),
            (LAYERS, rows_here, expand_weight.shape[2]),
            (LAYERS, rows_here, 3 * D),
            (LAYERS, width, D),
        ]
        finished = None
        grad_ada = None
        smalls = [None] * LAYERS
        for names in TAIL:
            if names[0] == "f":
                kinds = names[1:-1]
                layer = int(names[-1])
                sums = [moving[kind + names[-1]] for kind in kinds]
                if kinds[-1] == "C":
                    kinds, sums = kinds + "C", sums + [moving["C1"]]
                made, through = Gathered.finish(
                    sums, kinds,
                    None if layer else finished, layer, shapes, through,
                )
                finished = (finished or {}) | made
            elif names[0] == "m":
                layer = int(names[2])
                flat = moving["S0"].keep[layer * SMALL_ROWS : (layer + 1) * SMALL_ROWS]
                smalls[layer] = list(split_smalls(flat, items, heads, width))
                mods = gather_items(smalls[layer][0])
                smalls[layer][0] = mods
                grad_ada, through = ada_call(cond_first, mods, grad_ada, layer, through)
            else:
                through = act(names, through)
        grad_tokens = through
    else:
        partial = jnp.stack(
            [
                jnp.dot(cond_first, ada_weight[layer], preferred_element_type=FLOAT)
                for layer in range(LAYERS)
            ],
            axis=1,
        )
        if count == 2:
            total = partial[:items] + swap(partial[items:])
        else:
            total = lax.psum_scatter(partial, "batch", scatter_dimension=0, tiled=True)
        modulations = [
            (total[:, layer] + biases[layer]).reshape(items, 6, D) for layer in range(LAYERS)
        ]
        block_out, grad_tokens, bigs, smalls = general_forward_backward(
            tokens_in, cotangent, modulations, taps_all, qkv_weight, decay_weight, decay_bias,
            proj_weight, expand_weight, shrink_weight,
        )
    block_out = block_out.reshape(tokens_in.shape)
    grad_tokens = grad_tokens.reshape(tokens_in.shape)
    delta_mods, taps_grads, bias_grads = (
        jnp.stack([smalls[layer][k] for layer in range(LAYERS)]) for k in (0, 1, 3)
    )
    if fast:
        every_mod = delta_mods.transpose(1, 0, 2)
    else:
        every_mod = gather_items(delta_mods.transpose(1, 0, 2, 3)).reshape(
            count * items, LAYERS, 6 * D
        )
    if count == 2:
        taps_every = taps_grads + swap(taps_grads)
    else:
        taps_every = lax.psum(taps_grads, "batch")
    grad_taps = lax.dynamic_slice_in_dim(taps_every, place * width, width, 2)
    if not fast:
        grad_ada = jnp.zeros((LAYERS, rows_here, 6 * D), FLOAT)
        for item in range(count * items):
            grad_ada += (
                cond_first[item].astype(FLOAT)[None, :, None] * every_mod[item][:, None, :]
            )
    bias_width = ada_bias.shape[1]
    grad_ada_bias = lax.dynamic_slice_in_dim(
        jnp.sum(every_mod, axis=0), place * bias_width, bias_width, 1
    )
    if fast:
        grad_shrink, grad_expand, grad_qkv, grad_proj = (finished[k] for k in range(4))
        grad_decay = jnp.stack([jnp.transpose(smalls[layer][2]) for layer in range(LAYERS)])
    else:
        stack = lambda k: jnp.stack([bigs[layer][k] for layer in range(LAYERS)])
        grad_shrink, grad_proj = stack(0), stack(2)
        expand_parts, qkv_parts = stack(1), stack(3)
        grad_expand = jnp.concatenate([expand_parts[:, g] for g in range(count)], 2).astype(FLOAT)
        grad_qkv = jnp.concatenate(
            [
                qkv_parts[:, g, :, j * size : j * size + width]
                for j in range(3)
                for g in range(count)
            ],
            axis=2,
        ).astype(FLOAT)
        grad_decay = jnp.concatenate(
            [qkv_parts[:, g, :, width : width + heads] for g in range(count)], axis=2
        ).astype(FLOAT)
    return (
        block_out,
        grad_tokens,
        grad_ada,
        grad_ada_bias,
        grad_taps,
        grad_qkv,
        grad_decay,
        bias_grads,
        grad_proj,
        grad_expand,
        grad_shrink,
    )


def solution(mesh):
    return jax.shard_map(
        per_device,
        mesh=mesh,
        in_specs=(
            P("batch", "row", "col", None),
            P(),
            P(None, "batch", None),
            P(None, "batch"),
            P(None, None, "batch"),
            P(None, "batch", None),
            P(None, "batch", None),
            P(None, "batch"),
            P(None, "batch", None),
            P(None, "batch", None),
            P(None, "batch", None),
            P("batch", "row", "col", None),
        ),
        out_specs=(
            P("batch", "row", "col", None),
            P("batch", "row", "col", None),
            P(None, "batch", None),
            P(None, "batch"),
            P(None, None, "batch"),
            P(None, "batch", None),
            P(None, "batch", None),
            P(None, "batch"),
            P(None, "batch", None),
            P(None, "batch", None),
            P(None, "batch", None),
        ),
        check_vma=False,
    )
```

```python
import jax
import jax.numpy as jnp
from jax import lax
from jax.experimental import pallas as pl
from jax.experimental.pallas import tpu as pltpu
from jax.sharding import PartitionSpec as P

D = 1152
H = 16
HD = 72
LAYERS = 2
EPS = 1e-06
ACCURATE = lax.Precision.HIGHEST
FLOAT = jnp.float32
BFLOAT = jnp.bfloat16
LANES = 128
VMEM_LIMIT = 48 * 1024 * 1024
GRID_AXES = ("row", "col")
SMALL = pl.CostEstimate(flops=1, bytes_accessed=1, transcendentals=0)


def params():
    return pltpu.CompilerParams(vmem_limit_bytes=VMEM_LIMIT)


def padded_width(width):
    return -(-width // LANES) * LANES


def swap(value, axis="batch", bit=1):
    count = lax.axis_size(axis)
    return lax.ppermute(value, axis, [(i, i ^ bit) for i in range(count)])


def gather_items(own):
    if lax.axis_size("batch") == 2:
        return jnp.concatenate([own, swap(own)], axis=0)
    return lax.all_gather(own, "batch", axis=0, tiled=True)


def gather_last(own):
    if lax.axis_size("batch") == 2:
        other = swap(own)
        first = lax.axis_index("batch") == 0
        return jnp.concatenate([jnp.where(first, own, other), jnp.where(first, other, own)], -1)
    return lax.all_gather(own, "batch", axis=own.ndim - 1, tiled=True)


def reduce_items(partial):
    if lax.axis_size("batch") == 2:
        items = partial.shape[0] // 2
        return partial[:items] + swap(partial[items:].astype(BFLOAT)).astype(FLOAT)
    return lax.psum_scatter(partial, "batch", scatter_dimension=0, tiled=True)


def lines_out(values, axis):
    count, place = lax.axis_size(axis), lax.axis_index(axis)
    groups = values.reshape((count, -1) + values.shape[1:])
    blocks = []
    for k in range(count):
        block = lax.dynamic_index_in_dim(groups, place ^ k, 0, keepdims=False)
        blocks.append(block if k == 0 else swap(block, axis, k))
    return blocks


def lines_back(blocks, axis):
    count, place = lax.axis_size(axis), lax.axis_index(axis)
    received = [blocks[0]] + [swap(blocks[k], axis, k) for k in range(1, count)]
    stacked = jnp.stack(received)
    return jnp.concatenate(
        [lax.dynamic_index_in_dim(stacked, place ^ j, 0, keepdims=False) for j in range(count)]
    )


def halo(cells):
    return halo_edges([cells[:, 0], cells[:, -1], cells[:, :, 0], cells[:, :, -1]])


def beside(cells, sides, item):
    top, bottom, left, right = sides
    count, width = cells.shape[1], cells.shape[2]
    lefts, rights = left[item].astype(FLOAT), right[item].astype(FLOAT)
    at = lax.broadcasted_iota(jnp.int32, (width, cells.shape[3]), 0)
    rows = []
    for row in range(count + 2):
        if row == 0:
            here = top[item]
        elif row == count + 1:
            here = bottom[item]
        else:
            here = cells[item, row - 1]
        here = here.astype(FLOAT)
        before = jnp.where(at == 0, lefts[row : row + 1], pltpu.roll(here, 1, 0))
        after = jnp.where(at == width - 1, rights[row : row + 1], pltpu.roll(here, width - 1, 0))
        rows.append((before, here, after))
    return rows


def conv_forward_kernel(cells, *refs):
    sides, (taps, convolved, mixed) = refs[:4], refs[4:]
    weights = taps[...].astype(FLOAT)
    for item in range(cells.shape[0]):
        rows = beside(cells, sides, item)
        for row in range(cells.shape[1]):
            total = jnp.zeros(rows[0][1].shape, FLOAT)
            for a in range(3):
                for b in range(3):
                    total += weights[3 * a + b : 3 * a + b + 1] * rows[row + a][b]
            convolved[item, row] = total
            mixed[item, row] = (total * jax.nn.sigmoid(total)).astype(BFLOAT)


def conv_backward_kernel(cells, *refs):
    sides, delta, delta_sides, (taps, hidden, grads) = refs[:4], refs[4], refs[5:9], refs[9:]
    weights = taps[...].astype(FLOAT)
    sums = [jnp.zeros((cells.shape[2], cells.shape[3]), FLOAT) for _ in range(9)]
    for item in range(cells.shape[0]):
        rows = beside(cells, sides, item)
        for row in range(cells.shape[1]):
            here = delta[item, row].astype(FLOAT)
            for a in range(3):
                for b in range(3):
                    sums[3 * a + b] += rows[row + a][b] * here
        rows = beside(delta, delta_sides, item)
        for row in range(cells.shape[1]):
            total = jnp.zeros(rows[0][1].shape, FLOAT)
            for a in range(3):
                for b in range(3):
                    total += weights[3 * a + b : 3 * a + b + 1] * rows[row + 2 - a][2 - b]
            hidden[item, row] = total
    for tap in range(9):
        grads[tap : tap + 1] = jnp.sum(sums[tap], axis=0, keepdims=True)


def conv_specs(items, rows, cols, block):
    cells = pl.BlockSpec((items, rows, cols, block), lambda i: (0, 0, 0, i))
    side = lambda size: pl.BlockSpec((items, size, block), lambda i: (0, 0, i))
    taps = pl.BlockSpec((9, block), lambda i: (0, i))
    return [cells] + [side(size) for size in (cols, cols, rows + 2, rows + 2)], taps


def conv_forward(cells, sides, taps):
    items, rows, cols, width = cells.shape
    block = 3 * LANES
    specs, tap_spec = conv_specs(items, rows, cols, block)
    return pl.pallas_call(
        conv_forward_kernel,
        grid=(width // block,),
        in_specs=specs + [tap_spec],
        out_specs=[specs[0], specs[0]],
        out_shape=[
            jax.ShapeDtypeStruct(cells.shape, FLOAT),
            jax.ShapeDtypeStruct(cells.shape, BFLOAT),
        ],
        cost_estimate=SMALL,
        compiler_params=params(),
    )(cells, *sides, taps)


def conv_backward(cells, sides, delta, delta_sides, taps):
    items, rows, cols, width = cells.shape
    block = 3 * LANES
    specs, tap_spec = conv_specs(items, rows, cols, block)
    return pl.pallas_call(
        conv_backward_kernel,
        grid=(width // block,),
        in_specs=specs + specs + [tap_spec],
        out_specs=[specs[0], tap_spec],
        out_shape=[
            jax.ShapeDtypeStruct(cells.shape, FLOAT),
            jax.ShapeDtypeStruct((9, width), FLOAT),
        ],
        cost_estimate=SMALL,
        compiler_params=params(),
    )(cells, *sides, delta, *delta_sides, taps)


def scan_mask(place, rows, cols, along_cols, blocks):
    cells = rows * cols
    shape = (blocks * cells, blocks * cells)

    def line_and_position(index):
        block = index // cells
        inside = index - block * cells
        row = inside // cols
        col = inside - row * cols
        source = place ^ block
        if along_cols:
            return row, source * cols + col
        return col, source * rows + row

    line_t, at_t = line_and_position(lax.broadcasted_iota(jnp.int32, shape, 0))
    line_s, at_s = line_and_position(lax.broadcasted_iota(jnp.int32, shape, 1))
    return (line_t == line_s) & (at_s <= at_t)


def dot(left, right, contract=((1,), (0,)), precision=None):
    return lax.dot_general(
        left, right, (contract, ((), ())), precision=precision, preferred_element_type=FLOAT
    )


class Scan:
    def __init__(self, parts, mask, width):
        self.width = width
        self.padded = padded_width(width + 3 * (width // HD))
        self.heads = width // HD
        joined = jnp.concatenate([part[0] for part in parts], axis=0)
        size = self.padded
        self.queries = joined[:, :size]
        self.keys = joined[:, size : 2 * size]
        self.values = joined[:, 2 * size :]
        self.start = width - width // LANES * LANES
        self.block = width // LANES * LANES
        extra = self.queries[:, self.block : self.block + LANES].astype(FLOAT)
        logit = (
            extra
            + pltpu.roll(extra, LANES - self.heads, 1)
            + pltpu.roll(extra, LANES - 2 * self.heads, 1)
        )
        self.lane = lax.broadcasted_iota(jnp.int32, extra.shape, 1)
        self.is_logit = (self.lane >= self.start) & (self.lane < self.start + self.heads)
        self.logit = jnp.where(self.is_logit, logit, 0.0)
        small = jnp.exp(-jnp.abs(self.logit))
        logdecay = jnp.where(self.is_logit, jnp.minimum(self.logit, 0.0) - jnp.log(1.0 + small), 0.0)
        self.lower = jnp.where(mask, 1.0, 0.0).astype(FLOAT)
        self.mask = mask
        self.cumul = dot(self.lower, logdecay, precision=ACCURATE)
        self.cumul_rows = jnp.transpose(self.cumul)
        self.feature = lax.broadcasted_iota(jnp.int32, (1, size), 1)

    def of_head(self, head, array):
        inside = (self.feature >= head * HD) & (self.feature < head * HD + HD)
        return jnp.where(inside, array, jnp.zeros_like(array))

    def weights(self, head):
        at = self.start + head
        gap = self.cumul[:, at : at + 1] - self.cumul_rows[at : at + 1, :]
        return jnp.where(self.mask, jnp.exp(jnp.minimum(gap, 0.0)), 0.0)


SCALE = HD ** (-0.5)


def scan_forward_kernel(place, *refs, rows, cols, along_cols, width):
    count = len(refs) // 2
    parts, outs = refs[:count], refs[count:]
    mask = scan_mask(place[0], rows, cols, along_cols, count)
    scan = Scan(parts, mask, width)
    total = jnp.zeros(scan.queries.shape, FLOAT)
    for head in range(scan.heads):
        scores = dot(scan.of_head(head, scan.queries), scan.keys, ((1,), (1,))) * SCALE
        scores = (scores * scan.weights(head)).astype(BFLOAT)
        total += dot(scores, scan.of_head(head, scan.values))
    cells = rows * cols
    low = total.astype(BFLOAT)
    for k in range(count):
        outs[k][0] = low[k * cells : (k + 1) * cells, :width]


def scan_backward_kernel(place, *refs, rows, cols, along_cols, width):
    count = len(refs) // 3
    parts, deltas, outs = refs[:count], refs[count : 2 * count], refs[2 * count :]
    mask = scan_mask(place[0], rows, cols, along_cols, count)
    scan = Scan(parts, mask, width)
    joined = jnp.concatenate([part[0] for part in deltas], axis=0)
    short = scan.padded - width
    if short:
        joined = jnp.concatenate([joined, jnp.zeros((joined.shape[0], short), BFLOAT)], axis=1)
    shape = scan.queries.shape
    delta_query = jnp.zeros(shape, FLOAT)
    delta_key = jnp.zeros(shape, FLOAT)
    delta_value = jnp.zeros(shape, FLOAT)
    gap_rows = jnp.zeros(scan.lane.shape, FLOAT)
    gap_cols = jnp.zeros(scan.cumul_rows.shape, FLOAT)
    place_row = lax.broadcasted_iota(jnp.int32, gap_cols.shape, 0)
    for head in range(scan.heads):
        query = scan.of_head(head, scan.queries)
        delta = scan.of_head(head, joined)
        weights = scan.weights(head)
        scores = dot(query, scan.keys, ((1,), (1,))) * SCALE * weights
        delta_scores = dot(delta, scan.values, ((1,), (1,)))
        gap = delta_scores * scores
        at = scan.start + head
        gap_rows += jnp.where(scan.lane == at, jnp.sum(gap, axis=1, keepdims=True), 0.0)
        gap_cols += jnp.where(place_row == at, jnp.sum(gap, axis=0, keepdims=True), 0.0)
        inner = (delta_scores * weights * SCALE).astype(BFLOAT)
        delta_query += dot(inner, scan.of_head(head, scan.keys))
        delta_key += dot(inner, query, ((0,), (0,)))
        delta_value += dot(scores.astype(BFLOAT), delta, ((0,), (0,)))
    delta_cumul = gap_rows - jnp.transpose(gap_cols)
    delta_decay = dot(scan.lower, delta_cumul, ((0,), (0,)), ACCURATE)
    small = jnp.exp(-jnp.abs(scan.logit))
    keep = jnp.where(scan.logit >= 0.0, small, 1.0) / (1.0 + small)
    delta_logit = delta_decay * keep
    block = scan.block
    mixed = jnp.where(scan.is_logit, delta_logit, delta_query[:, block : block + LANES])
    pieces = [delta_query[:, :block]] if block else []
    pieces.append(mixed)
    if block + LANES < scan.padded:
        pieces.append(delta_query[:, block + LANES :])
    whole = jnp.concatenate(pieces + [delta_key, delta_value], axis=1).astype(BFLOAT)
    cells = rows * cols
    for k in range(count):
        outs[k][0] = whole[k * cells : (k + 1) * cells]


def scan_call(kernel, place, inputs, out_width, rows, cols, along_cols, width):
    count = lax.axis_size("col") if along_cols else lax.axis_size("row")
    items, cells = inputs[0].shape[:2]
    spec = lambda last: pl.BlockSpec((1, cells, last), lambda i, place: (i, 0, 0))

    def body(*refs):
        kernel(*refs, rows=rows, cols=cols, along_cols=along_cols, width=width)

    return pl.pallas_call(
        body,
        grid_spec=pltpu.PrefetchScalarGridSpec(
            num_scalar_prefetch=1,
            grid=(items,),
            in_specs=[spec(v.shape[2]) for v in inputs],
            out_specs=[spec(out_width)] * count,
        ),
        out_shape=[jax.ShapeDtypeStruct((items, cells, out_width), BFLOAT)] * count,
        cost_estimate=SMALL,
        compiler_params=params(),
    )(place.reshape(1).astype(jnp.int32), *inputs)


def pick(values, index):
    chosen = values[0]
    for k in range(1, len(values)):
        chosen = jnp.where(index == k, values[k], chosen)
    return chosen


def fetch_columns(pieces):
    count, place = lax.axis_size("batch"), lax.axis_index("batch")
    if count != 2:
        stacked = jnp.stack(pieces)
        return lax.all_to_all(stacked, "batch", 0, 0).reshape((-1,) + pieces[0].shape[1:])
    own, other = pick(pieces, place), pick(pieces, 1 - place)
    rows = own.shape[0]
    half = rows // 2
    core = lax.axis_index("row") % 2
    first = swap(lax.dynamic_slice_in_dim(other, core * half, half, 0))
    second = swap(first, "row", 1)
    whole = jnp.zeros((2 * rows,) + own.shape[1:], own.dtype)
    whole = lax.dynamic_update_slice_in_dim(whole, own, place * rows, 0)
    base = (1 - place) * rows
    whole = lax.dynamic_update_slice_in_dim(whole, first, base + core * half, 0)
    return lax.dynamic_update_slice_in_dim(whole, second, base + (1 - core) * half, 0)


def head_columns(qkv, decay, group, width):
    size = padded_width(width + 3 * (width // HD))
    heads = width // HD
    parts = []
    for j in range(3):
        piece = qkv[:, j * D + group * width : j * D + (group + 1) * width]
        filled = width
        parts.append(piece)
        if j == 0:
            parts.append(decay[:, group * heads : (group + 1) * heads])
            filled += heads
        if size > filled:
            parts.append(jnp.zeros((qkv.shape[0], size - filled), qkv.dtype))
    return jnp.concatenate(parts, axis=1)


def normalize(values):
    center = values - jnp.mean(values, axis=-1, keepdims=True)
    inverse = lax.rsqrt(jnp.mean(center * center, axis=-1, keepdims=True) + EPS)
    return center * inverse, inverse


def normalize_back(delta, normal, inverse):
    first = jnp.mean(delta, axis=-1, keepdims=True)
    second = jnp.mean(delta * normal, axis=-1, keepdims=True)
    return inverse * (delta - first - normal * second)


def embed_steps(steps):
    half = D // 2
    freqs = jnp.exp(-jnp.log(10000.0) * jnp.arange(half, dtype=FLOAT) / half)
    angles = steps.astype(FLOAT)[:, None] * freqs[None, :]
    return jnp.concatenate([jnp.cos(angles), jnp.sin(angles)], axis=1)


GELU_A = 0.7978845608028654
GELU_B = 0.044715


def gelu(z):
    return 0.5 * z * (1.0 + jnp.tanh(GELU_A * (z + GELU_B * z * z * z)))


def gelu_slope(z):
    t = jnp.tanh(GELU_A * (z + GELU_B * z * z * z))
    return 0.5 * (1.0 + t) + 0.5 * z * (1.0 - t * t) * GELU_A * (1.0 + 3.0 * GELU_B * z * z)


def matmul(left, right):
    return lax.dot_general(left, right, (((2,), (0,)), ((), ())), preferred_element_type=FLOAT)


def matmul_back(left, right):
    return lax.dot_general(left, right, (((2,), (1,)), ((), ())), preferred_element_type=FLOAT)


def weight_grad(left, right):
    return lax.dot_general(
        left, right, (((0, 1), (0, 1)), ((), ())), preferred_element_type=FLOAT
    )


SHARES = 16
SHARE_ROWS = 144
STAGES = (("row", 1), ("row", 2), ("col", 1), ("col", 2))


def share_place(stages):
    number = jnp.int32(0)
    for axis, bit in stages:
        number = 2 * number + (lax.axis_index(axis) // bit) % 2
    return number.reshape(1).astype(jnp.int32)


def product(act, delta):
    return lax.dot_general(act, delta, (((1,), (0,)), ((), ())), preferred_element_type=FLOAT)


def grad_send_kernel(place, act, delta, out):
    out[0] = product(act[0], delta[0]).astype(BFLOAT)


def grad_keep_kernel(place, act, delta, received, send, keep):
    value = (product(act[0], delta[0]) + received[0].astype(FLOAT)).astype(BFLOAT)
    first = pl.program_id(0) < SHARES // 4

    @pl.when(first)
    def _():
        send[0] = value

    @pl.when(jnp.logical_not(first))
    def _():
        keep[0] = value


class GradSum:
    def __init__(self, act, delta, act_index, delta_index, stages):
        self.act, self.delta, self.stages = act, delta, stages
        self.act_index, self.delta_index = act_index, delta_index
        self.place = share_place(stages)

    def call(self, kernel, position, extra, extra_specs, out_specs, out_shapes, through):
        tokens = self.act.shape[2]
        act_spec = pl.BlockSpec(
            (1, SHARE_ROWS, tokens), lambda i, m: self.act_index(position(i) ^ m[0])
        )
        delta_spec = pl.BlockSpec(
            (1, tokens, D), lambda i, m: self.delta_index(position(i) ^ m[0])
        )
        inputs = 3 + len(extra)

        def body(*refs):
            kernel(*refs[:inputs], *refs[inputs + 1 : -1])

        return pl.pallas_call(
            body,
            grid_spec=pltpu.PrefetchScalarGridSpec(
                num_scalar_prefetch=1,
                grid=(SHARES // 2,),
                in_specs=[act_spec, delta_spec] + extra_specs + [ANYWHERE],
                out_specs=out_specs + [ANYWHERE],
            ),
            out_shape=out_shapes + [jax.ShapeDtypeStruct(through.shape, through.dtype)],
            input_output_aliases={inputs: len(out_shapes)},
            cost_estimate=SMALL,
            compiler_params=params(),
        )(self.place, self.act, self.delta, *extra, through)

    def start(self, through):
        half = SHARES // 2
        block = (1, SHARE_ROWS, D)
        send, through = self.call(
            grad_send_kernel,
            lambda i: i + half,
            [],
            [],
            [pl.BlockSpec(block, lambda i, m: (i, 0, 0))],
            [jax.ShapeDtypeStruct((half, SHARE_ROWS, D), BFLOAT)],
            through,
        )
        self.flight = self.move(send, 0)
        return through

    def move(self, value, stage):
        axis, bit = self.stages[stage]
        return swap(value, axis, bit)

    def second(self, through):
        quarter = SHARES // 4
        block = (1, SHARE_ROWS, D)
        position = lambda i: i ^ quarter
        send, self.keep, through = self.call(
            grad_keep_kernel,
            position,
            [self.flight],
            [pl.BlockSpec(block, lambda i, m: (position(i), 0, 0))],
            [
                pl.BlockSpec(block, lambda i, m: (jnp.minimum(i, quarter - 1), 0, 0)),
                pl.BlockSpec(block, lambda i, m: (jnp.maximum(i - quarter, 0), 0, 0)),
            ],
            [jax.ShapeDtypeStruct((quarter, SHARE_ROWS, D), BFLOAT)] * 2,
            through,
        )
        self.flight = self.move(send, 1)
        self.state = 0
        return through

    works = ("halve", "halve", "add", "join", "join", "pass")
    own_state = 3
    offload = natural = False

    def advanced(self, outs):
        work = self.works[self.state]
        self.state += 1
        if work == "pass":
            self.keep, self.flight = outs
            self.pieces = [self.keep, self.flight]
            self.pieces += [self.move(piece, 0) for piece in self.pieces]
            return
        self.keep = outs[0]
        if not (self.offload and self.state == self.own_state):
            self.flight = self.onward(self.state, outs[-1])

    def onward(self, state, value):
        return self.move(value, (None, 2, 3, 3, 2, 1)[state])

    def done(self):
        return self.state == len(self.works)


class CrossGradSum(GradSum):
    works = ("halve", "halve", "add", "take", "join", "join", "pass")
    own_state = 4

    def onward(self, state, value):
        if state == 3:
            return self.cross(value)
        return self.move(value, (None, 2, 3, None, 3, 2, 1)[state])

    def cross(self, value):
        rows, cols = lax.axis_size("row"), lax.axis_size("col")
        pairs = []
        for x in range(2):
            for r in range(rows):
                for z in range(cols):
                    stays = r % 2 == x
                    to_x, to_r = (x, r) if stays else (1 - x, r ^ 1)
                    pairs.append(((x * rows + r) * cols + z, (to_x * rows + to_r) * cols + z))
        return lax.ppermute(value, ("batch", "row", "col"), pairs)


class Gathered:
    def __init__(self, sums):
        self.sums = sums

    def gather(self):
        self.collect(jnp.concatenate([one.keep for one in self.sums]))

    def collect(self, shares):
        whole = lax.all_gather(shares, GRID_AXES)
        for slot, one in enumerate(self.sums):
            one.whole, one.slot = whole, slot

    @staticmethod
    def finish(sums, kinds, previous, layer, shapes, through):
        block = (1, SHARE_ROWS, D)
        scalar = lax.axis_index("batch").reshape(1).astype(jnp.int32)

        def source(one):
            def index(i, m):
                core, y, low, high = i // 8, i // 4 % 2, i // 2 % 2, i % 2
                device = i if one.natural else (y * 2 + core) * 4 + high * 2 + low
                return (device, one.slot, 0, 0)

            return pl.BlockSpec((None,) + block, index)

        natural = sums[0].natural

        def expand(i, m):
            core, y = (i // 4 % 2, i // 8) if natural else (i // 8, i // 4 % 2)
            own = jnp.where(core == m[0], m[0], 1 - m[0])
            return (layer, i % 4, own * 2 + y)

        indices = (
            lambda i, m: (layer, i, 0),
            expand,
            lambda i, m: (0, i // 4, jnp.minimum(i % 4, 2)),
            lambda i, m: (0, i // 4, 0),
        )
        blocks = (block, block, (LAYERS,) + block[1:], (LAYERS,) + block[1:])
        targets = [k for kind in kinds[:3] for k in ((0,), (1,), (2, 3))["ABC".index(kind)]]
        kept = [k for k in targets if previous and k in previous]
        earlier = [previous[k] for k in kept]
        count, outs, given = len(earlier), len(targets), len(sums)

        def body(m, *refs):
            where = dict(zip(targets, refs[-1 - outs : -1]))
            last = pl.program_id(0) % 4 == 3
            done = 0
            for kind, ref in zip(kinds, refs):
                if kind != "C":
                    where["AB".index(kind)][0] = ref[0].astype(FLOAT)
                    continue

                at, done = done, done + 1

                @pl.when(last)
                def _(ref=ref, at=at):
                    where[3][at] = ref[0].astype(FLOAT)

                @pl.when(jnp.logical_not(last))
                def _(ref=ref, at=at):
                    where[2][at] = ref[0].astype(FLOAT)

        *results, through = pl.pallas_call(
            body,
            grid_spec=pltpu.PrefetchScalarGridSpec(
                num_scalar_prefetch=1,
                grid=(SHARES,),
                in_specs=[source(one) for one in sums] + [ANYWHERE] * (count + 1),
                out_specs=[pl.BlockSpec(blocks[k], indices[k]) for k in targets] + [ANYWHERE],
            ),
            out_shape=[jax.ShapeDtypeStruct(shapes[k], FLOAT) for k in targets]
            + [jax.ShapeDtypeStruct(through.shape, through.dtype)],
            input_output_aliases={1 + given + j: targets.index(k) for j, k in enumerate(kept)}
            | {1 + given + count: outs},
            cost_estimate=SMALL,
            compiler_params=params(),
        )(scalar, *[one.whole for one in sums], *earlier, through)
        return dict(zip(targets, results)), through


class Scattered(Gathered):
    def __init__(self):
        self.sums, self.group, self.shares = [], [], []

    def add(self, one, through):
        slot, tokens, dim = len(self.group), one.act.shape[2], len(self.shares) % 2
        one.offload = one.natural = True
        earlier = [self.buffer] if slot else []
        self.sums.append(one)
        self.group.append(one)
        count = len(earlier)
        shape = (1, SHARES) if dim else (SHARES, 2)
        place = lambda j: (slot, j, 0, 0) if dim else (j, slot, 0, 0)
        block = (1, 2) if dim else (2, 1)
        cross = isinstance(one, CrossGradSum)

        def body(act, delta, *refs):
            value = product(act[0], delta[0]).astype(BFLOAT)
            for k in range(2):
                part = value[k * SHARE_ROWS : (k + 1) * SHARE_ROWS]
                refs[count + 1][(0, k) if dim else (k, 0)] = part

        self.buffer, through = pl.pallas_call(
            body,
            grid=(SHARES // 2,),
            in_specs=[
                pl.BlockSpec(
                    (1, 2 * SHARE_ROWS, tokens), lambda j: (0, j % 4 if cross else j, 0)
                ),
                pl.BlockSpec((1, tokens, D), lambda j: (0, 0, j // 4 if cross else 0)),
            ]
            + [ANYWHERE] * (count + 1),
            out_specs=[pl.BlockSpec(block + (SHARE_ROWS, D), place), ANYWHERE],
            out_shape=[
                jax.ShapeDtypeStruct(shape + (SHARE_ROWS, D), BFLOAT),
                jax.ShapeDtypeStruct(through.shape, through.dtype),
            ],
            input_output_aliases={2 + k: k for k in range(count)} | {2 + count: 1},
            cost_estimate=SMALL,
            compiler_params=params(),
        )(one.act, one.delta, *earlier, through)
        return through

    def reduce(self):
        dim = len(self.shares) % 2
        summed = lax.psum_scatter(self.buffer, GRID_AXES, scatter_dimension=dim, tiled=True)
        self.shares.append(summed.reshape(-1, SHARE_ROWS, D))
        self.group = []

    def gather(self, after):
        shares = passed_by(self.shares, [after])
        shares = [part[slot] for part in shares for slot in range(part.shape[0])]
        for slot, one in enumerate(self.sums):
            if isinstance(one, CrossGradSum):
                shares[slot] = one.cross(shares[slot])
        self.collect(jnp.stack(shares))


class SmallSum:
    works = ("sum",) * 4

    def __init__(self, value):
        self.value, self.state = value, 0

    def start(self, through):
        self.keep, self.flight = self.value, self.move(0, self.value)
        return through

    def move(self, stage, value):
        return swap(value, *STAGES[stage])

    def advanced(self, outs):
        self.state += 1
        (self.keep,) = outs
        self.flight = None if self.done() else self.move(self.state, self.keep)

    def done(self):
        return self.state == len(self.works)


def tick_kernel(*refs, works):
    at, out = 0, 2 * len(works)
    for work in works:
        keep, flight = refs[at], refs[at + 1]
        at += 2
        count = keep.shape[0]
        if work == "sum":
            refs[out][...] = keep[...] + flight[...]
            out += 1
            continue
        if work == "join":
            refs[out][:count] = keep[...]
            refs[out][count:] = flight[...]
            out += 1
            continue
        for row in range(count):
            value = (keep[row].astype(FLOAT) + flight[row].astype(FLOAT)).astype(BFLOAT)
            if work == "add":
                refs[out][row] = value
            elif row < count // 2:
                refs[out][row] = value
            else:
                refs[out + 1][row - count // 2] = value
        out += 1 if work == "add" else 2


def tick(sums, through):
    if not sums:
        return through
    light = ("pass", "take")
    working = [one for one in sums if one.works[one.state] not in light]
    passing = [one for one in sums if one.works[one.state] in light]
    operands, shapes, counts, works = [], [], [], []
    for one in working:
        operands += [one.keep, one.flight]
        work, count = one.works[one.state], one.keep.shape[0]
        works.append(work)
        sizes = {"halve": [count // 2] * 2, "join": [2 * count]}.get(work, [count])
        counts.append(len(sizes))
        shapes += [
            jax.ShapeDtypeStruct((k,) + one.keep.shape[1:], one.keep.dtype) for k in sizes
        ]
    kept = lambda one: [one.flight] if one.works[one.state] == "take" else [one.keep, one.flight]
    passed = [value for one in passing for value in kept(one)] + [through]

    def body(*refs):
        ins, outs = refs[: len(operands)], refs[len(operands) + len(passed) :]
        tick_kernel(*ins, *outs, works=works)

    outs = pl.pallas_call(
        body,
        in_specs=[WHOLE] * len(operands) + [ANYWHERE] * len(passed),
        out_specs=[WHOLE] * len(shapes) + [ANYWHERE] * len(passed),
        out_shape=shapes + [jax.ShapeDtypeStruct(v.shape, v.dtype) for v in passed],
        input_output_aliases={
            len(operands) + k: len(shapes) + k for k in range(len(passed))
        },
        cost_estimate=SMALL,
        compiler_params=params(),
    )(*operands, *passed)
    at = 0
    for one, count in zip(working, counts):
        one.advanced(outs[at : at + count])
        at += count
    for one in passing:
        count = len(kept(one))
        one.advanced(outs[at : at + count])
        at += count
    return outs[-1]


def sum_small(value):
    for axis, bit in STAGES:
        value = value + swap(value, axis, bit)
    return value


def shrink_sum(act, outer_low):
    return GradSum(act[None], outer_low[None], lambda s: (0, s, 0), lambda s: (0, 0, 0), STAGES)


def expand_sum(act, inner_low):
    return CrossGradSum(
        act[None],
        inner_low[None],
        lambda s: (0, s // 8 * 4 + s % 4, 0),
        lambda s: (0, 0, s // 4 % 2),
        STAGES,
    )


def mixer_delta(own, other, branch, branch_other, places, width, size):
    tokens = own.shape[0]
    block = tokens // 4
    heads = width // HD

    def body(places, mine, theirs, low, low_other, out, logits):
        first = places[0] == 0
        values = mine[...].astype(FLOAT), theirs[...].astype(FLOAT)
        left = jnp.where(first, values[0], values[1])
        right = jnp.where(first, values[1], values[0])
        for j in range(3):
            part = slice(j * size, j * size + width)
            out[:, j * D : (j + 1) * D] = jnp.concatenate(
                [left[:, part], right[:, part]], axis=1
            ).astype(BFLOAT)
        half = pl.program_id(0) < 2

        @pl.when(half)
        def _():
            out[:, 3 * D :] = low[...]

        @pl.when(jnp.logical_not(half))
        def _():
            out[:, 3 * D :] = low_other[...]

        part = slice(width, width + heads)
        rest = jnp.zeros((block, LANES - 2 * heads), FLOAT)
        logits[...] = jnp.concatenate([left[:, part], right[:, part], rest], axis=1).astype(BFLOAT)

    return pl.pallas_call(
        body,
        grid_spec=pltpu.PrefetchScalarGridSpec(
            num_scalar_prefetch=1,
            grid=(4,),
            in_specs=[
                pl.BlockSpec((block, 3 * size), lambda i, m: (i, 0)),
                pl.BlockSpec((block, 3 * size), lambda i, m: (i ^ 2, 0)),
                pl.BlockSpec((block, D), lambda i, m: (jnp.minimum(i, 1), 0)),
                pl.BlockSpec((block, D), lambda i, m: (jnp.maximum(i - 2, 0), 0)),
            ],
            out_specs=[
                pl.BlockSpec((block, 4 * D), lambda i, m: (i, 0)),
                pl.BlockSpec((block, LANES), lambda i, m: (i, 0)),
            ],
        ),
        out_shape=[
            jax.ShapeDtypeStruct((tokens, 4 * D), BFLOAT),
            jax.ShapeDtypeStruct((tokens, LANES), BFLOAT),
        ],
        cost_estimate=SMALL,
        compiler_params=params(),
    )(places, own, other, branch, branch_other)


def mixer_sum(act, delta_project, branch, branch_other, places, width, size):
    delta, logits = mixer_delta(
        delta_project, swap(delta_project), branch, branch_other, places, width, size
    )
    return (
        GradSum(
            act,
            delta[None],
            lambda s: (jnp.where(s % 4 == 3, 1, 0), s // 4, 0),
            lambda s: (0, 0, s % 4),
            STAGES,
        ),
        logits,
    )


ITEMS = 2
ANYWHERE = pl.BlockSpec(memory_space=pl.ANY)
WHOLE = pl.BlockSpec(memory_space=pltpu.VMEM)


def call(body, shapes, arrays, places=None, held=(), after=(), scratch=()):
    first = 0 if places is None else 1
    count, kept, tied = len(arrays), len(held), len(after)

    def whole(*refs):
        ins = refs[first : first + count]
        far = refs[first + count : first + count + kept]
        at = first + count + kept + tied
        outs = refs[at : at + len(shapes)]
        body(refs[0] if first else None, ins, far, outs, refs[at + len(shapes) :])

    return pl.pallas_call(
        whole,
        in_specs=[pl.BlockSpec(memory_space=pltpu.SMEM)] * first
        + [WHOLE] * count
        + [ANYWHERE] * (kept + tied),
        out_specs=[WHOLE] * len(shapes),
        out_shape=[jax.ShapeDtypeStruct(*shape) for shape in shapes],
        scratch_shapes=list(scratch),
        cost_estimate=SMALL,
        compiler_params=params(),
    )(*([] if places is None else [places]), *arrays, *held, *after)


def edge_shapes(tile):
    rows, cols = tile
    sizes = [cols, cols, rows, rows]
    return [((ITEMS, size, D), BFLOAT) for size in sizes]


def put_edges(value, item, refs, tile):
    rows, cols = tile
    lines = [value[0], value[rows - 1]]
    for at in (0, cols - 1):
        lines.append(jnp.concatenate([value[r][at : at + 1] for r in range(rows)], axis=0))
    for ref, line in zip(refs, lines):
        ref[item] = line.astype(BFLOAT)


def halo_edges(edges):
    rows, cols = lax.axis_size("row"), lax.axis_size("col")
    first_row, last_row, first_col, last_col = edges
    top = lax.ppermute(last_row, "row", [(i, i + 1) for i in range(rows - 1)])
    bottom = lax.ppermute(first_row, "row", [(i + 1, i) for i in range(rows - 1)])
    to_right = jnp.concatenate([top[:, -1:], last_col, bottom[:, -1:]], axis=1)
    to_left = jnp.concatenate([top[:, :1], first_col, bottom[:, :1]], axis=1)
    left = lax.ppermute(to_right, "col", [(i, i + 1) for i in range(cols - 1)])
    right = lax.ppermute(to_left, "col", [(i + 1, i) for i in range(cols - 1)])
    return top, bottom, left, right


def modulated(value, mod, shift, scale):
    normal, inverse = normalize(value)
    return normal * (1.0 + mod[scale : scale + 1]) + mod[shift : shift + 1]


def enter_first(tokens, mod, tile):
    cells = (ITEMS,) + tile + (D,)

    def body(_, ins, far, outs, scratch):
        for i in range(ITEMS):
            hidden = modulated(ins[0][i].astype(FLOAT), ins[1][i], 0, 1).reshape(cells[1:])
            outs[0][i] = hidden.astype(BFLOAT)
            put_edges(hidden, i, outs[1:], tile)

    hidden, *edges = call(body, [(cells, BFLOAT)] + edge_shapes(tile), [tokens, mod])
    return hidden, edges


def enter_next(middle, own, received, mod_before, mod, tile):
    cells = (ITEMS,) + tile + (D,)
    count = middle.shape[1]

    def body(_, ins, far, outs, scratch):
        for i in range(ITEMS):
            at = slice(i * count, (i + 1) * count)
            outer = ins[1][at] + ins[2][at].astype(FLOAT)
            outs[1][i] = outer
            value = ins[0][i] + ins[3][i][5:6] * outer
            outs[0][i] = value
            hidden = modulated(value, ins[4][i], 0, 1).reshape(cells[1:])
            outs[2][i] = hidden.astype(BFLOAT)
            put_edges(hidden, i, outs[3:], tile)

    shapes = [(middle.shape, FLOAT), (middle.shape, FLOAT), (cells, BFLOAT)] + edge_shapes(tile)
    value, outer, hidden, *edges = call(body, shapes, [middle, own, received, mod_before, mod])
    return value, outer, hidden, edges


def leave(middle, own, received, mod):
    count = middle.shape[1]

    def body(_, ins, far, outs, scratch):
        for i in range(ITEMS):
            at = slice(i * count, (i + 1) * count)
            outer = ins[1][at] + ins[2][at].astype(FLOAT)
            outs[1][i] = outer
            outs[0][i] = (ins[0][i] + ins[3][i][5:6] * outer).astype(BFLOAT)

    return call(
        body, [(middle.shape, BFLOAT), (middle.shape, FLOAT)], [middle, own, received, mod]
    )


def gather_weight(far, scratch, sems, places, own):
    batch, quarter = places[0], places[1]
    rows = own.shape[0]
    size = rows // 4
    base = (1 - batch) * rows
    parts = [(own, batch * rows, rows)]
    for k in range(4):
        parts.append((far[k], base + (quarter ^ k) * size, size))
    copies = []
    for k, (source, start, count) in enumerate(parts):
        target = scratch.at[pl.ds(pl.multiple_of(start, 16), count)]
        copy = pltpu.make_async_copy(source, target, sems.at[k])
        copy.start()
        copies.append(copy)
    return copies


def split_logit(block, start, heads):
    lane = lax.broadcasted_iota(jnp.int32, block.shape, 1)
    here = (lane >= start) & (lane < start + heads)
    high = block.astype(BFLOAT).astype(FLOAT)
    rest = jnp.where(here, block - high, 0.0)
    middle = rest.astype(BFLOAT).astype(FLOAT)
    low = rest - middle
    return (
        jnp.where(here, high, block) + pltpu.roll(middle, heads, 1) + pltpu.roll(low, 2 * heads, 1)
    )


def project_call(own, other, weight, bias, places, cells, width):
    size = weight[0].shape[1] // 3
    block = width // LANES * LANES
    total = 2 * own.shape[0]
    count = total // cells

    def body(places, ins, far, outs, scratch):
        whole, joined, result, sems = scratch
        copies = gather_weight(far[1:], whole, sems, places, far[0])
        joined[: total // 2] = ins[0][...]
        joined[total // 2 :] = ins[1][...]
        for copy in copies:
            copy.wait()
        for part in range(3):
            columns = slice(part * size, (part + 1) * size)
            value = dot(joined[...], whole[:, columns])
            if part == 0:
                last = split_logit(
                    value[:, block : block + LANES] + ins[2][...], width - block, width // HD
                )
                result[:, :block] = value[:, :block].astype(BFLOAT)
                result[:, block : block + LANES] = last.astype(BFLOAT)
            else:
                result[:, columns] = value.astype(BFLOAT)
        for k in range(count):
            start = pl.multiple_of((places[2] ^ k) * cells, cells)
            outs[k][0] = result[pl.ds(start, cells)]

    return call(
        body,
        [((1, cells, 3 * size), BFLOAT)] * count,
        [own, other, bias],
        places,
        weight,
        scratch=[
            pltpu.VMEM((D, 3 * size), BFLOAT),
            pltpu.VMEM((total, D), BFLOAT),
            pltpu.VMEM((total, 3 * size), BFLOAT),
            pltpu.SemaphoreType.DMA((5,)),
        ],
    )


def halves_out(value, outs, columns, items_here):
    outs[0][:, columns] = value[:items_here]
    outs[1][:, columns] = value[items_here:].astype(BFLOAT)


COLUMNS = 384


def attend_out_call(blocks, weight, layer, places, cells, width):
    count = len(blocks)
    total = count * cells

    def body(places, ins, far, outs, scratch):
        whole, sems = scratch
        copy = pltpu.make_async_copy(far[0].at[layer], whole, sems.at[0])
        copy.start()
        for k in range(count):
            start = pl.multiple_of((places[2] ^ k) * cells, cells)
            outs[2][pl.ds(start, cells)] = ins[k][0]
        copy.wait()
        for at in range(0, D, COLUMNS):
            columns = slice(at, at + COLUMNS)
            halves_out(dot(outs[2][...], whole[:, columns]), outs, columns, total // 2)

    return call(
        body,
        [((total // 2, D), FLOAT), ((total // 2, D), BFLOAT), ((total, width), BFLOAT)],
        blocks,
        places,
        [weight],
        scratch=[pltpu.VMEM((width, D), BFLOAT), pltpu.SemaphoreType.DMA((1,))],
    )


def middle_call(tokens, own, received, mod):
    count = tokens.shape[1]

    def body(_, ins, far, outs, scratch):
        for i in range(ITEMS):
            at = slice(i * count, (i + 1) * count)
            branch = ins[1][at] + ins[2][at].astype(FLOAT)
            outs[0][i] = branch
            middle = ins[0][i].astype(FLOAT) + ins[3][i][2:3] * branch
            outs[1][i] = middle
            outs[2][at] = modulated(middle, ins[3][i], 3, 4).astype(BFLOAT)

    shape = tokens.shape
    return call(
        body,
        [(shape, FLOAT), (shape, FLOAT), ((ITEMS * count, D), BFLOAT)],
        [tokens, own, received, mod],
    )


def feed_call(own, other, expand, shrink, layer, places):
    total = 2 * own.shape[0]
    inner = shrink.shape[1]
    rows = expand[0].shape[1]
    tile = 256

    def body(places, ins, far, outs, scratch):
        wide, back, joined, sems = scratch
        start = pl.multiple_of(places[0] * inner, LANES)
        source = far[0].at[layer, :, pl.ds(start, inner)]
        copies = gather_weight(far[1:5], wide, sems, places, source)
        last = pltpu.make_async_copy(far[5].at[layer], back, sems.at[5])
        last.start()
        joined[: total // 2] = ins[0][...]
        joined[total // 2 :] = ins[1][...]
        for copy in copies:
            copy.wait()
        for at in range(0, inner, tile):
            columns = slice(at, at + tile)
            value = dot(joined[...], wide[:, columns])
            outs[2][:, columns] = value
            outs[3][:, columns] = gelu(value).astype(BFLOAT)
        last.wait()
        for at in range(0, D, COLUMNS):
            columns = slice(at, at + COLUMNS)
            halves_out(dot(outs[3][...], back[:, columns]), outs, columns, total // 2)

    return call(
        body,
        [
            ((total // 2, D), FLOAT),
            ((total // 2, D), BFLOAT),
            ((total, inner), FLOAT),
            ((total, inner), BFLOAT),
        ],
        [own, other],
        places,
        list(expand) + [shrink],
        scratch=[
            pltpu.VMEM((2 * rows, inner), BFLOAT),
            pltpu.VMEM((inner, D), BFLOAT),
            pltpu.VMEM((total, D), BFLOAT),
            pltpu.SemaphoreType.DMA((6,)),
        ],
    )


def turn_call(mixed, mixed_other, attend, second, second_other, active, places, through):
    tokens = attend.shape[0]
    width = attend.shape[1]
    padded = padded_width(width)
    inner = active.shape[1]
    half = mixed.shape[0]

    def turn(value):
        return jnp.transpose(value.astype(FLOAT)).astype(BFLOAT)

    def body(places, one, two, three, four, five, six, _, mixer, wide, long, __):
        first = places[0] == 0
        for ref, at in ((one, 0), (two, half)):
            value = turn(ref[...])
            mixer[0, :, at : at + half] = jnp.where(first, value[:width], value[width:])
        blank = jnp.zeros((tokens, padded - width), FLOAT)
        value = jnp.concatenate([three[...].astype(FLOAT), blank], axis=1)
        mixer[1] = jnp.transpose(value)[:width].astype(BFLOAT)
        wide[:, :half] = turn(four[...])
        wide[:, half:] = turn(five[...])
        for at in range(0, inner, 256):
            long[at : at + 256] = turn(six[:, at : at + 256])

    return pl.pallas_call(
        body,
        in_specs=[pl.BlockSpec(memory_space=pltpu.SMEM)] + [WHOLE] * 6 + [ANYWHERE],
        out_specs=[WHOLE] * 3 + [ANYWHERE],
        out_shape=[
            jax.ShapeDtypeStruct((2, width, tokens), BFLOAT),
            jax.ShapeDtypeStruct((D, tokens), BFLOAT),
            jax.ShapeDtypeStruct((inner, tokens), BFLOAT),
            jax.ShapeDtypeStruct(through.shape, through.dtype),
        ],
        input_output_aliases={7: 3},
        cost_estimate=SMALL,
        compiler_params=params(),
    )(places, mixed, mixed_other, attend, second, second_other, active, through)


def feed_back_call(own, other, inner_value, expand, shrink, layer, places):
    total = 2 * own.shape[0]
    inner = shrink.shape[1]
    rows = expand[0].shape[1]
    tile = 256

    def body(places, ins, far, outs, scratch):
        wide, back, joined, sems = scratch
        last = pltpu.make_async_copy(far[5].at[layer], back, sems.at[5])
        last.start()
        start = pl.multiple_of(places[0] * inner, LANES)
        source = far[0].at[layer, :, pl.ds(start, inner)]
        copies = gather_weight(far[1:5], wide, sems, places, source)
        joined[: total // 2] = ins[0][...]
        joined[total // 2 :] = ins[1][...]
        last.wait()
        for at in range(0, inner, tile):
            columns = slice(at, at + tile)
            value = dot(joined[...], back[at : at + tile], ((1,), (1,)))
            outs[2][:, columns] = (value * gelu_slope(ins[2][:, columns])).astype(BFLOAT)
        for copy in copies:
            copy.wait()
        for at in range(0, D, COLUMNS):
            columns = slice(at, at + COLUMNS)
            value = dot(outs[2][...], wide[at : at + COLUMNS], ((1,), (1,)))
            halves_out(value, outs, columns, total // 2)

    return call(
        body,
        [((total // 2, D), FLOAT), ((total // 2, D), BFLOAT), ((total, inner), BFLOAT)],
        [own, other, inner_value],
        places,
        list(expand) + [shrink],
        scratch=[
            pltpu.VMEM((2 * rows, inner), BFLOAT),
            pltpu.VMEM((inner, D), BFLOAT),
            pltpu.VMEM((total, D), BFLOAT),
            pltpu.SemaphoreType.DMA((6,)),
        ],
    )


def middle_back_call(delta, own, received, middle, branch, outer, mod):
    count = middle.shape[1]
    over = lambda v: jnp.sum(v, axis=0, keepdims=True)

    def body(_, ins, far, outs, scratch):
        for i in range(ITEMS):
            at = slice(i * count, (i + 1) * count)
            here = ins[0][i].astype(FLOAT)
            mod_here = ins[6][i]
            outs[2][i, 3:4] = over(here * ins[5][i])
            second = ins[1][at] + ins[2][at].astype(FLOAT)
            normal, inverse = normalize(ins[3][i])
            outs[2][i, 1:2] = over(second)
            outs[2][i, 2:3] = over(second * normal)
            total = here + normalize_back(second * (1.0 + mod_here[4:5]), normal, inverse)
            outs[0][i] = total
            outs[2][i, 0:1] = over(total * ins[4][i])
            outs[1][at] = (mod_here[2:3] * total).astype(BFLOAT)

    return call(
        body,
        [(middle.shape, FLOAT), ((ITEMS * count, D), BFLOAT), ((ITEMS, 4, D), FLOAT)],
        [delta, own, received, middle, branch, outer, mod],
    )


def attend_back_call(own, other, weight, layer, places, cells, width):
    total = 2 * own.shape[0]
    count = total // cells

    def body(places, ins, far, outs, scratch):
        whole, joined, result, sems = scratch
        copy = pltpu.make_async_copy(far[0].at[layer], whole, sems.at[0])
        copy.start()
        joined[: total // 2] = ins[0][...]
        joined[total // 2 :] = ins[1][...]
        copy.wait()
        result[...] = dot(joined[...], whole[...], ((1,), (1,))).astype(BFLOAT)
        for k in range(count):
            start = pl.multiple_of((places[2] ^ k) * cells, cells)
            outs[k][0] = result[pl.ds(start, cells)]

    return call(
        body,
        [((1, cells, width), BFLOAT)] * count,
        [own, other],
        places,
        [weight],
        scratch=[
            pltpu.VMEM((width, D), BFLOAT),
            pltpu.VMEM((total, D), BFLOAT),
            pltpu.VMEM((total, width), BFLOAT),
            pltpu.SemaphoreType.DMA((1,)),
        ],
    )


def project_back_call(blocks, weight, places, cells, width):
    count = len(blocks)
    total = count * cells
    wide = blocks[0].shape[2]

    def body(places, ins, far, outs, scratch):
        whole, sems = scratch
        copies = gather_weight(far[1:], whole, sems, places, far[0])
        for k in range(count):
            start = pl.multiple_of((places[2] ^ k) * cells, cells)
            outs[2][pl.ds(start, cells)] = ins[k][0]
        at = width // LANES * LANES
        logits = outs[2][:, at : at + LANES].astype(FLOAT)
        outs[3][...] = jnp.sum(logits, axis=0, keepdims=True)
        for copy in copies:
            copy.wait()
        for at in range(0, D, COLUMNS):
            columns = slice(at, at + COLUMNS)
            value = dot(outs[2][...], whole[at : at + COLUMNS], ((1,), (1,)))
            halves_out(value, outs, columns, total // 2)

    return call(
        body,
        [
            ((total // 2, D), FLOAT),
            ((total // 2, D), BFLOAT),
            ((total, wide), BFLOAT),
            ((1, LANES), FLOAT),
        ],
        blocks,
        places,
        weight,
        scratch=[pltpu.VMEM((D, wide), BFLOAT), pltpu.SemaphoreType.DMA((5,))],
    )


def conv_delta_call(own, received, convolved, tile):
    cells = convolved.shape
    count = tile[0] * tile[1]

    def body(_, ins, far, outs, scratch):
        for i in range(ITEMS):
            at = slice(i * count, (i + 1) * count)
            delta = (ins[0][at] + ins[1][at].astype(FLOAT)).reshape(cells[1:])
            value = ins[2][i]
            gate = jax.nn.sigmoid(value)
            delta = delta * gate * (1.0 + value * (1.0 - gate))
            outs[0][i] = delta.astype(BFLOAT)
            put_edges(delta, i, outs[1:], tile)

    delta, *edges = call(
        body, [(cells, BFLOAT)] + edge_shapes(tile), [own, received, convolved]
    )
    return delta, edges


def enter_back_call(delta_hidden, tokens, delta_middle, mod, mod_before):
    count = tokens.shape[1]
    over = lambda v: jnp.sum(v, axis=0, keepdims=True)
    lower = mod_before is not None

    def body(_, ins, far, outs, scratch):
        for i in range(ITEMS):
            at = slice(i * count, (i + 1) * count)
            here = ins[0][i].reshape(count, D)
            normal, inverse = normalize(ins[1][i].astype(FLOAT))
            outs[0][i, 0:1] = over(here)
            outs[0][i, 1:2] = over(here * normal)
            total = ins[2][i] + normalize_back(here * (1.0 + ins[3][i][1:2]), normal, inverse)
            if lower:
                outs[2][i] = total
                outs[1][at] = (ins[4][i][5:6] * total).astype(BFLOAT)
            else:
                outs[1][at] = total.astype(BFLOAT)

    shapes = [((ITEMS, 2, D), FLOAT), ((ITEMS * count, D), BFLOAT)]
    arrays = [delta_hidden, tokens, delta_middle, mod]
    if lower:
        shapes.append((tokens.shape, FLOAT))
        arrays.append(mod_before)
    return call(body, shapes, arrays)


def pack_kernel(places, qkv, decay, own, other, *, width):
    heads = width // HD
    size = padded_width(width + 3 * heads)
    value, extra = qkv[0].astype(FLOAT), decay[0].astype(FLOAT)
    rows = value.shape[0]
    pieces = []
    for group in range(2):
        parts = []
        for j in range(3):
            start = j * D + group * width
            parts.append(value[:, start : start + width])
            filled = width
            if j == 0:
                parts.append(extra[:, group * heads : (group + 1) * heads])
                filled += heads
            parts.append(jnp.zeros((rows, size - filled), FLOAT))
        pieces.append(jnp.concatenate(parts, axis=1).astype(BFLOAT))
    first = places[0] == 0
    own[...] = jnp.where(first, pieces[0], pieces[1])
    other[...] = jnp.where(first, pieces[1], pieces[0])


def pack_call(qkv, decay, layer, places, width):
    rows = qkv.shape[1]
    size = padded_width(width + 3 * (width // HD))

    def body(*refs):
        pack_kernel(*refs, width=width)

    out = pl.BlockSpec((SHARE_ROWS, 3 * size), lambda i, m: (i, 0))
    return pl.pallas_call(
        body,
        grid_spec=pltpu.PrefetchScalarGridSpec(
            num_scalar_prefetch=1,
            grid=(rows // SHARE_ROWS,),
            in_specs=[
                pl.BlockSpec((1, SHARE_ROWS, qkv.shape[2]), lambda i, m: (layer, i, 0)),
                pl.BlockSpec((1, SHARE_ROWS, decay.shape[2]), lambda i, m: (layer, i, 0)),
            ],
            out_specs=[out, out],
        ),
        out_shape=[jax.ShapeDtypeStruct((rows, 3 * size), BFLOAT)] * 2,
        cost_estimate=SMALL,
        compiler_params=params(),
    )(places, qkv, decay)


def passed_by(values, after):
    count = len(values)
    return pl.pallas_call(
        lambda *refs: None,
        in_specs=[ANYWHERE] * (count + len(after)),
        out_specs=[ANYWHERE] * count,
        out_shape=[jax.ShapeDtypeStruct(v.shape, v.dtype) for v in values],
        input_output_aliases={k: k for k in range(count)},
        cost_estimate=SMALL,
        compiler_params=params(),
    )(*values, *after)


def lines_swapped(blocks, axis):
    return [blocks[0]] + [swap(blocks[k], axis, k) for k in range(1, len(blocks))]


class Pair:
    def __init__(self, args, taps, tile):
        self.args, self.taps, self.tile = args, taps, tile
        self.modulations = [None] * LAYERS
        self.cells = tile[0] * tile[1]
        self.width = args["proj"].shape[1]
        self.heads = self.width // HD
        self.size = padded_width(self.width + 3 * self.heads)
        batch, row = lax.axis_index("batch"), lax.axis_index("row")
        quarter = row % 2 * 2 + row // 2
        self.places = [
            jnp.stack([batch, quarter, lax.axis_index(axis)]).astype(jnp.int32)
            for axis in ("col", "row")
        ]
        self.qkv, self.expand, self.bias = [], [], []
        self.pieces = {}
        self.quarter, self.batch = quarter, batch
        self.modulate()
        for layer in range(LAYERS):
            self.prepare(layer)
        for stage in range(3):
            self.fetch("qkv", 0, stage, [])

    def prepare(self, layer):
        args = self.args
        own, other = pack_call(args["qkv"], args["decay"], layer, self.places[0], self.width)
        part = own.shape[0] // 4
        self.pieces["qkv", layer] = lax.dynamic_slice_in_dim(other, self.quarter * part, part, 0)
        self.qkv.append([own])
        inner = args["shrink"].shape[1]
        piece = lax.dynamic_slice(
            args["expand"],
            (layer, self.quarter * part, (1 - self.batch) * inner),
            (1, part, inner),
        )
        self.pieces["expand", layer] = piece[0]
        self.expand.append([args["expand"]])
        start = self.width - self.width // LANES * LANES
        self.bias.append(
            jnp.pad(
                args["decay_bias"][layer].astype(FLOAT)[None],
                ((0, 0), (start, LANES - start - self.heads)),
            )
        )

    def modulate(self):
        cond = self.args["cond"]
        partial = jnp.stack(
            [
                jnp.dot(cond, self.args["ada"][layer], preferred_element_type=FLOAT)
                for layer in range(LAYERS)
            ],
            axis=1,
        )
        total = partial[:ITEMS] + swap(partial[ITEMS:])
        for layer in range(LAYERS):
            value = total[:, layer] + self.args["ada_bias"][layer]
            self.modulations[layer] = value.reshape(ITEMS, 6, D)

    def fetch(self, name, layer, stage, after):
        held = self.pieces[name, layer]
        if stage == 0:
            if after:
                (held,) = passed_by([held], after)
            self.pieces[name, layer] = [swap(held)]
        elif stage == 1:
            if after:
                held = passed_by(held, after)
            self.pieces[name, layer] = [held[0], swap(held[0], "row", 2)]
        else:
            if after:
                held = passed_by(held, after)
            into = self.qkv if name == "qkv" else self.expand
            into[layer] += list(held) + [swap(part, "row", 1) for part in held]

    def axis(self, layer):
        return "col" if layer % 2 == 0 else "row"

    def scan(self, kernel, layer, inputs, out_width):
        place = self.places[layer % 2][2]
        rows, cols = self.tile
        return scan_call(
            kernel, place, inputs, out_width, rows, cols, layer % 2 == 0, self.width
        )

    def forward(self, layer, hidden, edges, tokens):
        places, axis = self.places[layer % 2], self.axis(layer)
        mod = self.modulations[layer]
        sides = halo_edges(edges)
        convolved, mixed = conv_forward(hidden, sides, self.taps[layer])
        mixed = mixed.reshape(-1, D)
        mixed_other = swap(mixed)
        if layer == 0:
            self.fetch("expand", 0, 0, [hidden])
            self.fetch("expand", 0, 1, [mixed])
        else:
            self.fetch("expand", 1, 1, [mixed])
        parts = project_call(
            mixed, mixed_other, self.qkv[layer], self.bias[layer], places, self.cells, self.width
        )
        parts = list(parts)
        self.fetch("expand", layer, 2, [parts[0]])
        if layer + 1 < LAYERS:
            self.fetch("qkv", layer + 1, 0, [parts[0]])
        parts = lines_swapped(parts, axis)
        attends = self.scan(scan_forward_kernel, layer, parts, self.width)
        own, send, attend = attend_out_call(
            lines_swapped(attends, axis), self.args["proj"], layer, places, self.cells, self.width
        )
        if layer + 1 < LAYERS:
            self.fetch("qkv", layer + 1, 1, [own])
        branch, middle, second = middle_call(tokens, own, swap(send), mod)
        second_other = swap(second)
        if layer + 1 < LAYERS:
            self.fetch("qkv", layer + 1, 2, [second])
        own, send, inner, active = feed_call(
            second, second_other, self.expand[layer], self.args["shrink"], layer, places
        )
        if layer + 1 < LAYERS:
            self.fetch("expand", layer + 1, 0, [own])
        received = swap(send)
        mixer_act, second_act, active_act, own = turn_call(
            mixed, mixed_other, attend, second, second_other, active, places, own
        )
        saved = dict(
            tokens=tokens, hidden=hidden, sides=sides, convolved=convolved, parts=parts,
            branch=branch, middle=middle, inner=inner, mixer_act=mixer_act,
            second_act=second_act, active_act=active_act,
        )
        return middle, own, received, saved

    def backward(self, layer, delta, outer_low, outer_other, saved, tick):
        places, axis = self.places[layer % 2], self.axis(layer)
        mod = self.modulations[layer]
        both = lambda own, other: jnp.concatenate([own, other], axis=0)
        own, send, inner_low = feed_back_call(
            outer_low, outer_other, saved["inner"], self.expand[layer], self.args["shrink"],
            layer, places,
        )
        received = swap(send)
        shrink_pipe = shrink_sum(saved["active_act"], both(outer_low, outer_other))
        own = tick("P1", {"A": shrink_pipe}, own)
        delta_middle, branch_low, mod_b = middle_back_call(
            delta, own, received, saved["middle"], saved["branch"], saved["outer"], mod
        )
        branch_other = swap(branch_low)
        expand_pipe = expand_sum(saved["second_act"], inner_low)
        branch_low = tick("P2", {"B": expand_pipe}, branch_low)
        blocks = attend_back_call(
            branch_low, branch_other, self.args["proj"], layer, places, self.cells, self.width
        )
        sent = lines_swapped(blocks, axis)
        sent[0] = tick("P3", {}, sent[0])
        projects = self.scan(
            scan_backward_kernel, layer, list(saved["parts"]) + sent, 3 * self.size
        )
        sent = lines_swapped(projects, axis)
        sent[0] = tick("P4", {}, sent[0])
        own, send, delta_project, grad_bias = project_back_call(
            sent, self.qkv[layer], places, self.cells, self.width
        )
        received = swap(send)
        def mixer(after):
            (value,) = passed_by([delta_project], after)
            act = saved["mixer_act"]
            pipe, logits = mixer_sum(
                act, value, branch_low, branch_other, places, self.width, self.size
            )
            return pipe, dot(logits, act[0], ((0,), (1,)))[: 2 * self.heads]

        if not layer:
            mixer_pipe, grad_decay = mixer([])
        own = tick("P5", {}, own)
        delta_conv, edges = conv_delta_call(own, received, saved["convolved"], self.tile)
        delta_sides = halo_edges(edges)
        delta_conv = tick("P6", {}, delta_conv)
        if layer:
            mixer_pipe, grad_decay = mixer([delta_conv])
        top, bottom, left, right = delta_sides
        (left,) = passed_by([left], [right])
        left = tick("P8", {"C": mixer_pipe}, left)
        delta_sides = (top, bottom, left, right)
        delta_hidden, grad_taps = conv_backward(
            saved["hidden"], saved["sides"], delta_conv, delta_sides, self.taps[layer]
        )
        before = self.modulations[layer - 1] if layer else None
        mod_a, low, *rest = enter_back_call(
            delta_hidden, saved["tokens"], delta_middle, mod, before
        )
        low_other = swap(low) if rest else None

        small = SmallSum(join_smalls(mod_a, mod_b, grad_taps, grad_decay, grad_bias))
        low = tick("P7", {"S": small}, low)
        return rest[0] if rest else None, low, low_other


def pair_forward_backward(pair, tokens_in, cotangent, tick):
    tile = pair.tile
    shape = (ITEMS, pair.cells, D)
    tokens = tokens_in.reshape(shape)
    delta = cotangent.reshape(shape)
    hidden, edges = enter_first(tokens, pair.modulations[0], tile)
    stored = []
    for layer in range(LAYERS):
        middle, own, received, saved = pair.forward(layer, hidden, edges, tokens)
        stored.append(saved)
        mod = pair.modulations[layer]
        if layer + 1 < LAYERS:
            tokens, saved["outer"], hidden, edges = enter_next(
                middle, own, received, mod, pair.modulations[layer + 1], tile
            )
        else:
            block_out, saved["outer"] = leave(middle, own, received, mod)
    outer_low = (pair.modulations[-1][:, 5:6] * delta.astype(FLOAT)).astype(BFLOAT)
    outer_low = outer_low.reshape(-1, D)
    outer_other = swap(outer_low)
    for layer in reversed(range(LAYERS)):
        delta, outer_low, outer_other = pair.backward(
            layer, delta, outer_low, outer_other, stored[layer],
            lambda point, fresh, through, layer=layer: tick(layer, point, fresh, through),
        )
    return block_out, outer_low


def forward_layer(tokens, modulation, weights, layer, tile):
    taps, qkv, decay_bias, proj, expand, shrink = weights
    rows, cols = tile
    items, cells = tokens.shape[:2]
    width = proj.shape[0]
    heads = width // HD
    size = padded_width(width + 3 * heads)
    axis = "col" if layer % 2 == 0 else "row"
    mod = [modulation[:, k][:, None] for k in range(6)]
    normal, inverse = normalize(tokens)
    hidden = (normal * (1.0 + mod[1]) + mod[0]).astype(BFLOAT).reshape(items, rows, cols, D)
    sides = halo(hidden)
    convolved, mixed = conv_forward(hidden, sides, taps)
    mixed = gather_items(mixed.reshape(items, cells, D))
    project = matmul(mixed, qkv)
    logit = project[:, :, width : width + heads] + decay_bias.astype(FLOAT)
    high = logit.astype(BFLOAT)
    rest = logit - high.astype(FLOAT)
    middle_part = rest.astype(BFLOAT)
    low = (rest - middle_part.astype(FLOAT)).astype(BFLOAT)
    project = project.astype(BFLOAT)
    project = jnp.concatenate(
        [project[:, :, :width], high, middle_part, low, project[:, :, width + 3 * heads :]], axis=2
    )
    parts = lines_out(project, axis)
    place = lax.axis_index(axis)
    attends = scan_call(
        scan_forward_kernel, place, parts, width, rows, cols, layer % 2 == 0, width
    )
    attend = lines_back(attends, axis)
    branch = reduce_items(matmul(attend, proj))
    middle = tokens + mod[2] * branch
    normal2, inverse2 = normalize(middle)
    second = gather_items((normal2 * (1.0 + mod[4]) + mod[3]).astype(BFLOAT))
    inner = matmul(second, expand)
    active = gelu(inner).astype(BFLOAT)
    outer = reduce_items(matmul(active, shrink))
    result = middle + mod[5] * outer
    saved = (
        normal, inverse, hidden, sides, convolved, mixed, parts, attend, branch,
        normal2, inverse2, second, inner, active, outer,
    )
    return result, saved


def pipelined(width):
    shares = lax.axis_size("row") * lax.axis_size("col")
    square = lax.axis_size("row") == 4 and lax.axis_size("col") == 4
    return lax.axis_size("batch") == 2 and square and width == 4 * SHARE_ROWS and shares == SHARES


def backward_layer(delta, saved, modulation, weights, layer, tile):
    taps, qkv, decay_bias, proj, expand, shrink = weights
    (
        normal, inverse, hidden, sides, convolved, mixed, parts, attend, branch,
        normal2, inverse2, second, inner, active, outer,
    ) = saved
    rows, cols = tile
    items, cells = delta.shape[:2]
    width = proj.shape[0]
    heads = width // HD
    size = padded_width(width + 3 * heads)
    axis = "col" if layer % 2 == 0 else "row"
    mod = [modulation[:, k][:, None] for k in range(6)]
    over = lambda v: jnp.sum(v, axis=1)
    delta_gate2 = over(delta * outer)
    outer_low = gather_items((mod[5] * delta).astype(BFLOAT))
    grad_shrink = weight_grad(active, outer_low)
    inner_low = (matmul_back(outer_low, shrink) * gelu_slope(inner)).astype(BFLOAT)
    grad_expand = weight_grad(second, inner_low)
    delta_second = reduce_items(matmul_back(inner_low, expand))
    delta_shift2 = over(delta_second)
    delta_scale2 = over(delta_second * normal2)
    delta_middle = delta + normalize_back(delta_second * (1.0 + mod[4]), normal2, inverse2)
    delta_gate1 = over(delta_middle * branch)
    branch_low = gather_items((mod[2] * delta_middle).astype(BFLOAT))
    grad_proj = weight_grad(attend, branch_low)
    delta_attend = matmul_back(branch_low, proj).astype(BFLOAT)
    delta_parts = lines_out(delta_attend, axis)
    place = lax.axis_index(axis)
    projects = scan_call(
        scan_backward_kernel, place, list(parts) + delta_parts, 3 * size, rows, cols,
        layer % 2 == 0, width,
    )
    delta_project = lines_back(projects, axis)
    grad_qkv = weight_grad(mixed, delta_project)
    sums = (grad_shrink, grad_expand, grad_proj, grad_qkv)
    grad_decay_bias = jnp.sum(delta_project[:, :, width : width + heads].astype(FLOAT), axis=(0, 1))
    delta_mixed = reduce_items(matmul_back(delta_project, qkv)).reshape(convolved.shape)
    gate = jax.nn.sigmoid(convolved)
    delta_conv = (delta_mixed * gate * (1.0 + convolved * (1.0 - gate))).astype(BFLOAT)
    delta_sides = halo(delta_conv)
    delta_hidden, grad_taps = conv_backward(hidden, sides, delta_conv, delta_sides, taps)
    delta_hidden = delta_hidden.reshape(items, cells, D)
    delta_shift1 = over(delta_hidden)
    delta_scale1 = over(delta_hidden * normal)
    delta_tokens = delta_middle + normalize_back(delta_hidden * (1.0 + mod[1]), normal, inverse)
    delta_mod = jnp.stack(
        [delta_shift1, delta_scale1, delta_gate1, delta_shift2, delta_scale2, delta_gate2], axis=1
    )
    return delta_tokens, sums, (delta_mod, grad_taps, None, grad_decay_bias)


def sum_rows_here(grad):
    return lax.psum(grad.astype(BFLOAT), GRID_AXES).astype(FLOAT)


def sum_columns(grad):
    count = lax.axis_size("batch")
    low = grad.astype(BFLOAT).reshape((count, -1, grad.shape[1]))
    shares = lax.axis_size("row") * lax.axis_size("col")
    if count == 2 and low.shape[1] % shares == 0:
        share = lax.psum_scatter(low, GRID_AXES, scatter_dimension=1, tiled=True)
        place = lax.axis_index("batch")
        own = lax.dynamic_index_in_dim(share, place, 0, keepdims=False)
        other = swap(lax.dynamic_index_in_dim(share, 1 - place, 0, keepdims=False))
        both = jnp.stack([jnp.where(place == 0, own, other), jnp.where(place == 0, other, own)])
        return lax.all_gather(both, GRID_AXES, axis=1, tiled=True)
    total = lax.psum(low, GRID_AXES)
    return lax.all_to_all(total, "batch", 0, 0)


def ada_call(cond, mods, previous, layer, through):
    items, rows = cond.shape
    wide = mods.shape[1]
    block = 64
    previous = [] if previous is None else [previous]

    def body(columns, values, *refs):
        out = refs[-2]
        for at in range(0, wide, D):
            part = slice(at, at + D)
            total = columns[:, 0:1] * values[0:1, part]
            for item in range(1, items):
                total += columns[:, item : item + 1] * values[item : item + 1, part]
            out[0, :, part] = total

    count = len(previous)
    return pl.pallas_call(
        body,
        grid=(rows // block,),
        in_specs=[
            pl.BlockSpec((block, items), lambda i: (i, 0)),
            pl.BlockSpec((items, wide), lambda i: (0, 0)),
        ]
        + [ANYWHERE] * (count + 1),
        out_specs=[pl.BlockSpec((1, block, wide), lambda i: (layer, i, 0)), ANYWHERE],
        out_shape=[
            jax.ShapeDtypeStruct((LAYERS, rows, wide), FLOAT),
            jax.ShapeDtypeStruct(through.shape, through.dtype),
        ],
        input_output_aliases={2 + k: k for k in range(count)} | {2 + count: 1},
        cost_estimate=SMALL,
        compiler_params=params(),
    )(jnp.transpose(cond.astype(FLOAT)), mods, *previous, through)


SCHEDULE = {
    (1, "P1"): "aA1",
    (1, "P2"): "aB1rL1",
    (1, "P7"): "sC1",
    (0, "P1"): "kC1sA0",
    (0, "P3"): "gL1kA0",
    (0, "P4"): "sB0kB0",
    (0, "P5"): "tC1",
    (0, "P8"): "sC0kC0tC1tA0",
    (0, "P7"): "tC1tA0tB0sS0",
}
TAIL = (
    "tA0tB0tC0tS0",
    "tB0tC0tS0",
    "tB0tC0tS0gL0",
    "tS0",
    "mS1",
    "fAB1",
    "mS0",
    "fABC0",
)


SMALL_ROWS = 32


def join_smalls(mod_a, mod_b, grad_taps, grad_decay, grad_bias):
    heads = grad_decay.shape[0] // 2

    def body(_, ins, far, outs, scratch):
        out = outs[0]
        for i in range(ITEMS):
            out[6 * i : 6 * i + 2] = ins[0][i]
            out[6 * i + 2 : 6 * i + 6] = ins[1][i]
        out[12:21] = ins[2][...]
        out[21 : 21 + heads] = jnp.concatenate([ins[3][:heads], ins[3][heads:]], axis=1)
        bias = jnp.concatenate([ins[4][...], jnp.zeros((1, D - LANES), FLOAT)], axis=1)
        out[21 + heads : 22 + heads] = bias
        out[22 + heads :] = jnp.zeros((SMALL_ROWS - 22 - heads, D), FLOAT)

    return call(
        body, [((SMALL_ROWS, D), FLOAT)], [mod_a, mod_b, grad_taps, grad_decay, grad_bias]
    )[0]


def split_smalls(flat, items, heads, width):
    start = width - width // LANES * LANES
    decay = flat[21 : 21 + heads]
    return (
        flat[: items * 6].reshape(items, 6 * D),
        flat[12:21],
        jnp.concatenate([decay[:, :width], decay[:, width:]], axis=0),
        flat[21 + heads, start : start + heads],
    )


def general_forward_backward(
    tokens_in, cotangent, modulations, taps_all, qkv_weight, decay_weight, decay_bias,
    proj_weight, expand_weight, shrink_weight,
):
    count = lax.axis_size("batch")
    items, rows, cols = tokens_in.shape[:3]
    tile = (rows, cols)
    width = proj_weight.shape[1]
    weights = []
    for layer in range(LAYERS):
        qkv = fetch_columns(
            [head_columns(qkv_weight[layer], decay_weight[layer], g, width) for g in range(count)]
        )
        inner = expand_weight.shape[2] // count
        expand = fetch_columns(
            [expand_weight[layer][:, g * inner : (g + 1) * inner] for g in range(count)]
        )
        weights.append(
            (taps_all[layer], qkv, decay_bias[layer], proj_weight[layer], expand, shrink_weight[layer])
        )
    tokens = tokens_in.astype(FLOAT).reshape(items, rows * cols, D)
    stored = []
    for layer in range(LAYERS):
        tokens, saved = forward_layer(tokens, modulations[layer], weights[layer], layer, tile)
        stored.append(saved)
    delta = cotangent.astype(FLOAT).reshape(tokens.shape)
    bigs, smalls = [None] * LAYERS, [None] * LAYERS
    for layer in reversed(range(LAYERS)):
        delta, big, small = backward_layer(
            delta, stored[layer], modulations[layer], weights[layer], layer, tile
        )
        grad_shrink, grad_expand, grad_proj, grad_qkv = big
        bigs[layer] = (
            sum_rows_here(grad_shrink),
            sum_columns(grad_expand),
            sum_rows_here(grad_proj),
            sum_columns(grad_qkv),
        )
        smalls[layer] = tuple(
            None if part is None else lax.psum(part, GRID_AXES) for part in small
        )
    return tokens.astype(BFLOAT), delta.astype(BFLOAT), bigs, smalls


def per_device(
    tokens_in, timesteps, ada_weight, ada_bias, conv_taps, qkv_weight, decay_weight, decay_bias,
    proj_weight, expand_weight, shrink_weight, cotangent,
):
    count, place = lax.axis_size("batch"), lax.axis_index("batch")
    items, rows, cols = tokens_in.shape[:3]
    tile = (rows, cols)
    rows_here = ada_weight.shape[1]
    width = proj_weight.shape[1]
    heads = width // HD
    size = padded_width(width + 3 * heads)
    cond = jax.nn.silu(embed_steps(timesteps)).astype(BFLOAT)
    cond_slice = lax.dynamic_slice_in_dim(cond, place * rows_here, rows_here, 1)
    order = [0] if count != 2 else None
    if count == 2:
        cond_first = jnp.where(
            place == 0, cond_slice, jnp.concatenate([cond_slice[items:], cond_slice[:items]])
        )
    else:
        cond_first = cond_slice
    biases = gather_last(ada_bias).astype(FLOAT)
    taps_all = gather_last(conv_taps)
    fast = pipelined(width) and count * items == 4 and tile == (8, 8)
    hidden_units = shrink_weight.shape[1]
    if fast:
        moving = {}
        upper_sums = Scattered()

        def act(names, through):
            names = [names[at : at + 3] for at in range(0, len(names), 3)]
            steps = []
            for name in names + ["end"]:
                if name[0] == "t":
                    steps.append(moving[name[1:]])
                    continue
                through = tick(steps, through)
                steps = []
                one = moving.get(name[1:])
                if name[0] == "s":
                    through = one.start(through)
                elif name[0] == "k":
                    through = one.second(through)
                elif name == "gL1":
                    upper_sums.gather(through)
                elif name == "gL0":
                    Gathered([moving[name] for name in ("C1", "A0", "B0", "C0")]).gather()
                elif name[0] == "a":
                    through = upper_sums.add(one, through)
                elif name[0] == "r":
                    upper_sums.reduce()
            return through

        def step(layer, point, fresh, through):
            for name, one in fresh.items():
                moving[name if len(name) == 2 else name + str(layer)] = one
                if name in "ABC":
                    one.offload = True
            if "S" in fresh and not layer:
                moving["S0"] = SmallSum(
                    jnp.concatenate([moving["S0"].value, moving["S1"].value], axis=0)
                )
            return act(SCHEDULE.get((layer, point), ""), through)

        pair = Pair(
            dict(
                qkv=qkv_weight, decay=decay_weight, decay_bias=decay_bias, proj=proj_weight,
                expand=expand_weight, shrink=shrink_weight, cond=cond_first, ada=ada_weight,
                ada_bias=biases,
            ),
            taps_all,
            tile,
        )
        block_out, through = pair_forward_backward(pair, tokens_in, cotangent, step)
        shapes = [
            (LAYERS, hidden_units, D),
            (LAYERS, rows_here, expand_weight.shape[2]),
            (LAYERS, rows_here, 3 * D),
            (LAYERS, width, D),
        ]
        finished = None
        grad_ada = None
        smalls = [None] * LAYERS
        for names in TAIL:
            if names[0] == "f":
                kinds = names[1:-1]
                layer = int(names[-1])
                sums = [moving[kind + names[-1]] for kind in kinds]
                if kinds[-1] == "C":
                    kinds, sums = kinds + "C", sums + [moving["C1"]]
                made, through = Gathered.finish(
                    sums, kinds,
                    None if layer else finished, layer, shapes, through,
                )
                finished = (finished or {}) | made
            elif names[0] == "m":
                layer = int(names[2])
                flat = moving["S0"].keep[layer * SMALL_ROWS : (layer + 1) * SMALL_ROWS]
                smalls[layer] = list(split_smalls(flat, items, heads, width))
                mods = gather_items(smalls[layer][0])
                smalls[layer][0] = mods
                grad_ada, through = ada_call(cond_first, mods, grad_ada, layer, through)
            else:
                through = act(names, through)
        grad_tokens = through
    else:
        partial = jnp.stack(
            [
                jnp.dot(cond_first, ada_weight[layer], preferred_element_type=FLOAT)
                for layer in range(LAYERS)
            ],
            axis=1,
        )
        if count == 2:
            total = partial[:items] + swap(partial[items:])
        else:
            total = lax.psum_scatter(partial, "batch", scatter_dimension=0, tiled=True)
        modulations = [
            (total[:, layer] + biases[layer]).reshape(items, 6, D) for layer in range(LAYERS)
        ]
        block_out, grad_tokens, bigs, smalls = general_forward_backward(
            tokens_in, cotangent, modulations, taps_all, qkv_weight, decay_weight, decay_bias,
            proj_weight, expand_weight, shrink_weight,
        )
    block_out = block_out.reshape(tokens_in.shape)
    grad_tokens = grad_tokens.reshape(tokens_in.shape)
    delta_mods, taps_grads, bias_grads = (
        jnp.stack([smalls[layer][k] for layer in range(LAYERS)]) for k in (0, 1, 3)
    )
    if fast:
        every_mod = delta_mods.transpose(1, 0, 2)
    else:
        every_mod = gather_items(delta_mods.transpose(1, 0, 2, 3)).reshape(
            count * items, LAYERS, 6 * D
        )
    if count == 2:
        taps_every = taps_grads + swap(taps_grads)
    else:
        taps_every = lax.psum(taps_grads, "batch")
    grad_taps = lax.dynamic_slice_in_dim(taps_every, place * width, width, 2)
    if not fast:
        grad_ada = jnp.zeros((LAYERS, rows_here, 6 * D), FLOAT)
        for item in range(count * items):
            grad_ada += (
                cond_first[item].astype(FLOAT)[None, :, None] * every_mod[item][:, None, :]
            )
    bias_width = ada_bias.shape[1]
    grad_ada_bias = lax.dynamic_slice_in_dim(
        jnp.sum(every_mod, axis=0), place * bias_width, bias_width, 1
    )
    if fast:
        grad_shrink, grad_expand, grad_qkv, grad_proj = (finished[k] for k in range(4))
        grad_decay = jnp.stack([jnp.transpose(smalls[layer][2]) for layer in range(LAYERS)])
    else:
        stack = lambda k: jnp.stack([bigs[layer][k] for layer in range(LAYERS)])
        grad_shrink, grad_proj = stack(0), stack(2)
        expand_parts, qkv_parts = stack(1), stack(3)
        grad_expand = jnp.concatenate([expand_parts[:, g] for g in range(count)], 2).astype(FLOAT)
        grad_qkv = jnp.concatenate(
            [
                qkv_parts[:, g, :, j * size : j * size + width]
                for j in range(3)
                for g in range(count)
            ],
            axis=2,
        ).astype(FLOAT)
        grad_decay = jnp.concatenate(
            [qkv_parts[:, g, :, width : width + heads] for g in range(count)], axis=2
        ).astype(FLOAT)
    return (
        block_out,
        grad_tokens,
        grad_ada,
        grad_ada_bias,
        grad_taps,
        grad_qkv,
        grad_decay,
        bias_grads,
        grad_proj,
        grad_expand,
        grad_shrink,
    )


def solution(mesh):
    return jax.shard_map(
        per_device,
        mesh=mesh,
        in_specs=(
            P("batch", "row", "col", None),
            P(),
            P(None, "batch", None),
            P(None, "batch"),
            P(None, None, "batch"),
            P(None, "batch", None),
            P(None, "batch", None),
            P(None, "batch"),
            P(None, "batch", None),
            P(None, "batch", None),
            P(None, "batch", None),
            P("batch", "row", "col", None),
        ),
        out_specs=(
            P("batch", "row", "col", None),
            P("batch", "row", "col", None),
            P(None, "batch", None),
            P(None, "batch"),
            P(None, None, "batch"),
            P(None, "batch", None),
            P(None, "batch", None),
            P(None, "batch"),
            P(None, "batch", None),
            P(None, "batch", None),
            P(None, "batch", None),
        ),
        check_vma=False,
    )
```
